32 devices in a mesh: face: 8 (over y, x, core), band: 4 (over z).
Axes of the slice: x: 2, y: 2, z: 4, core: 2. Of those that a mesh axis runs over, the one named last changes fastest.
Arguments:
- coarse: bfloat16 [48, 128, 256], P('band', 'face'), may hold values from -6 to 6
- skip: bfloat16 [96, 256, 256], P('band', 'face'), may hold values from -6 to 6
- up_weight: bfloat16 [3, 3, 256, 256], replicated, may hold values from -0.25 to 0.25
- conv_weight: bfloat16 [3, 3, 256, 256], replicated, may hold values from -0.125 to 0.125
- cotangent: bfloat16 [96, 256, 256], P('band', 'face'), may hold values from -6 to 6
Outputs:
- decoded: bfloat16 [96, 256, 256], P('band', 'face')
- grad_coarse: bfloat16 [48, 128, 256], P('band', 'face')
- grad_up_weight: float32 [2304, 256], P('face', 'band')
- grad_conv_weight: float32 [2304, 256], P('face', 'band')
The draws below stay inside these ranges and needn't reach their ends.
All inputs are finite; a program needn't handle non-finite values.
Results may differ from the reference program's by a relative error of at most 0.0049.
Values may be sent and summed in bfloat16 or wider, within the bound.
No kernel may reach another device: no remote copies, remote signals or barrier semaphores. Data moves between devices by JAX's collectives and lax.ppermute only.
A program may use at most 128 MiB of HBM per device.

```python
import jax
import jax.numpy as jnp

C = 256
H = 48
W = 128


def shard_levels(stream_key, shape, pieces, low, top_value):
    gain, own = 1.0, jax.random.fold_in(stream_key, 6)
    for dim, shards_of in pieces:
        steps = jnp.exp(jax.random.uniform(jax.random.fold_in(own, dim), (shards_of,), jnp.float32, low / len(pieces), top_value / len(pieces)))
        gain = gain * jnp.repeat(steps, shape[dim] // shards_of).reshape([-1 if axis == dim else 1 for axis in range(len(shape))])
    return gain


def centred(rng, dims, spread, bound, split=(), dtype=jnp.bfloat16):
    level = shard_levels(rng, dims, split, -0.22, 0.18) if split else 1.0
    values = jax.random.normal(rng, dims, jnp.float32) * spread * level
    return jnp.minimum(jnp.maximum(values, -bound), bound).astype(dtype)


def setup_inputs(seed: int = 0) -> dict:
    keys = jax.random.split(jax.random.key(seed), 6)
    coarse = centred(keys[0], (H, W, C), 1.0, 6.0, ((0, 4), (1, 8)))
    skip = centred(keys[1], (2 * H, 2 * W, C), 1.0, 6.0, ((0, 4), (1, 8)))
    up_weight = centred(keys[2], (3, 3, C, C), (2 * C) ** -0.5, 0.25)
    conv_weight = centred(keys[3], (3, 3, C, C), (9 * C) ** -0.5, 0.125)
    cotangent = centred(keys[4], (2 * H, 2 * W, C), 1.0, 6.0, ((0, 4), (1, 8)))
    return dict(coarse=coarse, skip=skip, up_weight=up_weight, conv_weight=conv_weight, cotangent=cotangent)


forward_taps = ((1, 1), (0, 0), (1, 0))
backward_taps = ((1, 0), (0, 1), (1, 1))

def up_phases(extended, up_weight, n_rows, n_cols):
    channels = extended.shape[-1]
    totals = {}
    for row_tap in range(3):
        row_phase, row_off = forward_taps[row_tap]
        for col_tap in range(3):
            col_phase, col_off = forward_taps[col_tap]
            source = extended[row_off:row_off + n_rows, col_off:col_off + n_cols].reshape(-1, channels)
            term = jnp.dot(source, up_weight[row_tap, col_tap], preferred_element_type=jnp.float32)
            name = (row_phase, col_phase)
            totals[name] = totals[name] + term if name in totals else term
    per_row = []
    for row_phase in range(2):
        per_row.append(jnp.stack([totals[row_phase, col_phase].reshape(n_rows, n_cols, channels) for col_phase in range(2)], axis=2))
    return jnp.stack(per_row, axis=1)

def conv_forward(act_pad, conv_weight, n_rows, n_cols):
    channels = act_pad.shape[-1]
    total = jnp.zeros((n_rows * n_cols, channels), jnp.float32)
    for row_tap in range(3):
        for col_tap in range(3):
            source = act_pad[row_tap:row_tap + n_rows, col_tap:col_tap + n_cols].reshape(-1, channels)
            total = total + jnp.dot(source, conv_weight[row_tap, col_tap], preferred_element_type=jnp.float32)
    return total

def conv_backward(grad_pad, conv_weight, n_rows, n_cols):
    channels = grad_pad.shape[-1]
    total = jnp.zeros((n_rows * n_cols, channels), jnp.float32)
    for row_tap in range(3):
        for col_tap in range(3):
            source = grad_pad[2 - row_tap:2 - row_tap + n_rows, 2 - col_tap:2 - col_tap + n_cols].reshape(-1, channels)
            total = total + jnp.dot(source, conv_weight[row_tap, col_tap].T, preferred_element_type=jnp.float32)
    return total

def conv_wgrad(act_pad, grad_flat, n_rows, n_cols):
    channels = act_pad.shape[-1]
    blocks = []
    for row_tap in range(3):
        for col_tap in range(3):
            source = act_pad[row_tap:row_tap + n_rows, col_tap:col_tap + n_cols].reshape(-1, channels)
            blocks.append(jnp.dot(source.T, grad_flat, preferred_element_type=jnp.float32))
    return jnp.concatenate(blocks, axis=0)

def down_backward(grad_ext, coarse, up_weight, n_rows, n_cols):
    channels = coarse.shape[-1]
    coarse_flat = coarse.reshape(-1, channels)
    grad_in = jnp.zeros((n_rows * n_cols, channels), jnp.float32)
    blocks = []
    for row_tap in range(3):
        row_phase, row_start = backward_taps[row_tap]
        for col_tap in range(3):
            col_phase, col_start = backward_taps[col_tap]
            source = grad_ext[row_start:row_start + n_rows, row_phase, col_start:col_start + n_cols, col_phase].reshape(-1, channels)
            grad_in = grad_in + jnp.dot(source, up_weight[row_tap, col_tap].T, preferred_element_type=jnp.float32)
            blocks.append(jnp.dot(coarse_flat.T, source, preferred_element_type=jnp.float32))
    return (grad_in, jnp.concatenate(blocks, axis=0))

def wrap_pad(field):
    widened = jnp.concatenate([field[:, -1:], field, field[:, :1]], axis=1)
    return jnp.pad(widened, ((1, 1), (0, 0), (0, 0)))

def reference(coarse, skip, up_weight, conv_weight, cotangent):
    n_rows, n_cols, channels = coarse.shape
    extended = jnp.concatenate([coarse, coarse[:, :1]], axis=1)
    extended = jnp.pad(extended, ((0, 1), (0, 0), (0, 0)))
    upsampled = up_phases(extended, up_weight, n_rows, n_cols).reshape(2 * n_rows, 2 * n_cols, channels)
    preact = upsampled + skip.astype(jnp.float32)
    act = jax.nn.silu(preact).astype(jnp.bfloat16)
    act_pad = wrap_pad(act)
    decoded = conv_forward(act_pad, conv_weight, 2 * n_rows, 2 * n_cols)
    decoded = decoded.reshape(2 * n_rows, 2 * n_cols, channels).astype(jnp.bfloat16)
    grad_pad = wrap_pad(cotangent)
    grad_act = conv_backward(grad_pad, conv_weight, 2 * n_rows, 2 * n_cols).reshape(2 * n_rows, 2 * n_cols, channels)
    sigma = jax.nn.sigmoid(preact)
    grad_pre = (grad_act * sigma * (1.0 + preact * (1.0 - sigma))).astype(jnp.bfloat16)
    phased = grad_pre.reshape(n_rows, 2, n_cols, 2, channels)
    widened_grad = jnp.concatenate([phased[:, :, -1:], phased], axis=2)
    grad_ext = jnp.pad(widened_grad, ((1, 0), (0, 0), (0, 0), (0, 0), (0, 0)))
    grad_in, grad_up = down_backward(grad_ext, coarse, up_weight, n_rows, n_cols)
    grad_conv = conv_wgrad(act_pad, cotangent.reshape(-1, channels), 2 * n_rows, 2 * n_cols)
    grad_coarse = grad_in.reshape(n_rows, n_cols, channels).astype(jnp.bfloat16)
    return (decoded, grad_coarse, grad_up, grad_conv)
```

```python
import functools

import jax
import jax.numpy as jnp
from jax import lax
from jax.experimental import pallas as pl
from jax.experimental.pallas import tpu as pltpu
from jax.sharding import PartitionSpec as P

f32, bf16 = jnp.float32, jnp.bfloat16
forward_taps = ((1, 1), (0, 0), (1, 0))
backward_taps = ((1, 0), (0, 1), (1, 1))
MARGIN = 8
LANES = 128


def sds(shape, dtype):
    return jax.ShapeDtypeStruct(shape, dtype)


def kernel_call(body, outs, scratch, flops, *args):
    vmem = pl.BlockSpec(memory_space=pltpu.VMEM)
    smem = pl.BlockSpec(memory_space=pltpu.SMEM)
    moved = sum(a.size * a.dtype.itemsize for a in args)
    moved += sum(a.size * a.dtype.itemsize for a in outs)
    return pl.pallas_call(
        body,
        out_shape=tuple(outs),
        in_specs=[smem if a.dtype == jnp.int32 else vmem for a in args],
        out_specs=tuple(vmem for _ in outs),
        scratch_shapes=scratch,
        compiler_params=pltpu.CompilerParams(vmem_limit_bytes=44 * 2**20),
        cost_estimate=pl.CostEstimate(flops=flops, bytes_accessed=moved, transcendentals=0),
    )(*args)


def dot(a, b):
    return jnp.dot(a, b, preferred_element_type=f32)


def dot_nt(a, b):
    return lax.dot_general(a, b, (((1,), (1,)), ((), ())), preferred_element_type=f32)


def pairs(count, wrap):
    first = [(i, i ^ 1) for i in range(count)]
    second = []
    for i in range(count):
        j = i + 1 if i % 2 else i - 1
        if wrap or 0 <= j < count:
            second.append((i, j % count))
    return first, second


def exchange(to_before, to_after, axis, wrap):
    first, second = pairs(lax.axis_size(axis), wrap)
    even = lax.axis_index(axis) % 2 == 0
    to_first = jnp.where(even, to_after, to_before)
    to_second = jnp.where(even, to_before, to_after)
    got_first = lax.ppermute(to_first, axis, first)
    got_second = lax.ppermute(to_second, axis, second)
    before = jnp.where(even, got_second, got_first)
    after = jnp.where(even, got_first, got_second)
    return before, after


def rows_of(parts, total):
    stacked = jnp.concatenate(parts, axis=0)
    return jnp.pad(stacked, ((0, total - stacked.shape[0]), (0, 0)))


def up16(n):
    return (n + 15) // 16 * 16


def halves(n_rows, channels):
    return pltpu.VMEM((channels // LANES, n_rows, LANES), f32)


def put(ref, start, value, step=1):
    for part in range(ref.shape[0]):
        rows = pl.ds(start, value.shape[0], stride=step if step > 1 else None)
        ref[part, rows, :] = value[:, part * LANES : (part + 1) * LANES]


def get(ref, start, count, step=1):
    rows = pl.ds(start, count, stride=step if step > 1 else None)
    return jnp.concatenate([ref[part, rows, :] for part in range(ref.shape[0])], axis=1)


def put_edges(padded, stride, width, n_rows, left, right, upper, lower, corner):
    last = (n_rows + 1) * stride
    put(padded, stride + MARGIN - 1, left, stride)
    put(padded, stride + MARGIN + width, right, stride)
    put(padded, MARGIN - 1, upper[corner : corner + 1])
    put(padded, MARGIN + width, upper[corner + 1 : corner + 2])
    put(padded, last + MARGIN - 1, lower[corner : corner + 1])
    put(padded, last + MARGIN + width, lower[corner + 1 : corner + 2])


def three_shifts(padded, stride, width, n_rows, shifted):
    for row in range(n_rows):
        for shift in range(3):
            start = row * stride + MARGIN - 1 + shift
            shifted[shift, row] = get(padded, start, width).astype(bf16)


def split_by_core(place, partial, keep, send, groups, block):
    core = place[0]
    for group in range(groups):
        mine = pl.multiple_of((2 * group + core) * block, 16)
        theirs = pl.multiple_of((2 * group + 1 - core) * block, 16)
        keep[group] = partial[pl.ds(mine, block), :]
        send[group] = partial[pl.ds(theirs, block), :].astype(bf16)


def act_kernel(
    place, coarse, skip, cot, left, right, upper, lower, up_w,
    shifted, near, act, slope, keep, send, padded, pre, partial,
):
    n_rows, n_cols, channels = coarse.shape
    fine_rows, fine_cols, _ = skip.shape
    stride = fine_cols + 2 * MARGIN
    left_all, right_all = left[...].astype(f32), right[...].astype(f32)
    upper_all, lower_all = upper[...].astype(f32), lower[...].astype(f32)
    corner = fine_cols + n_cols
    for row in range(n_rows):
        near[0, row] = coarse[row]
        put(padded, row * stride, coarse[row].astype(f32))
    near[0, n_rows] = lower[fine_cols : fine_cols + n_cols]
    put(padded, n_rows * stride, lower_all[fine_cols : fine_cols + n_cols])
    put(padded, n_cols, right_all[fine_rows : fine_rows + n_rows], stride)
    put(padded, n_rows * stride + n_cols, lower_all[corner + 2 : corner + 3])
    for row in range(n_rows + 1):
        near[1, row] = get(padded, row * stride + 1, n_cols).astype(bf16)
    for row in range(n_rows + 1, near.shape[1]):
        for side in range(2):
            near[side, row] = jnp.zeros((n_cols, channels), bf16)
    sums = {}
    for k in range(3):
        row_phase, row_off = forward_taps[k]
        for l in range(3):
            col_phase, col_off = forward_taps[l]
            source = near[col_off, pl.ds(row_off, n_rows)].reshape(n_rows * n_cols, channels)
            term = dot(source, up_w[k, l])
            name = (row_phase, col_phase)
            sums[name] = sums[name] + term if name in sums else term
    for (row_phase, col_phase), total in sums.items():
        for row in range(n_rows):
            start = (2 * row + row_phase) * fine_cols + col_phase
            put(pre, start, total[row * n_cols : (row + 1) * n_cols], 2)
    preact = get(pre, 0, fine_rows * fine_cols) + skip[...].reshape(fine_rows * fine_cols, channels).astype(f32)
    sigma = jax.nn.sigmoid(preact)
    value = preact * sigma
    slope[...] = sigma + value * (1.0 - sigma)
    act_flat = value.astype(bf16)
    act[...] = act_flat.reshape(act.shape)
    put(padded, MARGIN, upper_all[:fine_cols])
    put(padded, (fine_rows + 1) * stride + MARGIN, lower_all[:fine_cols])
    for row in range(fine_rows):
        put(padded, (row + 1) * stride + MARGIN, cot[row].astype(f32))
    put_edges(
        padded, stride, fine_cols, fine_rows, left_all[:fine_rows], right_all[:fine_rows],
        upper_all, lower_all, corner,
    )
    three_shifts(padded, stride, fine_cols, fine_rows + 2, shifted)
    act_t = act_flat.T
    for k in range(3):
        for l in range(3):
            source = shifted[2 - l, pl.ds(2 - k, fine_rows)].reshape(-1, channels)
            partial[pl.ds((3 * k + l) * channels, channels), :] = dot(act_t, source)
    split_by_core(place, partial, keep, send, keep.shape[0], keep.shape[1])


def grad_kernel(place, shifted, slope, near, conv_w, grad, phases, keep, send, fine, partial):
    fine_rows, fine_cols = shifted.shape[1] - 2, shifted.shape[2]
    channels = shifted.shape[3]
    n_rows, n_cols = fine_rows // 2, fine_cols // 2
    total = jnp.zeros((fine_rows * fine_cols, channels), f32)
    for k in range(3):
        for l in range(3):
            source = shifted[2 - l, pl.ds(2 - k, fine_rows)].reshape(-1, channels)
            total = total + dot_nt(source, conv_w[k, l])
    rounded = (total * slope[...]).astype(bf16)
    grad[...] = rounded.reshape(grad.shape)
    put(fine, 0, rounded.astype(f32))
    for row_phase in range(2):
        for col_phase in range(2):
            for row in range(n_rows):
                start = (2 * row + row_phase) * fine_cols + col_phase
                phases[row_phase, col_phase, row] = get(fine, start, n_cols, 2).astype(bf16)
            for row in range(n_rows, phases.shape[2]):
                phases[row_phase, col_phase, row] = jnp.zeros((n_cols, channels), bf16)
    whole = phases.shape[2]
    turned = {}
    for row_off in range(2):
        for col_off in range(2):
            if row_off:
                cells = near[col_off, pl.ds(1, whole)]
            else:
                cells = near[col_off, pl.ds(0, whole)]
            turned[row_off, col_off] = cells.reshape(whole * n_cols, channels).T
    for k in range(3):
        row_phase, row_off = forward_taps[k]
        for l in range(3):
            col_phase, col_off = forward_taps[l]
            source = phases[row_phase, col_phase].reshape(whole * n_cols, channels)
            partial[pl.ds((3 * k + l) * channels, channels), :] = dot(
                turned[row_off, col_off], source
            )
    split_by_core(place, partial, keep, send, keep.shape[0], keep.shape[1])


def out_kernel(
    act, phases, left, right, upper, lower, conv_w, up_w, decoded, coarse_out,
    padded, shifted, moved,
):
    fine_rows, fine_cols, channels = act.shape
    n_rows, n_cols = fine_rows // 2, fine_cols // 2
    stride = fine_cols + 2 * MARGIN
    left_all, right_all = left[...].astype(f32), right[...].astype(f32)
    upper_all, lower_all = upper[...].astype(f32), lower[...].astype(f32)
    corner = 2 * fine_cols
    put(padded, MARGIN, upper_all[:fine_cols])
    put(padded, (fine_rows + 1) * stride + MARGIN, lower_all[:fine_cols])
    for row in range(fine_rows):
        put(padded, (row + 1) * stride + MARGIN, act[row].astype(f32))
    put_edges(
        padded, stride, fine_cols, fine_rows, left_all[:fine_rows], right_all[:fine_rows],
        upper_all, lower_all, corner,
    )
    three_shifts(padded, stride, fine_cols, fine_rows + 2, shifted)
    total = jnp.zeros((fine_rows * fine_cols, channels), f32)
    for k in range(3):
        for l in range(3):
            source = shifted[l, pl.ds(k, fine_rows)].reshape(-1, channels)
            total = total + dot(source, conv_w[k, l])
    decoded[...] = total.astype(bf16).reshape(decoded.shape)
    put(padded, 0, upper_all[fine_cols : 2 * fine_cols])
    moved[0, 0] = get(padded, 0, n_cols, 2).astype(bf16)
    moved[1, 0] = get(padded, 1, n_cols, 2).astype(bf16)
    for phase in range(2):
        for row in range(n_rows):
            moved[phase, 1 + row] = phases[1, phase, row]
    for row_phase in range(2):
        for row in range(n_rows):
            put(padded, (row + 1) * stride + MARGIN, phases[row_phase, 1, row].astype(f32))
        spare = (n_rows + 1) * stride
        put(padded, spare, left_all[fine_rows : 2 * fine_rows])
        put(padded, stride + MARGIN - 1, get(padded, spare + row_phase, n_rows, 2), stride)
        if row_phase:
            put(padded, MARGIN, moved[1, 0].astype(f32))
            put(padded, MARGIN - 1, upper_all[corner + 2 : corner + 3])
            for row in range(n_rows + 1):
                moved[2, row] = get(padded, row * stride + MARGIN - 1, n_cols).astype(bf16)
        else:
            for row in range(n_rows):
                moved[3, row] = get(padded, (row + 1) * stride + MARGIN - 1, n_cols).astype(bf16)
    total = jnp.zeros((n_rows * n_cols, channels), f32)
    for k in range(3):
        for l in range(3):
            if k == 1:
                if l == 0:
                    source = moved[3, pl.ds(0, n_rows)]
                else:
                    source = phases[0, l - 1, pl.ds(0, n_rows)]
            else:
                source = moved[(2, 0, 1)[l], pl.ds(k // 2, n_rows)]
            total = total + dot_nt(source.reshape(n_rows * n_cols, channels), up_w[k, l])
    coarse_out[...] = total.astype(bf16).reshape(coarse_out.shape)


def sum_kernel(place, keep, got, own, *messages):
    chip = place[1]
    own[...] = keep[chip] + got[chip].astype(f32)
    for k, message in enumerate(messages):
        other = chip ^ (k + 1)
        message[...] = (keep[other] + got[other].astype(f32)).astype(bf16)


def packing(rows, cols):
    side = max(1, 128 // cols)
    return side if rows % (16 * side) == 0 else 1


def plane_kernel(place, own, *refs):
    n_bands, peers = refs[-1].shape[0], refs[: -(refs[-1].shape[0] + 1)]
    outs, cut = refs[len(peers) : -1], refs[-1]
    total = own[...]
    for peer in peers:
        total = total + peer[...].astype(f32)
    cols = total.shape[1] // n_bands
    side = packing(total.shape[0], cols)
    rows = total.shape[0] // side
    for band in range(n_bands):
        for part in range(side):
            cut[band, :, part * cols : (part + 1) * cols] = total[
                part * rows : (part + 1) * rows, band * cols : (band + 1) * cols
            ]
    band = place[2]
    outs[0][...] = cut[band]
    for k in range(1, n_bands):
        outs[k][...] = cut[band ^ k].astype(bf16)


def last_kernel(own, *refs):
    peers, out = refs[:-1], refs[-1]
    total = own[...]
    for peer in peers:
        total = total + peer[...].astype(f32)
    rows, cols = total.shape[0], out.shape[1]
    for part in range(out.shape[0] // rows):
        out[part * rows : (part + 1) * rows, :] = total[:, part * cols : (part + 1) * cols]


def xor_pairs(count, bits):
    return [(i, i ^ bits) for i in range(count)]


def reduce_partial(place, keep, send):
    faces, bands = lax.axis_size("face"), lax.axis_size("band")
    groups, block, channels = keep.shape
    got = lax.ppermute(send, "face", xor_pairs(faces, 1))
    shape = (block, channels)
    own, *messages = kernel_call(
        sum_kernel, [sds(shape, f32)] + [sds(shape, bf16)] * (groups - 1), [], 0, place, keep, got
    )
    order = sorted(range(1, groups), key=lambda k: -bin(k).count("1"))
    got = [lax.ppermute(messages[k - 1], "face", xor_pairs(faces, 2 * k)) for k in order]
    cols = channels // bands
    side = packing(block, cols)
    shape = (block // side, cols * side)
    own, *messages = kernel_call(
        plane_kernel, [sds(shape, f32)] + [sds(shape, bf16)] * (bands - 1),
        [pltpu.VMEM((bands,) + shape, f32)], 0, place, own, *got,
    )
    order = sorted(range(1, bands), key=lambda k: -k)
    got = [lax.ppermute(messages[k - 1], "band", xor_pairs(bands, k)) for k in order]
    return kernel_call(last_kernel, [sds((block, cols), f32)], [], 0, own, *got)[0]


def local(coarse, skip, up_weight, conv_weight, cotangent):
    n_rows, n_cols, channels = coarse.shape
    fine_rows, fine_cols, _ = skip.shape
    faces = lax.axis_size("face")
    face, band = lax.axis_index("face"), lax.axis_index("band")
    place = jnp.stack([face % 2, face // 2, band]).astype(jnp.int32)
    groups, block = faces // 2, 9 * channels // faces

    size = up16(fine_rows + n_rows)
    left, right = exchange(
        rows_of([cotangent[:, 0], coarse[:, 0]], size),
        rows_of([cotangent[:, -1], coarse[:, -1]], size),
        "face", True,
    )
    size = up16(fine_cols + n_cols + 3)
    upper, lower = exchange(
        rows_of([cotangent[0], coarse[0], left[:1], right[:1], right[fine_rows : fine_rows + 1]], size),
        rows_of([cotangent[-1], coarse[-1], left[fine_rows - 1 : fine_rows], right[fine_rows - 1 : fine_rows]], size),
        "band", False,
    )

    fine_flat = (fine_rows * fine_cols, channels)
    cells = n_rows * n_cols
    stride = fine_cols + 2 * MARGIN
    padded = halves((fine_rows + 2) * stride, channels)
    flat = halves(fine_rows * fine_cols, channels)
    shift_shape = (3, fine_rows + 2, fine_cols, channels)
    whole = -(-cells // 256) * 256 // n_cols
    one_tap = 2 * cells * channels * channels
    partials = [sds((groups, block, channels), f32), sds((groups, block, channels), bf16)]
    partial = pltpu.VMEM((9 * channels, channels), f32)
    shifted, near, act, slope, keep_conv, send_conv = kernel_call(
        act_kernel,
        [
            sds(shift_shape, bf16), sds((2, whole + 1, n_cols, channels), bf16),
            sds(skip.shape, bf16), sds(fine_flat, f32), *partials,
        ],
        [padded, flat, partial],
        45 * one_tap, place, coarse, skip, cotangent, left, right, upper, lower, up_weight,
    )
    grad, phases, keep_up, send_up = kernel_call(
        grad_kernel,
        [sds(skip.shape, bf16), sds((2, 2, whole, n_cols, channels), bf16), *partials],
        [flat, partial],
        45 * one_tap, place, shifted, slope, near, conv_weight,
    )

    grad_conv = reduce_partial(place, keep_conv, send_conv)
    grad_up = reduce_partial(place, keep_up, send_up)

    size = up16(2 * fine_rows)
    left, right = exchange(
        rows_of([act[:, 0]], size), rows_of([act[:, -1], grad[:, -1]], size), "face", True
    )
    size = up16(2 * fine_cols + 3)
    blank = jnp.zeros((fine_cols, channels), bf16)
    upper, lower = exchange(
        rows_of([act[0], blank, left[:1], right[:1]], size),
        rows_of([act[-1], grad[-1], left[fine_rows - 1 : fine_rows], right[fine_rows - 1 : fine_rows], left[2 * fine_rows - 1 : 2 * fine_rows]], size),
        "band", False,
    )
    decoded, grad_coarse = kernel_call(
        out_kernel,
        [sds(skip.shape, bf16), sds(coarse.shape, bf16)],
        [padded, pltpu.VMEM(shift_shape, bf16), pltpu.VMEM((4, n_rows + 1, n_cols, channels), bf16)],
        45 * one_tap, act, phases, left, right, upper, lower, conv_weight, up_weight,
    )
    return (decoded, grad_coarse, grad_up, grad_conv)


def solution(mesh):
    return jax.shard_map(
        local,
        mesh=mesh,
        in_specs=(
            P("band", "face", None),
            P("band", "face", None),
            P(),
            P(),
            P("band", "face", None),
        ),
        out_specs=(
            P("band", "face", None),
            P("band", "face", None),
            P("face", "band"),
            P("face", "band"),
        ),
        check_vma=False,
    )
```

```python
import jax
import jax.numpy as jnp
from jax import lax
from jax.experimental import pallas as pl
from jax.experimental.pallas import tpu as pltpu
from jax.sharding import PartitionSpec as P

f32, bf16 = jnp.float32, jnp.bfloat16
forward_taps = ((1, 1), (0, 0), (1, 0))
backward_taps = ((1, 0), (0, 1), (1, 1))
MARGIN = 8
LANES = 128


def sds(shape, dtype):
    return jax.ShapeDtypeStruct(shape, dtype)


def kernel_call(body, outs, scratch, flops, *args, far=()):
    vmem = pl.BlockSpec(memory_space=pltpu.VMEM)
    smem = pl.BlockSpec(memory_space=pltpu.SMEM)
    anywhere = pl.BlockSpec(memory_space=pl.ANY)
    moved = sum(a.size * a.dtype.itemsize for a in args)
    moved += sum(a.size * a.dtype.itemsize for a in outs)
    return pl.pallas_call(
        body,
        out_shape=tuple(outs),
        in_specs=[
            anywhere if i in far else smem if a.dtype == jnp.int32 else vmem
            for i, a in enumerate(args)
        ],
        out_specs=tuple(vmem for _ in outs),
        scratch_shapes=scratch,
        compiler_params=pltpu.CompilerParams(vmem_limit_bytes=28 * 2**20),
        cost_estimate=pl.CostEstimate(flops=flops, bytes_accessed=moved, transcendentals=0),
    )(*args)


def dot(a, b):
    return jnp.dot(a, b, preferred_element_type=f32)


def dot_nt(a, b):
    return lax.dot_general(a, b, (((1,), (1,)), ((), ())), preferred_element_type=f32)


def pairs(count, wrap):
    first = [(i, i ^ 1) for i in range(count)]
    second = []
    for i in range(count):
        j = i + 1 if i % 2 else i - 1
        if wrap or 0 <= j < count:
            second.append((i, j % count))
    return first, second


def up16(n):
    return (n + 15) // 16 * 16


def halves(n_rows, channels):
    return pltpu.VMEM((channels // LANES, n_rows, LANES), f32)


def put(ref, start, value, step=1):
    for part in range(ref.shape[0]):
        rows = pl.ds(start, value.shape[0], stride=step if step > 1 else None)
        ref[part, rows, :] = value[:, part * LANES : (part + 1) * LANES]


def get(ref, start, count, step=1):
    rows = pl.ds(start, count, stride=step if step > 1 else None)
    return jnp.concatenate([ref[part, rows, :] for part in range(ref.shape[0])], axis=1)


def fill(ref, start, value):
    ref[start : start + value.shape[0], :] = value


def split_by_core(place, partial, keep, send):
    groups, block, _ = keep.shape
    for group in range(groups):
        mine = pl.multiple_of((2 * group + place[0]) * block, 16)
        theirs = pl.multiple_of((2 * group + 1 - place[0]) * block, 16)
        keep[group] = partial[pl.ds(mine, block), :]
        send[group] = partial[pl.ds(theirs, block), :].astype(bf16)


class Layout:
    def __init__(self, n_rows, n_cols):
        rows, cols = 2 * n_rows, 2 * n_cols
        self.cot, self.cot_2, self.skip, self.coarse = 0, rows, 2 * rows, 3 * rows
        self.face_size = up16(3 * rows + n_rows)
        self.row_cot, self.row_cot_2, self.row_skip = 0, cols, 2 * cols
        self.row_coarse, self.corner = 3 * cols, 3 * cols + n_cols
        self.band_size = self.corner + 16
        ring = (cols + 2 + 7) // 8 * 8
        self.top, self.bottom, self.left, self.right = 0, ring, 2 * ring, 2 * ring + rows
        self.ring_size = up16(2 * ring + 2 * rows)
        self.grad_left, self.grad_size = ring, up16(ring + rows)


COT, COT_2, SKIP, COARSE = (0, 1, 2), (3, 4, 5), (6, None, 7), (8, None, 9)


def face_message(place, coarse, skip, cot, first, second, cot_v, skip_v, coarse_v, flat, before, after, sems):
    rows, cols, _ = cot.shape
    n_rows, n_cols, _ = coarse.shape
    at = Layout(n_rows, n_cols)
    copies = [
        pltpu.make_async_copy(source, target, sems.at[i])
        for i, (source, target) in enumerate(((cot, cot_v), (skip, skip_v), (coarse, coarse_v)))
    ]
    for copy in copies:
        copy.start()
    before[...] = jnp.zeros_like(before)
    after[...] = jnp.zeros_like(after)
    copies[0].wait()
    put(flat, 0, cot_v[...].reshape(rows * cols, -1).astype(f32))
    fill(before, at.cot, get(flat, 0, rows, cols))
    fill(after, at.cot, get(flat, cols - 1, rows, cols))
    fill(after, at.cot_2, get(flat, cols - 2, rows, cols))
    copies[1].wait()
    put(flat, 0, skip_v[...].reshape(rows * cols, -1).astype(f32))
    fill(before, at.skip, get(flat, 0, rows, cols))
    fill(after, at.skip, get(flat, cols - 1, rows, cols))
    copies[2].wait()
    put(flat, 0, coarse_v[...].reshape(n_rows * n_cols, -1).astype(f32))
    fill(before, at.coarse, get(flat, 0, n_rows, n_cols))
    fill(after, at.coarse, get(flat, n_cols - 1, n_rows, n_cols))
    even = place[0] == 0
    first[...] = jnp.where(even, after[...], before[...]).astype(bf16)
    second[...] = jnp.where(even, before[...], after[...]).astype(bf16)


def band_message(place, coarse, skip, cot, got_first, got_second, first, second, left, right, before, after):
    rows, cols, channels = cot.shape
    n_rows, n_cols, _ = coarse.shape
    at = Layout(n_rows, n_cols)
    even = place[0] == 0
    one, two = got_first[...].astype(f32), got_second[...].astype(f32)
    left[...] = jnp.where(even, two, one)
    right[...] = jnp.where(even, one, two)
    for message, row, row_2, cell in ((before, 0, None, 0), (after, rows - 1, rows - 2, n_rows - 1)):
        fill(message, at.row_cot, cot[row].astype(f32))
        if row_2 is None:
            fill(message, at.row_cot_2, jnp.zeros((cols, channels), f32))
        else:
            fill(message, at.row_cot_2, cot[row_2].astype(f32))
        fill(message, at.row_skip, skip[row].astype(f32))
        fill(message, at.row_coarse, coarse[cell].astype(f32))
        fill(message, at.corner, jnp.zeros((16, channels), f32))
        corners = [
            (COT[0], left, at.cot + row), (COT[1], left, at.cot_2 + row), (COT[2], right, at.cot + row),
            (SKIP[0], left, at.skip + row), (SKIP[2], right, at.skip + row),
            (COARSE[0], left, at.coarse + cell), (COARSE[2], right, at.coarse + cell),
        ]
        if row_2 is not None:
            corners += [
                (COT_2[0], left, at.cot + row_2), (COT_2[1], left, at.cot_2 + row_2),
                (COT_2[2], right, at.cot + row_2),
            ]
        for corner, side, source in corners:
            fill(message, at.corner + corner, side[source : source + 1, :])
    even = lax.rem(place[2], 2) == 0
    first[...] = jnp.where(even, after[...], before[...]).astype(bf16)
    second[...] = jnp.where(even, before[...], after[...]).astype(bf16)


def act_kernel(
    place, coarse, skip, cot, left, right, got_first, got_second, up_w, conv_w,
    shifted, near, act, slope, keep, send, upper, lower, up_v, conv_v,
    padded, pre, partial, sems,
):
    n_rows, n_cols, channels = coarse.shape
    rows, cols, _ = skip.shape
    at = Layout(n_rows, n_cols)
    stride = cols + 2 * MARGIN
    copies = [
        pltpu.make_async_copy(up_w, up_v, sems.at[0]),
        pltpu.make_async_copy(conv_w, conv_v, sems.at[1]),
    ]
    for copy in copies:
        copy.start()
    even = lax.rem(place[2], 2) == 0
    one, two = got_first[...].astype(f32), got_second[...].astype(f32)
    upper[...] = jnp.where(even, two, one)
    lower[...] = jnp.where(even, one, two)
    for row in range(n_rows):
        near[0, row] = coarse[row]
        put(padded, row * stride, coarse[row].astype(f32))
    below = lower[at.row_coarse : at.row_coarse + n_cols, :]
    near[0, n_rows] = below.astype(bf16)
    put(padded, n_rows * stride, below)
    put(padded, n_cols, right[at.coarse : at.coarse + n_rows, :], stride)
    corner = at.corner + COARSE[2]
    put(padded, n_rows * stride + n_cols, lower[corner : corner + 1, :])
    for row in range(n_rows + 1):
        near[1, row] = get(padded, row * stride + 1, n_cols).astype(bf16)
    for row in range(n_rows + 1, near.shape[1]):
        for side in range(2):
            near[side, row] = jnp.zeros((n_cols, channels), bf16)
    put(padded, MARGIN, upper[at.row_cot : at.row_cot + cols, :])
    put(padded, (rows + 1) * stride + MARGIN, lower[at.row_cot : at.row_cot + cols, :])
    for row in range(rows):
        put(padded, (row + 1) * stride + MARGIN, cot[row].astype(f32))
    put(padded, stride + MARGIN - 1, left[at.cot : at.cot + rows, :], stride)
    put(padded, stride + MARGIN + cols, right[at.cot : at.cot + rows, :], stride)
    for row, message in ((0, upper), (rows + 1, lower)):
        for col, corner in ((-1, at.corner + COT[0]), (cols, at.corner + COT[2])):
            put(padded, row * stride + MARGIN + col, message[corner : corner + 1, :])
    for row in range(rows + 2):
        for shift in (0, 2):
            start = row * stride + MARGIN - 1 + shift
            shifted[shift, row] = get(padded, start, cols).astype(bf16)
    shifted[1, 0] = upper[at.row_cot : at.row_cot + cols, :].astype(bf16)
    shifted[1, rows + 1] = lower[at.row_cot : at.row_cot + cols, :].astype(bf16)
    for row in range(rows):
        shifted[1, row + 1] = cot[row]
    copies[0].wait()
    sums = {}
    for k in range(3):
        row_phase, row_off = forward_taps[k]
        for l in range(3):
            col_phase, col_off = forward_taps[l]
            source = near[col_off, pl.ds(row_off, n_rows)].reshape(n_rows * n_cols, channels)
            term = dot(source, up_v[k, l])
            name = (row_phase, col_phase)
            sums[name] = sums[name] + term if name in sums else term
    for (row_phase, col_phase), total in sums.items():
        for row in range(n_rows):
            start = (2 * row + row_phase) * cols + col_phase
            put(pre, start, total[row * n_cols : (row + 1) * n_cols], 2)
    preact = get(pre, 0, rows * cols) + skip[...].reshape(rows * cols, channels).astype(f32)
    sigma = jax.nn.sigmoid(preact)
    value = preact * sigma
    slope[...] = sigma + value * (1.0 - sigma)
    act_flat = value.astype(bf16)
    act[...] = act_flat.reshape(act.shape)
    act_t = act_flat.T
    for k in range(3):
        for l in range(3):
            source = shifted[2 - l, pl.ds(2 - k, rows)].reshape(-1, channels)
            partial[pl.ds((3 * k + l) * channels, channels), :] = dot(act_t, source)
    split_by_core(place, partial, keep, send)
    copies[1].wait()


def grad_kernel(place, shifted, slope, near, conv_w, phases, keep, send, fine, partial):
    rows, cols = shifted.shape[1] - 2, shifted.shape[2]
    channels = shifted.shape[3]
    n_rows, n_cols = rows // 2, cols // 2
    total = jnp.zeros((rows * cols, channels), f32)
    for k in range(3):
        for l in range(3):
            source = shifted[2 - l, pl.ds(2 - k, rows)].reshape(-1, channels)
            total = total + dot_nt(source, conv_w[k, l])
    put(fine, 0, (total * slope[...]).astype(bf16).astype(f32))
    whole = phases.shape[2]
    for row_phase in range(2):
        for col_phase in range(2):
            for row in range(n_rows):
                start = (2 * row + row_phase) * cols + col_phase
                phases[row_phase, col_phase, row] = get(fine, start, n_cols, 2).astype(bf16)
            for row in range(n_rows, whole):
                phases[row_phase, col_phase, row] = jnp.zeros((n_cols, channels), bf16)
    turned = {}
    for row_off in range(2):
        for col_off in range(2):
            cells = near[col_off, pl.ds(row_off, whole)]
            turned[row_off, col_off] = cells.reshape(whole * n_cols, channels).T
    for k in range(3):
        row_phase, row_off = forward_taps[k]
        for l in range(3):
            col_phase, col_off = forward_taps[l]
            source = phases[row_phase, col_phase].reshape(whole * n_cols, channels)
            partial[pl.ds((3 * k + l) * channels, channels), :] = dot(
                turned[row_off, col_off], source
            )
    split_by_core(place, partial, keep, send)


def out_kernel(
    place, coarse, cot, act, phases, left, right, upper, lower, conv_w, up_w,
    decoded, coarse_out, padded, shifted, moved, ring, wide,
):
    rows, cols, channels = act.shape
    n_rows, n_cols = rows // 2, cols // 2
    at = Layout(n_rows, n_cols)
    stride, step = cols + 2 * MARGIN, n_cols + 2 * MARGIN
    has_upper, has_lower = place[2] > 0, place[2] < place[3] - 1

    def corner(message, which):
        return message[at.corner + which : at.corner + which + 1, :]

    def cell(i, j):
        return (i + 1) * step + MARGIN + j

    for row in range(n_rows):
        put(wide, cell(row, 0), coarse[row].astype(f32))
    for row, message in ((-1, upper), (n_rows, lower)):
        put(wide, cell(row, 0), message[at.row_coarse : at.row_coarse + n_cols, :])
        put(wide, cell(row, -1), corner(message, COARSE[0]))
        put(wide, cell(row, n_cols), corner(message, COARSE[2]))
    put(wide, cell(0, -1), left[at.coarse : at.coarse + n_rows, :], step)
    put(wide, cell(0, n_cols), right[at.coarse : at.coarse + n_rows, :], step)
    total = jnp.zeros((at.ring_size, channels), f32)
    for k in range(3):
        for l in range(3):
            put(ring, 0, jnp.zeros((at.ring_size, channels), f32))
            for base, i in ((at.bottom, n_rows),) if k == 1 else ((at.top, k // 2 * -1),):
                start = cell(i, -1 if l == 2 else 0)
                put(ring, base + (l == 1), get(wide, start, n_cols + 1), 2)
            base, j = (at.right, n_cols) if l == 1 else (at.left, -(l // 2))
            start = cell(1 if k == 0 else 0, j)
            put(ring, base + (k != 1), get(wide, start, n_rows, step), 2)
            total = total + dot(get(ring, 0, at.ring_size).astype(bf16), up_w[k, l])
    put(ring, 0, jnp.zeros((at.ring_size, channels), f32))
    for base, message in ((at.top, upper), (at.bottom, lower)):
        put(ring, base + 1, message[at.row_skip : at.row_skip + cols, :])
        put(ring, base, corner(message, SKIP[0]))
        put(ring, base + cols + 1, corner(message, SKIP[2]))
    put(ring, at.left, left[at.skip : at.skip + rows, :])
    put(ring, at.right, right[at.skip : at.skip + rows, :])
    preact = total + get(ring, 0, at.ring_size)
    sigma = jax.nn.sigmoid(preact)
    value = preact * sigma
    slope = sigma + value * (1.0 - sigma)
    value = value.astype(bf16).astype(f32)
    for row in range(rows):
        put(padded, (row + 1) * stride + MARGIN, act[row].astype(f32))
    for row, base, exists in ((0, at.top, has_upper), (rows + 1, at.bottom, has_lower)):
        strip = value[base : base + cols + 2]
        put(padded, row * stride + MARGIN - 1, jnp.where(exists, strip, 0.0))
    put(padded, stride + MARGIN - 1, value[at.left : at.left + rows], stride)
    put(padded, stride + MARGIN + cols, value[at.right : at.right + rows], stride)
    for row in range(rows + 2):
        for shift in range(3):
            start = row * stride + MARGIN - 1 + shift
            shifted[shift, row] = get(padded, start, cols).astype(bf16)
    total = jnp.zeros((rows * cols, channels), f32)
    for k in range(3):
        for l in range(3):
            source = shifted[l, pl.ds(k, rows)].reshape(-1, channels)
            total = total + dot(source, conv_w[k, l])
    decoded[...] = total.astype(bf16).reshape(decoded.shape)

    def fine(p, q):
        return (p + 2) * stride + MARGIN + q

    for row in range(rows):
        put(wide, fine(row, 0), cot[row].astype(f32))
    for row, message, start, which in (
        (-1, upper, at.row_cot, COT), (-2, upper, at.row_cot_2, COT_2), (rows, lower, at.row_cot, COT),
    ):
        put(wide, fine(row, 0), message[start : start + cols, :])
        for col, one in ((-1, which[0]), (-2, which[1]), (cols, which[2])):
            put(wide, fine(row, col), corner(message, one))
    put(wide, fine(0, -1), left[at.cot : at.cot + rows, :], stride)
    put(wide, fine(0, -2), left[at.cot_2 : at.cot_2 + rows, :], stride)
    put(wide, fine(0, cols), right[at.cot : at.cot + rows, :], stride)
    total = jnp.zeros((at.grad_size, channels), f32)
    for k in range(3):
        for l in range(3):
            put(ring, at.top, get(wide, fine(-k, -l), cols + 1))
            put(ring, at.grad_left, get(wide, fine(1 - k, -l), rows, stride))
            source = get(ring, 0, at.grad_size).astype(bf16)
            total = total + dot_nt(source, conv_w[k, l])
    strip = (total[: cols + 1] * slope[at.top : at.top + cols + 1]).astype(bf16).astype(f32)
    put(ring, at.top, jnp.where(has_upper, strip, 0.0))
    strip = total[at.grad_left : at.grad_left + rows] * slope[at.left : at.left + rows]
    put(ring, at.grad_left, strip.astype(bf16).astype(f32))
    for phase, start in ((0, 1), (1, 2), (2, 0)):
        moved[phase, 0] = get(ring, at.top + start, n_cols, 2).astype(bf16)
    for phase in range(2):
        for row in range(n_rows):
            moved[phase, 1 + row] = phases[1, phase, row]
    for row_phase in range(2):
        for row in range(n_rows):
            put(padded, row * stride + MARGIN, phases[row_phase, 1, row].astype(f32))
        put(padded, MARGIN - 1, get(ring, at.grad_left + row_phase, n_rows, 2), stride)
        for row in range(n_rows):
            cells = get(padded, row * stride + MARGIN - 1, n_cols).astype(bf16)
            if row_phase:
                moved[2, 1 + row] = cells
            else:
                moved[3, row] = cells
    total = jnp.zeros((n_rows * n_cols, channels), f32)
    for k in range(3):
        for l in range(3):
            if k == 1:
                if l == 0:
                    source = moved[3, pl.ds(0, n_rows)]
                else:
                    source = phases[0, l - 1, pl.ds(0, n_rows)]
            else:
                source = moved[(2, 0, 1)[l], pl.ds(k // 2, n_rows)]
            total = total + dot_nt(source.reshape(n_rows * n_cols, channels), up_w[k, l])
    coarse_out[...] = total.astype(bf16).reshape(coarse_out.shape)


def sum_kernel(place, keep, got, own, *messages):
    chip = place[1]
    own[...] = keep[chip] + got[chip].astype(f32)
    for k, message in enumerate(messages):
        other = chip ^ (k + 1)
        message[...] = (keep[other] + got[other].astype(f32)).astype(bf16)


def packing(rows, cols):
    side = max(1, 128 // cols)
    return side if rows % (16 * side) == 0 else 1


def plane_kernel(place, own, *refs):
    n_bands, peers = refs[-1].shape[0], refs[: -(refs[-1].shape[0] + 1)]
    outs, cut = refs[len(peers) : -1], refs[-1]
    total = own[...]
    for peer in peers:
        total = total + peer[...].astype(f32)
    cols = total.shape[1] // n_bands
    side = packing(total.shape[0], cols)
    rows = total.shape[0] // side
    for band in range(n_bands):
        for part in range(side):
            cut[band, :, part * cols : (part + 1) * cols] = total[
                part * rows : (part + 1) * rows, band * cols : (band + 1) * cols
            ]
    band = place[2]
    outs[0][...] = cut[band]
    for k in range(1, n_bands):
        outs[k][...] = cut[band ^ k].astype(bf16)


def last_kernel(own, *refs):
    peers, out = refs[:-1], refs[-1]
    total = own[...]
    for peer in peers:
        total = total + peer[...].astype(f32)
    rows, cols = total.shape[0], out.shape[0]
    turned = total.T
    for part in range(out.shape[1] // rows):
        out[:, part * rows : (part + 1) * rows] = turned[part * cols : (part + 1) * cols, :]


def xor_pairs(count, bits):
    return [(i, i ^ bits) for i in range(count)]


def reduce_partial(place, keep, send):
    faces, bands = lax.axis_size("face"), lax.axis_size("band")
    groups, block, channels = keep.shape
    got = lax.ppermute(send, "face", xor_pairs(faces, 1))
    shape = (block, channels)
    own, *messages = kernel_call(
        sum_kernel, [sds(shape, f32)] + [sds(shape, bf16)] * (groups - 1), [], 0, place, keep, got
    )
    order = sorted(range(1, groups), key=lambda k: -bin(k).count("1"))
    got = [lax.ppermute(messages[k - 1], "face", xor_pairs(faces, 2 * k)) for k in order]
    cols = channels // bands
    side = packing(block, cols)
    shape = (block // side, cols * side)
    own, *messages = kernel_call(
        plane_kernel, [sds(shape, f32)] + [sds(shape, bf16)] * (bands - 1),
        [pltpu.VMEM((bands,) + shape, f32)], 0, place, own, *got,
    )
    order = sorted(range(1, bands), key=lambda k: -k)
    got = [lax.ppermute(messages[k - 1], "band", xor_pairs(bands, k)) for k in order]
    return kernel_call(last_kernel, [sds((cols, block), f32)], [], 0, own, *got)[0].T


def swap(first, second, axis, wrap):
    one, two = pairs(lax.axis_size(axis), wrap)
    return lax.ppermute(first, axis, one), lax.ppermute(second, axis, two)


def local(coarse, skip, up_weight, conv_weight, cotangent):
    n_rows, n_cols, channels = coarse.shape
    rows, cols, _ = skip.shape
    at = Layout(n_rows, n_cols)
    faces, bands = lax.axis_size("face"), lax.axis_size("band")
    face, band = lax.axis_index("face"), lax.axis_index("band")
    place = jnp.stack([face % 2, face // 2, band, bands]).astype(jnp.int32)
    groups, block = faces // 2, 9 * channels // faces

    flat = halves(rows * cols, channels)
    message = sds((at.face_size, channels), bf16)
    edges = pltpu.VMEM(message.shape, f32)
    first, second, cotangent, skip, coarse = kernel_call(
        face_message,
        [message, message, sds(cotangent.shape, bf16), sds(skip.shape, bf16), sds(coarse.shape, bf16)],
        [flat, edges, edges, pltpu.SemaphoreType.DMA((3,))],
        0, place, coarse, skip, cotangent, far=(1, 2, 3),
    )
    first, second = swap(first, second, "face", True)
    side = sds(message.shape, f32)
    message = sds((at.band_size, channels), bf16)
    edges = pltpu.VMEM(message.shape, f32)
    first, second, left, right = kernel_call(
        band_message, [message, message, side, side], [edges, edges],
        0, place, coarse, skip, cotangent, first, second,
    )
    first, second = swap(first, second, "band", False)

    cells = n_rows * n_cols
    stride = cols + 2 * MARGIN
    padded = halves((rows + 2) * stride, channels)
    shift_shape = (3, rows + 2, cols, channels)
    whole = -(-cells // 256) * 256 // n_cols
    one_tap = 2 * cells * channels * channels
    partials = [sds((groups, block, channels), f32), sds((groups, block, channels), bf16)]
    partial = pltpu.VMEM((9 * channels, channels), f32)
    side = sds(message.shape, f32)
    shifted, near, act, slope, keep_conv, send_conv, upper, lower, up_weight, conv_weight = kernel_call(
        act_kernel,
        [
            sds(shift_shape, bf16), sds((2, whole + 1, n_cols, channels), bf16),
            sds(skip.shape, bf16), sds((rows * cols, channels), f32), *partials, side, side,
            sds(up_weight.shape, bf16), sds(conv_weight.shape, bf16),
        ],
        [padded, flat, partial, pltpu.SemaphoreType.DMA((2,))],
        45 * one_tap, place, coarse, skip, cotangent, left, right, first, second,
        up_weight, conv_weight, far=(8, 9),
    )
    phases, keep_up, send_up = kernel_call(
        grad_kernel,
        [sds((2, 2, whole, n_cols, channels), bf16), *partials],
        [flat, partial],
        45 * one_tap, place, shifted, slope, near, conv_weight,
    )
    decoded, grad_coarse = kernel_call(
        out_kernel,
        [sds(skip.shape, bf16), sds(coarse.shape, bf16)],
        [
            padded, pltpu.VMEM(shift_shape, bf16), pltpu.VMEM((4, n_rows + 1, n_cols, channels), bf16),
            halves(at.ring_size, channels), halves((rows + 3) * stride, channels),
        ],
        60 * one_tap, place, coarse, cotangent, act, phases, left, right, upper, lower,
        conv_weight, up_weight,
    )
    grad_conv = reduce_partial(place, keep_conv, send_conv)
    grad_up = reduce_partial(place, keep_up, send_up)
    return (decoded, grad_coarse, grad_up, grad_conv)


def solution(mesh):
    return jax.shard_map(
        local,
        mesh=mesh,
        in_specs=(
            P("band", "face", None),
            P("band", "face", None),
            P(),
            P(),
            P("band", "face", None),
        ),
        out_specs=(
            P("band", "face", None),
            P("band", "face", None),
            P("face", "band"),
            P("face", "band"),
        ),
        check_vma=False,
    )
```

```python
import jax
import jax.numpy as jnp
from jax import lax
from jax.experimental import pallas as pl
from jax.experimental.pallas import tpu as pltpu
from jax.sharding import PartitionSpec as P

f32, bf16 = jnp.float32, jnp.bfloat16
forward_taps = ((1, 1), (0, 0), (1, 0))
backward_taps = ((1, 0), (0, 1), (1, 1))
MARGIN = 8
LANES = 128


def sds(shape, dtype):
    return jax.ShapeDtypeStruct(shape, dtype)


def kernel_call(body, outs, scratch, flops, *args, far=()):
    vmem = pl.BlockSpec(memory_space=pltpu.VMEM)
    smem = pl.BlockSpec(memory_space=pltpu.SMEM)
    anywhere = pl.BlockSpec(memory_space=pltpu.HBM)
    moved = sum(a.size * a.dtype.itemsize for a in args)
    moved += sum(a.size * a.dtype.itemsize for a in outs)
    return pl.pallas_call(
        body,
        out_shape=tuple(outs),
        in_specs=[
            anywhere if i in far else smem if a.dtype == jnp.int32 else vmem
            for i, a in enumerate(args)
        ],
        out_specs=tuple(vmem for _ in outs),
        scratch_shapes=scratch,
        compiler_params=pltpu.CompilerParams(vmem_limit_bytes=28 * 2**20),
        cost_estimate=pl.CostEstimate(flops=flops, bytes_accessed=moved, transcendentals=0),
    )(*args)


def dot(a, b):
    return jnp.dot(a, b, preferred_element_type=f32)


def dot_nt(a, b):
    return lax.dot_general(a, b, (((1,), (1,)), ((), ())), preferred_element_type=f32)


def pairs(count, wrap):
    first = [(i, i ^ 1) for i in range(count)]
    second = []
    for i in range(count):
        j = i + 1 if i % 2 else i - 1
        if wrap or 0 <= j < count:
            second.append((i, j % count))
    return first, second


def up16(n):
    return (n + 15) // 16 * 16


def halves(n_rows, channels):
    return pltpu.VMEM((channels // LANES, n_rows, LANES), f32)


def put(ref, start, value, step=1):
    for part in range(ref.shape[0]):
        rows = pl.ds(start, value.shape[0], stride=step if step > 1 else None)
        ref[part, rows, :] = value[:, part * LANES : (part + 1) * LANES]


def get(ref, start, count, step=1):
    rows = pl.ds(start, count, stride=step if step > 1 else None)
    return jnp.concatenate([ref[part, rows, :] for part in range(ref.shape[0])], axis=1)


def fill(ref, start, value):
    ref[start : start + value.shape[0], :] = value


def split_by_core(place, partial, keep, send):
    groups, block, _ = keep.shape
    for group in range(groups):
        mine = pl.multiple_of((2 * group + place[0]) * block, 16)
        theirs = pl.multiple_of((2 * group + 1 - place[0]) * block, 16)
        keep[group] = partial[pl.ds(mine, block), :]
        send[group] = partial[pl.ds(theirs, block), :].astype(bf16)


class Layout:
    def __init__(self, n_rows, n_cols):
        rows, cols = 2 * n_rows, 2 * n_cols
        self.cot, self.cot_2, self.skip, self.coarse = 0, rows, 2 * rows, 3 * rows
        self.face_size = up16(3 * rows + n_rows)
        self.row_cot, self.row_cot_2, self.row_skip = 0, cols, 2 * cols
        self.row_coarse, self.corner = 3 * cols, 3 * cols + n_cols
        self.band_size = self.corner + 16
        ring = (cols + 2 + 7) // 8 * 8
        self.top, self.bottom, self.left, self.right = 0, ring, 2 * ring, 2 * ring + rows
        self.ring_size = up16(2 * ring + 2 * rows)
        self.grad_left, self.grad_size = ring, up16(ring + rows)


COT, COT_2, SKIP, COARSE = (0, 1, 2), (3, 4, 5), (6, None, 7), (8, None, 9)


def face_message(place, coarse, skip, cot, first, second, cot_v, skip_v, coarse_v, flat, before, after, sems):
    rows, cols, _ = cot.shape
    n_rows, n_cols, _ = coarse.shape
    at = Layout(n_rows, n_cols)
    copies = [
        pltpu.make_async_copy(source, target, sems.at[i])
        for i, (source, target) in enumerate(((cot, cot_v), (skip, skip_v), (coarse, coarse_v)))
    ]
    for copy in copies:
        copy.start()
    before[...] = jnp.zeros_like(before)
    after[...] = jnp.zeros_like(after)
    copies[0].wait()
    put(flat, 0, cot_v[...].reshape(rows * cols, -1).astype(f32))
    fill(before, at.cot, get(flat, 0, rows, cols))
    fill(after, at.cot, get(flat, cols - 1, rows, cols))
    fill(after, at.cot_2, get(flat, cols - 2, rows, cols))
    copies[1].wait()
    put(flat, 0, skip_v[...].reshape(rows * cols, -1).astype(f32))
    fill(before, at.skip, get(flat, 0, rows, cols))
    fill(after, at.skip, get(flat, cols - 1, rows, cols))
    copies[2].wait()
    put(flat, 0, coarse_v[...].reshape(n_rows * n_cols, -1).astype(f32))
    fill(before, at.coarse, get(flat, 0, n_rows, n_cols))
    fill(after, at.coarse, get(flat, n_cols - 1, n_rows, n_cols))
    even = place[0] == 0
    first[...] = jnp.where(even, after[...], before[...]).astype(bf16)
    second[...] = jnp.where(even, before[...], after[...]).astype(bf16)


def band_message(place, coarse, skip, cot, got_first, got_second, first, second, left, right, before, after):
    rows, cols, channels = cot.shape
    n_rows, n_cols, _ = coarse.shape
    at = Layout(n_rows, n_cols)
    even = place[0] == 0
    one, two = got_first[...].astype(f32), got_second[...].astype(f32)
    left[...] = jnp.where(even, two, one)
    right[...] = jnp.where(even, one, two)
    for message, row, row_2, cell in ((before, 0, None, 0), (after, rows - 1, rows - 2, n_rows - 1)):
        fill(message, at.row_cot, cot[row].astype(f32))
        if row_2 is None:
            fill(message, at.row_cot_2, jnp.zeros((cols, channels), f32))
        else:
            fill(message, at.row_cot_2, cot[row_2].astype(f32))
        fill(message, at.row_skip, skip[row].astype(f32))
        fill(message, at.row_coarse, coarse[cell].astype(f32))
        fill(message, at.corner, jnp.zeros((16, channels), f32))
        corners = [
            (COT[0], left, at.cot + row), (COT[1], left, at.cot_2 + row), (COT[2], right, at.cot + row),
            (SKIP[0], left, at.skip + row), (SKIP[2], right, at.skip + row),
            (COARSE[0], left, at.coarse + cell), (COARSE[2], right, at.coarse + cell),
        ]
        if row_2 is not None:
            corners += [
                (COT_2[0], left, at.cot + row_2), (COT_2[1], left, at.cot_2 + row_2),
                (COT_2[2], right, at.cot + row_2),
            ]
        for corner, side, source in corners:
            fill(message, at.corner + corner, side[source : source + 1, :])
    even = lax.rem(place[2], 2) == 0
    first[...] = jnp.where(even, after[...], before[...]).astype(bf16)
    second[...] = jnp.where(even, before[...], after[...]).astype(bf16)


def act_kernel(
    place, coarse, skip, cot, left, right, got_first, got_second, up_w, conv_w,
    shifted, near, act, slope, keep, send, upper, lower, up_v, conv_v,
    padded, pre, partial, sems,
):
    n_rows, n_cols, channels = coarse.shape
    rows, cols, _ = skip.shape
    at = Layout(n_rows, n_cols)
    stride = cols + 2 * MARGIN
    copies = [
        pltpu.make_async_copy(up_w, up_v, sems.at[0]),
        pltpu.make_async_copy(conv_w, conv_v, sems.at[1]),
    ]
    for copy in copies:
        copy.start()
    even = lax.rem(place[2], 2) == 0
    one, two = got_first[...].astype(f32), got_second[...].astype(f32)
    upper[...] = jnp.where(even, two, one)
    lower[...] = jnp.where(even, one, two)
    for row in range(n_rows):
        near[0, row] = coarse[row]
        put(padded, row * stride, coarse[row].astype(f32))
    below = lower[at.row_coarse : at.row_coarse + n_cols, :]
    near[0, n_rows] = below.astype(bf16)
    put(padded, n_rows * stride, below)
    put(padded, n_cols, right[at.coarse : at.coarse + n_rows, :], stride)
    corner = at.corner + COARSE[2]
    put(padded, n_rows * stride + n_cols, lower[corner : corner + 1, :])
    for row in range(n_rows + 1):
        near[1, row] = get(padded, row * stride + 1, n_cols).astype(bf16)
    for row in range(n_rows + 1, near.shape[1]):
        for side in range(2):
            near[side, row] = jnp.zeros((n_cols, channels), bf16)
    put(padded, MARGIN, upper[at.row_cot : at.row_cot + cols, :])
    put(padded, (rows + 1) * stride + MARGIN, lower[at.row_cot : at.row_cot + cols, :])
    for row in range(rows):
        put(padded, (row + 1) * stride + MARGIN, cot[row].astype(f32))
    put(padded, stride + MARGIN - 1, left[at.cot : at.cot + rows, :], stride)
    put(padded, stride + MARGIN + cols, right[at.cot : at.cot + rows, :], stride)
    for row, message in ((0, upper), (rows + 1, lower)):
        for col, corner in ((-1, at.corner + COT[0]), (cols, at.corner + COT[2])):
            put(padded, row * stride + MARGIN + col, message[corner : corner + 1, :])
    for row in range(rows + 2):
        for shift in (0, 2):
            start = row * stride + MARGIN - 1 + shift
            shifted[shift, row] = get(padded, start, cols).astype(bf16)
    shifted[1, 0] = upper[at.row_cot : at.row_cot + cols, :].astype(bf16)
    shifted[1, rows + 1] = lower[at.row_cot : at.row_cot + cols, :].astype(bf16)
    for row in range(rows):
        shifted[1, row + 1] = cot[row]
    copies[0].wait()
    sums = {}
    for k in range(3):
        row_phase, row_off = forward_taps[k]
        for l in range(3):
            col_phase, col_off = forward_taps[l]
            source = near[col_off, pl.ds(row_off, n_rows)].reshape(n_rows * n_cols, channels)
            term = dot(source, up_v[k, l])
            name = (row_phase, col_phase)
            sums[name] = sums[name] + term if name in sums else term
    for (row_phase, col_phase), total in sums.items():
        for row in range(n_rows):
            start = (2 * row + row_phase) * cols + col_phase
            put(pre, start, total[row * n_cols : (row + 1) * n_cols], 2)
    preact = get(pre, 0, rows * cols) + skip[...].reshape(rows * cols, channels).astype(f32)
    sigma = jax.nn.sigmoid(preact)
    value = preact * sigma
    slope[...] = sigma + value * (1.0 - sigma)
    act_flat = value.astype(bf16)
    act[...] = act_flat.reshape(act.shape)
    act_t = act_flat.T
    for k in range(3):
        for l in range(3):
            source = shifted[2 - l, pl.ds(2 - k, rows)].reshape(-1, channels)
            partial[pl.ds((3 * k + l) * channels, channels), :] = dot(act_t, source)
    split_by_core(place, partial, keep, send)
    copies[1].wait()


def grad_kernel(shifted, slope, conv_w, phases, fine):
    rows, cols = shifted.shape[1] - 2, shifted.shape[2]
    channels = shifted.shape[3]
    n_rows, n_cols = rows // 2, cols // 2
    total = jnp.zeros((rows * cols, channels), f32)
    for k in range(3):
        for l in range(3):
            source = shifted[2 - l, pl.ds(2 - k, rows)].reshape(-1, channels)
            total = total + dot_nt(source, conv_w[k, l])
    put(fine, 0, (total * slope[...]).astype(bf16).astype(f32))
    whole = phases.shape[2]
    for row_phase in range(2):
        for col_phase in range(2):
            for row in range(n_rows):
                start = (2 * row + row_phase) * cols + col_phase
                phases[row_phase, col_phase, row] = get(fine, start, n_cols, 2).astype(bf16)
            for row in range(n_rows, whole):
                phases[row_phase, col_phase, row] = jnp.zeros((n_cols, channels), bf16)


def up_kernel(place, near, phases, keep, send, partial):
    _, _, whole, n_cols, channels = phases.shape
    turned = {}
    for row_off in range(2):
        for col_off in range(2):
            cells = near[col_off, pl.ds(row_off, whole)]
            turned[row_off, col_off] = cells.reshape(whole * n_cols, channels).T
    for k in range(3):
        row_phase, row_off = forward_taps[k]
        for l in range(3):
            col_phase, col_off = forward_taps[l]
            source = phases[row_phase, col_phase].reshape(whole * n_cols, channels)
            partial[pl.ds((3 * k + l) * channels, channels), :] = dot(
                turned[row_off, col_off], source
            )
    split_by_core(place, partial, keep, send)


def out_kernel(
    place, coarse, cot, act, phases, left, right, upper, lower, conv_w, up_w,
    decoded, coarse_out, padded, shifted, moved, ring, wide,
):
    rows, cols, channels = act.shape
    n_rows, n_cols = rows // 2, cols // 2
    at = Layout(n_rows, n_cols)
    stride, step = cols + 2 * MARGIN, n_cols + 2 * MARGIN
    has_upper, has_lower = place[2] > 0, place[2] < place[3] - 1

    def corner(message, which):
        return message[at.corner + which : at.corner + which + 1, :]

    def cell(i, j):
        return (i + 1) * step + MARGIN + j

    for row in range(n_rows):
        put(wide, cell(row, 0), coarse[row].astype(f32))
    for row, message in ((-1, upper), (n_rows, lower)):
        put(wide, cell(row, 0), message[at.row_coarse : at.row_coarse + n_cols, :])
        put(wide, cell(row, -1), corner(message, COARSE[0]))
        put(wide, cell(row, n_cols), corner(message, COARSE[2]))
    put(wide, cell(0, -1), left[at.coarse : at.coarse + n_rows, :], step)
    put(wide, cell(0, n_cols), right[at.coarse : at.coarse + n_rows, :], step)
    total = jnp.zeros((at.ring_size, channels), f32)
    for k in range(3):
        for l in range(3):
            put(ring, 0, jnp.zeros((at.ring_size, channels), f32))
            for base, i in ((at.bottom, n_rows),) if k == 1 else ((at.top, k // 2 * -1),):
                start = cell(i, -1 if l == 2 else 0)
                put(ring, base + (l == 1), get(wide, start, n_cols + 1), 2)
            base, j = (at.right, n_cols) if l == 1 else (at.left, -(l // 2))
            start = cell(1 if k == 0 else 0, j)
            put(ring, base + (k != 1), get(wide, start, n_rows, step), 2)
            total = total + dot(get(ring, 0, at.ring_size).astype(bf16), up_w[k, l])
    put(ring, 0, jnp.zeros((at.ring_size, channels), f32))
    for base, message in ((at.top, upper), (at.bottom, lower)):
        put(ring, base + 1, message[at.row_skip : at.row_skip + cols, :])
        put(ring, base, corner(message, SKIP[0]))
        put(ring, base + cols + 1, corner(message, SKIP[2]))
    put(ring, at.left, left[at.skip : at.skip + rows, :])
    put(ring, at.right, right[at.skip : at.skip + rows, :])
    preact = total + get(ring, 0, at.ring_size)
    sigma = jax.nn.sigmoid(preact)
    value = preact * sigma
    slope = sigma + value * (1.0 - sigma)
    value = value.astype(bf16).astype(f32)
    for row in range(rows):
        put(padded, (row + 1) * stride + MARGIN, act[row].astype(f32))
    for row, base, exists in ((0, at.top, has_upper), (rows + 1, at.bottom, has_lower)):
        strip = value[base : base + cols + 2]
        put(padded, row * stride + MARGIN - 1, jnp.where(exists, strip, 0.0))
    put(padded, stride + MARGIN - 1, value[at.left : at.left + rows], stride)
    put(padded, stride + MARGIN + cols, value[at.right : at.right + rows], stride)
    for row in range(rows + 2):
        for shift in range(3):
            start = row * stride + MARGIN - 1 + shift
            shifted[shift, row] = get(padded, start, cols).astype(bf16)
    total = jnp.zeros((rows * cols, channels), f32)
    for k in range(3):
        for l in range(3):
            source = shifted[l, pl.ds(k, rows)].reshape(-1, channels)
            total = total + dot(source, conv_w[k, l])
    decoded[...] = total.astype(bf16).reshape(decoded.shape)

    def fine(p, q):
        return (p + 2) * stride + MARGIN + q

    for row in range(rows):
        put(wide, fine(row, 0), cot[row].astype(f32))
    for row, message, start, which in (
        (-1, upper, at.row_cot, COT), (-2, upper, at.row_cot_2, COT_2), (rows, lower, at.row_cot, COT),
    ):
        put(wide, fine(row, 0), message[start : start + cols, :])
        for col, one in ((-1, which[0]), (-2, which[1]), (cols, which[2])):
            put(wide, fine(row, col), corner(message, one))
    put(wide, fine(0, -1), left[at.cot : at.cot + rows, :], stride)
    put(wide, fine(0, -2), left[at.cot_2 : at.cot_2 + rows, :], stride)
    put(wide, fine(0, cols), right[at.cot : at.cot + rows, :], stride)
    total = jnp.zeros((at.grad_size, channels), f32)
    for k in range(3):
        for l in range(3):
            put(ring, at.top, get(wide, fine(-k, -l), cols + 1))
            put(ring, at.grad_left, get(wide, fine(1 - k, -l), rows, stride))
            source = get(ring, 0, at.grad_size).astype(bf16)
            total = total + dot_nt(source, conv_w[k, l])
    strip = (total[: cols + 1] * slope[at.top : at.top + cols + 1]).astype(bf16).astype(f32)
    put(ring, at.top, jnp.where(has_upper, strip, 0.0))
    strip = total[at.grad_left : at.grad_left + rows] * slope[at.left : at.left + rows]
    put(ring, at.grad_left, strip.astype(bf16).astype(f32))
    for phase, start in ((0, 1), (1, 2), (2, 0)):
        moved[phase, 0] = get(ring, at.top + start, n_cols, 2).astype(bf16)
    for phase in range(2):
        for row in range(n_rows):
            moved[phase, 1 + row] = phases[1, phase, row]
    for row_phase in range(2):
        for row in range(n_rows):
            put(padded, row * stride + MARGIN, phases[row_phase, 1, row].astype(f32))
        put(padded, MARGIN - 1, get(ring, at.grad_left + row_phase, n_rows, 2), stride)
        for row in range(n_rows):
            cells = get(padded, row * stride + MARGIN - 1, n_cols).astype(bf16)
            if row_phase:
                moved[2, 1 + row] = cells
            else:
                moved[3, row] = cells
    total = jnp.zeros((n_rows * n_cols, channels), f32)
    for k in range(3):
        for l in range(3):
            if k == 1:
                if l == 0:
                    source = moved[3, pl.ds(0, n_rows)]
                else:
                    source = phases[0, l - 1, pl.ds(0, n_rows)]
            else:
                source = moved[(2, 0, 1)[l], pl.ds(k // 2, n_rows)]
            total = total + dot_nt(source.reshape(n_rows * n_cols, channels), up_w[k, l])
    coarse_out[...] = total.astype(bf16).reshape(coarse_out.shape)


def sum_kernel(place, keep, got, own, *messages):
    chip = place[1]
    own[...] = keep[chip] + got[chip].astype(f32)
    for k, message in enumerate(messages):
        other = chip ^ (k + 1)
        message[...] = (keep[other] + got[other].astype(f32)).astype(bf16)


def packing(rows, cols):
    side = max(1, 128 // cols)
    return side if rows % (16 * side) == 0 else 1


def plane_kernel(place, own, *refs):
    n_bands, peers = refs[-1].shape[0], refs[: -(refs[-1].shape[0] + 1)]
    outs, cut = refs[len(peers) : -1], refs[-1]
    total = own[...]
    for peer in peers:
        total = total + peer[...].astype(f32)
    cols = total.shape[1] // n_bands
    side = packing(total.shape[0], cols)
    rows = total.shape[0] // side
    for band in range(n_bands):
        for part in range(side):
            cut[band, :, part * cols : (part + 1) * cols] = total[
                part * rows : (part + 1) * rows, band * cols : (band + 1) * cols
            ]
    band = place[2]
    outs[0][...] = cut[band]
    for k in range(1, n_bands):
        outs[k][...] = cut[band ^ k].astype(bf16)


def last_kernel(own, *refs):
    peers, out = refs[:-1], refs[-1]
    total = own[...]
    for peer in peers:
        total = total + peer[...].astype(f32)
    rows, cols = total.shape[0], out.shape[0]
    turned = total.T
    for part in range(out.shape[1] // rows):
        out[:, part * rows : (part + 1) * rows] = turned[part * cols : (part + 1) * cols, :]


def xor_pairs(count, bits):
    return [(i, i ^ bits) for i in range(count)]


def core_sum(place, keep, send):
    groups, block, channels = keep.shape
    got = lax.ppermute(send, "face", xor_pairs(lax.axis_size("face"), 1))
    shape = (block, channels)
    outs = [sds(shape, f32)] + [sds(shape, bf16)] * (groups - 1)
    own, *messages = kernel_call(sum_kernel, outs, [], 0, place, keep, got)
    return own, messages


def plane_swap(messages):
    faces = lax.axis_size("face")
    order = sorted(range(1, faces // 2), key=lambda k: -bin(k).count("1"))
    return [lax.ppermute(messages[k - 1], "face", xor_pairs(faces, 2 * k)) for k in order]


def band_sum(place, own, got):
    bands = lax.axis_size("band")
    block, channels = own.shape
    cols = channels // bands
    side = packing(block, cols)
    shape = (block // side, cols * side)
    own, *messages = kernel_call(
        plane_kernel, [sds(shape, f32)] + [sds(shape, bf16)] * (bands - 1),
        [pltpu.VMEM((bands,) + shape, f32)], 0, place, own, *got,
    )
    order = sorted(range(1, bands), key=lambda k: -k)
    got = [lax.ppermute(messages[k - 1], "band", xor_pairs(bands, k)) for k in order]
    return kernel_call(last_kernel, [sds((cols, block), f32)], [], 0, own, *got)[0].T


def after(value, *others):
    return lax.optimization_barrier((value, *others))[0]


def swap(first, second, axis, wrap):
    one, two = pairs(lax.axis_size(axis), wrap)
    return lax.ppermute(first, axis, one), lax.ppermute(second, axis, two)


def local(coarse, skip, up_weight, conv_weight, cotangent):
    n_rows, n_cols, channels = coarse.shape
    rows, cols, _ = skip.shape
    at = Layout(n_rows, n_cols)
    faces, bands = lax.axis_size("face"), lax.axis_size("band")
    face, band = lax.axis_index("face"), lax.axis_index("band")
    place = jnp.stack([face % 2, face // 2, band, bands]).astype(jnp.int32)
    groups, block = faces // 2, 9 * channels // faces

    flat = halves(rows * cols, channels)
    message = sds((at.face_size, channels), bf16)
    edges = pltpu.VMEM(message.shape, f32)
    first, second, cotangent, skip, coarse = kernel_call(
        face_message,
        [message, message, sds(cotangent.shape, bf16), sds(skip.shape, bf16), sds(coarse.shape, bf16)],
        [flat, edges, edges, pltpu.SemaphoreType.DMA((3,))],
        0, place, coarse, skip, cotangent, far=(1, 2, 3),
    )
    first, second = swap(first, second, "face", True)
    side = sds(message.shape, f32)
    message = sds((at.band_size, channels), bf16)
    edges = pltpu.VMEM(message.shape, f32)
    first, second, left, right = kernel_call(
        band_message, [message, message, side, side], [edges, edges],
        0, place, coarse, skip, cotangent, first, second,
    )
    first, second = swap(first, second, "band", False)

    cells = n_rows * n_cols
    stride = cols + 2 * MARGIN
    padded = halves((rows + 2) * stride, channels)
    shift_shape = (3, rows + 2, cols, channels)
    whole = -(-cells // 256) * 256 // n_cols
    one_tap = 2 * cells * channels * channels
    partials = [sds((groups, block, channels), f32), sds((groups, block, channels), bf16)]
    partial = pltpu.VMEM((9 * channels, channels), f32)
    side = sds(message.shape, f32)
    shifted, near, act, slope, keep_conv, send_conv, upper, lower, up_weight, conv_weight = kernel_call(
        act_kernel,
        [
            sds(shift_shape, bf16), sds((2, whole + 1, n_cols, channels), bf16),
            sds(skip.shape, bf16), sds((rows * cols, channels), f32), *partials, side, side,
            sds(up_weight.shape, bf16), sds(conv_weight.shape, bf16),
        ],
        [padded, flat, partial, pltpu.SemaphoreType.DMA((2,))],
        45 * one_tap, place, coarse, skip, cotangent, left, right, first, second,
        up_weight, conv_weight, far=(8, 9),
    )
    own_conv, to_plane = core_sum(place, keep_conv, send_conv)
    from_plane = plane_swap(to_plane)
    phases = kernel_call(
        grad_kernel,
        [sds((2, 2, whole, n_cols, channels), bf16)],
        [flat],
        36 * one_tap, shifted, slope, conv_weight,
    )[0]
    keep_up, send_up = kernel_call(
        up_kernel, partials, [partial], 9 * one_tap, place, after(near, to_plane[0]), phases
    )
    own_up, to_plane = core_sum(place, keep_up, send_up)
    decoded, grad_coarse = kernel_call(
        out_kernel,
        [sds(skip.shape, bf16), sds(coarse.shape, bf16)],
        [
            padded, pltpu.VMEM(shift_shape, bf16), pltpu.VMEM((4, n_rows + 1, n_cols, channels), bf16),
            halves(at.ring_size, channels), halves((rows + 3) * stride, channels),
        ],
        60 * one_tap, place, coarse, cotangent, after(act, to_plane[0]), phases, left, right,
        upper, lower, conv_weight, up_weight,
    )
    grad_conv = band_sum(place, after(own_conv, decoded), from_plane)
    grad_up = band_sum(place, own_up, plane_swap(to_plane))
    return (decoded, grad_coarse, grad_up, grad_conv)


def solution(mesh):
    return jax.shard_map(
        local,
        mesh=mesh,
        in_specs=(
            P("band", "face", None),
            P("band", "face", None),
            P(),
            P(),
            P("band", "face", None),
        ),
        out_specs=(
            P("band", "face", None),
            P("band", "face", None),
            P("face", "band"),
            P("face", "band"),
        ),
        check_vma=False,
    )
```

```python
import jax
import jax.numpy as jnp
from jax import lax
from jax.experimental import pallas as pl
from jax.experimental.pallas import tpu as pltpu
from jax.sharding import PartitionSpec as P

f32, bf16 = jnp.float32, jnp.bfloat16
forward_taps = ((1, 1), (0, 0), (1, 0))
backward_taps = ((1, 0), (0, 1), (1, 1))
MARGIN = 8
LANES = 128


def sds(shape, dtype):
    return jax.ShapeDtypeStruct(shape, dtype)


def kernel_call(body, outs, scratch, flops, *args, far=()):
    vmem = pl.BlockSpec(memory_space=pltpu.VMEM)
    smem = pl.BlockSpec(memory_space=pltpu.SMEM)
    hbm = pl.BlockSpec(memory_space=pltpu.HBM)
    moved = sum(a.size * a.dtype.itemsize for a in args)
    moved += sum(a.size * a.dtype.itemsize for a in outs)
    args = [
        pltpu.with_memory_space_constraint(a, pltpu.HBM) if i in far else a
        for i, a in enumerate(args)
    ]
    return pl.pallas_call(
        body,
        out_shape=tuple(outs),
        in_specs=[
            hbm if i in far else smem if a.dtype == jnp.int32 else vmem
            for i, a in enumerate(args)
        ],
        out_specs=tuple(vmem for _ in outs),
        scratch_shapes=scratch,
        compiler_params=pltpu.CompilerParams(vmem_limit_bytes=28 * 2**20),
        cost_estimate=pl.CostEstimate(flops=flops, bytes_accessed=moved, transcendentals=0),
    )(*args)


def dot(a, b):
    return jnp.dot(a, b, preferred_element_type=f32)


def dot_nt(a, b):
    return lax.dot_general(a, b, (((1,), (1,)), ((), ())), preferred_element_type=f32)


def pairs(count, wrap):
    first = [(i, i ^ 1) for i in range(count)]
    second = []
    for i in range(count):
        j = i + 1 if i % 2 else i - 1
        if wrap or 0 <= j < count:
            second.append((i, j % count))
    return first, second


def up16(n):
    return (n + 15) // 16 * 16


def halves(n_rows, channels):
    return pltpu.VMEM((channels // LANES, n_rows, LANES), f32)


def put(ref, start, value, step=1):
    for part in range(ref.shape[0]):
        rows = pl.ds(start, value.shape[0], stride=step if step > 1 else None)
        ref[part, rows, :] = value[:, part * LANES : (part + 1) * LANES]


def get(ref, start, count, step=1):
    rows = pl.ds(start, count, stride=step if step > 1 else None)
    return jnp.concatenate([ref[part, rows, :] for part in range(ref.shape[0])], axis=1)


def fill(ref, start, value):
    ref[start : start + value.shape[0], :] = value


def split_by_core(place, partial, keep, send):
    groups, block, _ = keep.shape
    for group in range(groups):
        mine = pl.multiple_of((2 * group + place[0]) * block, 16)
        theirs = pl.multiple_of((2 * group + 1 - place[0]) * block, 16)
        keep[group] = partial[pl.ds(mine, block), :]
        send[group] = partial[pl.ds(theirs, block), :].astype(bf16)


class Layout:
    def __init__(self, n_rows, n_cols):
        rows, cols = 2 * n_rows, 2 * n_cols
        self.cot, self.cot_2, self.skip, self.coarse = 0, rows, 2 * rows, 3 * rows
        self.face_size = up16(3 * rows + n_rows)
        self.row_cot, self.row_cot_2, self.row_skip = 0, cols, 2 * cols
        self.row_coarse, self.corner = 3 * cols, 3 * cols + n_cols
        self.band_size = self.corner + 16
        ring = (cols + 2 + 7) // 8 * 8
        self.top, self.bottom, self.left, self.right = 0, ring, 2 * ring, 2 * ring + rows
        self.ring_size = up16(2 * ring + 2 * rows)
        self.grad_left, self.grad_size = ring, up16(ring + rows)


COT, COT_2, SKIP, COARSE = (0, 1, 2), (3, 4, 5), (6, None, 7), (8, None, 9)


def face_message(place, coarse, skip, cot, first, second, cot_v, skip_v, coarse_v, flat, before, after, sems):
    rows, cols, _ = cot.shape
    n_rows, n_cols, _ = coarse.shape
    at = Layout(n_rows, n_cols)
    copies = [
        pltpu.make_async_copy(source, target, sems.at[i])
        for i, (source, target) in enumerate(((cot, cot_v), (skip, skip_v), (coarse, coarse_v)))
    ]
    for copy in copies:
        copy.start()
    before[...] = jnp.zeros_like(before)
    after[...] = jnp.zeros_like(after)
    copies[0].wait()
    put(flat, 0, cot_v[...].reshape(rows * cols, -1).astype(f32))
    fill(before, at.cot, get(flat, 0, rows, cols))
    fill(after, at.cot, get(flat, cols - 1, rows, cols))
    fill(after, at.cot_2, get(flat, cols - 2, rows, cols))
    copies[1].wait()
    put(flat, 0, skip_v[...].reshape(rows * cols, -1).astype(f32))
    fill(before, at.skip, get(flat, 0, rows, cols))
    fill(after, at.skip, get(flat, cols - 1, rows, cols))
    copies[2].wait()
    put(flat, 0, coarse_v[...].reshape(n_rows * n_cols, -1).astype(f32))
    fill(before, at.coarse, get(flat, 0, n_rows, n_cols))
    fill(after, at.coarse, get(flat, n_cols - 1, n_rows, n_cols))
    even = place[0] == 0
    first[...] = jnp.where(even, after[...], before[...]).astype(bf16)
    second[...] = jnp.where(even, before[...], after[...]).astype(bf16)


def band_message(place, coarse, skip, cot, got_first, got_second, first, second, left, right, before, after):
    rows, cols, channels = cot.shape
    n_rows, n_cols, _ = coarse.shape
    at = Layout(n_rows, n_cols)
    even = place[0] == 0
    one, two = got_first[...].astype(f32), got_second[...].astype(f32)
    left[...] = jnp.where(even, two, one)
    right[...] = jnp.where(even, one, two)
    for message, row, row_2, cell in ((before, 0, None, 0), (after, rows - 1, rows - 2, n_rows - 1)):
        fill(message, at.row_cot, cot[row].astype(f32))
        if row_2 is None:
            fill(message, at.row_cot_2, jnp.zeros((cols, channels), f32))
        else:
            fill(message, at.row_cot_2, cot[row_2].astype(f32))
        fill(message, at.row_skip, skip[row].astype(f32))
        fill(message, at.row_coarse, coarse[cell].astype(f32))
        fill(message, at.corner, jnp.zeros((16, channels), f32))
        corners = [
            (COT[0], left, at.cot + row), (COT[1], left, at.cot_2 + row), (COT[2], right, at.cot + row),
            (SKIP[0], left, at.skip + row), (SKIP[2], right, at.skip + row),
            (COARSE[0], left, at.coarse + cell), (COARSE[2], right, at.coarse + cell),
        ]
        if row_2 is not None:
            corners += [
                (COT_2[0], left, at.cot + row_2), (COT_2[1], left, at.cot_2 + row_2),
                (COT_2[2], right, at.cot + row_2),
            ]
        for corner, side, source in corners:
            fill(message, at.corner + corner, side[source : source + 1, :])
    even = lax.rem(place[2], 2) == 0
    first[...] = jnp.where(even, after[...], before[...]).astype(bf16)
    second[...] = jnp.where(even, before[...], after[...]).astype(bf16)


def act_kernel(
    place, coarse, skip, cot, left, right, got_first, got_second, up_w, conv_w,
    shifted, near, act, slope, keep, send, upper, lower, up_v, conv_v,
    padded, pre, partial, sems,
):
    n_rows, n_cols, channels = coarse.shape
    rows, cols, _ = skip.shape
    at = Layout(n_rows, n_cols)
    stride = cols + 2 * MARGIN
    copies = [
        pltpu.make_async_copy(up_w, up_v, sems.at[0]),
        pltpu.make_async_copy(conv_w, conv_v, sems.at[1]),
    ]
    for copy in copies:
        copy.start()
    even = lax.rem(place[2], 2) == 0
    one, two = got_first[...].astype(f32), got_second[...].astype(f32)
    upper[...] = jnp.where(even, two, one)
    lower[...] = jnp.where(even, one, two)
    for row in range(n_rows):
        near[0, row] = coarse[row]
        put(padded, row * stride, coarse[row].astype(f32))
    below = lower[at.row_coarse : at.row_coarse + n_cols, :]
    near[0, n_rows] = below.astype(bf16)
    put(padded, n_rows * stride, below)
    put(padded, n_cols, right[at.coarse : at.coarse + n_rows, :], stride)
    corner = at.corner + COARSE[2]
    put(padded, n_rows * stride + n_cols, lower[corner : corner + 1, :])
    for row in range(n_rows + 1):
        near[1, row] = get(padded, row * stride + 1, n_cols).astype(bf16)
    for row in range(n_rows + 1, near.shape[1]):
        for side in range(2):
            near[side, row] = jnp.zeros((n_cols, channels), bf16)
    put(padded, MARGIN, upper[at.row_cot : at.row_cot + cols, :])
    put(padded, (rows + 1) * stride + MARGIN, lower[at.row_cot : at.row_cot + cols, :])
    for row in range(rows):
        put(padded, (row + 1) * stride + MARGIN, cot[row].astype(f32))
    put(padded, stride + MARGIN - 1, left[at.cot : at.cot + rows, :], stride)
    put(padded, stride + MARGIN + cols, right[at.cot : at.cot + rows, :], stride)
    for row, message in ((0, upper), (rows + 1, lower)):
        for col, corner in ((-1, at.corner + COT[0]), (cols, at.corner + COT[2])):
            put(padded, row * stride + MARGIN + col, message[corner : corner + 1, :])
    for row in range(rows + 2):
        for shift in (0, 2):
            start = row * stride + MARGIN - 1 + shift
            shifted[shift, row] = get(padded, start, cols).astype(bf16)
    shifted[1, 0] = upper[at.row_cot : at.row_cot + cols, :].astype(bf16)
    shifted[1, rows + 1] = lower[at.row_cot : at.row_cot + cols, :].astype(bf16)
    for row in range(rows):
        shifted[1, row + 1] = cot[row]
    copies[0].wait()
    sums = {}
    for k in range(3):
        row_phase, row_off = forward_taps[k]
        for l in range(3):
            col_phase, col_off = forward_taps[l]
            source = near[col_off, pl.ds(row_off, n_rows)].reshape(n_rows * n_cols, channels)
            term = dot(source, up_v[k, l])
            name = (row_phase, col_phase)
            sums[name] = sums[name] + term if name in sums else term
    for (row_phase, col_phase), total in sums.items():
        for row in range(n_rows):
            start = (2 * row + row_phase) * cols + col_phase
            put(pre, start, total[row * n_cols : (row + 1) * n_cols], 2)
    preact = get(pre, 0, rows * cols) + skip[...].reshape(rows * cols, channels).astype(f32)
    sigma = jax.nn.sigmoid(preact)
    value = preact * sigma
    slope[...] = sigma + value * (1.0 - sigma)
    act_flat = value.astype(bf16)
    act[...] = act_flat.reshape(act.shape)
    act_t = act_flat.T
    for k in range(3):
        for l in range(3):
            source = shifted[2 - l, pl.ds(2 - k, rows)].reshape(-1, channels)
            partial[pl.ds((3 * k + l) * channels, channels), :] = dot(act_t, source)
    split_by_core(place, partial, keep, send)
    copies[1].wait()


def grad_kernel(shifted, slope, conv_w, phases, fine):
    rows, cols = shifted.shape[1] - 2, shifted.shape[2]
    channels = shifted.shape[3]
    n_rows, n_cols = rows // 2, cols // 2
    total = jnp.zeros((rows * cols, channels), f32)
    for k in range(3):
        for l in range(3):
            source = shifted[2 - l, pl.ds(2 - k, rows)].reshape(-1, channels)
            total = total + dot_nt(source, conv_w[k, l])
    put(fine, 0, (total * slope[...]).astype(bf16).astype(f32))
    whole = phases.shape[2]
    for row_phase in range(2):
        for col_phase in range(2):
            for row in range(n_rows):
                start = (2 * row + row_phase) * cols + col_phase
                phases[row_phase, col_phase, row] = get(fine, start, n_cols, 2).astype(bf16)
            for row in range(n_rows, whole):
                phases[row_phase, col_phase, row] = jnp.zeros((n_cols, channels), bf16)


def up_kernel(place, near, phases, keep, send, partial):
    _, _, whole, n_cols, channels = phases.shape
    turned = {}
    for row_off in range(2):
        for col_off in range(2):
            cells = near[col_off, pl.ds(row_off, whole)]
            turned[row_off, col_off] = cells.reshape(whole * n_cols, channels).T
    for k in range(3):
        row_phase, row_off = forward_taps[k]
        for l in range(3):
            col_phase, col_off = forward_taps[l]
            source = phases[row_phase, col_phase].reshape(whole * n_cols, channels)
            partial[pl.ds((3 * k + l) * channels, channels), :] = dot(
                turned[row_off, col_off], source
            )
    split_by_core(place, partial, keep, send)


def out_kernel(
    place, coarse, cot, act, phases, left, right, upper, lower, conv_w, up_w,
    decoded, coarse_out, padded, shifted, moved, ring, wide,
):
    rows, cols, channels = act.shape
    n_rows, n_cols = rows // 2, cols // 2
    at = Layout(n_rows, n_cols)
    stride, step = cols + 2 * MARGIN, n_cols + 2 * MARGIN
    has_upper, has_lower = place[2] > 0, place[2] < place[3] - 1

    def corner(message, which):
        return message[at.corner + which : at.corner + which + 1, :]

    def cell(i, j):
        return (i + 1) * step + MARGIN + j

    for row in range(n_rows):
        put(wide, cell(row, 0), coarse[row].astype(f32))
    for row, message in ((-1, upper), (n_rows, lower)):
        put(wide, cell(row, 0), message[at.row_coarse : at.row_coarse + n_cols, :])
        put(wide, cell(row, -1), corner(message, COARSE[0]))
        put(wide, cell(row, n_cols), corner(message, COARSE[2]))
    put(wide, cell(0, -1), left[at.coarse : at.coarse + n_rows, :], step)
    put(wide, cell(0, n_cols), right[at.coarse : at.coarse + n_rows, :], step)
    total = jnp.zeros((at.ring_size, channels), f32)
    for k in range(3):
        for l in range(3):
            put(ring, 0, jnp.zeros((at.ring_size, channels), f32))
            for base, i in ((at.bottom, n_rows),) if k == 1 else ((at.top, k // 2 * -1),):
                start = cell(i, -1 if l == 2 else 0)
                put(ring, base + (l == 1), get(wide, start, n_cols + 1), 2)
            base, j = (at.right, n_cols) if l == 1 else (at.left, -(l // 2))
            start = cell(1 if k == 0 else 0, j)
            put(ring, base + (k != 1), get(wide, start, n_rows, step), 2)
            total = total + dot(get(ring, 0, at.ring_size).astype(bf16), up_w[k, l])
    put(ring, 0, jnp.zeros((at.ring_size, channels), f32))
    for base, message in ((at.top, upper), (at.bottom, lower)):
        put(ring, base + 1, message[at.row_skip : at.row_skip + cols, :])
        put(ring, base, corner(message, SKIP[0]))
        put(ring, base + cols + 1, corner(message, SKIP[2]))
    put(ring, at.left, left[at.skip : at.skip + rows, :])
    put(ring, at.right, right[at.skip : at.skip + rows, :])
    preact = total + get(ring, 0, at.ring_size)
    sigma = jax.nn.sigmoid(preact)
    value = preact * sigma
    slope = sigma + value * (1.0 - sigma)
    value = value.astype(bf16).astype(f32)
    for row in range(rows):
        put(padded, (row + 1) * stride + MARGIN, act[row].astype(f32))
    for row, base, exists in ((0, at.top, has_upper), (rows + 1, at.bottom, has_lower)):
        strip = value[base : base + cols + 2]
        put(padded, row * stride + MARGIN - 1, jnp.where(exists, strip, 0.0))
    put(padded, stride + MARGIN - 1, value[at.left : at.left + rows], stride)
    put(padded, stride + MARGIN + cols, value[at.right : at.right + rows], stride)
    for row in range(rows + 2):
        for shift in range(3):
            start = row * stride + MARGIN - 1 + shift
            shifted[shift, row] = get(padded, start, cols).astype(bf16)
    total = jnp.zeros((rows * cols, channels), f32)
    for k in range(3):
        for l in range(3):
            source = shifted[l, pl.ds(k, rows)].reshape(-1, channels)
            total = total + dot(source, conv_w[k, l])
    decoded[...] = total.astype(bf16).reshape(decoded.shape)

    def fine(p, q):
        return (p + 2) * stride + MARGIN + q

    for row in range(rows):
        put(wide, fine(row, 0), cot[row].astype(f32))
    for row, message, start, which in (
        (-1, upper, at.row_cot, COT), (-2, upper, at.row_cot_2, COT_2), (rows, lower, at.row_cot, COT),
    ):
        put(wide, fine(row, 0), message[start : start + cols, :])
        for col, one in ((-1, which[0]), (-2, which[1]), (cols, which[2])):
            put(wide, fine(row, col), corner(message, one))
    put(wide, fine(0, -1), left[at.cot : at.cot + rows, :], stride)
    put(wide, fine(0, -2), left[at.cot_2 : at.cot_2 + rows, :], stride)
    put(wide, fine(0, cols), right[at.cot : at.cot + rows, :], stride)
    total = jnp.zeros((at.grad_size, channels), f32)
    for k in range(3):
        for l in range(3):
            put(ring, at.top, get(wide, fine(-k, -l), cols + 1))
            put(ring, at.grad_left, get(wide, fine(1 - k, -l), rows, stride))
            source = get(ring, 0, at.grad_size).astype(bf16)
            total = total + dot_nt(source, conv_w[k, l])
    strip = (total[: cols + 1] * slope[at.top : at.top + cols + 1]).astype(bf16).astype(f32)
    put(ring, at.top, jnp.where(has_upper, strip, 0.0))
    strip = total[at.grad_left : at.grad_left + rows] * slope[at.left : at.left + rows]
    put(ring, at.grad_left, strip.astype(bf16).astype(f32))
    for phase, start in ((0, 1), (1, 2), (2, 0)):
        moved[phase, 0] = get(ring, at.top + start, n_cols, 2).astype(bf16)
    for phase in range(2):
        for row in range(n_rows):
            moved[phase, 1 + row] = phases[1, phase, row]
    for row_phase in range(2):
        for row in range(n_rows):
            put(padded, row * stride + MARGIN, phases[row_phase, 1, row].astype(f32))
        put(padded, MARGIN - 1, get(ring, at.grad_left + row_phase, n_rows, 2), stride)
        for row in range(n_rows):
            cells = get(padded, row * stride + MARGIN - 1, n_cols).astype(bf16)
            if row_phase:
                moved[2, 1 + row] = cells
            else:
                moved[3, row] = cells
    total = jnp.zeros((n_rows * n_cols, channels), f32)
    for k in range(3):
        for l in range(3):
            if k == 1:
                if l == 0:
                    source = moved[3, pl.ds(0, n_rows)]
                else:
                    source = phases[0, l - 1, pl.ds(0, n_rows)]
            else:
                source = moved[(2, 0, 1)[l], pl.ds(k // 2, n_rows)]
            total = total + dot_nt(source.reshape(n_rows * n_cols, channels), up_w[k, l])
    coarse_out[...] = total.astype(bf16).reshape(coarse_out.shape)


def sum_kernel(place, keep, got, own, *messages):
    chip = place[1]
    own[...] = keep[chip] + got[chip].astype(f32)
    for k, message in enumerate(messages):
        other = chip ^ (k + 1)
        message[...] = (keep[other] + got[other].astype(f32)).astype(bf16)


def packing(rows, cols):
    side = max(1, 128 // cols)
    return side if rows % (16 * side) == 0 else 1


def plane_kernel(place, own, *refs):
    n_bands, peers = refs[-1].shape[0], refs[: -(refs[-1].shape[0] + 1)]
    outs, cut = refs[len(peers) : -1], refs[-1]
    total = own[...]
    for peer in peers:
        total = total + peer[...].astype(f32)
    cols = total.shape[1] // n_bands
    side = packing(total.shape[0], cols)
    rows = total.shape[0] // side
    for band in range(n_bands):
        for part in range(side):
            cut[band, :, part * cols : (part + 1) * cols] = total[
                part * rows : (part + 1) * rows, band * cols : (band + 1) * cols
            ]
    band = place[2]
    outs[0][...] = cut[band]
    for k in range(1, n_bands):
        outs[k][...] = cut[band ^ k].astype(bf16)


def last_kernel(own, *refs):
    peers, out = refs[:-1], refs[-1]
    total = own[...]
    for peer in peers:
        total = total + peer[...].astype(f32)
    rows, cols = total.shape[0], out.shape[0]
    turned = total.T
    for part in range(out.shape[1] // rows):
        out[:, part * rows : (part + 1) * rows] = turned[part * cols : (part + 1) * cols, :]


def xor_pairs(count, bits):
    return [(i, i ^ bits) for i in range(count)]


def core_sum(place, keep, send):
    groups, block, channels = keep.shape
    got = lax.ppermute(send, "face", xor_pairs(lax.axis_size("face"), 1))
    shape = (block, channels)
    outs = [sds(shape, f32)] + [sds(shape, bf16)] * (groups - 1)
    own, *messages = kernel_call(sum_kernel, outs, [], 0, place, keep, got)
    return own, messages


def plane_swap(messages):
    faces = lax.axis_size("face")
    order = sorted(range(1, faces // 2), key=lambda k: -bin(k).count("1"))
    return [lax.ppermute(messages[k - 1], "face", xor_pairs(faces, 2 * k)) for k in order]


def band_sum(place, own, got):
    bands = lax.axis_size("band")
    block, channels = own.shape
    cols = channels // bands
    side = packing(block, cols)
    shape = (block // side, cols * side)
    own, *messages = kernel_call(
        plane_kernel, [sds(shape, f32)] + [sds(shape, bf16)] * (bands - 1),
        [pltpu.VMEM((bands,) + shape, f32)], 0, place, own, *got,
    )
    order = sorted(range(1, bands), key=lambda k: -k)
    got = [lax.ppermute(messages[k - 1], "band", xor_pairs(bands, k)) for k in order]
    return kernel_call(last_kernel, [sds((cols, block), f32)], [], 0, own, *got)[0].T


def after(value, *others):
    return lax.optimization_barrier((value, *others))[0]


def swap(first, second, axis, wrap):
    one, two = pairs(lax.axis_size(axis), wrap)
    return lax.ppermute(first, axis, one), lax.ppermute(second, axis, two)


def local(coarse, skip, up_weight, conv_weight, cotangent):
    n_rows, n_cols, channels = coarse.shape
    rows, cols, _ = skip.shape
    at = Layout(n_rows, n_cols)
    faces, bands = lax.axis_size("face"), lax.axis_size("band")
    face, band = lax.axis_index("face"), lax.axis_index("band")
    place = jnp.stack([face % 2, face // 2, band, bands]).astype(jnp.int32)
    groups, block = faces // 2, 9 * channels // faces

    flat = halves(rows * cols, channels)
    message = sds((at.face_size, channels), bf16)
    edges = pltpu.VMEM(message.shape, f32)
    first, second, cotangent, skip, coarse = kernel_call(
        face_message,
        [message, message, sds(cotangent.shape, bf16), sds(skip.shape, bf16), sds(coarse.shape, bf16)],
        [flat, edges, edges, pltpu.SemaphoreType.DMA((3,))],
        0, place, coarse, skip, cotangent, far=(1, 2, 3),
    )
    first, second = swap(first, second, "face", True)
    side = sds(message.shape, f32)
    message = sds((at.band_size, channels), bf16)
    edges = pltpu.VMEM(message.shape, f32)
    first, second, left, right = kernel_call(
        band_message, [message, message, side, side], [edges, edges],
        0, place, coarse, skip, cotangent, first, second,
    )
    first, second = swap(first, second, "band", False)

    cells = n_rows * n_cols
    stride = cols + 2 * MARGIN
    padded = halves((rows + 2) * stride, channels)
    shift_shape = (3, rows + 2, cols, channels)
    whole = -(-cells // 256) * 256 // n_cols
    one_tap = 2 * cells * channels * channels
    partials = [sds((groups, block, channels), f32), sds((groups, block, channels), bf16)]
    partial = pltpu.VMEM((9 * channels, channels), f32)
    side = sds(message.shape, f32)
    shifted, near, act, slope, keep_conv, send_conv, upper, lower, up_weight, conv_weight = kernel_call(
        act_kernel,
        [
            sds(shift_shape, bf16), sds((2, whole + 1, n_cols, channels), bf16),
            sds(skip.shape, bf16), sds((rows * cols, channels), f32), *partials, side, side,
            sds(up_weight.shape, bf16), sds(conv_weight.shape, bf16),
        ],
        [padded, flat, partial, pltpu.SemaphoreType.DMA((2,))],
        45 * one_tap, place, coarse, skip, cotangent, left, right, first, second,
        up_weight, conv_weight, far=(8, 9),
    )
    own_conv, to_plane = core_sum(place, keep_conv, send_conv)
    from_plane = plane_swap(to_plane)
    phases = kernel_call(
        grad_kernel,
        [sds((2, 2, whole, n_cols, channels), bf16)],
        [flat],
        36 * one_tap, shifted, slope, conv_weight,
    )[0]
    keep_up, send_up = kernel_call(
        up_kernel, partials, [partial], 9 * one_tap, place, after(near, to_plane[0]), phases
    )
    own_up, to_plane = core_sum(place, keep_up, send_up)
    decoded, grad_coarse = kernel_call(
        out_kernel,
        [sds(skip.shape, bf16), sds(coarse.shape, bf16)],
        [
            padded, pltpu.VMEM(shift_shape, bf16), pltpu.VMEM((4, n_rows + 1, n_cols, channels), bf16),
            halves(at.ring_size, channels), halves((rows + 3) * stride, channels),
        ],
        60 * one_tap, place, coarse, cotangent, after(act, to_plane[0]), phases, left, right,
        upper, lower, conv_weight, up_weight,
    )
    grad_conv = band_sum(place, after(own_conv, decoded), from_plane)
    grad_up = band_sum(place, own_up, plane_swap(to_plane))
    return (decoded, grad_coarse, grad_up, grad_conv)


def solution(mesh):
    return jax.shard_map(
        local,
        mesh=mesh,
        in_specs=(
            P("band", "face", None),
            P("band", "face", None),
            P(),
            P(),
            P("band", "face", None),
        ),
        out_specs=(
            P("band", "face", None),
            P("band", "face", None),
            P("face", "band"),
            P("face", "band"),
        ),
        check_vma=False,
    )
```

```python
import jax
import jax.numpy as jnp
from jax import lax
from jax.experimental import pallas as pl
from jax.experimental.pallas import tpu as pltpu
from jax.sharding import PartitionSpec as P

f32, bf16 = jnp.float32, jnp.bfloat16
forward_taps = ((1, 1), (0, 0), (1, 0))
backward_taps = ((1, 0), (0, 1), (1, 1))
MARGIN = 8
LANES = 128


def sds(shape, dtype):
    return jax.ShapeDtypeStruct(shape, dtype)


def kernel_call(body, outs, scratch, flops, *args, far=()):
    vmem = pl.BlockSpec(memory_space=pltpu.VMEM)
    smem = pl.BlockSpec(memory_space=pltpu.SMEM)
    hbm = pl.BlockSpec(memory_space=pltpu.HBM)
    moved = sum(a.size * a.dtype.itemsize for a in args)
    moved += sum(a.size * a.dtype.itemsize for a in outs)
    args = [
        pltpu.with_memory_space_constraint(a, pltpu.HBM) if i in far else a
        for i, a in enumerate(args)
    ]
    return pl.pallas_call(
        body,
        out_shape=tuple(outs),
        in_specs=[
            hbm if i in far else smem if a.dtype == jnp.int32 else vmem
            for i, a in enumerate(args)
        ],
        out_specs=tuple(vmem for _ in outs),
        scratch_shapes=scratch,
        compiler_params=pltpu.CompilerParams(vmem_limit_bytes=28 * 2**20),
        cost_estimate=pl.CostEstimate(flops=flops, bytes_accessed=moved, transcendentals=0),
    )(*args)


def dot(a, b):
    return jnp.dot(a, b, preferred_element_type=f32)


def dot_nt(a, b):
    return lax.dot_general(a, b, (((1,), (1,)), ((), ())), preferred_element_type=f32)


def pairs(count, wrap):
    first = [(i, i ^ 1) for i in range(count)]
    second = []
    for i in range(count):
        j = i + 1 if i % 2 else i - 1
        if wrap or 0 <= j < count:
            second.append((i, j % count))
    return first, second


def up16(n):
    return (n + 15) // 16 * 16


def halves(n_rows, channels):
    return pltpu.VMEM((channels // LANES, n_rows, LANES), f32)


def put(ref, start, value, step=1):
    for part in range(ref.shape[0]):
        rows = pl.ds(start, value.shape[0], stride=step if step > 1 else None)
        ref[part, rows, :] = value[:, part * LANES : (part + 1) * LANES]


def get(ref, start, count, step=1):
    rows = pl.ds(start, count, stride=step if step > 1 else None)
    return jnp.concatenate([ref[part, rows, :] for part in range(ref.shape[0])], axis=1)


def fill(ref, start, value):
    ref[start : start + value.shape[0], :] = value


def split_by_core(place, partial, keep, send):
    groups, block, _ = keep.shape
    for group in range(groups):
        mine = pl.multiple_of((2 * group + place[0]) * block, 16)
        theirs = pl.multiple_of((2 * group + 1 - place[0]) * block, 16)
        keep[group] = partial[pl.ds(mine, block), :]
        send[group] = partial[pl.ds(theirs, block), :].astype(bf16)


class Layout:
    def __init__(self, n_rows, n_cols):
        rows, cols = 2 * n_rows, 2 * n_cols
        self.cot, self.cot_2, self.skip, self.coarse = 0, rows, 2 * rows, 3 * rows
        self.face_size = up16(3 * rows + n_rows)
        self.row_cot, self.row_cot_2, self.row_skip = 0, cols, 2 * cols
        self.row_coarse, self.corner = 3 * cols, 3 * cols + n_cols
        self.band_size = self.corner + 16
        ring = (cols + 2 + 7) // 8 * 8
        self.top, self.bottom, self.left, self.right = 0, ring, 2 * ring, 2 * ring + rows
        self.ring_size = up16(2 * ring + 2 * rows)
        self.grad_left, self.grad_size = ring, up16(ring + rows)


COT, COT_2, SKIP, COARSE = (0, 1, 2), (3, 4, 5), (6, None, 7), (8, None, 9)


def face_message(place, coarse, skip, cot, first, second, cot_v, skip_v, coarse_v, flat, before, after, sems):
    rows, cols, _ = cot.shape
    n_rows, n_cols, _ = coarse.shape
    at = Layout(n_rows, n_cols)
    copies = [
        pltpu.make_async_copy(source, target, sems.at[i])
        for i, (source, target) in enumerate(((cot, cot_v), (skip, skip_v), (coarse, coarse_v)))
    ]
    for copy in copies:
        copy.start()
    before[...] = jnp.zeros_like(before)
    after[...] = jnp.zeros_like(after)
    copies[0].wait()
    put(flat, 0, cot_v[...].reshape(rows * cols, -1).astype(f32))
    fill(before, at.cot, get(flat, 0, rows, cols))
    fill(after, at.cot, get(flat, cols - 1, rows, cols))
    fill(after, at.cot_2, get(flat, cols - 2, rows, cols))
    copies[1].wait()
    put(flat, 0, skip_v[...].reshape(rows * cols, -1).astype(f32))
    fill(before, at.skip, get(flat, 0, rows, cols))
    fill(after, at.skip, get(flat, cols - 1, rows, cols))
    copies[2].wait()
    put(flat, 0, coarse_v[...].reshape(n_rows * n_cols, -1).astype(f32))
    fill(before, at.coarse, get(flat, 0, n_rows, n_cols))
    fill(after, at.coarse, get(flat, n_cols - 1, n_rows, n_cols))
    even = place[0] == 0
    first[...] = jnp.where(even, after[...], before[...]).astype(bf16)
    second[...] = jnp.where(even, before[...], after[...]).astype(bf16)


def band_message(place, coarse, skip, cot, got_first, got_second, first, second, left, right, before, after):
    rows, cols, channels = cot.shape
    n_rows, n_cols, _ = coarse.shape
    at = Layout(n_rows, n_cols)
    even = place[0] == 0
    one, two = got_first[...].astype(f32), got_second[...].astype(f32)
    left[...] = jnp.where(even, two, one)
    right[...] = jnp.where(even, one, two)
    for message, row, row_2, cell in ((before, 0, None, 0), (after, rows - 1, rows - 2, n_rows - 1)):
        fill(message, at.row_cot, cot[row].astype(f32))
        if row_2 is None:
            fill(message, at.row_cot_2, jnp.zeros((cols, channels), f32))
        else:
            fill(message, at.row_cot_2, cot[row_2].astype(f32))
        fill(message, at.row_skip, skip[row].astype(f32))
        fill(message, at.row_coarse, coarse[cell].astype(f32))
        fill(message, at.corner, jnp.zeros((16, channels), f32))
        corners = [
            (COT[0], left, at.cot + row), (COT[1], left, at.cot_2 + row), (COT[2], right, at.cot + row),
            (SKIP[0], left, at.skip + row), (SKIP[2], right, at.skip + row),
            (COARSE[0], left, at.coarse + cell), (COARSE[2], right, at.coarse + cell),
        ]
        if row_2 is not None:
            corners += [
                (COT_2[0], left, at.cot + row_2), (COT_2[1], left, at.cot_2 + row_2),
                (COT_2[2], right, at.cot + row_2),
            ]
        for corner, side, source in corners:
            fill(message, at.corner + corner, side[source : source + 1, :])
    even = lax.rem(place[2], 2) == 0
    first[...] = jnp.where(even, after[...], before[...]).astype(bf16)
    second[...] = jnp.where(even, before[...], after[...]).astype(bf16)


def act_kernel(
    place, coarse, skip, cot, left, right, got_first, got_second, up_w, conv_w,
    shifted, near, act, slope, keep, send, upper, lower, conv_v, padded, pre, partial, sem,
):
    n_rows, n_cols, channels = coarse.shape
    rows, cols, _ = skip.shape
    at = Layout(n_rows, n_cols)
    stride = cols + 2 * MARGIN
    copy = pltpu.make_async_copy(conv_w, conv_v, sem)
    copy.start()
    even = lax.rem(place[2], 2) == 0
    one, two = got_first[...].astype(f32), got_second[...].astype(f32)
    upper[...] = jnp.where(even, two, one)
    lower[...] = jnp.where(even, one, two)
    for row in range(n_rows):
        near[0, row] = coarse[row]
        put(padded, row * stride, coarse[row].astype(f32))
    below = lower[at.row_coarse : at.row_coarse + n_cols, :]
    near[0, n_rows] = below.astype(bf16)
    put(padded, n_rows * stride, below)
    put(padded, n_cols, right[at.coarse : at.coarse + n_rows, :], stride)
    corner = at.corner + COARSE[2]
    put(padded, n_rows * stride + n_cols, lower[corner : corner + 1, :])
    for row in range(n_rows + 1):
        near[1, row] = get(padded, row * stride + 1, n_cols).astype(bf16)
    for row in range(n_rows + 1, near.shape[1]):
        for side in range(2):
            near[side, row] = jnp.zeros((n_cols, channels), bf16)
    put(padded, MARGIN, upper[at.row_cot : at.row_cot + cols, :])
    put(padded, (rows + 1) * stride + MARGIN, lower[at.row_cot : at.row_cot + cols, :])
    for row in range(rows):
        put(padded, (row + 1) * stride + MARGIN, cot[row].astype(f32))
    put(padded, stride + MARGIN - 1, left[at.cot : at.cot + rows, :], stride)
    put(padded, stride + MARGIN + cols, right[at.cot : at.cot + rows, :], stride)
    for row, message in ((0, upper), (rows + 1, lower)):
        for col, corner in ((-1, at.corner + COT[0]), (cols, at.corner + COT[2])):
            put(padded, row * stride + MARGIN + col, message[corner : corner + 1, :])
    for row in range(rows + 2):
        for shift in (0, 2):
            start = row * stride + MARGIN - 1 + shift
            shifted[shift, row] = get(padded, start, cols).astype(bf16)
    shifted[1, 0] = upper[at.row_cot : at.row_cot + cols, :].astype(bf16)
    shifted[1, rows + 1] = lower[at.row_cot : at.row_cot + cols, :].astype(bf16)
    for row in range(rows):
        shifted[1, row + 1] = cot[row]
    sums = {}
    for k in range(3):
        row_phase, row_off = forward_taps[k]
        for l in range(3):
            col_phase, col_off = forward_taps[l]
            source = near[col_off, pl.ds(row_off, n_rows)].reshape(n_rows * n_cols, channels)
            term = dot(source, up_w[k, l])
            name = (row_phase, col_phase)
            sums[name] = sums[name] + term if name in sums else term
    for (row_phase, col_phase), total in sums.items():
        for row in range(n_rows):
            start = (2 * row + row_phase) * cols + col_phase
            put(pre, start, total[row * n_cols : (row + 1) * n_cols], 2)
    preact = get(pre, 0, rows * cols) + skip[...].reshape(rows * cols, channels).astype(f32)
    sigma = jax.nn.sigmoid(preact)
    value = preact * sigma
    slope[...] = sigma + value * (1.0 - sigma)
    act_flat = value.astype(bf16)
    act[...] = act_flat.reshape(act.shape)
    act_t = act_flat.T
    for k in range(3):
        for l in range(3):
            source = shifted[2 - l, pl.ds(2 - k, rows)].reshape(-1, channels)
            partial[pl.ds((3 * k + l) * channels, channels), :] = dot(act_t, source)
    split_by_core(place, partial, keep, send)
    copy.wait()


def grad_kernel(shifted, slope, conv_w, phases, fine):
    rows, cols = shifted.shape[1] - 2, shifted.shape[2]
    channels = shifted.shape[3]
    n_rows, n_cols = rows // 2, cols // 2
    total = jnp.zeros((rows * cols, channels), f32)
    for k in range(3):
        for l in range(3):
            source = shifted[2 - l, pl.ds(2 - k, rows)].reshape(-1, channels)
            total = total + dot_nt(source, conv_w[k, l])
    put(fine, 0, (total * slope[...]).astype(bf16).astype(f32))
    whole = phases.shape[2]
    for row_phase in range(2):
        for col_phase in range(2):
            for row in range(n_rows):
                start = (2 * row + row_phase) * cols + col_phase
                phases[row_phase, col_phase, row] = get(fine, start, n_cols, 2).astype(bf16)
            for row in range(n_rows, whole):
                phases[row_phase, col_phase, row] = jnp.zeros((n_cols, channels), bf16)


def up_kernel(place, near, phases, keep, send, partial):
    _, _, whole, n_cols, channels = phases.shape
    turned = {}
    for row_off in range(2):
        for col_off in range(2):
            cells = near[col_off, pl.ds(row_off, whole)]
            turned[row_off, col_off] = cells.reshape(whole * n_cols, channels).T
    for k in range(3):
        row_phase, row_off = forward_taps[k]
        for l in range(3):
            col_phase, col_off = forward_taps[l]
            source = phases[row_phase, col_phase].reshape(whole * n_cols, channels)
            partial[pl.ds((3 * k + l) * channels, channels), :] = dot(
                turned[row_off, col_off], source
            )
    split_by_core(place, partial, keep, send)


def out_kernel(
    place, coarse, cot, act, phases, left, right, upper, lower, conv_w, up_w,
    decoded, coarse_out, padded, shifted, moved, ring, wide,
):
    rows, cols, channels = act.shape
    n_rows, n_cols = rows // 2, cols // 2
    at = Layout(n_rows, n_cols)
    stride, step = cols + 2 * MARGIN, n_cols + 2 * MARGIN
    has_upper, has_lower = place[2] > 0, place[2] < place[3] - 1

    def corner(message, which):
        return message[at.corner + which : at.corner + which + 1, :]

    def cell(i, j):
        return (i + 1) * step + MARGIN + j

    for row in range(n_rows):
        put(wide, cell(row, 0), coarse[row].astype(f32))
    for row, message in ((-1, upper), (n_rows, lower)):
        put(wide, cell(row, 0), message[at.row_coarse : at.row_coarse + n_cols, :])
        put(wide, cell(row, -1), corner(message, COARSE[0]))
        put(wide, cell(row, n_cols), corner(message, COARSE[2]))
    put(wide, cell(0, -1), left[at.coarse : at.coarse + n_rows, :], step)
    put(wide, cell(0, n_cols), right[at.coarse : at.coarse + n_rows, :], step)
    total = jnp.zeros((at.ring_size, channels), f32)
    for k in range(3):
        for l in range(3):
            put(ring, 0, jnp.zeros((at.ring_size, channels), f32))
            for base, i in ((at.bottom, n_rows),) if k == 1 else ((at.top, k // 2 * -1),):
                start = cell(i, -1 if l == 2 else 0)
                put(ring, base + (l == 1), get(wide, start, n_cols + 1), 2)
            base, j = (at.right, n_cols) if l == 1 else (at.left, -(l // 2))
            start = cell(1 if k == 0 else 0, j)
            put(ring, base + (k != 1), get(wide, start, n_rows, step), 2)
            total = total + dot(get(ring, 0, at.ring_size).astype(bf16), up_w[k, l])
    put(ring, 0, jnp.zeros((at.ring_size, channels), f32))
    for base, message in ((at.top, upper), (at.bottom, lower)):
        put(ring, base + 1, message[at.row_skip : at.row_skip + cols, :])
        put(ring, base, corner(message, SKIP[0]))
        put(ring, base + cols + 1, corner(message, SKIP[2]))
    put(ring, at.left, left[at.skip : at.skip + rows, :])
    put(ring, at.right, right[at.skip : at.skip + rows, :])
    preact = total + get(ring, 0, at.ring_size)
    sigma = jax.nn.sigmoid(preact)
    value = preact * sigma
    slope = sigma + value * (1.0 - sigma)
    value = value.astype(bf16).astype(f32)
    for row in range(rows):
        put(padded, (row + 1) * stride + MARGIN, act[row].astype(f32))
    for row, base, exists in ((0, at.top, has_upper), (rows + 1, at.bottom, has_lower)):
        strip = value[base : base + cols + 2]
        put(padded, row * stride + MARGIN - 1, jnp.where(exists, strip, 0.0))
    put(padded, stride + MARGIN - 1, value[at.left : at.left + rows], stride)
    put(padded, stride + MARGIN + cols, value[at.right : at.right + rows], stride)
    for row in range(rows + 2):
        for shift in range(3):
            start = row * stride + MARGIN - 1 + shift
            shifted[shift, row] = get(padded, start, cols).astype(bf16)
    total = jnp.zeros((rows * cols, channels), f32)
    for k in range(3):
        for l in range(3):
            source = shifted[l, pl.ds(k, rows)].reshape(-1, channels)
            total = total + dot(source, conv_w[k, l])
    decoded[...] = total.astype(bf16).reshape(decoded.shape)

    def fine(p, q):
        return (p + 2) * stride + MARGIN + q

    for row in range(rows):
        put(wide, fine(row, 0), cot[row].astype(f32))
    for row, message, start, which in (
        (-1, upper, at.row_cot, COT), (-2, upper, at.row_cot_2, COT_2), (rows, lower, at.row_cot, COT),
    ):
        put(wide, fine(row, 0), message[start : start + cols, :])
        for col, one in ((-1, which[0]), (-2, which[1]), (cols, which[2])):
            put(wide, fine(row, col), corner(message, one))
    put(wide, fine(0, -1), left[at.cot : at.cot + rows, :], stride)
    put(wide, fine(0, -2), left[at.cot_2 : at.cot_2 + rows, :], stride)
    put(wide, fine(0, cols), right[at.cot : at.cot + rows, :], stride)
    total = jnp.zeros((at.grad_size, channels), f32)
    for k in range(3):
        for l in range(3):
            put(ring, at.top, get(wide, fine(-k, -l), cols + 1))
            put(ring, at.grad_left, get(wide, fine(1 - k, -l), rows, stride))
            source = get(ring, 0, at.grad_size).astype(bf16)
            total = total + dot_nt(source, conv_w[k, l])
    strip = (total[: cols + 1] * slope[at.top : at.top + cols + 1]).astype(bf16).astype(f32)
    put(ring, at.top, jnp.where(has_upper, strip, 0.0))
    strip = total[at.grad_left : at.grad_left + rows] * slope[at.left : at.left + rows]
    put(ring, at.grad_left, strip.astype(bf16).astype(f32))
    for phase, start in ((0, 1), (1, 2), (2, 0)):
        moved[phase, 0] = get(ring, at.top + start, n_cols, 2).astype(bf16)
    for phase in range(2):
        for row in range(n_rows):
            moved[phase, 1 + row] = phases[1, phase, row]
    for row_phase in range(2):
        for row in range(n_rows):
            put(padded, row * stride + MARGIN, phases[row_phase, 1, row].astype(f32))
        put(padded, MARGIN - 1, get(ring, at.grad_left + row_phase, n_rows, 2), stride)
        for row in range(n_rows):
            cells = get(padded, row * stride + MARGIN - 1, n_cols).astype(bf16)
            if row_phase:
                moved[2, 1 + row] = cells
            else:
                moved[3, row] = cells
    total = jnp.zeros((n_rows * n_cols, channels), f32)
    for k in range(3):
        for l in range(3):
            if k == 1:
                if l == 0:
                    source = moved[3, pl.ds(0, n_rows)]
                else:
                    source = phases[0, l - 1, pl.ds(0, n_rows)]
            else:
                source = moved[(2, 0, 1)[l], pl.ds(k // 2, n_rows)]
            total = total + dot_nt(source.reshape(n_rows * n_cols, channels), up_w[k, l])
    coarse_out[...] = total.astype(bf16).reshape(coarse_out.shape)


def halving(count):
    bits = (count // 2).bit_length() - 1
    return [[(step + core) % bits for step in range(bits)] for core in range(2)]


def mask_of(slot, order):
    last = len(order) - 1
    return sum(1 << bit for step, bit in enumerate(order) if slot >> (last - step) & 1)


def core_kernel(place, keep, got, own, message):
    slots, half = keep.shape[0], own.shape[0]
    even, odd = halving(2 * slots)
    for slot in range(slots):
        chip = place[1] ^ jnp.where(place[0] == 0, mask_of(slot, even), mask_of(slot, odd))
        total = keep[chip] + got[chip].astype(f32)
        if slot < half:
            own[slot] = total
        else:
            message[slot - half] = total.astype(bf16)


def plane_kernel(before, got, own, message):
    half = own.shape[0]
    for slot in range(2 * half):
        total = before[slot] + got[slot].astype(f32)
        if slot < half:
            own[slot] = total
        else:
            message[slot - half] = total.astype(bf16)


def band_kernel(place, conv, got_conv, up, got_up, own, *refs):
    n_bands, messages, cut = len(refs), refs[:-1], refs[-1]
    conv_total = conv[0] + got_conv[0].astype(f32)
    up_total = up[0] + got_up[0].astype(f32)
    cols = conv_total.shape[1] // n_bands
    for band in range(n_bands):
        cut[band, :, :cols] = conv_total[:, band * cols : (band + 1) * cols]
        cut[band, :, cols:] = up_total[:, band * cols : (band + 1) * cols]
    own[...] = cut[place[2]]
    for k, message in enumerate(messages):
        message[...] = cut[place[2] ^ (k + 1)].astype(bf16)


def last_kernel(own, *refs):
    peers, (conv, up) = refs[:-2], refs[-2:]
    total = own[...]
    for peer in peers:
        total = total + peer[...].astype(f32)
    turned = total.T
    conv[...] = turned[: conv.shape[0]]
    up[...] = turned[conv.shape[0] :]


def xor_pairs(count, bits):
    return [(i, i ^ bits) for i in range(count)]


def core_sum(place, keep, send):
    groups, block, channels = keep.shape
    got = lax.ppermute(send, "face", xor_pairs(lax.axis_size("face"), 1))
    shape = (groups // 2, block, channels)
    return kernel_call(core_kernel, [sds(shape, f32), sds(shape, bf16)], [], 0, place, keep, got)


def plane_swap(message, step):
    faces = lax.axis_size("face")
    orders = halving(faces)
    return lax.ppermute(message, "face", [(i, i ^ 2 << orders[i % 2][step]) for i in range(faces)])


def plane_sum(own, got):
    half, block, channels = own.shape
    shape = (half // 2, block, channels)
    return kernel_call(plane_kernel, [sds(shape, f32), sds(shape, bf16)], [], 0, own, got)


def band_sum(place, conv, got_conv, up, got_up):
    bands = lax.axis_size("band")
    _, block, channels = conv.shape
    cols = channels // bands
    shape = (block, 2 * cols)
    own, *messages = kernel_call(
        band_kernel, [sds(shape, f32)] + [sds(shape, bf16)] * (bands - 1),
        [pltpu.VMEM((bands,) + shape, f32)], 0, place, conv, got_conv, up, got_up,
    )
    got = [lax.ppermute(messages[k - 1], "band", xor_pairs(bands, k)) for k in range(bands - 1, 0, -1)]
    return [a.T for a in kernel_call(last_kernel, [sds((cols, block), f32)] * 2, [], 0, own, *got)]


def after(value, *others):
    return lax.optimization_barrier((value, *others))[0]


def swap(first, second, axis, wrap):
    one, two = pairs(lax.axis_size(axis), wrap)
    return lax.ppermute(first, axis, one), lax.ppermute(second, axis, two)


def local(coarse, skip, up_weight, conv_weight, cotangent):
    n_rows, n_cols, channels = coarse.shape
    rows, cols, _ = skip.shape
    at = Layout(n_rows, n_cols)
    faces, bands = lax.axis_size("face"), lax.axis_size("band")
    face, band = lax.axis_index("face"), lax.axis_index("band")
    place = jnp.stack([face % 2, face // 2, band, bands]).astype(jnp.int32)
    groups, block = faces // 2, 9 * channels // faces

    flat = halves(rows * cols, channels)
    message = sds((at.face_size, channels), bf16)
    edges = pltpu.VMEM(message.shape, f32)
    first, second, cotangent, skip, coarse = kernel_call(
        face_message,
        [message, message, sds(cotangent.shape, bf16), sds(skip.shape, bf16), sds(coarse.shape, bf16)],
        [flat, edges, edges, pltpu.SemaphoreType.DMA((3,))],
        0, place, coarse, skip, cotangent, far=(1, 2, 3),
    )
    first, second = swap(first, second, "face", True)
    side = sds(message.shape, f32)
    message = sds((at.band_size, channels), bf16)
    edges = pltpu.VMEM(message.shape, f32)
    first, second, left, right = kernel_call(
        band_message, [message, message, side, side], [edges, edges],
        0, place, coarse, skip, cotangent, first, second,
    )
    first, second = swap(first, second, "band", False)

    cells = n_rows * n_cols
    stride = cols + 2 * MARGIN
    padded = halves((rows + 2) * stride, channels)
    shift_shape = (3, rows + 2, cols, channels)
    whole = -(-cells // 256) * 256 // n_cols
    one_tap = 2 * cells * channels * channels
    partials = [sds((groups, block, channels), f32), sds((groups, block, channels), bf16)]
    partial = pltpu.VMEM((9 * channels, channels), f32)
    side = sds(message.shape, f32)
    shifted, near, act, slope, keep_conv, send_conv, upper, lower, conv_weight = kernel_call(
        act_kernel,
        [
            sds(shift_shape, bf16), sds((2, whole + 1, n_cols, channels), bf16),
            sds(skip.shape, bf16), sds((rows * cols, channels), f32), *partials, side, side,
            sds(conv_weight.shape, bf16),
        ],
        [padded, flat, partial, pltpu.SemaphoreType.DMA],
        45 * one_tap, place, coarse, skip, cotangent, left, right, first, second,
        up_weight, conv_weight, far=(9,),
    )
    own_conv, to_conv = core_sum(place, keep_conv, send_conv)
    got_conv = plane_swap(to_conv, 0)
    phases = kernel_call(
        grad_kernel,
        [sds((2, 2, whole, n_cols, channels), bf16)],
        [flat],
        0, shifted, slope, conv_weight,
    )[0]
    keep_up, send_up = kernel_call(
        up_kernel, partials, [partial], 0, place, after(near, to_conv), phases
    )
    own_up, to_up = core_sum(place, keep_up, send_up)
    got_up = plane_swap(to_up, 0)
    steps = (faces // 2).bit_length() - 1
    for step in range(1, steps):
        own_conv, to_conv = plane_sum(after(own_conv, to_up), got_conv)
        got_conv = plane_swap(to_conv, step)
        if step == 1:
            decoded, grad_coarse = kernel_call(
                out_kernel,
                [sds(skip.shape, bf16), sds(coarse.shape, bf16)],
                [
                    padded, pltpu.VMEM(shift_shape, bf16),
                    pltpu.VMEM((4, n_rows + 1, n_cols, channels), bf16),
                    halves(at.ring_size, channels), halves((rows + 3) * stride, channels),
                ],
                0, place, coarse, cotangent, after(act, to_conv), phases, left, right,
                upper, lower, conv_weight, up_weight,
            )
            own_up = after(own_up, decoded)
        own_up, to_up = plane_sum(own_up, got_up)
        got_up = plane_swap(to_up, step)
    grad_conv, grad_up = band_sum(place, own_conv, got_conv, own_up, got_up)
    return (decoded, grad_coarse, grad_up, grad_conv)


def solution(mesh):
    return jax.shard_map(
        local,
        mesh=mesh,
        in_specs=(
            P("band", "face", None),
            P("band", "face", None),
            P(),
            P(),
            P("band", "face", None),
        ),
        out_specs=(
            P("band", "face", None),
            P("band", "face", None),
            P("face", "band"),
            P("face", "band"),
        ),
        check_vma=False,
    )
```

```python
import jax
import jax.numpy as jnp
from jax import lax
from jax.experimental import pallas as pl
from jax.experimental.pallas import tpu as pltpu
from jax.sharding import PartitionSpec as P

f32, bf16 = jnp.float32, jnp.bfloat16
forward_taps = ((1, 1), (0, 0), (1, 0))
backward_taps = ((1, 0), (0, 1), (1, 1))
MARGIN = 8
LANES = 128


def sds(shape, dtype):
    return jax.ShapeDtypeStruct(shape, dtype)


def kernel_call(body, outs, scratch, flops, *args, far=()):
    vmem = pl.BlockSpec(memory_space=pltpu.VMEM)
    smem = pl.BlockSpec(memory_space=pltpu.SMEM)
    hbm = pl.BlockSpec(memory_space=pltpu.HBM)
    moved = sum(a.size * a.dtype.itemsize for a in args)
    moved += sum(a.size * a.dtype.itemsize for a in outs)
    args = [
        pltpu.with_memory_space_constraint(a, pltpu.HBM) if i in far else a
        for i, a in enumerate(args)
    ]
    return pl.pallas_call(
        body,
        out_shape=tuple(outs),
        in_specs=[
            hbm if i in far else smem if a.dtype == jnp.int32 else vmem
            for i, a in enumerate(args)
        ],
        out_specs=tuple(vmem for _ in outs),
        scratch_shapes=scratch,
        compiler_params=pltpu.CompilerParams(vmem_limit_bytes=28 * 2**20),
        cost_estimate=pl.CostEstimate(flops=flops, bytes_accessed=moved, transcendentals=0),
    )(*args)


def dot(a, b):
    return jnp.dot(a, b, preferred_element_type=f32)


def dot_nt(a, b):
    return lax.dot_general(a, b, (((1,), (1,)), ((), ())), preferred_element_type=f32)


def pairs(count, wrap):
    first = [(i, i ^ 1) for i in range(count)]
    second = []
    for i in range(count):
        j = i + 1 if i % 2 else i - 1
        if wrap or 0 <= j < count:
            second.append((i, j % count))
    return first, second


def up16(n):
    return (n + 15) // 16 * 16


def halves(n_rows, channels):
    return pltpu.VMEM((channels // LANES, n_rows, LANES), f32)


def put(ref, start, value, step=1):
    for part in range(ref.shape[0]):
        rows = pl.ds(start, value.shape[0], stride=step if step > 1 else None)
        ref[part, rows, :] = value[:, part * LANES : (part + 1) * LANES]


def get(ref, start, count, step=1):
    rows = pl.ds(start, count, stride=step if step > 1 else None)
    return jnp.concatenate([ref[part, rows, :] for part in range(ref.shape[0])], axis=1)


def fill(ref, start, value):
    ref[start : start + value.shape[0], :] = value


def other_core(place, partial, send):
    groups, block, _ = send.shape
    for group in range(groups):
        theirs = pl.multiple_of((2 * group + 1 - place[0]) * block, 16)
        send[group] = partial[pl.ds(theirs, block), :].astype(bf16)


class Layout:
    def __init__(self, n_rows, n_cols):
        rows, cols = 2 * n_rows, 2 * n_cols
        self.cot, self.cot_2, self.skip, self.coarse = 0, rows, 2 * rows, 3 * rows
        self.face_size = up16(3 * rows + n_rows)
        self.row_cot, self.row_cot_2, self.row_skip = 0, cols, 2 * cols
        self.row_coarse, self.corner = 3 * cols, 3 * cols + n_cols
        self.band_size = self.corner + 16
        ring = (cols + 2 + 7) // 8 * 8
        self.top, self.bottom, self.left, self.right = 0, ring, 2 * ring, 2 * ring + rows
        self.ring_size = up16(2 * ring + 2 * rows)
        self.grad_left, self.grad_size = ring, up16(ring + rows)


COT, COT_2, SKIP, COARSE = (0, 1, 2), (3, 4, 5), (6, None, 7), (8, None, 9)


def face_message(place, coarse, skip, cot, first, second, cot_v, skip_v, coarse_v, flat, before, after, sems):
    rows, cols, _ = cot.shape
    n_rows, n_cols, _ = coarse.shape
    at = Layout(n_rows, n_cols)
    copies = [
        pltpu.make_async_copy(source, target, sems.at[i])
        for i, (source, target) in enumerate(((cot, cot_v), (skip, skip_v), (coarse, coarse_v)))
    ]
    for copy in copies:
        copy.start()
    before[...] = jnp.zeros_like(before)
    after[...] = jnp.zeros_like(after)
    for copy, array, start, start_2 in (
        (copies[0], cot_v, at.cot, at.cot_2), (copies[1], skip_v, at.skip, None), (copies[2], coarse_v, at.coarse, None),
    ):
        copy.wait()
        n, width, channels = array.shape
        put(flat, 0, array[:, :16, :].astype(f32)[:, :8, :].reshape(n * 8, channels))
        put(flat, n * 8, array[:, width - 16 :, :].astype(f32)[:, 8:, :].reshape(n * 8, channels))
        fill(before, start, get(flat, 0, n, 8))
        fill(after, start, get(flat, n * 8 + 7, n, 8))
        if start_2 is not None:
            fill(after, start_2, get(flat, n * 8 + 6, n, 8))
    even = place[0] == 0
    first[...] = jnp.where(even, after[...], before[...]).astype(bf16)
    second[...] = jnp.where(even, before[...], after[...]).astype(bf16)


def band_message(place, coarse, skip, cot, got_first, got_second, first, second, left, right, before, after):
    rows, cols, channels = cot.shape
    n_rows, n_cols, _ = coarse.shape
    at = Layout(n_rows, n_cols)
    even = place[0] == 0
    one, two = got_first[...].astype(f32), got_second[...].astype(f32)
    left[...] = jnp.where(even, two, one)
    right[...] = jnp.where(even, one, two)
    for message, row, row_2, cell in ((before, 0, None, 0), (after, rows - 1, rows - 2, n_rows - 1)):
        fill(message, at.row_cot, cot[row].astype(f32))
        if row_2 is None:
            fill(message, at.row_cot_2, jnp.zeros((cols, channels), f32))
        else:
            fill(message, at.row_cot_2, cot[row_2].astype(f32))
        fill(message, at.row_skip, skip[row].astype(f32))
        fill(message, at.row_coarse, coarse[cell].astype(f32))
        fill(message, at.corner, jnp.zeros((16, channels), f32))
        corners = [
            (COT[0], left, at.cot + row), (COT[1], left, at.cot_2 + row), (COT[2], right, at.cot + row),
            (SKIP[0], left, at.skip + row), (SKIP[2], right, at.skip + row),
            (COARSE[0], left, at.coarse + cell), (COARSE[2], right, at.coarse + cell),
        ]
        if row_2 is not None:
            corners += [
                (COT_2[0], left, at.cot + row_2), (COT_2[1], left, at.cot_2 + row_2),
                (COT_2[2], right, at.cot + row_2),
            ]
        for corner, side, source in corners:
            fill(message, at.corner + corner, side[source : source + 1, :])
    even = lax.rem(place[2], 2) == 0
    first[...] = jnp.where(even, after[...], before[...]).astype(bf16)
    second[...] = jnp.where(even, before[...], after[...]).astype(bf16)


def act_kernel(
    place, coarse, skip, cot, left, right, got_first, got_second, up_w, conv_w,
    shifted, near, act, slope, partial, send, upper, lower, conv_v, padded, pre, sem,
):
    n_rows, n_cols, channels = coarse.shape
    rows, cols, _ = skip.shape
    at = Layout(n_rows, n_cols)
    stride = cols + 2 * MARGIN
    copy = pltpu.make_async_copy(conv_w, conv_v, sem)
    copy.start()
    even = lax.rem(place[2], 2) == 0
    one, two = got_first[...].astype(f32), got_second[...].astype(f32)
    upper[...] = jnp.where(even, two, one)
    lower[...] = jnp.where(even, one, two)
    for row in range(n_rows):
        near[0, row] = coarse[row]
        put(padded, row * stride, coarse[row].astype(f32))
    below = lower[at.row_coarse : at.row_coarse + n_cols, :]
    near[0, n_rows] = below.astype(bf16)
    put(padded, n_rows * stride, below)
    put(padded, n_cols, right[at.coarse : at.coarse + n_rows, :], stride)
    corner = at.corner + COARSE[2]
    put(padded, n_rows * stride + n_cols, lower[corner : corner + 1, :])
    for row in range(n_rows + 1):
        near[1, row] = get(padded, row * stride + 1, n_cols).astype(bf16)
    for row in range(n_rows + 1, near.shape[1]):
        for side in range(2):
            near[side, row] = jnp.zeros((n_cols, channels), bf16)
    put(padded, MARGIN, upper[at.row_cot : at.row_cot + cols, :])
    put(padded, (rows + 1) * stride + MARGIN, lower[at.row_cot : at.row_cot + cols, :])
    for row in range(rows):
        put(padded, (row + 1) * stride + MARGIN, cot[row].astype(f32))
    put(padded, stride + MARGIN - 1, left[at.cot : at.cot + rows, :], stride)
    put(padded, stride + MARGIN + cols, right[at.cot : at.cot + rows, :], stride)
    for row, message in ((0, upper), (rows + 1, lower)):
        for col, corner in ((-1, at.corner + COT[0]), (cols, at.corner + COT[2])):
            put(padded, row * stride + MARGIN + col, message[corner : corner + 1, :])
    for row in range(rows + 2):
        for shift in (0, 2):
            start = row * stride + MARGIN - 1 + shift
            shifted[shift, row] = get(padded, start, cols).astype(bf16)
    shifted[1, 0] = upper[at.row_cot : at.row_cot + cols, :].astype(bf16)
    shifted[1, rows + 1] = lower[at.row_cot : at.row_cot + cols, :].astype(bf16)
    for row in range(rows):
        shifted[1, row + 1] = cot[row]
    sums = {}
    for k in range(3):
        row_phase, row_off = forward_taps[k]
        for l in range(3):
            col_phase, col_off = forward_taps[l]
            source = near[col_off, pl.ds(row_off, n_rows)].reshape(n_rows * n_cols, channels)
            term = dot(source, up_w[k, l])
            name = (row_phase, col_phase)
            sums[name] = sums[name] + term if name in sums else term
    for (row_phase, col_phase), total in sums.items():
        for row in range(n_rows):
            start = (2 * row + row_phase) * cols + col_phase
            put(pre, start, total[row * n_cols : (row + 1) * n_cols], 2)
    preact = get(pre, 0, rows * cols) + skip[...].reshape(rows * cols, channels).astype(f32)
    sigma = jax.nn.sigmoid(preact)
    value = preact * sigma
    slope[...] = sigma + value * (1.0 - sigma)
    act_flat = value.astype(bf16)
    act[...] = act_flat.reshape(act.shape)
    act_t = act_flat.T
    for k in range(3):
        for l in range(3):
            source = shifted[2 - l, pl.ds(2 - k, rows)].reshape(-1, channels)
            partial[pl.ds((3 * k + l) * channels, channels), :] = dot(act_t, source)
    other_core(place, partial, send)
    copy.wait()


def grad_kernel(shifted, slope, conv_w, phases, fine):
    rows, cols = shifted.shape[1] - 2, shifted.shape[2]
    channels = shifted.shape[3]
    n_rows, n_cols = rows // 2, cols // 2
    total = jnp.zeros((rows * cols, channels), f32)
    for k in range(3):
        for l in range(3):
            source = shifted[2 - l, pl.ds(2 - k, rows)].reshape(-1, channels)
            total = total + dot_nt(source, conv_w[k, l])
    put(fine, 0, (total * slope[...]).astype(bf16).astype(f32))
    whole = phases.shape[2]
    for row_phase in range(2):
        for col_phase in range(2):
            for row in range(n_rows):
                start = (2 * row + row_phase) * cols + col_phase
                phases[row_phase, col_phase, row] = get(fine, start, n_cols, 2).astype(bf16)
            for row in range(n_rows, whole):
                phases[row_phase, col_phase, row] = jnp.zeros((n_cols, channels), bf16)


def up_kernel(place, near, phases, partial, send):
    _, _, whole, n_cols, channels = phases.shape
    turned = {}
    for row_off in range(2):
        for col_off in range(2):
            cells = near[col_off, pl.ds(row_off, whole)]
            turned[row_off, col_off] = cells.reshape(whole * n_cols, channels).T
    for k in range(3):
        row_phase, row_off = forward_taps[k]
        for l in range(3):
            col_phase, col_off = forward_taps[l]
            source = phases[row_phase, col_phase].reshape(whole * n_cols, channels)
            partial[pl.ds((3 * k + l) * channels, channels), :] = dot(
                turned[row_off, col_off], source
            )
    other_core(place, partial, send)


def ring_kernel(
    place, coarse, cot, left, right, upper, lower, conv_w, up_w, ring_act, ring_grad, ring, wide,
):
    rows, cols, channels = cot.shape
    n_rows, n_cols = rows // 2, cols // 2
    at = Layout(n_rows, n_cols)
    stride, step = cols + 2 * MARGIN, n_cols + 2 * MARGIN
    has_upper, has_lower = place[2] > 0, place[2] < place[3] - 1

    def corner(message, which):
        return message[at.corner + which : at.corner + which + 1, :]

    def cell(i, j):
        return (i + 1) * step + MARGIN + j

    for row in range(n_rows):
        put(wide, cell(row, 0), coarse[row].astype(f32))
    for row, message in ((-1, upper), (n_rows, lower)):
        put(wide, cell(row, 0), message[at.row_coarse : at.row_coarse + n_cols, :])
        put(wide, cell(row, -1), corner(message, COARSE[0]))
        put(wide, cell(row, n_cols), corner(message, COARSE[2]))
    put(wide, cell(0, -1), left[at.coarse : at.coarse + n_rows, :], step)
    put(wide, cell(0, n_cols), right[at.coarse : at.coarse + n_rows, :], step)
    total = jnp.zeros((at.ring_size, channels), f32)
    for k in range(3):
        for l in range(3):
            put(ring, 0, jnp.zeros((at.ring_size, channels), f32))
            for base, i in ((at.bottom, n_rows),) if k == 1 else ((at.top, k // 2 * -1),):
                start = cell(i, -1 if l == 2 else 0)
                put(ring, base + (l == 1), get(wide, start, n_cols + 1), 2)
            base, j = (at.right, n_cols) if l == 1 else (at.left, -(l // 2))
            start = cell(1 if k == 0 else 0, j)
            put(ring, base + (k != 1), get(wide, start, n_rows, step), 2)
            total = total + dot(get(ring, 0, at.ring_size).astype(bf16), up_w[k, l])
    put(ring, 0, jnp.zeros((at.ring_size, channels), f32))
    for base, message in ((at.top, upper), (at.bottom, lower)):
        put(ring, base + 1, message[at.row_skip : at.row_skip + cols, :])
        put(ring, base, corner(message, SKIP[0]))
        put(ring, base + cols + 1, corner(message, SKIP[2]))
    put(ring, at.left, left[at.skip : at.skip + rows, :])
    put(ring, at.right, right[at.skip : at.skip + rows, :])
    preact = total + get(ring, 0, at.ring_size)
    sigma = jax.nn.sigmoid(preact)
    value = preact * sigma
    slope = sigma + value * (1.0 - sigma)
    value = value.astype(bf16).astype(f32)
    ring_act[...] = value
    for base, exists in ((at.top, has_upper), (at.bottom, has_lower)):
        strip = value[base : base + cols + 2]
        ring_act[base : base + cols + 2, :] = jnp.where(exists, strip, 0.0)

    def fine(p, q):
        return (p + 2) * stride + MARGIN + q

    for row in range(rows):
        put(wide, fine(row, 0), cot[row].astype(f32))
    for row, message, start, which in (
        (-1, upper, at.row_cot, COT), (-2, upper, at.row_cot_2, COT_2), (rows, lower, at.row_cot, COT),
    ):
        put(wide, fine(row, 0), message[start : start + cols, :])
        for col, one in ((-1, which[0]), (-2, which[1]), (cols, which[2])):
            put(wide, fine(row, col), corner(message, one))
    put(wide, fine(0, -1), left[at.cot : at.cot + rows, :], stride)
    put(wide, fine(0, -2), left[at.cot_2 : at.cot_2 + rows, :], stride)
    put(wide, fine(0, cols), right[at.cot : at.cot + rows, :], stride)
    total = jnp.zeros((at.grad_size, channels), f32)
    for k in range(3):
        for l in range(3):
            put(ring, at.top, get(wide, fine(-k, -l), cols + 1))
            put(ring, at.grad_left, get(wide, fine(1 - k, -l), rows, stride))
            source = get(ring, 0, at.grad_size).astype(bf16)
            total = total + dot_nt(source, conv_w[k, l])
    strip = (total[: cols + 1] * slope[at.top : at.top + cols + 1]).astype(bf16).astype(f32)
    put(ring_grad, at.top, jnp.where(has_upper, strip, 0.0))
    strip = total[at.grad_left : at.grad_left + rows] * slope[at.left : at.left + rows]
    put(ring_grad, at.grad_left, strip.astype(bf16).astype(f32))


def decoded_kernel(act, ring_act, conv_w, decoded, padded, shifted):
    rows, cols, channels = act.shape
    at = Layout(rows // 2, cols // 2)
    stride = cols + 2 * MARGIN
    for row in range(rows):
        put(padded, (row + 1) * stride + MARGIN, act[row].astype(f32))
    for row, base in ((0, at.top), (rows + 1, at.bottom)):
        put(padded, row * stride + MARGIN - 1, ring_act[base : base + cols + 2, :])
    put(padded, stride + MARGIN - 1, ring_act[at.left : at.left + rows, :], stride)
    put(padded, stride + MARGIN + cols, ring_act[at.right : at.right + rows, :], stride)
    for row in range(rows + 2):
        for shift in range(3):
            start = row * stride + MARGIN - 1 + shift
            shifted[shift, row] = get(padded, start, cols).astype(bf16)
    total = jnp.zeros((rows * cols, channels), f32)
    for k in range(3):
        for l in range(3):
            source = shifted[l, pl.ds(k, rows)].reshape(-1, channels)
            total = total + dot(source, conv_w[k, l])
    decoded[...] = total.astype(bf16).reshape(decoded.shape)

def coarse_kernel(phases, ring_grad, up_w, coarse_out, padded, moved):
    n_rows, n_cols, channels = coarse_out.shape
    at = Layout(n_rows, n_cols)
    stride = n_cols + 2 * MARGIN
    for phase, start in ((0, 1), (1, 2), (2, 0)):
        moved[phase, 0] = get(ring_grad, at.top + start, n_cols, 2).astype(bf16)
    for phase in range(2):
        for row in range(n_rows):
            moved[phase, 1 + row] = phases[1, phase, row]
    for row_phase in range(2):
        for row in range(n_rows):
            put(padded, row * stride + MARGIN, phases[row_phase, 1, row].astype(f32))
        put(padded, MARGIN - 1, get(ring_grad, at.grad_left + row_phase, n_rows, 2), stride)
        for row in range(n_rows):
            cells = get(padded, row * stride + MARGIN - 1, n_cols).astype(bf16)
            if row_phase:
                moved[2, 1 + row] = cells
            else:
                moved[3, row] = cells
    total = jnp.zeros((n_rows * n_cols, channels), f32)
    for k in range(3):
        for l in range(3):
            if k == 1:
                if l == 0:
                    source = moved[3, pl.ds(0, n_rows)]
                else:
                    source = phases[0, l - 1, pl.ds(0, n_rows)]
            else:
                source = moved[(2, 0, 1)[l], pl.ds(k // 2, n_rows)]
            total = total + dot_nt(source.reshape(n_rows * n_cols, channels), up_w[k, l])
    coarse_out[...] = total.astype(bf16).reshape(coarse_out.shape)


def halving(count):
    bits = (count // 2).bit_length() - 1
    return [[(step + core) % bits for step in range(bits)] for core in range(2)]


def mask_of(slot, order):
    last = len(order) - 1
    return sum(1 << bit for step, bit in enumerate(order) if slot >> (last - step) & 1)


def core_kernel(place, partial, got, own, message):
    slots, half, block = got.shape[0], own.shape[0], got.shape[1]
    even, odd = halving(2 * slots)
    for slot in range(slots):
        chip = place[1] ^ jnp.where(place[0] == 0, mask_of(slot, even), mask_of(slot, odd))
        mine = pl.multiple_of((2 * chip + place[0]) * block, 16)
        total = partial[pl.ds(mine, block), :] + got[chip].astype(f32)
        if slot < half:
            own[slot] = total
        else:
            message[slot - half] = total.astype(bf16)


def plane_kernel(before, got, own, message):
    half = own.shape[0]
    for slot in range(2 * half):
        total = before[slot] + got[slot].astype(f32)
        if slot < half:
            own[slot] = total
        else:
            message[slot - half] = total.astype(bf16)


def band_kernel(place, conv, got_conv, up, got_up, own, *refs):
    n_bands, messages, cut = len(refs), refs[:-1], refs[-1]
    conv_total = conv[0] + got_conv[0].astype(f32)
    up_total = up[0] + got_up[0].astype(f32)
    cols = conv_total.shape[1] // n_bands
    for band in range(n_bands):
        cut[band, :, :cols] = conv_total[:, band * cols : (band + 1) * cols]
        cut[band, :, cols:] = up_total[:, band * cols : (band + 1) * cols]
    own[...] = cut[place[2]]
    for k, message in enumerate(messages):
        message[...] = cut[place[2] ^ (k + 1)].astype(bf16)


def last_kernel(own, *refs):
    peers, (conv, up) = refs[:-2], refs[-2:]
    total = own[...]
    for peer in peers:
        total = total + peer[...].astype(f32)
    turned = total.T
    conv[...] = turned[: conv.shape[0]]
    up[...] = turned[conv.shape[0] :]


def xor_pairs(count, bits):
    return [(i, i ^ bits) for i in range(count)]


def core_sum(place, partial, send):
    groups, block, channels = send.shape
    got = lax.ppermute(send, "face", xor_pairs(lax.axis_size("face"), 1))
    shape = (groups // 2, block, channels)
    return kernel_call(core_kernel, [sds(shape, f32), sds(shape, bf16)], [], 0, place, partial, got)


def plane_swap(message, step):
    faces = lax.axis_size("face")
    orders = halving(faces)
    return lax.ppermute(message, "face", [(i, i ^ 2 << orders[i % 2][step]) for i in range(faces)])


def plane_sum(own, got):
    half, block, channels = own.shape
    shape = (half // 2, block, channels)
    return kernel_call(plane_kernel, [sds(shape, f32), sds(shape, bf16)], [], 0, own, got)


def band_sum(place, conv, got_conv, up, got_up):
    bands = lax.axis_size("band")
    _, block, channels = conv.shape
    cols = channels // bands
    shape = (block, 2 * cols)
    own, *messages = kernel_call(
        band_kernel, [sds(shape, f32)] + [sds(shape, bf16)] * (bands - 1),
        [pltpu.VMEM((bands,) + shape, f32)], 0, place, conv, got_conv, up, got_up,
    )
    got = [lax.ppermute(messages[k - 1], "band", xor_pairs(bands, k)) for k in range(bands - 1, 0, -1)]
    return [a.T for a in kernel_call(last_kernel, [sds((cols, block), f32)] * 2, [], 0, own, *got)]


def after(value, *others):
    return lax.optimization_barrier((value, *others))[0]


def swap(first, second, axis, wrap):
    one, two = pairs(lax.axis_size(axis), wrap)
    return lax.ppermute(first, axis, one), lax.ppermute(second, axis, two)


def local(coarse, skip, up_weight, conv_weight, cotangent):
    n_rows, n_cols, channels = coarse.shape
    rows, cols, _ = skip.shape
    at = Layout(n_rows, n_cols)
    faces, bands = lax.axis_size("face"), lax.axis_size("band")
    face, band = lax.axis_index("face"), lax.axis_index("band")
    place = jnp.stack([face % 2, face // 2, band, bands]).astype(jnp.int32)
    groups, block = faces // 2, 9 * channels // faces

    flat = halves(rows * cols, channels)
    message = sds((at.face_size, channels), bf16)
    edges = pltpu.VMEM(message.shape, f32)
    first, second, cotangent, skip, coarse = kernel_call(
        face_message,
        [message, message, sds(cotangent.shape, bf16), sds(skip.shape, bf16), sds(coarse.shape, bf16)],
        [flat, edges, edges, pltpu.SemaphoreType.DMA((3,))],
        0, place, coarse, skip, cotangent, far=(1, 2, 3),
    )
    first, second = swap(first, second, "face", True)
    side = sds(message.shape, f32)
    message = sds((at.band_size, channels), bf16)
    edges = pltpu.VMEM(message.shape, f32)
    first, second, left, right = kernel_call(
        band_message, [message, message, side, side], [edges, edges],
        0, place, coarse, skip, cotangent, first, second,
    )
    first, second = swap(first, second, "band", False)

    cells = n_rows * n_cols
    stride = cols + 2 * MARGIN
    padded = halves((rows + 2) * stride, channels)
    shift_shape = (3, rows + 2, cols, channels)
    whole = -(-cells // 256) * 256 // n_cols
    one_tap = 2 * cells * channels * channels
    partials = [sds((9 * channels, channels), f32), sds((groups, block, channels), bf16)]
    side = sds(message.shape, f32)
    shifted, near, act, slope, part_conv, send_conv, upper, lower, conv_weight = kernel_call(
        act_kernel,
        [
            sds(shift_shape, bf16), sds((2, whole + 1, n_cols, channels), bf16),
            sds(skip.shape, bf16), sds((rows * cols, channels), f32), *partials, side, side,
            sds(conv_weight.shape, bf16),
        ],
        [padded, flat, pltpu.SemaphoreType.DMA],
        45 * one_tap, place, coarse, skip, cotangent, left, right, first, second,
        up_weight, conv_weight, far=(9,),
    )
    own_conv, to_conv = core_sum(place, part_conv, send_conv)
    got_conv = plane_swap(to_conv, 0)
    phases = kernel_call(
        grad_kernel,
        [sds((2, 2, whole, n_cols, channels), bf16)],
        [flat],
        0, shifted, slope, conv_weight,
    )[0]
    part_up, send_up = kernel_call(
        up_kernel, partials, [], 0, place, after(near, to_conv), phases
    )
    own_up, to_up = core_sum(place, part_up, send_up)
    got_up = plane_swap(to_up, 0)
    ring_act, ring_grad = kernel_call(
        ring_kernel,
        [
            sds((at.ring_size, channels), f32),
            sds((channels // LANES, at.grad_size, LANES), f32),
        ],
        [halves(at.ring_size, channels), halves((rows + 3) * stride, channels)],
        0, place, coarse, cotangent, after(left, to_up), right, upper, lower, conv_weight, up_weight,
    )
    own_conv = after(own_conv, ring_act)
    steps = (faces // 2).bit_length() - 1
    for step in range(1, steps):
        own_conv, to_conv = plane_sum(own_conv, got_conv)
        got_conv = plane_swap(to_conv, step)
        if step == 1:
            decoded = kernel_call(
                decoded_kernel, [sds(skip.shape, bf16)], [padded, pltpu.VMEM(shift_shape, bf16)],
                0, act, after(ring_act, to_conv), conv_weight,
            )[0]
            own_up = after(own_up, decoded)
        own_up, to_up = plane_sum(own_up, got_up)
        got_up = plane_swap(to_up, step)
        if step == 1:
            grad_coarse = kernel_call(
                coarse_kernel, [sds(coarse.shape, bf16)],
                [
                    halves(n_rows * (n_cols + 2 * MARGIN), channels),
                    pltpu.VMEM((4, n_rows + 1, n_cols, channels), bf16),
                ],
                0, phases, after(ring_grad, to_up), up_weight,
            )[0]
            own_up = after(own_up, grad_coarse)
    grad_conv, grad_up = band_sum(place, own_conv, got_conv, own_up, got_up)
    return (decoded, grad_coarse, grad_up, grad_conv)


def solution(mesh):
    return jax.shard_map(
        local,
        mesh=mesh,
        in_specs=(
            P("band", "face", None),
            P("band", "face", None),
            P(),
            P(),
            P("band", "face", None),
        ),
        out_specs=(
            P("band", "face", None),
            P("band", "face", None),
            P("face", "band"),
            P("face", "band"),
        ),
        check_vma=False,
    )
```

```python
import jax
import jax.numpy as jnp
from jax import lax
from jax.experimental import pallas as pl
from jax.experimental.pallas import tpu as pltpu
from jax.sharding import PartitionSpec as P

f32, bf16 = jnp.float32, jnp.bfloat16
forward_taps = ((1, 1), (0, 0), (1, 0))
backward_taps = ((1, 0), (0, 1), (1, 1))
MARGIN = 8
LANES = 128


def sds(shape, dtype):
    return jax.ShapeDtypeStruct(shape, dtype)


def kernel_call(body, outs, scratch, flops, *args, far=()):
    vmem = pl.BlockSpec(memory_space=pltpu.VMEM)
    hbm = pl.BlockSpec(memory_space=pltpu.HBM)
    moved = sum(a.size * a.dtype.itemsize for a in args)
    moved += sum(a.size * a.dtype.itemsize for a in outs)
    args = [
        pltpu.with_memory_space_constraint(a, pltpu.HBM) if i in far else a
        for i, a in enumerate(args)
    ]
    return pl.pallas_call(
        body,
        out_shape=tuple(outs),
        in_specs=[hbm if i in far else vmem for i in range(len(args))],
        out_specs=tuple(vmem for _ in outs),
        scratch_shapes=scratch,
        compiler_params=pltpu.CompilerParams(vmem_limit_bytes=28 * 2**20),
        cost_estimate=pl.CostEstimate(flops=flops, bytes_accessed=moved, transcendentals=0),
    )(*args)


def place_of():
    face = lax.axis_index("face")
    return lax.rem(face, 2), lax.div(face, 2), lax.axis_index("band"), lax.axis_size("band")


def dot(a, b):
    return jnp.dot(a, b, preferred_element_type=f32)


def dot_nt(a, b):
    return lax.dot_general(a, b, (((1,), (1,)), ((), ())), preferred_element_type=f32)


def pairs(count, wrap):
    first = [(i, i ^ 1) for i in range(count)]
    second = []
    for i in range(count):
        j = i + 1 if i % 2 else i - 1
        if wrap or 0 <= j < count:
            second.append((i, j % count))
    return first, second


def up16(n):
    return (n + 15) // 16 * 16


def halves(n_rows, channels):
    return pltpu.VMEM((channels // LANES, n_rows, LANES), f32)


def put(ref, start, value, step=1):
    for part in range(ref.shape[0]):
        rows = pl.ds(start, value.shape[0], stride=step if step > 1 else None)
        ref[part, rows, :] = value[:, part * LANES : (part + 1) * LANES]


def get(ref, start, count, step=1):
    rows = pl.ds(start, count, stride=step if step > 1 else None)
    return jnp.concatenate([ref[part, rows, :] for part in range(ref.shape[0])], axis=1)


def fill(ref, start, value):
    ref[start : start + value.shape[0], :] = value


def other_core(partial, send):
    core = place_of()[0]
    groups, block, _ = send.shape
    for group in range(groups):
        theirs = pl.multiple_of((2 * group + 1 - core) * block, 16)
        send[group] = partial[pl.ds(theirs, block), :].astype(bf16)


class Layout:
    def __init__(self, n_rows, n_cols):
        rows, cols = 2 * n_rows, 2 * n_cols
        self.cot, self.cot_2, self.skip, self.coarse = 0, rows, 2 * rows, 3 * rows
        self.face_size = up16(3 * rows + n_rows)
        self.row_cot, self.row_cot_2, self.row_skip = 0, cols, 2 * cols
        self.row_coarse, self.corner = 3 * cols, 3 * cols + n_cols
        self.band_size = self.corner + 16
        ring = (cols + 2 + 7) // 8 * 8
        self.top, self.bottom, self.left, self.right = 0, ring, 2 * ring, 2 * ring + rows
        self.ring_size = up16(2 * ring + 2 * rows)
        self.grad_left, self.grad_size = ring, up16(ring + rows)


COT, COT_2, SKIP, COARSE = (0, 1, 2), (3, 4, 5), (6, None, 7), (8, None, 9)


def face_message(coarse, skip, cot, first, second, cot_v, skip_v, coarse_v, flat, before, after, sems):
    rows, cols, _ = cot.shape
    n_rows, n_cols, _ = coarse.shape
    at = Layout(n_rows, n_cols)
    copies = [
        pltpu.make_async_copy(source, target, sems.at[i])
        for i, (source, target) in enumerate(((cot, cot_v), (skip, skip_v), (coarse, coarse_v)))
    ]
    for copy in copies:
        copy.start()
    before[...] = jnp.zeros_like(before)
    after[...] = jnp.zeros_like(after)
    for copy, array, start, start_2 in (
        (copies[0], cot_v, at.cot, at.cot_2), (copies[1], skip_v, at.skip, None), (copies[2], coarse_v, at.coarse, None),
    ):
        copy.wait()
        n, width, channels = array.shape
        put(flat, 0, array[:, :16, :].astype(f32)[:, :8, :].reshape(n * 8, channels))
        put(flat, n * 8, array[:, width - 16 :, :].astype(f32)[:, 8:, :].reshape(n * 8, channels))
        fill(before, start, get(flat, 0, n, 8))
        fill(after, start, get(flat, n * 8 + 7, n, 8))
        if start_2 is not None:
            fill(after, start_2, get(flat, n * 8 + 6, n, 8))
    even = place_of()[0] == 0
    first[...] = jnp.where(even, after[...], before[...]).astype(bf16)
    second[...] = jnp.where(even, before[...], after[...]).astype(bf16)


def band_message(coarse, skip, cot, got_first, got_second, first, second, left, right, before, after):
    rows, cols, channels = cot.shape
    n_rows, n_cols, _ = coarse.shape
    at = Layout(n_rows, n_cols)
    even = place_of()[0] == 0
    one, two = got_first[...].astype(f32), got_second[...].astype(f32)
    left[...] = jnp.where(even, two, one)
    right[...] = jnp.where(even, one, two)
    for message, row, row_2, cell in ((before, 0, None, 0), (after, rows - 1, rows - 2, n_rows - 1)):
        fill(message, at.row_cot, cot[row].astype(f32))
        if row_2 is None:
            fill(message, at.row_cot_2, jnp.zeros((cols, channels), f32))
        else:
            fill(message, at.row_cot_2, cot[row_2].astype(f32))
        fill(message, at.row_skip, skip[row].astype(f32))
        fill(message, at.row_coarse, coarse[cell].astype(f32))
        fill(message, at.corner, jnp.zeros((16, channels), f32))
        corners = [
            (COT[0], left, at.cot + row), (COT[1], left, at.cot_2 + row), (COT[2], right, at.cot + row),
            (SKIP[0], left, at.skip + row), (SKIP[2], right, at.skip + row),
            (COARSE[0], left, at.coarse + cell), (COARSE[2], right, at.coarse + cell),
        ]
        if row_2 is not None:
            corners += [
                (COT_2[0], left, at.cot + row_2), (COT_2[1], left, at.cot_2 + row_2),
                (COT_2[2], right, at.cot + row_2),
            ]
        for corner, side, source in corners:
            fill(message, at.corner + corner, side[source : source + 1, :])
    even = lax.rem(place_of()[2], 2) == 0
    first[...] = jnp.where(even, after[...], before[...]).astype(bf16)
    second[...] = jnp.where(even, before[...], after[...]).astype(bf16)


def act_kernel(
    coarse, skip, cot, left, right, got_first, got_second, up_w, conv_w,
    shifted, near, act, slope, partial, send, upper, lower, conv_v, padded, pre, sem,
):
    n_rows, n_cols, channels = coarse.shape
    rows, cols, _ = skip.shape
    at = Layout(n_rows, n_cols)
    stride = cols + 2 * MARGIN
    copy = pltpu.make_async_copy(conv_w, conv_v, sem)
    copy.start()
    even = lax.rem(place_of()[2], 2) == 0
    one, two = got_first[...].astype(f32), got_second[...].astype(f32)
    upper[...] = jnp.where(even, two, one)
    lower[...] = jnp.where(even, one, two)
    for row in range(n_rows):
        near[0, row] = coarse[row]
        put(padded, row * stride, coarse[row].astype(f32))
    below = lower[at.row_coarse : at.row_coarse + n_cols, :]
    near[0, n_rows] = below.astype(bf16)
    put(padded, n_rows * stride, below)
    put(padded, n_cols, right[at.coarse : at.coarse + n_rows, :], stride)
    corner = at.corner + COARSE[2]
    put(padded, n_rows * stride + n_cols, lower[corner : corner + 1, :])
    for row in range(n_rows + 1):
        near[1, row] = get(padded, row * stride + 1, n_cols).astype(bf16)
    for row in range(n_rows + 1, near.shape[1]):
        for side in range(2):
            near[side, row] = jnp.zeros((n_cols, channels), bf16)
    put(padded, MARGIN, upper[at.row_cot : at.row_cot + cols, :])
    put(padded, (rows + 1) * stride + MARGIN, lower[at.row_cot : at.row_cot + cols, :])
    for row in range(rows):
        put(padded, (row + 1) * stride + MARGIN, cot[row].astype(f32))
    put(padded, stride + MARGIN - 1, left[at.cot : at.cot + rows, :], stride)
    put(padded, stride + MARGIN + cols, right[at.cot : at.cot + rows, :], stride)
    for row, message in ((0, upper), (rows + 1, lower)):
        for col, corner in ((-1, at.corner + COT[0]), (cols, at.corner + COT[2])):
            put(padded, row * stride + MARGIN + col, message[corner : corner + 1, :])
    for row in range(rows + 2):
        for shift in (0, 2):
            start = row * stride + MARGIN - 1 + shift
            shifted[shift, row] = get(padded, start, cols).astype(bf16)
    shifted[1, 0] = upper[at.row_cot : at.row_cot + cols, :].astype(bf16)
    shifted[1, rows + 1] = lower[at.row_cot : at.row_cot + cols, :].astype(bf16)
    for row in range(rows):
        shifted[1, row + 1] = cot[row]
    sums = {}
    for k in range(3):
        row_phase, row_off = forward_taps[k]
        for l in range(3):
            col_phase, col_off = forward_taps[l]
            source = near[col_off, pl.ds(row_off, n_rows)].reshape(n_rows * n_cols, channels)
            term = dot(source, up_w[k, l])
            name = (row_phase, col_phase)
            sums[name] = sums[name] + term if name in sums else term
    for (row_phase, col_phase), total in sums.items():
        for row in range(n_rows):
            start = (2 * row + row_phase) * cols + col_phase
            put(pre, start, total[row * n_cols : (row + 1) * n_cols], 2)
    preact = get(pre, 0, rows * cols) + skip[...].reshape(rows * cols, channels).astype(f32)
    sigma = jax.nn.sigmoid(preact)
    value = preact * sigma
    slope[...] = sigma + value * (1.0 - sigma)
    act_flat = value.astype(bf16)
    act[...] = act_flat.reshape(act.shape)
    act_t = act_flat.T
    for k in range(3):
        for l in range(3):
            source = shifted[2 - l, pl.ds(2 - k, rows)].reshape(-1, channels)
            partial[pl.ds((3 * k + l) * channels, channels), :] = dot(act_t, source)
    other_core(partial, send)
    copy.wait()


def grad_kernel(shifted, slope, conv_w, phases, fine):
    rows, cols = shifted.shape[1] - 2, shifted.shape[2]
    channels = shifted.shape[3]
    n_rows, n_cols = rows // 2, cols // 2
    total = jnp.zeros((rows * cols, channels), f32)
    for k in range(3):
        for l in range(3):
            source = shifted[2 - l, pl.ds(2 - k, rows)].reshape(-1, channels)
            total = total + dot_nt(source, conv_w[k, l])
    put(fine, 0, (total * slope[...]).astype(bf16).astype(f32))
    whole = phases.shape[2]
    for row_phase in range(2):
        for col_phase in range(2):
            for row in range(n_rows):
                start = (2 * row + row_phase) * cols + col_phase
                phases[row_phase, col_phase, row] = get(fine, start, n_cols, 2).astype(bf16)
            for row in range(n_rows, whole):
                phases[row_phase, col_phase, row] = jnp.zeros((n_cols, channels), bf16)


def up_kernel(near, phases, partial, send):
    _, _, whole, n_cols, channels = phases.shape
    turned = {}
    for row_off in range(2):
        for col_off in range(2):
            cells = near[col_off, pl.ds(row_off, whole)]
            turned[row_off, col_off] = cells.reshape(whole * n_cols, channels).T
    for k in range(3):
        row_phase, row_off = forward_taps[k]
        for l in range(3):
            col_phase, col_off = forward_taps[l]
            source = phases[row_phase, col_phase].reshape(whole * n_cols, channels)
            partial[pl.ds((3 * k + l) * channels, channels), :] = dot(
                turned[row_off, col_off], source
            )
    other_core(partial, send)


def ring_kernel(
    coarse, cot, left, right, upper, lower, conv_w, up_w, ring_act, ring_grad, ring, wide,
):
    rows, cols, channels = cot.shape
    n_rows, n_cols = rows // 2, cols // 2
    at = Layout(n_rows, n_cols)
    stride, step = cols + 2 * MARGIN, n_cols + 2 * MARGIN
    _, _, band, n_bands = place_of()
    has_upper, has_lower = band > 0, band < n_bands - 1

    def corner(message, which):
        return message[at.corner + which : at.corner + which + 1, :]

    def cell(i, j):
        return (i + 1) * step + MARGIN + j

    for row in range(n_rows):
        put(wide, cell(row, 0), coarse[row].astype(f32))
    for row, message in ((-1, upper), (n_rows, lower)):
        put(wide, cell(row, 0), message[at.row_coarse : at.row_coarse + n_cols, :])
        put(wide, cell(row, -1), corner(message, COARSE[0]))
        put(wide, cell(row, n_cols), corner(message, COARSE[2]))
    put(wide, cell(0, -1), left[at.coarse : at.coarse + n_rows, :], step)
    put(wide, cell(0, n_cols), right[at.coarse : at.coarse + n_rows, :], step)
    total = jnp.zeros((at.ring_size, channels), f32)
    for k in range(3):
        for l in range(3):
            put(ring, 0, jnp.zeros((at.ring_size, channels), f32))
            for base, i in ((at.bottom, n_rows),) if k == 1 else ((at.top, k // 2 * -1),):
                start = cell(i, -1 if l == 2 else 0)
                put(ring, base + (l == 1), get(wide, start, n_cols + 1), 2)
            base, j = (at.right, n_cols) if l == 1 else (at.left, -(l // 2))
            start = cell(1 if k == 0 else 0, j)
            put(ring, base + (k != 1), get(wide, start, n_rows, step), 2)
            total = total + dot(get(ring, 0, at.ring_size).astype(bf16), up_w[k, l])
    put(ring, 0, jnp.zeros((at.ring_size, channels), f32))
    for base, message in ((at.top, upper), (at.bottom, lower)):
        put(ring, base + 1, message[at.row_skip : at.row_skip + cols, :])
        put(ring, base, corner(message, SKIP[0]))
        put(ring, base + cols + 1, corner(message, SKIP[2]))
    put(ring, at.left, left[at.skip : at.skip + rows, :])
    put(ring, at.right, right[at.skip : at.skip + rows, :])
    preact = total + get(ring, 0, at.ring_size)
    sigma = jax.nn.sigmoid(preact)
    value = preact * sigma
    slope = sigma + value * (1.0 - sigma)
    value = value.astype(bf16).astype(f32)
    ring_act[...] = value
    for base, exists in ((at.top, has_upper), (at.bottom, has_lower)):
        strip = value[base : base + cols + 2]
        ring_act[base : base + cols + 2, :] = jnp.where(exists, strip, 0.0)

    def fine(p, q):
        return (p + 2) * stride + MARGIN + q

    for row in range(rows):
        put(wide, fine(row, 0), cot[row].astype(f32))
    for row, message, start, which in (
        (-1, upper, at.row_cot, COT), (-2, upper, at.row_cot_2, COT_2), (rows, lower, at.row_cot, COT),
    ):
        put(wide, fine(row, 0), message[start : start + cols, :])
        for col, one in ((-1, which[0]), (-2, which[1]), (cols, which[2])):
            put(wide, fine(row, col), corner(message, one))
    put(wide, fine(0, -1), left[at.cot : at.cot + rows, :], stride)
    put(wide, fine(0, -2), left[at.cot_2 : at.cot_2 + rows, :], stride)
    put(wide, fine(0, cols), right[at.cot : at.cot + rows, :], stride)
    total = jnp.zeros((at.grad_size, channels), f32)
    for k in range(3):
        for l in range(3):
            put(ring, at.top, get(wide, fine(-k, -l), cols + 1))
            put(ring, at.grad_left, get(wide, fine(1 - k, -l), rows, stride))
            source = get(ring, 0, at.grad_size).astype(bf16)
            total = total + dot_nt(source, conv_w[k, l])
    strip = (total[: cols + 1] * slope[at.top : at.top + cols + 1]).astype(bf16).astype(f32)
    put(ring_grad, at.top, jnp.where(has_upper, strip, 0.0))
    strip = total[at.grad_left : at.grad_left + rows] * slope[at.left : at.left + rows]
    put(ring_grad, at.grad_left, strip.astype(bf16).astype(f32))


def decoded_kernel(act, ring_act, conv_w, decoded, padded, shifted):
    rows, cols, channels = act.shape
    at = Layout(rows // 2, cols // 2)
    stride = cols + 2 * MARGIN
    for row in range(rows):
        put(padded, (row + 1) * stride + MARGIN, act[row].astype(f32))
    for row, base in ((0, at.top), (rows + 1, at.bottom)):
        put(padded, row * stride + MARGIN - 1, ring_act[base : base + cols + 2, :])
    put(padded, stride + MARGIN - 1, ring_act[at.left : at.left + rows, :], stride)
    put(padded, stride + MARGIN + cols, ring_act[at.right : at.right + rows, :], stride)
    for row in range(rows + 2):
        for shift in range(3):
            start = row * stride + MARGIN - 1 + shift
            shifted[shift, row] = get(padded, start, cols).astype(bf16)
    total = jnp.zeros((rows * cols, channels), f32)
    for k in range(3):
        for l in range(3):
            source = shifted[l, pl.ds(k, rows)].reshape(-1, channels)
            total = total + dot(source, conv_w[k, l])
    decoded[...] = total.astype(bf16).reshape(decoded.shape)

def coarse_kernel(phases, ring_grad, up_w, coarse_out, padded, moved):
    n_rows, n_cols, channels = coarse_out.shape
    at = Layout(n_rows, n_cols)
    stride = n_cols + 2 * MARGIN
    for phase, start in ((0, 1), (1, 2), (2, 0)):
        moved[phase, 0] = get(ring_grad, at.top + start, n_cols, 2).astype(bf16)
    for phase in range(2):
        for row in range(n_rows):
            moved[phase, 1 + row] = phases[1, phase, row]
    for row_phase in range(2):
        for row in range(n_rows):
            put(padded, row * stride + MARGIN, phases[row_phase, 1, row].astype(f32))
        put(padded, MARGIN - 1, get(ring_grad, at.grad_left + row_phase, n_rows, 2), stride)
        for row in range(n_rows):
            cells = get(padded, row * stride + MARGIN - 1, n_cols).astype(bf16)
            if row_phase:
                moved[2, 1 + row] = cells
            else:
                moved[3, row] = cells
    total = jnp.zeros((n_rows * n_cols, channels), f32)
    for k in range(3):
        for l in range(3):
            if k == 1:
                if l == 0:
                    source = moved[3, pl.ds(0, n_rows)]
                else:
                    source = phases[0, l - 1, pl.ds(0, n_rows)]
            else:
                source = moved[(2, 0, 1)[l], pl.ds(k // 2, n_rows)]
            total = total + dot_nt(source.reshape(n_rows * n_cols, channels), up_w[k, l])
    coarse_out[...] = total.astype(bf16).reshape(coarse_out.shape)


def halving(count):
    bits = (count // 2).bit_length() - 1
    return [[(step + core) % bits for step in range(bits)] for core in range(2)]


def mask_of(slot, order):
    last = len(order) - 1
    return sum(1 << bit for step, bit in enumerate(order) if slot >> (last - step) & 1)


def core_kernel(partial, got, own, message):
    slots, half, block = got.shape[0], own.shape[0], got.shape[1]
    core, chip, _, _ = place_of()
    even, odd = halving(2 * slots)
    for slot in range(slots):
        target = chip ^ jnp.where(core == 0, mask_of(slot, even), mask_of(slot, odd))
        mine = pl.multiple_of((2 * target + core) * block, 16)
        total = partial[pl.ds(mine, block), :] + got[target].astype(f32)
        if slot < half:
            own[slot] = total
        else:
            message[slot - half] = total.astype(bf16)


def plane_kernel(before, got, own, message):
    half = own.shape[0]
    for slot in range(2 * half):
        total = before[slot] + got[slot].astype(f32)
        if slot < half:
            own[slot] = total
        else:
            message[slot - half] = total.astype(bf16)


def band_kernel(conv, got_conv, up, got_up, own, *refs):
    n_bands, messages, cut = len(refs), refs[:-1], refs[-1]
    conv_total = conv[0] + got_conv[0].astype(f32)
    up_total = up[0] + got_up[0].astype(f32)
    cols = conv_total.shape[1] // n_bands
    for band in range(n_bands):
        cut[band, :, :cols] = conv_total[:, band * cols : (band + 1) * cols]
        cut[band, :, cols:] = up_total[:, band * cols : (band + 1) * cols]
    band = place_of()[2]
    own[...] = cut[band]
    for k, message in enumerate(messages):
        message[...] = cut[lax.rem(band + k + 1, n_bands)].astype(bf16)


def last_kernel(own, *refs):
    peers, (conv, up) = refs[:-2], refs[-2:]
    total = own[...]
    for peer in peers:
        total = total + peer[...].astype(f32)
    turned = total.T
    conv[...] = turned[: conv.shape[0]]
    up[...] = turned[conv.shape[0] :]


def xor_pairs(count, bits):
    return [(i, i ^ bits) for i in range(count)]


def core_sum(partial, send):
    groups, block, channels = send.shape
    got = lax.ppermute(send, "face", xor_pairs(lax.axis_size("face"), 1))
    shape = (groups // 2, block, channels)
    return kernel_call(core_kernel, [sds(shape, f32), sds(shape, bf16)], [], 0, partial, got)


def plane_swap(message, step):
    faces = lax.axis_size("face")
    orders = halving(faces)
    return lax.ppermute(message, "face", [(i, i ^ 2 << orders[i % 2][step]) for i in range(faces)])


def plane_sum(own, got):
    half, block, channels = own.shape
    shape = (half // 2, block, channels)
    return kernel_call(plane_kernel, [sds(shape, f32), sds(shape, bf16)], [], 0, own, got)


def band_sum(conv, got_conv, up, got_up):
    bands = lax.axis_size("band")
    _, block, channels = conv.shape
    cols = channels // bands
    shape = (block, 2 * cols)
    own, *messages = kernel_call(
        band_kernel, [sds(shape, f32)] + [sds(shape, bf16)] * (bands - 1),
        [pltpu.VMEM((bands,) + shape, f32)], 0, conv, got_conv, up, got_up,
    )
    got = [
        lax.ppermute(messages[k - 1], "band", [(i, (i + k) % bands) for i in range(bands)])
        for k in range(1, bands)
    ]
    return [a.T for a in kernel_call(last_kernel, [sds((cols, block), f32)] * 2, [], 0, own, *got)]


def after(value, *others):
    return lax.optimization_barrier((value, *others))[0]


def swap(first, second, axis, wrap):
    one, two = pairs(lax.axis_size(axis), wrap)
    return lax.ppermute(first, axis, one), lax.ppermute(second, axis, two)


def local(coarse, skip, up_weight, conv_weight, cotangent):
    n_rows, n_cols, channels = coarse.shape
    rows, cols, _ = skip.shape
    at = Layout(n_rows, n_cols)
    faces = lax.axis_size("face")
    groups, block = faces // 2, 9 * channels // faces

    flat = halves(rows * cols, channels)
    message = sds((at.face_size, channels), bf16)
    edges = pltpu.VMEM(message.shape, f32)
    first, second, cotangent, skip, coarse = kernel_call(
        face_message,
        [message, message, sds(cotangent.shape, bf16), sds(skip.shape, bf16), sds(coarse.shape, bf16)],
        [flat, edges, edges, pltpu.SemaphoreType.DMA((3,))],
        0, coarse, skip, cotangent, far=(0, 1, 2),
    )
    first, second = swap(first, second, "face", True)
    side = sds(message.shape, f32)
    message = sds((at.band_size, channels), bf16)
    edges = pltpu.VMEM(message.shape, f32)
    first, second, left, right = kernel_call(
        band_message, [message, message, side, side], [edges, edges],
        0, coarse, skip, cotangent, first, second,
    )
    first, second = swap(first, second, "band", False)

    cells = n_rows * n_cols
    stride = cols + 2 * MARGIN
    padded = halves((rows + 2) * stride, channels)
    shift_shape = (3, rows + 2, cols, channels)
    whole = -(-cells // 256) * 256 // n_cols
    partials = [sds((9 * channels, channels), f32), sds((groups, block, channels), bf16)]
    side = sds(message.shape, f32)
    shifted, near, act, slope, part_conv, send_conv, upper, lower, conv_weight = kernel_call(
        act_kernel,
        [
            sds(shift_shape, bf16), sds((2, whole + 1, n_cols, channels), bf16),
            sds(skip.shape, bf16), sds((rows * cols, channels), f32), *partials, side, side,
            sds(conv_weight.shape, bf16),
        ],
        [padded, flat, pltpu.SemaphoreType.DMA],
        0, coarse, skip, cotangent, left, right, first, second, up_weight, conv_weight, far=(8,),
    )
    phases = kernel_call(
        grad_kernel, [sds((2, 2, whole, n_cols, channels), bf16)], [flat],
        0, shifted, slope, conv_weight,
    )[0]
    part_up, send_up = kernel_call(up_kernel, partials, [], 0, near, phases)
    own_conv, to_conv = core_sum(after(part_conv, send_up), send_conv)
    got_conv = plane_swap(to_conv, 0)
    own_up, to_up = core_sum(after(part_up, to_conv), send_up)
    got_up = plane_swap(to_up, 0)
    ring_act, ring_grad = kernel_call(
        ring_kernel,
        [
            sds((at.ring_size, channels), f32),
            sds((channels // LANES, at.grad_size, LANES), f32),
        ],
        [halves(at.ring_size, channels), halves((rows + 3) * stride, channels)],
        0, coarse, cotangent, after(left, to_up), right, upper, lower, conv_weight, up_weight,
    )
    own_conv = after(own_conv, ring_act)
    steps = (faces // 2).bit_length() - 1
    for step in range(1, steps):
        own_conv, to_conv = plane_sum(own_conv, got_conv)
        got_conv = plane_swap(to_conv, step)
        if step == 1:
            decoded = kernel_call(
                decoded_kernel, [sds(skip.shape, bf16)], [padded, pltpu.VMEM(shift_shape, bf16)],
                0, act, after(ring_act, to_conv), conv_weight,
            )[0]
            own_up = after(own_up, decoded)
        own_up, to_up = plane_sum(own_up, got_up)
        got_up = plane_swap(to_up, step)
        if step == 1:
            grad_coarse = kernel_call(
                coarse_kernel, [sds(coarse.shape, bf16)],
                [
                    halves(n_rows * (n_cols + 2 * MARGIN), channels),
                    pltpu.VMEM((4, n_rows + 1, n_cols, channels), bf16),
                ],
                0, phases, after(ring_grad, to_up), up_weight,
            )[0]
            own_up = after(own_up, grad_coarse)
    grad_conv, grad_up = band_sum(own_conv, got_conv, own_up, got_up)
    return (decoded, grad_coarse, grad_up, grad_conv)


def solution(mesh):
    return jax.shard_map(
        local,
        mesh=mesh,
        in_specs=(
            P("band", "face", None),
            P("band", "face", None),
            P(),
            P(),
            P("band", "face", None),
        ),
        out_specs=(
            P("band", "face", None),
            P("band", "face", None),
            P("face", "band"),
            P("face", "band"),
        ),
        check_vma=False,
    )
```

```python
import jax
import jax.numpy as jnp
from jax import lax
from jax.experimental import pallas as pl
from jax.experimental.pallas import tpu as pltpu
from jax.sharding import PartitionSpec as P

f32, bf16 = jnp.float32, jnp.bfloat16
forward_taps = ((1, 1), (0, 0), (1, 0))
backward_taps = ((1, 0), (0, 1), (1, 1))
MARGIN = 8
LANES = 128


def sds(shape, dtype):
    return jax.ShapeDtypeStruct(shape, dtype)


def kernel_call(body, outs, scratch, flops, *args, far=()):
    vmem = pl.BlockSpec(memory_space=pltpu.VMEM)
    hbm = pl.BlockSpec(memory_space=pltpu.HBM)
    moved = sum(a.size * a.dtype.itemsize for a in args)
    moved += sum(a.size * a.dtype.itemsize for a in outs)
    args = [
        pltpu.with_memory_space_constraint(a, pltpu.HBM) if i in far else a
        for i, a in enumerate(args)
    ]
    return pl.pallas_call(
        body,
        out_shape=tuple(outs),
        in_specs=[hbm if i in far else vmem for i in range(len(args))],
        out_specs=tuple(vmem for _ in outs),
        scratch_shapes=scratch,
        compiler_params=pltpu.CompilerParams(vmem_limit_bytes=28 * 2**20),
        cost_estimate=pl.CostEstimate(flops=flops, bytes_accessed=moved, transcendentals=0),
    )(*args)


def place_of():
    face = lax.axis_index("face")
    return lax.rem(face, 2), lax.div(face, 2), lax.axis_index("band"), lax.axis_size("band")


def dot(a, b):
    return jnp.dot(a, b, preferred_element_type=f32)


def dot_nt(a, b):
    return lax.dot_general(a, b, (((1,), (1,)), ((), ())), preferred_element_type=f32)


def pairs(count, wrap):
    first = [(i, i ^ 1) for i in range(count)]
    second = []
    for i in range(count):
        j = i + 1 if i % 2 else i - 1
        if wrap or 0 <= j < count:
            second.append((i, j % count))
    return first, second


def up16(n):
    return (n + 15) // 16 * 16


def halves(n_rows, channels):
    return pltpu.VMEM((channels // LANES, n_rows, LANES), f32)


def put(ref, start, value, step=1):
    for part in range(ref.shape[0]):
        rows = pl.ds(start, value.shape[0], stride=step if step > 1 else None)
        ref[part, rows, :] = value[:, part * LANES : (part + 1) * LANES]


def get(ref, start, count, step=1):
    rows = pl.ds(start, count, stride=step if step > 1 else None)
    return jnp.concatenate([ref[part, rows, :] for part in range(ref.shape[0])], axis=1)


def fill(ref, start, value):
    ref[start : start + value.shape[0], :] = value


def other_core(partial, send):
    core = place_of()[0]
    groups, block, _ = send.shape
    for group in range(groups):
        theirs = pl.multiple_of((2 * group + 1 - core) * block, 16)
        send[group] = partial[pl.ds(theirs, block), :].astype(bf16)


class Layout:
    def __init__(self, n_rows, n_cols):
        rows, cols = 2 * n_rows, 2 * n_cols
        self.cot, self.cot_2, self.skip, self.coarse = 0, rows, 2 * rows, 3 * rows
        self.face_size = up16(3 * rows + n_rows)
        self.row_cot, self.row_cot_2, self.row_skip = 0, cols, 2 * cols
        self.row_coarse, self.corner = 3 * cols, 3 * cols + n_cols
        self.band_size = self.corner + 16
        ring = (cols + 2 + 7) // 8 * 8
        self.top, self.bottom, self.left, self.right = 0, ring, 2 * ring, 2 * ring + rows
        self.ring_size = up16(2 * ring + 2 * rows)
        self.grad_left, self.grad_size = ring, up16(ring + rows)


COT, COT_2, SKIP, COARSE = (0, 1, 2), (3, 4, 5), (6, None, 7), (8, None, 9)


def face_message(coarse, skip, cot, first, second, cot_v, skip_v, coarse_v, flat, before, after, sems):
    rows, cols, _ = cot.shape
    n_rows, n_cols, _ = coarse.shape
    at = Layout(n_rows, n_cols)
    copies = [
        pltpu.make_async_copy(source, target, sems.at[i])
        for i, (source, target) in enumerate(((cot, cot_v), (skip, skip_v), (coarse, coarse_v)))
    ]
    for copy in copies:
        copy.start()
    before[...] = jnp.zeros_like(before)
    after[...] = jnp.zeros_like(after)
    for copy, array, start, start_2 in (
        (copies[0], cot_v, at.cot, at.cot_2), (copies[1], skip_v, at.skip, None), (copies[2], coarse_v, at.coarse, None),
    ):
        copy.wait()
        n, width, channels = array.shape
        put(flat, 0, array[:, :16, :].astype(f32)[:, :8, :].reshape(n * 8, channels))
        put(flat, n * 8, array[:, width - 16 :, :].astype(f32)[:, 8:, :].reshape(n * 8, channels))
        fill(before, start, get(flat, 0, n, 8))
        fill(after, start, get(flat, n * 8 + 7, n, 8))
        if start_2 is not None:
            fill(after, start_2, get(flat, n * 8 + 6, n, 8))
    even = place_of()[0] == 0
    first[...] = jnp.where(even, after[...], before[...]).astype(bf16)
    second[...] = jnp.where(even, before[...], after[...]).astype(bf16)


def band_message(coarse, skip, cot, got_first, got_second, first, second, left, right, before, after):
    rows, cols, channels = cot.shape
    n_rows, n_cols, _ = coarse.shape
    at = Layout(n_rows, n_cols)
    even = place_of()[0] == 0
    one, two = got_first[...].astype(f32), got_second[...].astype(f32)
    left[...] = jnp.where(even, two, one)
    right[...] = jnp.where(even, one, two)
    for message, row, row_2, cell in ((before, 0, None, 0), (after, rows - 1, rows - 2, n_rows - 1)):
        fill(message, at.row_cot, cot[row].astype(f32))
        if row_2 is None:
            fill(message, at.row_cot_2, jnp.zeros((cols, channels), f32))
        else:
            fill(message, at.row_cot_2, cot[row_2].astype(f32))
        fill(message, at.row_skip, skip[row].astype(f32))
        fill(message, at.row_coarse, coarse[cell].astype(f32))
        fill(message, at.corner, jnp.zeros((16, channels), f32))
        corners = [
            (COT[0], left, at.cot + row), (COT[1], left, at.cot_2 + row), (COT[2], right, at.cot + row),
            (SKIP[0], left, at.skip + row), (SKIP[2], right, at.skip + row),
            (COARSE[0], left, at.coarse + cell), (COARSE[2], right, at.coarse + cell),
        ]
        if row_2 is not None:
            corners += [
                (COT_2[0], left, at.cot + row_2), (COT_2[1], left, at.cot_2 + row_2),
                (COT_2[2], right, at.cot + row_2),
            ]
        for corner, side, source in corners:
            fill(message, at.corner + corner, side[source : source + 1, :])
    even = lax.rem(place_of()[2], 2) == 0
    first[...] = jnp.where(even, after[...], before[...]).astype(bf16)
    second[...] = jnp.where(even, before[...], after[...]).astype(bf16)


def act_kernel(
    coarse, skip, cot, left, right, got_second, got_first, up_w, conv_w,
    shifted, near, act, slope, partial, send, upper, lower, conv_v, padded, pre, sem,
):
    n_rows, n_cols, channels = coarse.shape
    rows, cols, _ = skip.shape
    at = Layout(n_rows, n_cols)
    stride = cols + 2 * MARGIN
    copy = pltpu.make_async_copy(conv_w, conv_v, sem)
    copy.start()
    even = lax.rem(place_of()[2], 2) == 0
    one, two = got_first[...].astype(f32), got_second[...].astype(f32)
    upper[...] = jnp.where(even, two, one)
    lower[...] = jnp.where(even, one, two)
    for row in range(n_rows):
        near[0, row] = coarse[row]
        put(padded, row * stride, coarse[row].astype(f32))
    below = lower[at.row_coarse : at.row_coarse + n_cols, :]
    near[0, n_rows] = below.astype(bf16)
    put(padded, n_rows * stride, below)
    put(padded, n_cols, right[at.coarse : at.coarse + n_rows, :], stride)
    corner = at.corner + COARSE[2]
    put(padded, n_rows * stride + n_cols, lower[corner : corner + 1, :])
    for row in range(n_rows + 1):
        near[1, row] = get(padded, row * stride + 1, n_cols).astype(bf16)
    for row in range(n_rows + 1, near.shape[1]):
        for side in range(2):
            near[side, row] = jnp.zeros((n_cols, channels), bf16)
    put(padded, MARGIN, upper[at.row_cot : at.row_cot + cols, :])
    put(padded, (rows + 1) * stride + MARGIN, lower[at.row_cot : at.row_cot + cols, :])
    for row in range(rows):
        put(padded, (row + 1) * stride + MARGIN, cot[row].astype(f32))
    put(padded, stride + MARGIN - 1, left[at.cot : at.cot + rows, :], stride)
    put(padded, stride + MARGIN + cols, right[at.cot : at.cot + rows, :], stride)
    for row, message in ((0, upper), (rows + 1, lower)):
        for col, corner in ((-1, at.corner + COT[0]), (cols, at.corner + COT[2])):
            put(padded, row * stride + MARGIN + col, message[corner : corner + 1, :])
    for row in range(rows + 2):
        for shift in (0, 2):
            start = row * stride + MARGIN - 1 + shift
            shifted[shift, row] = get(padded, start, cols).astype(bf16)
    shifted[1, 0] = upper[at.row_cot : at.row_cot + cols, :].astype(bf16)
    shifted[1, rows + 1] = lower[at.row_cot : at.row_cot + cols, :].astype(bf16)
    for row in range(rows):
        shifted[1, row + 1] = cot[row]
    sums = {}
    for k in range(3):
        row_phase, row_off = forward_taps[k]
        for l in range(3):
            col_phase, col_off = forward_taps[l]
            source = near[col_off, pl.ds(row_off, n_rows)].reshape(n_rows * n_cols, channels)
            term = dot(source, up_w[k, l])
            name = (row_phase, col_phase)
            sums[name] = sums[name] + term if name in sums else term
    for (row_phase, col_phase), total in sums.items():
        for row in range(n_rows):
            start = (2 * row + row_phase) * cols + col_phase
            put(pre, start, total[row * n_cols : (row + 1) * n_cols], 2)
    preact = get(pre, 0, rows * cols) + skip[...].reshape(rows * cols, channels).astype(f32)
    sigma = jax.nn.sigmoid(preact)
    value = preact * sigma
    slope[...] = sigma + value * (1.0 - sigma)
    act_flat = value.astype(bf16)
    act[...] = act_flat.reshape(act.shape)
    act_t = act_flat.T
    for k in range(3):
        for l in range(3):
            source = shifted[2 - l, pl.ds(2 - k, rows)].reshape(-1, channels)
            partial[pl.ds((3 * k + l) * channels, channels), :] = dot(act_t, source)
    other_core(partial, send)
    copy.wait()


def grad_kernel(shifted, slope, conv_w, phases, fine):
    rows, cols = shifted.shape[1] - 2, shifted.shape[2]
    channels = shifted.shape[3]
    n_rows, n_cols = rows // 2, cols // 2
    total = jnp.zeros((rows * cols, channels), f32)
    for k in range(3):
        for l in range(3):
            source = shifted[2 - l, pl.ds(2 - k, rows)].reshape(-1, channels)
            total = total + dot_nt(source, conv_w[k, l])
    put(fine, 0, (total * slope[...]).astype(bf16).astype(f32))
    whole = phases.shape[2]
    for row_phase in range(2):
        for col_phase in range(2):
            for row in range(n_rows):
                start = (2 * row + row_phase) * cols + col_phase
                phases[row_phase, col_phase, row] = get(fine, start, n_cols, 2).astype(bf16)
            for row in range(n_rows, whole):
                phases[row_phase, col_phase, row] = jnp.zeros((n_cols, channels), bf16)


def up_kernel(near, phases, partial, send):
    _, _, whole, n_cols, channels = phases.shape
    turned = {}
    for row_off in range(2):
        for col_off in range(2):
            cells = near[col_off, pl.ds(row_off, whole)]
            turned[row_off, col_off] = cells.reshape(whole * n_cols, channels).T
    for k in range(3):
        row_phase, row_off = forward_taps[k]
        for l in range(3):
            col_phase, col_off = forward_taps[l]
            source = phases[row_phase, col_phase].reshape(whole * n_cols, channels)
            partial[pl.ds((3 * k + l) * channels, channels), :] = dot(
                turned[row_off, col_off], source
            )
    other_core(partial, send)


def ring_kernel(
    coarse, cot, left, right, upper, lower, conv_w, up_w, ring_act, ring_grad, ring, wide,
):
    rows, cols, channels = cot.shape
    n_rows, n_cols = rows // 2, cols // 2
    at = Layout(n_rows, n_cols)
    stride, step = cols + 2 * MARGIN, n_cols + 2 * MARGIN
    _, _, band, n_bands = place_of()
    has_upper, has_lower = band > 0, band < n_bands - 1

    def corner(message, which):
        return message[at.corner + which : at.corner + which + 1, :]

    def cell(i, j):
        return (i + 1) * step + MARGIN + j

    for row in range(n_rows):
        put(wide, cell(row, 0), coarse[row].astype(f32))
    for row, message in ((-1, upper), (n_rows, lower)):
        put(wide, cell(row, 0), message[at.row_coarse : at.row_coarse + n_cols, :])
        put(wide, cell(row, -1), corner(message, COARSE[0]))
        put(wide, cell(row, n_cols), corner(message, COARSE[2]))
    put(wide, cell(0, -1), left[at.coarse : at.coarse + n_rows, :], step)
    put(wide, cell(0, n_cols), right[at.coarse : at.coarse + n_rows, :], step)
    total = jnp.zeros((at.ring_size, channels), f32)
    for k in range(3):
        for l in range(3):
            put(ring, 0, jnp.zeros((at.ring_size, channels), f32))
            for base, i in ((at.bottom, n_rows),) if k == 1 else ((at.top, k // 2 * -1),):
                start = cell(i, -1 if l == 2 else 0)
                put(ring, base + (l == 1), get(wide, start, n_cols + 1), 2)
            base, j = (at.right, n_cols) if l == 1 else (at.left, -(l // 2))
            start = cell(1 if k == 0 else 0, j)
            put(ring, base + (k != 1), get(wide, start, n_rows, step), 2)
            total = total + dot(get(ring, 0, at.ring_size).astype(bf16), up_w[k, l])
    put(ring, 0, jnp.zeros((at.ring_size, channels), f32))
    for base, message in ((at.top, upper), (at.bottom, lower)):
        put(ring, base + 1, message[at.row_skip : at.row_skip + cols, :])
        put(ring, base, corner(message, SKIP[0]))
        put(ring, base + cols + 1, corner(message, SKIP[2]))
    put(ring, at.left, left[at.skip : at.skip + rows, :])
    put(ring, at.right, right[at.skip : at.skip + rows, :])
    preact = total + get(ring, 0, at.ring_size)
    sigma = jax.nn.sigmoid(preact)
    value = preact * sigma
    slope = sigma + value * (1.0 - sigma)
    value = value.astype(bf16).astype(f32)
    ring_act[...] = value
    for base, exists in ((at.top, has_upper), (at.bottom, has_lower)):
        strip = value[base : base + cols + 2]
        ring_act[base : base + cols + 2, :] = jnp.where(exists, strip, 0.0)

    def fine(p, q):
        return (p + 2) * stride + MARGIN + q

    for row in range(rows):
        put(wide, fine(row, 0), cot[row].astype(f32))
    for row, message, start, which in (
        (-1, upper, at.row_cot, COT), (-2, upper, at.row_cot_2, COT_2), (rows, lower, at.row_cot, COT),
    ):
        put(wide, fine(row, 0), message[start : start + cols, :])
        for col, one in ((-1, which[0]), (-2, which[1]), (cols, which[2])):
            put(wide, fine(row, col), corner(message, one))
    put(wide, fine(0, -1), left[at.cot : at.cot + rows, :], stride)
    put(wide, fine(0, -2), left[at.cot_2 : at.cot_2 + rows, :], stride)
    put(wide, fine(0, cols), right[at.cot : at.cot + rows, :], stride)
    total = jnp.zeros((at.grad_size, channels), f32)
    for k in range(3):
        for l in range(3):
            put(ring, at.top, get(wide, fine(-k, -l), cols + 1))
            put(ring, at.grad_left, get(wide, fine(1 - k, -l), rows, stride))
            source = get(ring, 0, at.grad_size).astype(bf16)
            total = total + dot_nt(source, conv_w[k, l])
    strip = (total[: cols + 1] * slope[at.top : at.top + cols + 1]).astype(bf16).astype(f32)
    put(ring_grad, at.top, jnp.where(has_upper, strip, 0.0))
    strip = total[at.grad_left : at.grad_left + rows] * slope[at.left : at.left + rows]
    put(ring_grad, at.grad_left, strip.astype(bf16).astype(f32))


def decoded_kernel(act, ring_act, conv_w, decoded, padded, shifted):
    rows, cols, channels = act.shape
    at = Layout(rows // 2, cols // 2)
    stride = cols + 2 * MARGIN
    for row in range(rows):
        put(padded, (row + 1) * stride + MARGIN, act[row].astype(f32))
    for row, base in ((0, at.top), (rows + 1, at.bottom)):
        put(padded, row * stride + MARGIN - 1, ring_act[base : base + cols + 2, :])
    put(padded, stride + MARGIN - 1, ring_act[at.left : at.left + rows, :], stride)
    put(padded, stride + MARGIN + cols, ring_act[at.right : at.right + rows, :], stride)
    for row in range(rows + 2):
        for shift in range(3):
            start = row * stride + MARGIN - 1 + shift
            shifted[shift, row] = get(padded, start, cols).astype(bf16)
    total = jnp.zeros((rows * cols, channels), f32)
    for k in range(3):
        for l in range(3):
            source = shifted[l, pl.ds(k, rows)].reshape(-1, channels)
            total = total + dot(source, conv_w[k, l])
    decoded[...] = total.astype(bf16).reshape(decoded.shape)

def coarse_kernel(phases, ring_grad, up_w, coarse_out, padded, moved):
    n_rows, n_cols, channels = coarse_out.shape
    at = Layout(n_rows, n_cols)
    stride = n_cols + 2 * MARGIN
    for phase, start in ((0, 1), (1, 2), (2, 0)):
        moved[phase, 0] = get(ring_grad, at.top + start, n_cols, 2).astype(bf16)
    for phase in range(2):
        for row in range(n_rows):
            moved[phase, 1 + row] = phases[1, phase, row]
    for row_phase in range(2):
        for row in range(n_rows):
            put(padded, row * stride + MARGIN, phases[row_phase, 1, row].astype(f32))
        put(padded, MARGIN - 1, get(ring_grad, at.grad_left + row_phase, n_rows, 2), stride)
        for row in range(n_rows):
            cells = get(padded, row * stride + MARGIN - 1, n_cols).astype(bf16)
            if row_phase:
                moved[2, 1 + row] = cells
            else:
                moved[3, row] = cells
    total = jnp.zeros((n_rows * n_cols, channels), f32)
    for k in range(3):
        for l in range(3):
            if k == 1:
                if l == 0:
                    source = moved[3, pl.ds(0, n_rows)]
                else:
                    source = phases[0, l - 1, pl.ds(0, n_rows)]
            else:
                source = moved[(2, 0, 1)[l], pl.ds(k // 2, n_rows)]
            total = total + dot_nt(source.reshape(n_rows * n_cols, channels), up_w[k, l])
    coarse_out[...] = total.astype(bf16).reshape(coarse_out.shape)


def halving(count):
    bits = (count // 2).bit_length() - 1
    return [[(step + core) % bits for step in range(bits)] for core in range(2)]


def mask_of(slot, order):
    last = len(order) - 1
    return sum(1 << bit for step, bit in enumerate(order) if slot >> (last - step) & 1)


def core_kernel(partial, got, own, message):
    slots, half, block = got.shape[0], own.shape[0], got.shape[1]
    core, chip, _, _ = place_of()
    even, odd = halving(2 * slots)
    for slot in range(slots):
        target = chip ^ jnp.where(core == 0, mask_of(slot, even), mask_of(slot, odd))
        mine = pl.multiple_of((2 * target + core) * block, 16)
        total = partial[pl.ds(mine, block), :] + got[target].astype(f32)
        if slot < half:
            own[slot] = total
        else:
            message[slot - half] = total.astype(bf16)


def plane_kernel(before, got, own, message):
    half = own.shape[0]
    for slot in range(2 * half):
        total = before[slot] + got[slot].astype(f32)
        if slot < half:
            own[slot] = total
        else:
            message[slot - half] = total.astype(bf16)


def band_kernel(conv, got_conv, up, got_up, own, *refs):
    n_bands, messages, cut = len(refs), refs[:-1], refs[-1]
    conv_total = conv[0] + got_conv[0].astype(f32)
    up_total = up[0] + got_up[0].astype(f32)
    cols = conv_total.shape[1] // n_bands
    for band in range(n_bands):
        cut[band, :, :cols] = conv_total[:, band * cols : (band + 1) * cols]
        cut[band, :, cols:] = up_total[:, band * cols : (band + 1) * cols]
    band = place_of()[2]
    own[...] = cut[band]
    for k, message in enumerate(messages):
        message[...] = cut[lax.rem(band + k + 1, n_bands)].astype(bf16)


def last_kernel(own, *refs):
    peers, (conv, up) = refs[:-2], refs[-2:]
    total = own[...]
    for peer in peers:
        total = total + peer[...].astype(f32)
    turned = total.T
    conv[...] = turned[: conv.shape[0]]
    up[...] = turned[conv.shape[0] :]


def xor_pairs(count, bits):
    return [(i, i ^ bits) for i in range(count)]


def core_sum(partial, send):
    groups, block, channels = send.shape
    got = lax.ppermute(send, "face", xor_pairs(lax.axis_size("face"), 1))
    shape = (groups // 2, block, channels)
    return kernel_call(core_kernel, [sds(shape, f32), sds(shape, bf16)], [], 0, partial, got)


def plane_swap(message, step):
    faces = lax.axis_size("face")
    orders = halving(faces)
    return lax.ppermute(message, "face", [(i, i ^ 2 << orders[i % 2][step]) for i in range(faces)])


def plane_sum(own, got):
    half, block, channels = own.shape
    shape = (half // 2, block, channels)
    return kernel_call(plane_kernel, [sds(shape, f32), sds(shape, bf16)], [], 0, own, got)


def band_sum(conv, got_conv, up, got_up):
    bands = lax.axis_size("band")
    _, block, channels = conv.shape
    cols = channels // bands
    shape = (block, 2 * cols)
    own, *messages = kernel_call(
        band_kernel, [sds(shape, f32)] + [sds(shape, bf16)] * (bands - 1),
        [pltpu.VMEM((bands,) + shape, f32)], 0, conv, got_conv, up, got_up,
    )
    got = [
        lax.ppermute(messages[k - 1], "band", [(i, (i + k) % bands) for i in range(bands)])
        for k in range(1, bands)
    ]
    return [a.T for a in kernel_call(last_kernel, [sds((cols, block), f32)] * 2, [], 0, own, *got)]


def after(value, *others):
    return lax.optimization_barrier((value, *others))[0]


def swap(first, second, axis, wrap):
    one, two = pairs(lax.axis_size(axis), wrap)
    return lax.ppermute(first, axis, one), lax.ppermute(second, axis, two)


def local(coarse, skip, up_weight, conv_weight, cotangent):
    n_rows, n_cols, channels = coarse.shape
    rows, cols, _ = skip.shape
    at = Layout(n_rows, n_cols)
    faces = lax.axis_size("face")
    groups, block = faces // 2, 9 * channels // faces

    flat = halves(rows * cols, channels)
    message = sds((at.face_size, channels), bf16)
    edges = pltpu.VMEM(message.shape, f32)
    first, second, cotangent, skip, coarse = kernel_call(
        face_message,
        [message, message, sds(cotangent.shape, bf16), sds(skip.shape, bf16), sds(coarse.shape, bf16)],
        [flat, edges, edges, pltpu.SemaphoreType.DMA((3,))],
        0, coarse, skip, cotangent, far=(0, 1, 2),
    )
    first, second = swap(first, second, "face", True)
    side = sds(message.shape, f32)
    message = sds((at.band_size, channels), bf16)
    edges = pltpu.VMEM(message.shape, f32)
    first, second, left, right = kernel_call(
        band_message, [message, message, side, side], [edges, edges],
        0, coarse, skip, cotangent, first, second,
    )
    first, second = swap(first, second, "band", False)

    cells = n_rows * n_cols
    stride = cols + 2 * MARGIN
    padded = halves((rows + 2) * stride, channels)
    shift_shape = (3, rows + 2, cols, channels)
    whole = -(-cells // 256) * 256 // n_cols
    partials = [sds((9 * channels, channels), f32), sds((groups, block, channels), bf16)]
    side = sds(message.shape, f32)
    shifted, near, act, slope, part_conv, send_conv, upper, lower, conv_weight = kernel_call(
        act_kernel,
        [
            sds(shift_shape, bf16), sds((2, whole + 1, n_cols, channels), bf16),
            sds(skip.shape, bf16), sds((rows * cols, channels), f32), *partials, side, side,
            sds(conv_weight.shape, bf16),
        ],
        [padded, flat, pltpu.SemaphoreType.DMA],
        0, coarse, skip, cotangent, left, right, second, first, up_weight, conv_weight, far=(8,),
    )
    phases = kernel_call(
        grad_kernel, [sds((2, 2, whole, n_cols, channels), bf16)], [flat],
        0, shifted, slope, conv_weight,
    )[0]
    part_up, send_up = kernel_call(up_kernel, partials, [], 0, near, phases)
    own_conv, to_conv = core_sum(after(part_conv, send_up), send_conv)
    got_conv = plane_swap(to_conv, 0)
    own_up, to_up = core_sum(after(part_up, to_conv), send_up)
    got_up = plane_swap(to_up, 0)
    ring_act, ring_grad = kernel_call(
        ring_kernel,
        [
            sds((at.ring_size, channels), f32),
            sds((channels // LANES, at.grad_size, LANES), f32),
        ],
        [halves(at.ring_size, channels), halves((rows + 3) * stride, channels)],
        0, coarse, cotangent, after(left, to_up), right, upper, lower, conv_weight, up_weight,
    )
    own_conv = after(own_conv, ring_act)
    steps = (faces // 2).bit_length() - 1
    for step in range(1, steps):
        own_conv, to_conv = plane_sum(own_conv, got_conv)
        got_conv = plane_swap(to_conv, step)
        if step == 1:
            decoded = kernel_call(
                decoded_kernel, [sds(skip.shape, bf16)], [padded, pltpu.VMEM(shift_shape, bf16)],
                0, act, after(ring_act, to_conv), conv_weight,
            )[0]
            own_up = after(own_up, decoded)
        own_up, to_up = plane_sum(own_up, got_up)
        got_up = plane_swap(to_up, step)
        if step == 1:
            grad_coarse = kernel_call(
                coarse_kernel, [sds(coarse.shape, bf16)],
                [
                    halves(n_rows * (n_cols + 2 * MARGIN), channels),
                    pltpu.VMEM((4, n_rows + 1, n_cols, channels), bf16),
                ],
                0, phases, after(ring_grad, to_up), up_weight,
            )[0]
            own_up = after(own_up, grad_coarse)
    grad_conv, grad_up = band_sum(own_conv, got_conv, own_up, got_up)
    return (decoded, grad_coarse, grad_up, grad_conv)


def solution(mesh):
    return jax.shard_map(
        local,
        mesh=mesh,
        in_specs=(
            P("band", "face", None),
            P("band", "face", None),
            P(),
            P(),
            P("band", "face", None),
        ),
        out_specs=(
            P("band", "face", None),
            P("band", "face", None),
            P("face", "band"),
            P("face", "band"),
        ),
        check_vma=False,
    )
```

```python
import jax
import jax.numpy as jnp
from jax import lax
from jax.experimental import pallas as pl
from jax.experimental.pallas import tpu as pltpu
from jax.sharding import PartitionSpec as P

f32, bf16 = jnp.float32, jnp.bfloat16
forward_taps = ((1, 1), (0, 0), (1, 0))
backward_taps = ((1, 0), (0, 1), (1, 1))
MARGIN = 8
LANES = 128


def sds(shape, dtype):
    return jax.ShapeDtypeStruct(shape, dtype)


def kernel_call(body, outs, scratch, flops, *args, far=(), changed=None):
    vmem = pl.BlockSpec(memory_space=pltpu.VMEM)
    hbm = pl.BlockSpec(memory_space=pltpu.HBM)
    moved = sum(a.size * a.dtype.itemsize for a in args)
    moved += sum(a.size * a.dtype.itemsize for a in outs)
    args = [
        pltpu.with_memory_space_constraint(a, pltpu.HBM) if i in far else a
        for i, a in enumerate(args)
    ]
    return pl.pallas_call(
        body,
        out_shape=tuple(outs),
        in_specs=[hbm if i in far else vmem for i in range(len(args))],
        out_specs=tuple(vmem for _ in outs),
        scratch_shapes=scratch,
        input_output_aliases=changed or {},
        compiler_params=pltpu.CompilerParams(vmem_limit_bytes=28 * 2**20),
        cost_estimate=pl.CostEstimate(flops=flops, bytes_accessed=moved, transcendentals=0),
    )(*args)


def place_of():
    face = lax.axis_index("face")
    return lax.rem(face, 2), lax.div(face, 2), lax.axis_index("band"), lax.axis_size("band")


def dot(a, b):
    return jnp.dot(a, b, preferred_element_type=f32)


def dot_nt(a, b):
    return lax.dot_general(a, b, (((1,), (1,)), ((), ())), preferred_element_type=f32)


def pairs(count, wrap):
    first = [(i, i ^ 1) for i in range(count)]
    second = []
    for i in range(count):
        j = i + 1 if i % 2 else i - 1
        if wrap or 0 <= j < count:
            second.append((i, j % count))
    return first, second


def up16(n):
    return (n + 15) // 16 * 16


def halves(n_rows, channels):
    return pltpu.VMEM((channels // LANES, n_rows, LANES), f32)


def put(ref, start, value, step=1):
    for part in range(ref.shape[0]):
        rows = pl.ds(start, value.shape[0], stride=step if step > 1 else None)
        ref[part, rows, :] = value[:, part * LANES : (part + 1) * LANES]


def get(ref, start, count, step=1):
    rows = pl.ds(start, count, stride=step if step > 1 else None)
    return jnp.concatenate([ref[part, rows, :] for part in range(ref.shape[0])], axis=1)


def fill(ref, start, value):
    ref[start : start + value.shape[0], :] = value


def other_core(partial, send):
    core = place_of()[0]
    groups, block, _ = send.shape
    for group in range(groups):
        theirs = pl.multiple_of((2 * group + 1 - core) * block, 16)
        send[group] = partial[pl.ds(theirs, block), :].astype(bf16)


class Layout:
    def __init__(self, n_rows, n_cols):
        rows, cols = 2 * n_rows, 2 * n_cols
        self.cot, self.cot_2, self.skip, self.coarse = 0, rows, 2 * rows, 3 * rows
        self.face_size = up16(3 * rows + n_rows)
        self.row_cot, self.row_cot_2, self.row_skip = 0, cols, 2 * cols
        self.row_coarse, self.corner = 3 * cols, 3 * cols + n_cols
        self.band_size = self.corner + 16
        ring = (cols + 2 + 7) // 8 * 8
        self.top, self.bottom, self.left, self.right = 0, ring, 2 * ring, 2 * ring + rows
        self.ring_size = up16(2 * ring + 2 * rows)
        self.grad_left, self.grad_size = ring, up16(ring + rows)


COT, COT_2, SKIP, COARSE = (0, 1, 2), (3, 4, 5), (6, None, 7), (8, None, 9)


def face_message(coarse, skip, cot, first, second, cot_v, skip_v, coarse_v, flat, before, after, sems):
    rows, cols, _ = cot.shape
    n_rows, n_cols, _ = coarse.shape
    at = Layout(n_rows, n_cols)
    copies = [
        pltpu.make_async_copy(source, target, sems.at[i])
        for i, (source, target) in enumerate(((cot, cot_v), (skip, skip_v), (coarse, coarse_v)))
    ]
    for copy in copies:
        copy.start()
    before[...] = jnp.zeros_like(before)
    after[...] = jnp.zeros_like(after)
    for copy, array, start, start_2 in (
        (copies[0], cot_v, at.cot, at.cot_2), (copies[1], skip_v, at.skip, None), (copies[2], coarse_v, at.coarse, None),
    ):
        copy.wait()
        n, width, channels = array.shape
        put(flat, 0, array[:, :16, :].astype(f32)[:, :8, :].reshape(n * 8, channels))
        put(flat, n * 8, array[:, width - 16 :, :].astype(f32)[:, 8:, :].reshape(n * 8, channels))
        fill(before, start, get(flat, 0, n, 8))
        fill(after, start, get(flat, n * 8 + 7, n, 8))
        if start_2 is not None:
            fill(after, start_2, get(flat, n * 8 + 6, n, 8))
    even = place_of()[0] == 0
    first[...] = jnp.where(even, after[...], before[...]).astype(bf16)
    second[...] = jnp.where(even, before[...], after[...]).astype(bf16)


def band_message(coarse, skip, cot, got_first, got_second, first, second, left, right, before, after):
    rows, cols, channels = cot.shape
    n_rows, n_cols, _ = coarse.shape
    at = Layout(n_rows, n_cols)
    even = place_of()[0] == 0
    one, two = got_first[...].astype(f32), got_second[...].astype(f32)
    left[...] = jnp.where(even, two, one)
    right[...] = jnp.where(even, one, two)
    for message, row, row_2, cell in ((before, 0, None, 0), (after, rows - 1, rows - 2, n_rows - 1)):
        fill(message, at.row_cot, cot[row].astype(f32))
        if row_2 is None:
            fill(message, at.row_cot_2, jnp.zeros((cols, channels), f32))
        else:
            fill(message, at.row_cot_2, cot[row_2].astype(f32))
        fill(message, at.row_skip, skip[row].astype(f32))
        fill(message, at.row_coarse, coarse[cell].astype(f32))
        fill(message, at.corner, jnp.zeros((16, channels), f32))
        corners = [
            (COT[0], left, at.cot + row), (COT[1], left, at.cot_2 + row), (COT[2], right, at.cot + row),
            (SKIP[0], left, at.skip + row), (SKIP[2], right, at.skip + row),
            (COARSE[0], left, at.coarse + cell), (COARSE[2], right, at.coarse + cell),
        ]
        if row_2 is not None:
            corners += [
                (COT_2[0], left, at.cot + row_2), (COT_2[1], left, at.cot_2 + row_2),
                (COT_2[2], right, at.cot + row_2),
            ]
        for corner, side, source in corners:
            fill(message, at.corner + corner, side[source : source + 1, :])
    even = lax.rem(place_of()[2], 2) == 0
    first[...] = jnp.where(even, after[...], before[...]).astype(bf16)
    second[...] = jnp.where(even, before[...], after[...]).astype(bf16)


def inner_kernel(
    coarse, skip, cot, left, right, up_w, conv_w,
    shifted, near, act, slope, partial, last_pre, conv_v, padded, pre, sem,
):
    n_rows, n_cols, channels = coarse.shape
    rows, cols, _ = skip.shape
    at = Layout(n_rows, n_cols)
    stride = cols + 2 * MARGIN
    copy = pltpu.make_async_copy(conv_w, conv_v, sem)
    copy.start()
    for row in range(n_rows):
        near[0, row] = coarse[row]
        put(padded, row * stride, coarse[row].astype(f32))
    put(padded, n_cols, right[at.coarse : at.coarse + n_rows, :], stride)
    for row in range(n_rows):
        near[1, row] = get(padded, row * stride + 1, n_cols).astype(bf16)
    for row in range(n_rows, near.shape[1]):
        for side in range(2):
            near[side, row] = jnp.zeros((n_cols, channels), bf16)
    sums = {}
    for k in range(3):
        row_phase, row_off = forward_taps[k]
        for l in range(3):
            col_phase, col_off = forward_taps[l]
            source = near[col_off, pl.ds(row_off, n_rows)].reshape(n_rows * n_cols, channels)
            term = dot(source, up_w[k, l])
            name = (row_phase, col_phase)
            sums[name] = sums[name] + term if name in sums else term
    for (row_phase, col_phase), total in sums.items():
        for row in range(n_rows):
            start = (2 * row + row_phase) * cols + col_phase
            put(pre, start, total[row * n_cols : (row + 1) * n_cols], 2)
    for row in range(rows):
        put(padded, row * stride + MARGIN, cot[row].astype(f32))
    put(padded, MARGIN - 1, left[at.cot : at.cot + rows, :], stride)
    put(padded, MARGIN + cols, right[at.cot : at.cot + rows, :], stride)
    for row in range(rows):
        for shift in (0, 2):
            start = row * stride + MARGIN - 1 + shift
            shifted[shift, row + 1] = get(padded, start, cols).astype(bf16)
        shifted[1, row + 1] = cot[row]
    for shift in range(3):
        shifted[shift, 0] = jnp.zeros((cols, channels), bf16)
        shifted[shift, rows + 1] = jnp.zeros((cols, channels), bf16)
    preact = get(pre, 0, rows * cols) + skip[...].reshape(rows * cols, channels).astype(f32)
    last_pre[...] = preact[(rows - 1) * cols :]
    sigma = jax.nn.sigmoid(preact)
    value = preact * sigma
    slope[...] = sigma + value * (1.0 - sigma)
    row_of = lax.broadcasted_iota(jnp.int32, value.shape, 0)
    act_flat = jnp.where(row_of < (rows - 1) * cols, value, 0.0).astype(bf16)
    act[...] = act_flat.reshape(act.shape)
    act_t = act_flat.T
    for k in range(3):
        for l in range(3):
            source = shifted[2 - l, pl.ds(2 - k, rows)].reshape(-1, channels)
            partial[pl.ds((3 * k + l) * channels, channels), :] = dot(act_t, source)
    copy.wait()


def act_kernel(
    got_second, got_first, right, up_w, last_pre, shifted_in, near_in, act_in, slope_in, partial_in,
    shifted, near, act, slope, partial, send, upper, lower, padded, pre,
):
    rows, cols, channels = act.shape
    n_rows, n_cols = rows // 2, cols // 2
    at = Layout(n_rows, n_cols)
    even = lax.rem(place_of()[2], 2) == 0
    one, two = got_first[...].astype(f32), got_second[...].astype(f32)
    upper[...] = jnp.where(even, two, one)
    lower[...] = jnp.where(even, one, two)
    below = lower[at.row_coarse : at.row_coarse + n_cols, :]
    corner = at.corner + COARSE[2]
    put(padded, 0, below)
    put(padded, n_cols, lower[corner : corner + 1, :])
    cells = [below.astype(bf16), get(padded, 1, n_cols).astype(bf16)]
    near[0, n_rows] = cells[0]
    near[1, n_rows] = cells[1]
    put(pre, 0, dot(cells[0], up_w[0, 1]), 2)
    put(pre, 1, dot(cells[1], up_w[0, 0]) + dot(cells[0], up_w[0, 2]), 2)
    preact = last_pre[...] + get(pre, 0, cols)
    sigma = jax.nn.sigmoid(preact)
    value = preact * sigma
    slope[(rows - 1) * cols :, :] = sigma + value * (1.0 - sigma)
    last = value.astype(bf16)
    act[rows - 1] = last
    for row, message in ((0, upper), (rows + 1, lower)):
        centre = message[at.row_cot : at.row_cot + cols, :]
        put(padded, MARGIN, centre)
        for col, one in ((-1, COT[0]), (cols, COT[2])):
            put(padded, MARGIN + col, message[at.corner + one : at.corner + one + 1, :])
        shifted[0, row] = get(padded, MARGIN - 1, cols).astype(bf16)
        shifted[1, row] = centre.astype(bf16)
        shifted[2, row] = get(padded, MARGIN + 1, cols).astype(bf16)
    last_t = last.T
    both_t = jnp.concatenate([last, act_in[0]], axis=0).T
    for k in range(3):
        for l in range(3):
            beside = shifted[2 - l, rows + 1 - k]
            if k == 2:
                term = dot(both_t, jnp.concatenate([beside, shifted[2 - l, 0]], axis=0))
            else:
                term = dot(last_t, beside)
            tap = pl.ds((3 * k + l) * channels, channels)
            partial[tap, :] = partial_in[tap, :] + term
    other_core(partial, send)


def grad_kernel(shifted, slope, conv_w, phases, fine):
    rows, cols = shifted.shape[1] - 2, shifted.shape[2]
    channels = shifted.shape[3]
    n_rows, n_cols = rows // 2, cols // 2
    total = jnp.zeros((rows * cols, channels), f32)
    for k in range(3):
        for l in range(3):
            source = shifted[2 - l, pl.ds(2 - k, rows)].reshape(-1, channels)
            total = total + dot_nt(source, conv_w[k, l])
    put(fine, 0, (total * slope[...]).astype(bf16).astype(f32))
    whole = phases.shape[2]
    for row_phase in range(2):
        for col_phase in range(2):
            for row in range(n_rows):
                start = (2 * row + row_phase) * cols + col_phase
                phases[row_phase, col_phase, row] = get(fine, start, n_cols, 2).astype(bf16)
            for row in range(n_rows, whole):
                phases[row_phase, col_phase, row] = jnp.zeros((n_cols, channels), bf16)


def up_kernel(near, phases, partial, send):
    _, _, whole, n_cols, channels = phases.shape
    turned = {}
    for row_off in range(2):
        for col_off in range(2):
            cells = near[col_off, pl.ds(row_off, whole)]
            turned[row_off, col_off] = cells.reshape(whole * n_cols, channels).T
    for k in range(3):
        row_phase, row_off = forward_taps[k]
        for l in range(3):
            col_phase, col_off = forward_taps[l]
            source = phases[row_phase, col_phase].reshape(whole * n_cols, channels)
            partial[pl.ds((3 * k + l) * channels, channels), :] = dot(
                turned[row_off, col_off], source
            )
    other_core(partial, send)


def ring_kernel(
    coarse, cot, left, right, upper, lower, conv_w, up_w, ring_act, ring_grad, ring, wide,
):
    rows, cols, channels = cot.shape
    n_rows, n_cols = rows // 2, cols // 2
    at = Layout(n_rows, n_cols)
    stride, step = cols + 2 * MARGIN, n_cols + 2 * MARGIN
    _, _, band, n_bands = place_of()
    has_upper, has_lower = band > 0, band < n_bands - 1

    def corner(message, which):
        return message[at.corner + which : at.corner + which + 1, :]

    def cell(i, j):
        return (i + 1) * step + MARGIN + j

    for row in range(n_rows):
        put(wide, cell(row, 0), coarse[row].astype(f32))
    for row, message in ((-1, upper), (n_rows, lower)):
        put(wide, cell(row, 0), message[at.row_coarse : at.row_coarse + n_cols, :])
        put(wide, cell(row, -1), corner(message, COARSE[0]))
        put(wide, cell(row, n_cols), corner(message, COARSE[2]))
    put(wide, cell(0, -1), left[at.coarse : at.coarse + n_rows, :], step)
    put(wide, cell(0, n_cols), right[at.coarse : at.coarse + n_rows, :], step)
    total = jnp.zeros((at.ring_size, channels), f32)
    for k in range(3):
        for l in range(3):
            put(ring, 0, jnp.zeros((at.ring_size, channels), f32))
            for base, i in ((at.bottom, n_rows),) if k == 1 else ((at.top, k // 2 * -1),):
                start = cell(i, -1 if l == 2 else 0)
                put(ring, base + (l == 1), get(wide, start, n_cols + 1), 2)
            base, j = (at.right, n_cols) if l == 1 else (at.left, -(l // 2))
            start = cell(1 if k == 0 else 0, j)
            put(ring, base + (k != 1), get(wide, start, n_rows, step), 2)
            total = total + dot(get(ring, 0, at.ring_size).astype(bf16), up_w[k, l])
    put(ring, 0, jnp.zeros((at.ring_size, channels), f32))
    for base, message in ((at.top, upper), (at.bottom, lower)):
        put(ring, base + 1, message[at.row_skip : at.row_skip + cols, :])
        put(ring, base, corner(message, SKIP[0]))
        put(ring, base + cols + 1, corner(message, SKIP[2]))
    put(ring, at.left, left[at.skip : at.skip + rows, :])
    put(ring, at.right, right[at.skip : at.skip + rows, :])
    preact = total + get(ring, 0, at.ring_size)
    sigma = jax.nn.sigmoid(preact)
    value = preact * sigma
    slope = sigma + value * (1.0 - sigma)
    value = value.astype(bf16).astype(f32)
    ring_act[...] = value
    for base, exists in ((at.top, has_upper), (at.bottom, has_lower)):
        strip = value[base : base + cols + 2]
        ring_act[base : base + cols + 2, :] = jnp.where(exists, strip, 0.0)

    def fine(p, q):
        return (p + 2) * stride + MARGIN + q

    for row in range(rows):
        put(wide, fine(row, 0), cot[row].astype(f32))
    for row, message, start, which in (
        (-1, upper, at.row_cot, COT), (-2, upper, at.row_cot_2, COT_2), (rows, lower, at.row_cot, COT),
    ):
        put(wide, fine(row, 0), message[start : start + cols, :])
        for col, one in ((-1, which[0]), (-2, which[1]), (cols, which[2])):
            put(wide, fine(row, col), corner(message, one))
    put(wide, fine(0, -1), left[at.cot : at.cot + rows, :], stride)
    put(wide, fine(0, -2), left[at.cot_2 : at.cot_2 + rows, :], stride)
    put(wide, fine(0, cols), right[at.cot : at.cot + rows, :], stride)
    total = jnp.zeros((at.grad_size, channels), f32)
    for k in range(3):
        for l in range(3):
            put(ring, at.top, get(wide, fine(-k, -l), cols + 1))
            put(ring, at.grad_left, get(wide, fine(1 - k, -l), rows, stride))
            source = get(ring, 0, at.grad_size).astype(bf16)
            total = total + dot_nt(source, conv_w[k, l])
    strip = (total[: cols + 1] * slope[at.top : at.top + cols + 1]).astype(bf16).astype(f32)
    put(ring_grad, at.top, jnp.where(has_upper, strip, 0.0))
    strip = total[at.grad_left : at.grad_left + rows] * slope[at.left : at.left + rows]
    put(ring_grad, at.grad_left, strip.astype(bf16).astype(f32))


def decoded_kernel(act, ring_act, conv_w, decoded, padded, shifted):
    rows, cols, channels = act.shape
    at = Layout(rows // 2, cols // 2)
    stride = cols + 2 * MARGIN
    for row in range(rows):
        put(padded, (row + 1) * stride + MARGIN, act[row].astype(f32))
    for row, base in ((0, at.top), (rows + 1, at.bottom)):
        put(padded, row * stride + MARGIN - 1, ring_act[base : base + cols + 2, :])
    put(padded, stride + MARGIN - 1, ring_act[at.left : at.left + rows, :], stride)
    put(padded, stride + MARGIN + cols, ring_act[at.right : at.right + rows, :], stride)
    for row in range(rows + 2):
        for shift in range(3):
            start = row * stride + MARGIN - 1 + shift
            shifted[shift, row] = get(padded, start, cols).astype(bf16)
    total = jnp.zeros((rows * cols, channels), f32)
    for k in range(3):
        for l in range(3):
            source = shifted[l, pl.ds(k, rows)].reshape(-1, channels)
            total = total + dot(source, conv_w[k, l])
    decoded[...] = total.astype(bf16).reshape(decoded.shape)

def coarse_kernel(phases, ring_grad, up_w, coarse_out, padded, moved):
    n_rows, n_cols, channels = coarse_out.shape
    at = Layout(n_rows, n_cols)
    stride = n_cols + 2 * MARGIN
    for phase, start in ((0, 1), (1, 2), (2, 0)):
        moved[phase, 0] = get(ring_grad, at.top + start, n_cols, 2).astype(bf16)
    for phase in range(2):
        for row in range(n_rows):
            moved[phase, 1 + row] = phases[1, phase, row]
    for row_phase in range(2):
        for row in range(n_rows):
            put(padded, row * stride + MARGIN, phases[row_phase, 1, row].astype(f32))
        put(padded, MARGIN - 1, get(ring_grad, at.grad_left + row_phase, n_rows, 2), stride)
        for row in range(n_rows):
            cells = get(padded, row * stride + MARGIN - 1, n_cols).astype(bf16)
            if row_phase:
                moved[2, 1 + row] = cells
            else:
                moved[3, row] = cells
    total = jnp.zeros((n_rows * n_cols, channels), f32)
    for k in range(3):
        for l in range(3):
            if k == 1:
                if l == 0:
                    source = moved[3, pl.ds(0, n_rows)]
                else:
                    source = phases[0, l - 1, pl.ds(0, n_rows)]
            else:
                source = moved[(2, 0, 1)[l], pl.ds(k // 2, n_rows)]
            total = total + dot_nt(source.reshape(n_rows * n_cols, channels), up_w[k, l])
    coarse_out[...] = total.astype(bf16).reshape(coarse_out.shape)


def halving(count):
    bits = (count // 2).bit_length() - 1
    return [[(step + core) % bits for step in range(bits)] for core in range(2)]


def mask_of(slot, order):
    last = len(order) - 1
    return sum(1 << bit for step, bit in enumerate(order) if slot >> (last - step) & 1)


def core_kernel(partial, got, own, message):
    slots, half, block = got.shape[0], own.shape[0], got.shape[1]
    core, chip, _, _ = place_of()
    even, odd = halving(2 * slots)
    for slot in range(slots):
        target = chip ^ jnp.where(core == 0, mask_of(slot, even), mask_of(slot, odd))
        mine = pl.multiple_of((2 * target + core) * block, 16)
        total = partial[pl.ds(mine, block), :] + got[target].astype(f32)
        if slot < half:
            own[slot] = total
        else:
            message[slot - half] = total.astype(bf16)


def plane_kernel(before, got, own, message):
    half = own.shape[0]
    for slot in range(2 * half):
        total = before[slot] + got[slot].astype(f32)
        if slot < half:
            own[slot] = total
        else:
            message[slot - half] = total.astype(bf16)


def band_kernel(conv, got_conv, up, got_up, own, *refs):
    n_bands, messages, cut = len(refs), refs[:-1], refs[-1]
    conv_total = conv[0] + got_conv[0].astype(f32)
    up_total = up[0] + got_up[0].astype(f32)
    cols = conv_total.shape[1] // n_bands
    for band in range(n_bands):
        cut[band, :, :cols] = conv_total[:, band * cols : (band + 1) * cols]
        cut[band, :, cols:] = up_total[:, band * cols : (band + 1) * cols]
    band = place_of()[2]
    own[...] = cut[band]
    for k, message in enumerate(messages):
        message[...] = cut[lax.rem(band + k + 1, n_bands)].astype(bf16)


def last_kernel(own, *refs):
    peers, (conv, up) = refs[:-2], refs[-2:]
    total = own[...]
    for peer in peers:
        total = total + peer[...].astype(f32)
    turned = total.T
    conv[...] = turned[: conv.shape[0]]
    up[...] = turned[conv.shape[0] :]


def xor_pairs(count, bits):
    return [(i, i ^ bits) for i in range(count)]


def core_sum(partial, send):
    groups, block, channels = send.shape
    got = lax.ppermute(send, "face", xor_pairs(lax.axis_size("face"), 1))
    shape = (groups // 2, block, channels)
    return kernel_call(core_kernel, [sds(shape, f32), sds(shape, bf16)], [], 0, partial, got)


def plane_swap(message, step):
    faces = lax.axis_size("face")
    orders = halving(faces)
    return lax.ppermute(message, "face", [(i, i ^ 2 << orders[i % 2][step]) for i in range(faces)])


def plane_sum(own, got):
    half, block, channels = own.shape
    shape = (half // 2, block, channels)
    return kernel_call(plane_kernel, [sds(shape, f32), sds(shape, bf16)], [], 0, own, got)


def band_sum(conv, got_conv, up, got_up):
    bands = lax.axis_size("band")
    _, block, channels = conv.shape
    cols = channels // bands
    shape = (block, 2 * cols)
    own, *messages = kernel_call(
        band_kernel, [sds(shape, f32)] + [sds(shape, bf16)] * (bands - 1),
        [pltpu.VMEM((bands,) + shape, f32)], 0, conv, got_conv, up, got_up,
    )
    got = [
        lax.ppermute(messages[k - 1], "band", [(i, (i + k) % bands) for i in range(bands)])
        for k in range(1, bands)
    ]
    return [a.T for a in kernel_call(last_kernel, [sds((cols, block), f32)] * 2, [], 0, own, *got)]


def after(value, *others):
    return lax.optimization_barrier((value, *others))[0]


def swap(first, second, axis, wrap):
    one, two = pairs(lax.axis_size(axis), wrap)
    return lax.ppermute(first, axis, one), lax.ppermute(second, axis, two)


def local(coarse, skip, up_weight, conv_weight, cotangent):
    n_rows, n_cols, channels = coarse.shape
    rows, cols, _ = skip.shape
    at = Layout(n_rows, n_cols)
    faces = lax.axis_size("face")
    groups, block = faces // 2, 9 * channels // faces

    flat = halves(rows * cols, channels)
    message = sds((at.face_size, channels), bf16)
    edges = pltpu.VMEM(message.shape, f32)
    first, second, cotangent, skip, coarse = kernel_call(
        face_message,
        [message, message, sds(cotangent.shape, bf16), sds(skip.shape, bf16), sds(coarse.shape, bf16)],
        [flat, edges, edges, pltpu.SemaphoreType.DMA((3,))],
        0, coarse, skip, cotangent, far=(0, 1, 2),
    )
    first, second = swap(first, second, "face", True)
    side = sds(message.shape, f32)
    message = sds((at.band_size, channels), bf16)
    edges = pltpu.VMEM(message.shape, f32)
    first, second, left, right = kernel_call(
        band_message, [message, message, side, side], [edges, edges],
        0, coarse, skip, cotangent, first, second,
    )
    first, second = swap(first, second, "band", False)

    cells = n_rows * n_cols
    stride = cols + 2 * MARGIN
    padded = halves((rows + 2) * stride, channels)
    shift_shape = (3, rows + 2, cols, channels)
    whole = -(-cells // 256) * 256 // n_cols
    part = sds((9 * channels, channels), f32)
    blocks = [
        sds(shift_shape, bf16), sds((2, whole + 1, n_cols, channels), bf16),
        sds(skip.shape, bf16), sds((rows * cols, channels), f32), part,
    ]
    *inner, last_pre, conv_weight = kernel_call(
        inner_kernel,
        [*blocks, sds((cols, channels), f32), sds(conv_weight.shape, bf16)],
        [halves(rows * stride, channels), flat, pltpu.SemaphoreType.DMA],
        0, coarse, skip, cotangent, left, right, up_weight, conv_weight, far=(6,),
    )
    send = sds((groups, block, channels), bf16)
    side = sds(message.shape, f32)
    shifted, near, act, slope, part_conv, send_conv, upper, lower = kernel_call(
        act_kernel, [*blocks, send, side, side],
        [halves(stride, channels), halves(cols, channels)],
        0, second, first, right, up_weight, last_pre, *inner, changed={5 + i: i for i in range(5)},
    )
    phases = kernel_call(
        grad_kernel, [sds((2, 2, whole, n_cols, channels), bf16)], [flat],
        0, shifted, slope, conv_weight,
    )[0]
    part_up, send_up = kernel_call(up_kernel, [part, send], [], 0, near, phases)
    own_conv, to_conv = core_sum(after(part_conv, send_up), send_conv)
    got_conv = plane_swap(to_conv, 0)
    own_up, to_up = core_sum(after(part_up, to_conv), send_up)
    got_up = plane_swap(to_up, 0)
    ring_act, ring_grad = kernel_call(
        ring_kernel,
        [
            sds((at.ring_size, channels), f32),
            sds((channels // LANES, at.grad_size, LANES), f32),
        ],
        [halves(at.ring_size, channels), halves((rows + 3) * stride, channels)],
        0, coarse, cotangent, after(left, to_up), right, upper, lower, conv_weight, up_weight,
    )
    own_conv = after(own_conv, ring_act)
    steps = (faces // 2).bit_length() - 1
    for step in range(1, steps):
        own_conv, to_conv = plane_sum(own_conv, got_conv)
        got_conv = plane_swap(to_conv, step)
        if step == 1:
            decoded = kernel_call(
                decoded_kernel, [sds(skip.shape, bf16)], [padded, pltpu.VMEM(shift_shape, bf16)],
                0, act, after(ring_act, to_conv), conv_weight,
            )[0]
            own_up = after(own_up, decoded)
        own_up, to_up = plane_sum(own_up, got_up)
        got_up = plane_swap(to_up, step)
        if step == 1:
            grad_coarse = kernel_call(
                coarse_kernel, [sds(coarse.shape, bf16)],
                [
                    halves(n_rows * (n_cols + 2 * MARGIN), channels),
                    pltpu.VMEM((4, n_rows + 1, n_cols, channels), bf16),
                ],
                0, phases, after(ring_grad, to_up), up_weight,
            )[0]
            own_up = after(own_up, grad_coarse)
    grad_conv, grad_up = band_sum(own_conv, got_conv, own_up, got_up)
    return (decoded, grad_coarse, grad_up, grad_conv)


def solution(mesh):
    return jax.shard_map(
        local,
        mesh=mesh,
        in_specs=(
            P("band", "face", None),
            P("band", "face", None),
            P(),
            P(),
            P("band", "face", None),
        ),
        out_specs=(
            P("band", "face", None),
            P("band", "face", None),
            P("face", "band"),
            P("face", "band"),
        ),
        check_vma=False,
    )
```

```python
import jax
import jax.numpy as jnp
from jax import lax
from jax.experimental import pallas as pl
from jax.experimental.pallas import tpu as pltpu
from jax.sharding import PartitionSpec as P

f32, bf16 = jnp.float32, jnp.bfloat16
forward_taps = ((1, 1), (0, 0), (1, 0))
backward_taps = ((1, 0), (0, 1), (1, 1))
MARGIN = 8
LANES = 128


def sds(shape, dtype):
    return jax.ShapeDtypeStruct(shape, dtype)


def kernel_call(body, outs, scratch, flops, *args, far=(), changed=None):
    vmem = pl.BlockSpec(memory_space=pltpu.VMEM)
    hbm = pl.BlockSpec(memory_space=pltpu.HBM)
    moved = sum(a.size * a.dtype.itemsize for a in args)
    moved += sum(a.size * a.dtype.itemsize for a in outs)
    args = [
        pltpu.with_memory_space_constraint(a, pltpu.HBM) if i in far else a
        for i, a in enumerate(args)
    ]
    return pl.pallas_call(
        body,
        out_shape=tuple(outs),
        in_specs=[hbm if i in far else vmem for i in range(len(args))],
        out_specs=tuple(vmem for _ in outs),
        scratch_shapes=scratch,
        input_output_aliases=changed or {},
        compiler_params=pltpu.CompilerParams(vmem_limit_bytes=28 * 2**20),
        cost_estimate=pl.CostEstimate(flops=flops, bytes_accessed=moved, transcendentals=0),
    )(*args)


def place_of():
    face = lax.axis_index("face")
    return lax.rem(face, 2), lax.div(face, 2), lax.axis_index("band"), lax.axis_size("band")


def dot(a, b):
    return jnp.dot(a, b, preferred_element_type=f32)


def dot_nt(a, b):
    return lax.dot_general(a, b, (((1,), (1,)), ((), ())), preferred_element_type=f32)


def pairs(count, wrap):
    first = [(i, i ^ 1) for i in range(count)]
    second = []
    for i in range(count):
        j = i + 1 if i % 2 else i - 1
        if wrap or 0 <= j < count:
            second.append((i, j % count))
    return first, second


def up16(n):
    return (n + 15) // 16 * 16


def halves(n_rows, channels):
    return pltpu.VMEM((channels // LANES, n_rows, LANES), f32)


def put(ref, start, value, step=1):
    for part in range(ref.shape[0]):
        rows = pl.ds(start, value.shape[0], stride=step if step > 1 else None)
        ref[part, rows, :] = value[:, part * LANES : (part + 1) * LANES]


def get(ref, start, count, step=1):
    rows = pl.ds(start, count, stride=step if step > 1 else None)
    return jnp.concatenate([ref[part, rows, :] for part in range(ref.shape[0])], axis=1)


def fill(ref, start, value):
    ref[start : start + value.shape[0], :] = value


def other_core(partial, send):
    core = place_of()[0]
    groups, block, _ = send.shape
    for group in range(groups):
        theirs = pl.multiple_of((2 * group + 1 - core) * block, 16)
        send[group] = partial[pl.ds(theirs, block), :].astype(bf16)


class Layout:
    def __init__(self, n_rows, n_cols):
        rows, cols = 2 * n_rows, 2 * n_cols
        self.cot, self.cot_2, self.skip, self.coarse = 0, rows, 2 * rows, 3 * rows
        self.face_size = up16(3 * rows + n_rows)
        self.row_cot, self.row_cot_2, self.row_skip = 0, cols, 2 * cols
        self.row_coarse, self.corner = 3 * cols, 3 * cols + n_cols
        self.band_size = self.corner + 16
        ring = (cols + 2 + 7) // 8 * 8
        self.top, self.bottom, self.left, self.right = 0, ring, 2 * ring, 2 * ring + rows
        self.ring_size = up16(2 * ring + 2 * rows)
        self.grad_left, self.grad_size = ring, up16(ring + rows)


COT, COT_2, SKIP, COARSE = (0, 1, 2), (3, 4, 5), (6, None, 7), (8, None, 9)


def face_message(coarse, skip, cot, first, second, cot_v, skip_v, coarse_v, flat, before, after, sems):
    rows, cols, _ = cot.shape
    n_rows, n_cols, _ = coarse.shape
    at = Layout(n_rows, n_cols)
    copies = [
        pltpu.make_async_copy(source, target, sems.at[i])
        for i, (source, target) in enumerate(((cot, cot_v), (skip, skip_v), (coarse, coarse_v)))
    ]
    for copy in copies:
        copy.start()
    before[...] = jnp.zeros_like(before)
    after[...] = jnp.zeros_like(after)
    for copy, array, start, start_2 in (
        (copies[0], cot_v, at.cot, at.cot_2), (copies[1], skip_v, at.skip, None), (copies[2], coarse_v, at.coarse, None),
    ):
        copy.wait()
        n, width, channels = array.shape
        put(flat, 0, array[:, :16, :].astype(f32)[:, :8, :].reshape(n * 8, channels))
        put(flat, n * 8, array[:, width - 16 :, :].astype(f32)[:, 8:, :].reshape(n * 8, channels))
        fill(before, start, get(flat, 0, n, 8))
        fill(after, start, get(flat, n * 8 + 7, n, 8))
        if start_2 is not None:
            fill(after, start_2, get(flat, n * 8 + 6, n, 8))
    even = place_of()[0] == 0
    first[...] = jnp.where(even, after[...], before[...]).astype(bf16)
    second[...] = jnp.where(even, before[...], after[...]).astype(bf16)


def band_message(coarse, skip, cot, got_first, got_second, first, second, left, right, before, after):
    rows, cols, channels = cot.shape
    n_rows, n_cols, _ = coarse.shape
    at = Layout(n_rows, n_cols)
    even = place_of()[0] == 0
    one, two = got_first[...].astype(f32), got_second[...].astype(f32)
    left[...] = jnp.where(even, two, one)
    right[...] = jnp.where(even, one, two)
    for message, row, row_2, cell in ((before, 0, None, 0), (after, rows - 1, rows - 2, n_rows - 1)):
        fill(message, at.row_cot, cot[row].astype(f32))
        if row_2 is None:
            fill(message, at.row_cot_2, jnp.zeros((cols, channels), f32))
        else:
            fill(message, at.row_cot_2, cot[row_2].astype(f32))
        fill(message, at.row_skip, skip[row].astype(f32))
        fill(message, at.row_coarse, coarse[cell].astype(f32))
        fill(message, at.corner, jnp.zeros((16, channels), f32))
        corners = [
            (COT[0], left, at.cot + row), (COT[1], left, at.cot_2 + row), (COT[2], right, at.cot + row),
            (SKIP[0], left, at.skip + row), (SKIP[2], right, at.skip + row),
            (COARSE[0], left, at.coarse + cell), (COARSE[2], right, at.coarse + cell),
        ]
        if row_2 is not None:
            corners += [
                (COT_2[0], left, at.cot + row_2), (COT_2[1], left, at.cot_2 + row_2),
                (COT_2[2], right, at.cot + row_2),
            ]
        for corner, side, source in corners:
            fill(message, at.corner + corner, side[source : source + 1, :])
    even = lax.rem(place_of()[2], 2) == 0
    first[...] = jnp.where(even, after[...], before[...]).astype(bf16)
    second[...] = jnp.where(even, before[...], after[...]).astype(bf16)


def inner_kernel(
    coarse, skip, cot, left, right, up_w, conv_w,
    shifted, near, act, slope, partial, last_pre, conv_v, grad_act, padded, pre, sem,
):
    n_rows, n_cols, channels = coarse.shape
    rows, cols, _ = skip.shape
    at = Layout(n_rows, n_cols)
    stride = cols + 2 * MARGIN
    copy = pltpu.make_async_copy(conv_w, conv_v, sem)
    copy.start()
    for row in range(n_rows):
        near[0, row] = coarse[row]
        put(padded, row * stride, coarse[row].astype(f32))
    put(padded, n_cols, right[at.coarse : at.coarse + n_rows, :], stride)
    for row in range(n_rows):
        near[1, row] = get(padded, row * stride + 1, n_cols).astype(bf16)
    for row in range(n_rows, near.shape[1]):
        for side in range(2):
            near[side, row] = jnp.zeros((n_cols, channels), bf16)
    sums = {}
    for k in range(3):
        row_phase, row_off = forward_taps[k]
        for l in range(3):
            col_phase, col_off = forward_taps[l]
            source = near[col_off, pl.ds(row_off, n_rows)].reshape(n_rows * n_cols, channels)
            term = dot(source, up_w[k, l])
            name = (row_phase, col_phase)
            sums[name] = sums[name] + term if name in sums else term
    for (row_phase, col_phase), total in sums.items():
        for row in range(n_rows):
            start = (2 * row + row_phase) * cols + col_phase
            put(pre, start, total[row * n_cols : (row + 1) * n_cols], 2)
    for row in range(rows):
        put(padded, row * stride + MARGIN, cot[row].astype(f32))
    put(padded, MARGIN - 1, left[at.cot : at.cot + rows, :], stride)
    put(padded, MARGIN + cols, right[at.cot : at.cot + rows, :], stride)
    for row in range(rows):
        for shift in (0, 2):
            start = row * stride + MARGIN - 1 + shift
            shifted[shift, row + 1] = get(padded, start, cols).astype(bf16)
        shifted[1, row + 1] = cot[row]
    for shift in range(3):
        shifted[shift, 0] = jnp.zeros((cols, channels), bf16)
        shifted[shift, rows + 1] = jnp.zeros((cols, channels), bf16)
    preact = get(pre, 0, rows * cols) + skip[...].reshape(rows * cols, channels).astype(f32)
    last_pre[...] = preact[(rows - 1) * cols :]
    sigma = jax.nn.sigmoid(preact)
    value = preact * sigma
    slope[...] = sigma + value * (1.0 - sigma)
    row_of = lax.broadcasted_iota(jnp.int32, value.shape, 0)
    act_flat = jnp.where(row_of < (rows - 1) * cols, value, 0.0).astype(bf16)
    act[...] = act_flat.reshape(act.shape)
    act_t = act_flat.T
    for k in range(3):
        for l in range(3):
            source = shifted[2 - l, pl.ds(2 - k, rows)].reshape(-1, channels)
            partial[pl.ds((3 * k + l) * channels, channels), :] = dot(act_t, source)
    copy.wait()
    total = jnp.zeros((rows * cols, channels), f32)
    for k in range(3):
        for l in range(3):
            source = shifted[2 - l, pl.ds(2 - k, rows)].reshape(-1, channels)
            total = total + dot_nt(source, conv_v[k, l])
    grad_act[...] = total


def act_kernel(
    got_second, got_first, right, up_w, last_pre, shifted_in, near_in, act_in, slope_in, partial_in,
    shifted, near, act, slope, partial, send, upper, lower, padded, pre,
):
    rows, cols, channels = act.shape
    n_rows, n_cols = rows // 2, cols // 2
    at = Layout(n_rows, n_cols)
    even = lax.rem(place_of()[2], 2) == 0
    one, two = got_first[...].astype(f32), got_second[...].astype(f32)
    upper[...] = jnp.where(even, two, one)
    lower[...] = jnp.where(even, one, two)
    below = lower[at.row_coarse : at.row_coarse + n_cols, :]
    corner = at.corner + COARSE[2]
    put(padded, 0, below)
    put(padded, n_cols, lower[corner : corner + 1, :])
    cells = [below.astype(bf16), get(padded, 1, n_cols).astype(bf16)]
    near[0, n_rows] = cells[0]
    near[1, n_rows] = cells[1]
    put(pre, 0, dot(cells[0], up_w[0, 1]), 2)
    put(pre, 1, dot(cells[1], up_w[0, 0]) + dot(cells[0], up_w[0, 2]), 2)
    preact = last_pre[...] + get(pre, 0, cols)
    sigma = jax.nn.sigmoid(preact)
    value = preact * sigma
    slope[(rows - 1) * cols :, :] = sigma + value * (1.0 - sigma)
    last = value.astype(bf16)
    act[rows - 1] = last
    for row, message in ((0, upper), (rows + 1, lower)):
        centre = message[at.row_cot : at.row_cot + cols, :]
        put(padded, MARGIN, centre)
        for col, one in ((-1, COT[0]), (cols, COT[2])):
            put(padded, MARGIN + col, message[at.corner + one : at.corner + one + 1, :])
        shifted[0, row] = get(padded, MARGIN - 1, cols).astype(bf16)
        shifted[1, row] = centre.astype(bf16)
        shifted[2, row] = get(padded, MARGIN + 1, cols).astype(bf16)
    last_t = last.T
    both_t = jnp.concatenate([last, act_in[0]], axis=0).T
    for k in range(3):
        for l in range(3):
            beside = shifted[2 - l, rows + 1 - k]
            if k == 2:
                term = dot(both_t, jnp.concatenate([beside, shifted[2 - l, 0]], axis=0))
            else:
                term = dot(last_t, beside)
            tap = pl.ds((3 * k + l) * channels, channels)
            partial[tap, :] = partial_in[tap, :] + term
    other_core(partial, send)


def grad_kernel(shifted, slope, grad_act, conv_w, phases, fine):
    rows, cols = shifted.shape[1] - 2, shifted.shape[2]
    channels = shifted.shape[3]
    n_rows, n_cols = rows // 2, cols // 2
    first = jnp.zeros((cols, channels), f32)
    last = jnp.zeros((cols, channels), f32)
    for l in range(3):
        first = first + dot_nt(shifted[2 - l, 0], conv_w[2, l])
        last = last + dot_nt(shifted[2 - l, rows + 1], conv_w[0, l])
    cells = rows * cols
    put(fine, 0, (grad_act[...] * slope[...]).astype(bf16).astype(f32))
    total = (grad_act[:cols, :] + first) * slope[:cols, :]
    put(fine, 0, total.astype(bf16).astype(f32))
    total = (grad_act[cells - cols :, :] + last) * slope[cells - cols :, :]
    put(fine, cells - cols, total.astype(bf16).astype(f32))
    whole = phases.shape[2]
    for row_phase in range(2):
        for col_phase in range(2):
            for row in range(n_rows):
                start = (2 * row + row_phase) * cols + col_phase
                phases[row_phase, col_phase, row] = get(fine, start, n_cols, 2).astype(bf16)
            for row in range(n_rows, whole):
                phases[row_phase, col_phase, row] = jnp.zeros((n_cols, channels), bf16)


def up_kernel(near, phases, partial, send):
    _, _, whole, n_cols, channels = phases.shape
    turned = {}
    for row_off in range(2):
        for col_off in range(2):
            cells = near[col_off, pl.ds(row_off, whole)]
            turned[row_off, col_off] = cells.reshape(whole * n_cols, channels).T
    for k in range(3):
        row_phase, row_off = forward_taps[k]
        for l in range(3):
            col_phase, col_off = forward_taps[l]
            source = phases[row_phase, col_phase].reshape(whole * n_cols, channels)
            partial[pl.ds((3 * k + l) * channels, channels), :] = dot(
                turned[row_off, col_off], source
            )
    other_core(partial, send)


def ring_kernel(
    coarse, cot, left, right, upper, lower, conv_w, up_w, ring_act, ring_grad, ring, wide,
):
    rows, cols, channels = cot.shape
    n_rows, n_cols = rows // 2, cols // 2
    at = Layout(n_rows, n_cols)
    stride, step = cols + 2 * MARGIN, n_cols + 2 * MARGIN
    _, _, band, n_bands = place_of()
    has_upper, has_lower = band > 0, band < n_bands - 1

    def corner(message, which):
        return message[at.corner + which : at.corner + which + 1, :]

    def cell(i, j):
        return (i + 1) * step + MARGIN + j

    for row in range(n_rows):
        put(wide, cell(row, 0), coarse[row].astype(f32))
    for row, message in ((-1, upper), (n_rows, lower)):
        put(wide, cell(row, 0), message[at.row_coarse : at.row_coarse + n_cols, :])
        put(wide, cell(row, -1), corner(message, COARSE[0]))
        put(wide, cell(row, n_cols), corner(message, COARSE[2]))
    put(wide, cell(0, -1), left[at.coarse : at.coarse + n_rows, :], step)
    put(wide, cell(0, n_cols), right[at.coarse : at.coarse + n_rows, :], step)
    total = jnp.zeros((at.ring_size, channels), f32)
    for k in range(3):
        for l in range(3):
            put(ring, 0, jnp.zeros((at.ring_size, channels), f32))
            for base, i in ((at.bottom, n_rows),) if k == 1 else ((at.top, k // 2 * -1),):
                start = cell(i, -1 if l == 2 else 0)
                put(ring, base + (l == 1), get(wide, start, n_cols + 1), 2)
            base, j = (at.right, n_cols) if l == 1 else (at.left, -(l // 2))
            start = cell(1 if k == 0 else 0, j)
            put(ring, base + (k != 1), get(wide, start, n_rows, step), 2)
            total = total + dot(get(ring, 0, at.ring_size).astype(bf16), up_w[k, l])
    put(ring, 0, jnp.zeros((at.ring_size, channels), f32))
    for base, message in ((at.top, upper), (at.bottom, lower)):
        put(ring, base + 1, message[at.row_skip : at.row_skip + cols, :])
        put(ring, base, corner(message, SKIP[0]))
        put(ring, base + cols + 1, corner(message, SKIP[2]))
    put(ring, at.left, left[at.skip : at.skip + rows, :])
    put(ring, at.right, right[at.skip : at.skip + rows, :])
    preact = total + get(ring, 0, at.ring_size)
    sigma = jax.nn.sigmoid(preact)
    value = preact * sigma
    slope = sigma + value * (1.0 - sigma)
    value = value.astype(bf16).astype(f32)
    ring_act[...] = value
    for base, exists in ((at.top, has_upper), (at.bottom, has_lower)):
        strip = value[base : base + cols + 2]
        ring_act[base : base + cols + 2, :] = jnp.where(exists, strip, 0.0)

    def fine(p, q):
        return (p + 2) * stride + MARGIN + q

    for row in range(rows):
        put(wide, fine(row, 0), cot[row].astype(f32))
    for row, message, start, which in (
        (-1, upper, at.row_cot, COT), (-2, upper, at.row_cot_2, COT_2), (rows, lower, at.row_cot, COT),
    ):
        put(wide, fine(row, 0), message[start : start + cols, :])
        for col, one in ((-1, which[0]), (-2, which[1]), (cols, which[2])):
            put(wide, fine(row, col), corner(message, one))
    put(wide, fine(0, -1), left[at.cot : at.cot + rows, :], stride)
    put(wide, fine(0, -2), left[at.cot_2 : at.cot_2 + rows, :], stride)
    put(wide, fine(0, cols), right[at.cot : at.cot + rows, :], stride)
    total = jnp.zeros((at.grad_size, channels), f32)
    for k in range(3):
        for l in range(3):
            put(ring, at.top, get(wide, fine(-k, -l), cols + 1))
            put(ring, at.grad_left, get(wide, fine(1 - k, -l), rows, stride))
            source = get(ring, 0, at.grad_size).astype(bf16)
            total = total + dot_nt(source, conv_w[k, l])
    strip = (total[: cols + 1] * slope[at.top : at.top + cols + 1]).astype(bf16).astype(f32)
    put(ring_grad, at.top, jnp.where(has_upper, strip, 0.0))
    strip = total[at.grad_left : at.grad_left + rows] * slope[at.left : at.left + rows]
    put(ring_grad, at.grad_left, strip.astype(bf16).astype(f32))


def decoded_kernel(act, ring_act, conv_w, decoded, padded, shifted):
    rows, cols, channels = act.shape
    at = Layout(rows // 2, cols // 2)
    stride = cols + 2 * MARGIN
    for row in range(rows):
        put(padded, (row + 1) * stride + MARGIN, act[row].astype(f32))
    for row, base in ((0, at.top), (rows + 1, at.bottom)):
        put(padded, row * stride + MARGIN - 1, ring_act[base : base + cols + 2, :])
    put(padded, stride + MARGIN - 1, ring_act[at.left : at.left + rows, :], stride)
    put(padded, stride + MARGIN + cols, ring_act[at.right : at.right + rows, :], stride)
    for row in range(rows + 2):
        for shift in range(3):
            start = row * stride + MARGIN - 1 + shift
            shifted[shift, row] = get(padded, start, cols).astype(bf16)
    total = jnp.zeros((rows * cols, channels), f32)
    for k in range(3):
        for l in range(3):
            source = shifted[l, pl.ds(k, rows)].reshape(-1, channels)
            total = total + dot(source, conv_w[k, l])
    decoded[...] = total.astype(bf16).reshape(decoded.shape)

def coarse_kernel(phases, ring_grad, up_w, coarse_out, padded, moved):
    n_rows, n_cols, channels = coarse_out.shape
    at = Layout(n_rows, n_cols)
    stride = n_cols + 2 * MARGIN
    for phase, start in ((0, 1), (1, 2), (2, 0)):
        moved[phase, 0] = get(ring_grad, at.top + start, n_cols, 2).astype(bf16)
    for phase in range(2):
        for row in range(n_rows):
            moved[phase, 1 + row] = phases[1, phase, row]
    for row_phase in range(2):
        for row in range(n_rows):
            put(padded, row * stride + MARGIN, phases[row_phase, 1, row].astype(f32))
        put(padded, MARGIN - 1, get(ring_grad, at.grad_left + row_phase, n_rows, 2), stride)
        for row in range(n_rows):
            cells = get(padded, row * stride + MARGIN - 1, n_cols).astype(bf16)
            if row_phase:
                moved[2, 1 + row] = cells
            else:
                moved[3, row] = cells
    total = jnp.zeros((n_rows * n_cols, channels), f32)
    for k in range(3):
        for l in range(3):
            if k == 1:
                if l == 0:
                    source = moved[3, pl.ds(0, n_rows)]
                else:
                    source = phases[0, l - 1, pl.ds(0, n_rows)]
            else:
                source = moved[(2, 0, 1)[l], pl.ds(k // 2, n_rows)]
            total = total + dot_nt(source.reshape(n_rows * n_cols, channels), up_w[k, l])
    coarse_out[...] = total.astype(bf16).reshape(coarse_out.shape)


def halving(count):
    bits = (count // 2).bit_length() - 1
    return [[(step + core) % bits for step in range(bits)] for core in range(2)]


def mask_of(slot, order):
    last = len(order) - 1
    return sum(1 << bit for step, bit in enumerate(order) if slot >> (last - step) & 1)


def core_kernel(partial, got, own, message):
    slots, half, block = got.shape[0], own.shape[0], got.shape[1]
    core, chip, _, _ = place_of()
    even, odd = halving(2 * slots)
    for slot in range(slots):
        target = chip ^ jnp.where(core == 0, mask_of(slot, even), mask_of(slot, odd))
        mine = pl.multiple_of((2 * target + core) * block, 16)
        total = partial[pl.ds(mine, block), :] + got[target].astype(f32)
        if slot < half:
            own[slot] = total
        else:
            message[slot - half] = total.astype(bf16)


def plane_kernel(before, got, own, message):
    half = own.shape[0]
    for slot in range(2 * half):
        total = before[slot] + got[slot].astype(f32)
        if slot < half:
            own[slot] = total
        else:
            message[slot - half] = total.astype(bf16)


def band_kernel(conv, got_conv, up, got_up, own, *refs):
    n_bands, messages, cut = len(refs), refs[:-1], refs[-1]
    conv_total = conv[0] + got_conv[0].astype(f32)
    up_total = up[0] + got_up[0].astype(f32)
    cols = conv_total.shape[1] // n_bands
    for band in range(n_bands):
        cut[band, :, :cols] = conv_total[:, band * cols : (band + 1) * cols]
        cut[band, :, cols:] = up_total[:, band * cols : (band + 1) * cols]
    band = place_of()[2]
    own[...] = cut[band]
    for k, message in enumerate(messages):
        message[...] = cut[lax.rem(band + k + 1, n_bands)].astype(bf16)


def last_kernel(own, *refs):
    peers, (conv, up) = refs[:-2], refs[-2:]
    total = own[...]
    for peer in peers:
        total = total + peer[...].astype(f32)
    turned = total.T
    conv[...] = turned[: conv.shape[0]]
    up[...] = turned[conv.shape[0] :]


def xor_pairs(count, bits):
    return [(i, i ^ bits) for i in range(count)]


def core_sum(partial, send):
    groups, block, channels = send.shape
    got = lax.ppermute(send, "face", xor_pairs(lax.axis_size("face"), 1))
    shape = (groups // 2, block, channels)
    return kernel_call(core_kernel, [sds(shape, f32), sds(shape, bf16)], [], 0, partial, got)


def plane_swap(message, step):
    faces = lax.axis_size("face")
    orders = halving(faces)
    return lax.ppermute(message, "face", [(i, i ^ 2 << orders[i % 2][step]) for i in range(faces)])


def plane_sum(own, got):
    half, block, channels = own.shape
    shape = (half // 2, block, channels)
    return kernel_call(plane_kernel, [sds(shape, f32), sds(shape, bf16)], [], 0, own, got)


def band_sum(conv, got_conv, up, got_up):
    bands = lax.axis_size("band")
    _, block, channels = conv.shape
    cols = channels // bands
    shape = (block, 2 * cols)
    own, *messages = kernel_call(
        band_kernel, [sds(shape, f32)] + [sds(shape, bf16)] * (bands - 1),
        [pltpu.VMEM((bands,) + shape, f32)], 0, conv, got_conv, up, got_up,
    )
    got = [
        lax.ppermute(messages[k - 1], "band", [(i, (i + k) % bands) for i in range(bands)])
        for k in range(1, bands)
    ]
    return [a.T for a in kernel_call(last_kernel, [sds((cols, block), f32)] * 2, [], 0, own, *got)]


def after(value, *others):
    return lax.optimization_barrier((value, *others))[0]


def swap(first, second, axis, wrap):
    one, two = pairs(lax.axis_size(axis), wrap)
    return lax.ppermute(first, axis, one), lax.ppermute(second, axis, two)


def local(coarse, skip, up_weight, conv_weight, cotangent):
    n_rows, n_cols, channels = coarse.shape
    rows, cols, _ = skip.shape
    at = Layout(n_rows, n_cols)
    faces = lax.axis_size("face")
    groups, block = faces // 2, 9 * channels // faces

    flat = halves(rows * cols, channels)
    message = sds((at.face_size, channels), bf16)
    edges = pltpu.VMEM(message.shape, f32)
    first, second, cotangent, skip, coarse = kernel_call(
        face_message,
        [message, message, sds(cotangent.shape, bf16), sds(skip.shape, bf16), sds(coarse.shape, bf16)],
        [flat, edges, edges, pltpu.SemaphoreType.DMA((3,))],
        0, coarse, skip, cotangent, far=(0, 1, 2),
    )
    first, second = swap(first, second, "face", True)
    side = sds(message.shape, f32)
    message = sds((at.band_size, channels), bf16)
    edges = pltpu.VMEM(message.shape, f32)
    first, second, left, right = kernel_call(
        band_message, [message, message, side, side], [edges, edges],
        0, coarse, skip, cotangent, first, second,
    )
    first, second = swap(first, second, "band", False)

    cells = n_rows * n_cols
    stride = cols + 2 * MARGIN
    padded = halves((rows + 2) * stride, channels)
    shift_shape = (3, rows + 2, cols, channels)
    whole = -(-cells // 256) * 256 // n_cols
    part = sds((9 * channels, channels), f32)
    blocks = [
        sds(shift_shape, bf16), sds((2, whole + 1, n_cols, channels), bf16),
        sds(skip.shape, bf16), sds((rows * cols, channels), f32), part,
    ]
    *inner, last_pre, conv_weight, grad_act = kernel_call(
        inner_kernel,
        [
            *blocks, sds((cols, channels), f32), sds(conv_weight.shape, bf16),
            sds((rows * cols, channels), f32),
        ],
        [halves(rows * stride, channels), flat, pltpu.SemaphoreType.DMA],
        0, coarse, skip, cotangent, left, right, up_weight, conv_weight, far=(6,),
    )
    send = sds((groups, block, channels), bf16)
    side = sds(message.shape, f32)
    shifted, near, act, slope, part_conv, send_conv, upper, lower = kernel_call(
        act_kernel, [*blocks, send, side, side],
        [halves(stride, channels), halves(cols, channels)],
        0, second, first, right, up_weight, last_pre, *inner, changed={5 + i: i for i in range(5)},
    )
    phases = kernel_call(
        grad_kernel, [sds((2, 2, whole, n_cols, channels), bf16)], [flat],
        0, shifted, slope, grad_act, conv_weight,
    )[0]
    part_up, send_up = kernel_call(up_kernel, [part, send], [], 0, near, phases)
    own_conv, to_conv = core_sum(after(part_conv, send_up), send_conv)
    got_conv = plane_swap(to_conv, 0)
    own_up, to_up = core_sum(after(part_up, to_conv), send_up)
    got_up = plane_swap(to_up, 0)
    ring_act, ring_grad = kernel_call(
        ring_kernel,
        [
            sds((at.ring_size, channels), f32),
            sds((channels // LANES, at.grad_size, LANES), f32),
        ],
        [halves(at.ring_size, channels), halves((rows + 3) * stride, channels)],
        0, coarse, cotangent, after(left, to_up), right, upper, lower, conv_weight, up_weight,
    )
    own_conv = after(own_conv, ring_act)
    steps = (faces // 2).bit_length() - 1
    for step in range(1, steps):
        own_conv, to_conv = plane_sum(own_conv, got_conv)
        got_conv = plane_swap(to_conv, step)
        if step == 1:
            decoded = kernel_call(
                decoded_kernel, [sds(skip.shape, bf16)], [padded, pltpu.VMEM(shift_shape, bf16)],
                0, act, after(ring_act, to_conv), conv_weight,
            )[0]
            own_up = after(own_up, decoded)
        own_up, to_up = plane_sum(own_up, got_up)
        got_up = plane_swap(to_up, step)
        if step == 1:
            grad_coarse = kernel_call(
                coarse_kernel, [sds(coarse.shape, bf16)],
                [
                    halves(n_rows * (n_cols + 2 * MARGIN), channels),
                    pltpu.VMEM((4, n_rows + 1, n_cols, channels), bf16),
                ],
                0, phases, after(ring_grad, to_up), up_weight,
            )[0]
            own_up = after(own_up, grad_coarse)
    grad_conv, grad_up = band_sum(own_conv, got_conv, own_up, got_up)
    return (decoded, grad_coarse, grad_up, grad_conv)


def solution(mesh):
    return jax.shard_map(
        local,
        mesh=mesh,
        in_specs=(
            P("band", "face", None),
            P("band", "face", None),
            P(),
            P(),
            P("band", "face", None),
        ),
        out_specs=(
            P("band", "face", None),
            P("band", "face", None),
            P("face", "band"),
            P("face", "band"),
        ),
        check_vma=False,
    )
```

```python
import jax
import jax.numpy as jnp
from jax import lax
from jax.experimental import pallas as pl
from jax.experimental.pallas import tpu as pltpu
from jax.sharding import PartitionSpec as P

f32, bf16 = jnp.float32, jnp.bfloat16
forward_taps = ((1, 1), (0, 0), (1, 0))
backward_taps = ((1, 0), (0, 1), (1, 1))
MARGIN = 8
LANES = 128


def sds(shape, dtype):
    return jax.ShapeDtypeStruct(shape, dtype)


def kernel_call(body, outs, scratch, flops, *args, far=(), changed=None):
    vmem = pl.BlockSpec(memory_space=pltpu.VMEM)
    hbm = pl.BlockSpec(memory_space=pltpu.HBM)
    moved = sum(a.size * a.dtype.itemsize for a in args)
    moved += sum(a.size * a.dtype.itemsize for a in outs)
    args = [
        pltpu.with_memory_space_constraint(a, pltpu.HBM) if i in far else a
        for i, a in enumerate(args)
    ]
    return pl.pallas_call(
        body,
        out_shape=tuple(outs),
        in_specs=[hbm if i in far else vmem for i in range(len(args))],
        out_specs=tuple(vmem for _ in outs),
        scratch_shapes=scratch,
        input_output_aliases=changed or {},
        compiler_params=pltpu.CompilerParams(vmem_limit_bytes=28 * 2**20),
        cost_estimate=pl.CostEstimate(flops=flops, bytes_accessed=moved, transcendentals=0),
    )(*args)


def place_of():
    face = lax.axis_index("face")
    return lax.rem(face, 2), lax.div(face, 2), lax.axis_index("band"), lax.axis_size("band")


def dot(a, b):
    return jnp.dot(a, b, preferred_element_type=f32)


def dot_nt(a, b):
    return lax.dot_general(a, b, (((1,), (1,)), ((), ())), preferred_element_type=f32)


def pairs(count, wrap):
    first = [(i, i ^ 1) for i in range(count)]
    second = []
    for i in range(count):
        j = i + 1 if i % 2 else i - 1
        if wrap or 0 <= j < count:
            second.append((i, j % count))
    return first, second


def up16(n):
    return (n + 15) // 16 * 16


def halves(n_rows, channels):
    return pltpu.VMEM((channels // LANES, n_rows, LANES), f32)


def put(ref, start, value, step=1):
    for part in range(ref.shape[0]):
        rows = pl.ds(start, value.shape[0], stride=step if step > 1 else None)
        ref[part, rows, :] = value[:, part * LANES : (part + 1) * LANES]


def get(ref, start, count, step=1):
    rows = pl.ds(start, count, stride=step if step > 1 else None)
    return jnp.concatenate([ref[part, rows, :] for part in range(ref.shape[0])], axis=1)


def fill(ref, start, value):
    ref[start : start + value.shape[0], :] = value


def other_core(partial, send):
    core = place_of()[0]
    groups, block, _ = send.shape
    for group in range(groups):
        theirs = pl.multiple_of((2 * group + 1 - core) * block, 16)
        send[group] = partial[pl.ds(theirs, block), :].astype(bf16)


class Layout:
    def __init__(self, n_rows, n_cols):
        rows, cols = 2 * n_rows, 2 * n_cols
        self.cot, self.cot_2, self.skip, self.coarse = 0, rows, 2 * rows, 3 * rows
        self.face_size = up16(3 * rows + n_rows)
        self.row_cot, self.row_cot_2, self.row_skip = 0, cols, 2 * cols
        self.row_coarse, self.corner = 3 * cols, 3 * cols + n_cols
        self.band_size = self.corner + 16
        ring = (cols + 2 + 7) // 8 * 8
        self.top, self.bottom, self.left, self.right = 0, ring, 2 * ring, 2 * ring + rows
        self.ring_size = up16(2 * ring + 2 * rows)
        self.grad_left, self.grad_size = ring, up16(ring + rows)


COT, COT_2, SKIP, COARSE = (0, 1, 2), (3, 4, 5), (6, None, 7), (8, None, 9)


def face_message(coarse, skip, cot, first, second, cot_v, skip_v, coarse_v, flat, before, after, sems):
    rows, cols, _ = cot.shape
    n_rows, n_cols, _ = coarse.shape
    at = Layout(n_rows, n_cols)
    copies = [
        pltpu.make_async_copy(source, target, sems.at[i])
        for i, (source, target) in enumerate(((cot, cot_v), (skip, skip_v), (coarse, coarse_v)))
    ]
    for copy in copies:
        copy.start()
    before[...] = jnp.zeros_like(before)
    after[...] = jnp.zeros_like(after)
    for copy, array, start, start_2 in (
        (copies[0], cot_v, at.cot, at.cot_2), (copies[1], skip_v, at.skip, None), (copies[2], coarse_v, at.coarse, None),
    ):
        copy.wait()
        n, width, channels = array.shape
        put(flat, 0, array[:, :16, :].astype(f32)[:, :8, :].reshape(n * 8, channels))
        put(flat, n * 8, array[:, width - 16 :, :].astype(f32)[:, 8:, :].reshape(n * 8, channels))
        fill(before, start, get(flat, 0, n, 8))
        fill(after, start, get(flat, n * 8 + 7, n, 8))
        if start_2 is not None:
            fill(after, start_2, get(flat, n * 8 + 6, n, 8))
    even = place_of()[0] == 0
    first[...] = jnp.where(even, after[...], before[...]).astype(bf16)
    second[...] = jnp.where(even, before[...], after[...]).astype(bf16)


def band_message(coarse, skip, cot, got_first, got_second, first, second, left, right, before, after):
    rows, cols, channels = cot.shape
    n_rows, n_cols, _ = coarse.shape
    at = Layout(n_rows, n_cols)
    even = place_of()[0] == 0
    one, two = got_first[...].astype(f32), got_second[...].astype(f32)
    left[...] = jnp.where(even, two, one)
    right[...] = jnp.where(even, one, two)
    for message, row, row_2, cell in ((before, 0, None, 0), (after, rows - 1, rows - 2, n_rows - 1)):
        fill(message, at.row_cot, cot[row].astype(f32))
        if row_2 is None:
            fill(message, at.row_cot_2, jnp.zeros((cols, channels), f32))
        else:
            fill(message, at.row_cot_2, cot[row_2].astype(f32))
        fill(message, at.row_skip, skip[row].astype(f32))
        fill(message, at.row_coarse, coarse[cell].astype(f32))
        fill(message, at.corner, jnp.zeros((16, channels), f32))
        corners = [
            (COT[0], left, at.cot + row), (COT[1], left, at.cot_2 + row), (COT[2], right, at.cot + row),
            (SKIP[0], left, at.skip + row), (SKIP[2], right, at.skip + row),
            (COARSE[0], left, at.coarse + cell), (COARSE[2], right, at.coarse + cell),
        ]
        if row_2 is not None:
            corners += [
                (COT_2[0], left, at.cot + row_2), (COT_2[1], left, at.cot_2 + row_2),
                (COT_2[2], right, at.cot + row_2),
            ]
        for corner, side, source in corners:
            fill(message, at.corner + corner, side[source : source + 1, :])
    even = lax.rem(place_of()[2], 2) == 0
    first[...] = jnp.where(even, after[...], before[...]).astype(bf16)
    second[...] = jnp.where(even, before[...], after[...]).astype(bf16)


def inner_kernel(
    coarse, skip, cot, left, right, up_w, conv_w,
    shifted, near, act, slope, partial, last_pre, conv_v, grad_act, padded, pre, sem,
):
    n_rows, n_cols, channels = coarse.shape
    rows, cols, _ = skip.shape
    at = Layout(n_rows, n_cols)
    stride = cols + 2 * MARGIN
    copy = pltpu.make_async_copy(conv_w, conv_v, sem)
    copy.start()
    for row in range(n_rows):
        near[0, row] = coarse[row]
        put(padded, row * stride, coarse[row].astype(f32))
    put(padded, n_cols, right[at.coarse : at.coarse + n_rows, :], stride)
    for row in range(n_rows):
        near[1, row] = get(padded, row * stride + 1, n_cols).astype(bf16)
    for row in range(n_rows, near.shape[1]):
        for side in range(2):
            near[side, row] = jnp.zeros((n_cols, channels), bf16)
    sums = {}
    for k in range(3):
        row_phase, row_off = forward_taps[k]
        for l in range(3):
            col_phase, col_off = forward_taps[l]
            source = near[col_off, pl.ds(row_off, n_rows)].reshape(n_rows * n_cols, channels)
            term = dot(source, up_w[k, l])
            name = (row_phase, col_phase)
            sums[name] = sums[name] + term if name in sums else term
    for (row_phase, col_phase), total in sums.items():
        for row in range(n_rows):
            start = (2 * row + row_phase) * cols + col_phase
            put(pre, start, total[row * n_cols : (row + 1) * n_cols], 2)
    for row in range(rows):
        put(padded, row * stride + MARGIN, cot[row].astype(f32))
    put(padded, MARGIN - 1, left[at.cot : at.cot + rows, :], stride)
    put(padded, MARGIN + cols, right[at.cot : at.cot + rows, :], stride)
    for row in range(rows):
        for shift in (0, 2):
            start = row * stride + MARGIN - 1 + shift
            shifted[shift, row + 1] = get(padded, start, cols).astype(bf16)
        shifted[1, row + 1] = cot[row]
    for shift in range(3):
        shifted[shift, 0] = jnp.zeros((cols, channels), bf16)
        shifted[shift, rows + 1] = jnp.zeros((cols, channels), bf16)
    preact = get(pre, 0, rows * cols) + skip[...].reshape(rows * cols, channels).astype(f32)
    last_pre[...] = preact[(rows - 1) * cols :]
    sigma = jax.nn.sigmoid(preact)
    value = preact * sigma
    slope[...] = sigma + value * (1.0 - sigma)
    row_of = lax.broadcasted_iota(jnp.int32, value.shape, 0)
    act_flat = jnp.where(row_of < (rows - 1) * cols, value, 0.0).astype(bf16)
    act[...] = act_flat.reshape(act.shape)
    act_t = act_flat.T
    for k in range(3):
        for l in range(3):
            source = shifted[2 - l, pl.ds(2 - k, rows)].reshape(-1, channels)
            partial[pl.ds((3 * k + l) * channels, channels), :] = dot(act_t, source)
    copy.wait()
    total = jnp.zeros((rows * cols, channels), f32)
    for k in range(3):
        for l in range(3):
            source = shifted[2 - l, pl.ds(2 - k, rows)].reshape(-1, channels)
            total = total + dot_nt(source, conv_v[k, l])
    grad_act[...] = total


def act_kernel(
    got_second, got_first, right, up_w, last_pre, shifted_in, near_in, act_in, slope_in, partial_in,
    shifted, near, act, slope, partial, send, upper, lower, padded, pre,
):
    rows, cols, channels = act.shape
    n_rows, n_cols = rows // 2, cols // 2
    at = Layout(n_rows, n_cols)
    even = lax.rem(place_of()[2], 2) == 0
    one, two = got_first[...].astype(f32), got_second[...].astype(f32)
    upper[...] = jnp.where(even, two, one)
    lower[...] = jnp.where(even, one, two)
    below = lower[at.row_coarse : at.row_coarse + n_cols, :]
    corner = at.corner + COARSE[2]
    put(padded, 0, below)
    put(padded, n_cols, lower[corner : corner + 1, :])
    cells = [below.astype(bf16), get(padded, 1, n_cols).astype(bf16)]
    near[0, n_rows] = cells[0]
    near[1, n_rows] = cells[1]
    put(pre, 0, dot(cells[0], up_w[0, 1]), 2)
    put(pre, 1, dot(cells[1], up_w[0, 0]) + dot(cells[0], up_w[0, 2]), 2)
    preact = last_pre[...] + get(pre, 0, cols)
    sigma = jax.nn.sigmoid(preact)
    value = preact * sigma
    slope[(rows - 1) * cols :, :] = sigma + value * (1.0 - sigma)
    last = value.astype(bf16)
    act[rows - 1] = last
    for row, message in ((0, upper), (rows + 1, lower)):
        centre = message[at.row_cot : at.row_cot + cols, :]
        put(padded, MARGIN, centre)
        for col, one in ((-1, COT[0]), (cols, COT[2])):
            put(padded, MARGIN + col, message[at.corner + one : at.corner + one + 1, :])
        shifted[0, row] = get(padded, MARGIN - 1, cols).astype(bf16)
        shifted[1, row] = centre.astype(bf16)
        shifted[2, row] = get(padded, MARGIN + 1, cols).astype(bf16)
    last_t = last.T
    both_t = jnp.concatenate([last, act_in[0]], axis=0).T
    for k in range(3):
        for l in range(3):
            beside = shifted[2 - l, rows + 1 - k]
            if k == 2:
                term = dot(both_t, jnp.concatenate([beside, shifted[2 - l, 0]], axis=0))
            else:
                term = dot(last_t, beside)
            tap = pl.ds((3 * k + l) * channels, channels)
            partial[tap, :] = partial_in[tap, :] + term
    other_core(partial, send)


def grad_kernel(shifted, slope, grad_act, conv_w, phases, fine):
    rows, cols = shifted.shape[1] - 2, shifted.shape[2]
    channels = shifted.shape[3]
    n_rows, n_cols = rows // 2, cols // 2
    first = jnp.zeros((cols, channels), f32)
    last = jnp.zeros((cols, channels), f32)
    for l in range(3):
        first = first + dot_nt(shifted[2 - l, 0], conv_w[2, l])
        last = last + dot_nt(shifted[2 - l, rows + 1], conv_w[0, l])
    cells = rows * cols
    put(fine, 0, (grad_act[...] * slope[...]).astype(bf16).astype(f32))
    total = (grad_act[:cols, :] + first) * slope[:cols, :]
    put(fine, 0, total.astype(bf16).astype(f32))
    total = (grad_act[cells - cols :, :] + last) * slope[cells - cols :, :]
    put(fine, cells - cols, total.astype(bf16).astype(f32))
    whole = phases.shape[2]
    for row_phase in range(2):
        for col_phase in range(2):
            for row in range(n_rows):
                start = (2 * row + row_phase) * cols + col_phase
                phases[row_phase, col_phase, row] = get(fine, start, n_cols, 2).astype(bf16)
            for row in range(n_rows, whole):
                phases[row_phase, col_phase, row] = jnp.zeros((n_cols, channels), bf16)


def up_kernel(near, phases, partial, send):
    _, _, whole, n_cols, channels = phases.shape
    turned = {}
    for row_off in range(2):
        for col_off in range(2):
            cells = near[col_off, pl.ds(row_off, whole)]
            turned[row_off, col_off] = cells.reshape(whole * n_cols, channels).T
    for k in range(3):
        row_phase, row_off = forward_taps[k]
        for l in range(3):
            col_phase, col_off = forward_taps[l]
            source = phases[row_phase, col_phase].reshape(whole * n_cols, channels)
            partial[pl.ds((3 * k + l) * channels, channels), :] = dot(
                turned[row_off, col_off], source
            )
    other_core(partial, send)


def ring_kernel(
    coarse, cot, left, right, upper, lower, conv_w, up_w, ring_act, ring_grad, ring, wide,
):
    rows, cols, channels = cot.shape
    n_rows, n_cols = rows // 2, cols // 2
    at = Layout(n_rows, n_cols)
    stride, step = cols + 2 * MARGIN, n_cols + 2 * MARGIN
    _, _, band, n_bands = place_of()
    has_upper, has_lower = band > 0, band < n_bands - 1

    def corner(message, which):
        return message[at.corner + which : at.corner + which + 1, :]

    def cell(i, j):
        return (i + 1) * step + MARGIN + j

    for row in range(n_rows):
        put(wide, cell(row, 0), coarse[row].astype(f32))
    for row, message in ((-1, upper), (n_rows, lower)):
        put(wide, cell(row, 0), message[at.row_coarse : at.row_coarse + n_cols, :])
        put(wide, cell(row, -1), corner(message, COARSE[0]))
        put(wide, cell(row, n_cols), corner(message, COARSE[2]))
    put(wide, cell(0, -1), left[at.coarse : at.coarse + n_rows, :], step)
    put(wide, cell(0, n_cols), right[at.coarse : at.coarse + n_rows, :], step)
    total = jnp.zeros((at.ring_size, channels), f32)
    for k in range(3):
        for l in range(3):
            put(ring, 0, jnp.zeros((at.ring_size, channels), f32))
            for base, i in ((at.bottom, n_rows),) if k == 1 else ((at.top, k // 2 * -1),):
                start = cell(i, -1 if l == 2 else 0)
                put(ring, base + (l == 1), get(wide, start, n_cols + 1), 2)
            base, j = (at.right, n_cols) if l == 1 else (at.left, -(l // 2))
            start = cell(1 if k == 0 else 0, j)
            put(ring, base + (k != 1), get(wide, start, n_rows, step), 2)
            total = total + dot(get(ring, 0, at.ring_size).astype(bf16), up_w[k, l])
    put(ring, 0, jnp.zeros((at.ring_size, channels), f32))
    for base, message in ((at.top, upper), (at.bottom, lower)):
        put(ring, base + 1, message[at.row_skip : at.row_skip + cols, :])
        put(ring, base, corner(message, SKIP[0]))
        put(ring, base + cols + 1, corner(message, SKIP[2]))
    put(ring, at.left, left[at.skip : at.skip + rows, :])
    put(ring, at.right, right[at.skip : at.skip + rows, :])
    preact = total + get(ring, 0, at.ring_size)
    sigma = jax.nn.sigmoid(preact)
    value = preact * sigma
    slope = sigma + value * (1.0 - sigma)
    value = value.astype(bf16).astype(f32)
    ring_act[...] = value
    for base, exists in ((at.top, has_upper), (at.bottom, has_lower)):
        strip = value[base : base + cols + 2]
        ring_act[base : base + cols + 2, :] = jnp.where(exists, strip, 0.0)

    def fine(p, q):
        return (p + 2) * stride + MARGIN + q

    for row in range(rows):
        put(wide, fine(row, 0), cot[row].astype(f32))
    for row, message, start, which in (
        (-1, upper, at.row_cot, COT), (-2, upper, at.row_cot_2, COT_2), (rows, lower, at.row_cot, COT),
    ):
        put(wide, fine(row, 0), message[start : start + cols, :])
        for col, one in ((-1, which[0]), (-2, which[1]), (cols, which[2])):
            put(wide, fine(row, col), corner(message, one))
    put(wide, fine(0, -1), left[at.cot : at.cot + rows, :], stride)
    put(wide, fine(0, -2), left[at.cot_2 : at.cot_2 + rows, :], stride)
    put(wide, fine(0, cols), right[at.cot : at.cot + rows, :], stride)
    total = jnp.zeros((at.grad_size, channels), f32)
    for k in range(3):
        for l in range(3):
            put(ring, at.top, get(wide, fine(-k, -l), cols + 1))
            put(ring, at.grad_left, get(wide, fine(1 - k, -l), rows, stride))
            source = get(ring, 0, at.grad_size).astype(bf16)
            total = total + dot_nt(source, conv_w[k, l])
    strip = (total[: cols + 1] * slope[at.top : at.top + cols + 1]).astype(bf16).astype(f32)
    put(ring_grad, at.top, jnp.where(has_upper, strip, 0.0))
    strip = total[at.grad_left : at.grad_left + rows] * slope[at.left : at.left + rows]
    put(ring_grad, at.grad_left, strip.astype(bf16).astype(f32))


def decoded_kernel(act, ring_act, conv_w, decoded, padded, shifted):
    rows, cols, channels = act.shape
    at = Layout(rows // 2, cols // 2)
    stride = cols + 2 * MARGIN
    for row in range(rows):
        put(padded, (row + 1) * stride + MARGIN, act[row].astype(f32))
    for row, base in ((0, at.top), (rows + 1, at.bottom)):
        put(padded, row * stride + MARGIN - 1, ring_act[base : base + cols + 2, :])
    put(padded, stride + MARGIN - 1, ring_act[at.left : at.left + rows, :], stride)
    put(padded, stride + MARGIN + cols, ring_act[at.right : at.right + rows, :], stride)
    for row in range(rows + 2):
        for shift in range(3):
            start = row * stride + MARGIN - 1 + shift
            shifted[shift, row] = get(padded, start, cols).astype(bf16)
    total = jnp.zeros((rows * cols, channels), f32)
    for k in range(3):
        for l in range(3):
            source = shifted[l, pl.ds(k, rows)].reshape(-1, channels)
            total = total + dot(source, conv_w[k, l])
    decoded[...] = total.astype(bf16).reshape(decoded.shape)

def coarse_kernel(phases, ring_grad, up_w, coarse_out, padded, moved):
    n_rows, n_cols, channels = coarse_out.shape
    at = Layout(n_rows, n_cols)
    stride = n_cols + 2 * MARGIN
    for phase, start in ((0, 1), (1, 2), (2, 0)):
        moved[phase, 0] = get(ring_grad, at.top + start, n_cols, 2).astype(bf16)
    for phase in range(2):
        for row in range(n_rows):
            moved[phase, 1 + row] = phases[1, phase, row]
    for row_phase in range(2):
        for row in range(n_rows):
            put(padded, row * stride + MARGIN, phases[row_phase, 1, row].astype(f32))
        put(padded, MARGIN - 1, get(ring_grad, at.grad_left + row_phase, n_rows, 2), stride)
        for row in range(n_rows):
            cells = get(padded, row * stride + MARGIN - 1, n_cols).astype(bf16)
            if row_phase:
                moved[2, 1 + row] = cells
            else:
                moved[3, row] = cells
    total = jnp.zeros((n_rows * n_cols, channels), f32)
    for k in range(3):
        for l in range(3):
            if k == 1:
                if l == 0:
                    source = moved[3, pl.ds(0, n_rows)]
                else:
                    source = phases[0, l - 1, pl.ds(0, n_rows)]
            else:
                source = moved[(2, 0, 1)[l], pl.ds(k // 2, n_rows)]
            total = total + dot_nt(source.reshape(n_rows * n_cols, channels), up_w[k, l])
    coarse_out[...] = total.astype(bf16).reshape(coarse_out.shape)


def halving(count):
    bits = (count // 2).bit_length() - 1
    return [[(step + core) % bits for step in range(bits)] for core in range(2)]


def mask_of(slot, order):
    last = len(order) - 1
    return sum(1 << bit for step, bit in enumerate(order) if slot >> (last - step) & 1)


def core_kernel(partial, got, own, message):
    slots, half, block = got.shape[0], own.shape[0], got.shape[1]
    core, chip, _, _ = place_of()
    even, odd = halving(2 * slots)
    for slot in range(slots):
        target = chip ^ jnp.where(core == 0, mask_of(slot, even), mask_of(slot, odd))
        mine = pl.multiple_of((2 * target + core) * block, 16)
        total = partial[pl.ds(mine, block), :] + got[target].astype(f32)
        if slot < half:
            own[slot] = total
        else:
            message[slot - half] = total.astype(bf16)


def plane_kernel(before, got, own, message):
    half = own.shape[0]
    for slot in range(2 * half):
        total = before[slot] + got[slot].astype(f32)
        if slot < half:
            own[slot] = total
        else:
            message[slot - half] = total.astype(bf16)


def packing(rows, cols):
    side = max(1, LANES // cols)
    return side if rows % (16 * side) == 0 else 1


def conv_band_kernel(conv, got, own, message, cut):
    n_bands, _, cols = cut.shape
    total = conv[0] + got[0].astype(f32)
    for band in range(n_bands):
        cut[band] = total[:, band * cols : (band + 1) * cols]
    band = place_of()[2]
    for slot in range(n_bands // 2):
        lanes = slice(slot * cols, (slot + 1) * cols)
        own[:, lanes] = cut[band ^ (2 * slot)]
        message[:, lanes] = cut[band ^ (2 * slot + 1)].astype(bf16)


def band_kernel(conv, got_conv, up, got_up, own, *refs):
    messages, cut = refs[:-1], refs[-1]
    n_bands, rows, cols = cut.shape
    conv_total = conv[...] + got_conv[...].astype(f32)
    up_total = up[0] + got_up[0].astype(f32)
    for band in range(n_bands):
        cut[band] = up_total[:, band * cols : (band + 1) * cols]
    band = place_of()[2]
    own[:, :cols] = conv_total[:, :cols]
    own[:, cols:] = cut[band]
    for k, message in enumerate(messages, 1):
        piece = cut[band ^ k].astype(bf16)
        if k % 2:
            side = packing(rows, cols)
            for part in range(side):
                some = piece[part * rows // side : (part + 1) * rows // side]
                message[:, part * cols : (part + 1) * cols] = some
        else:
            message[:, :cols] = conv_total[:, k // 2 * cols : (k // 2 + 1) * cols].astype(bf16)
            message[:, cols:] = piece


def last_kernel(own, *refs):
    peers, (conv, up, total) = refs[:-3], refs[-3:]
    rows, cols = own.shape[0], own.shape[1] // 2
    total[...] = own[...]
    for peer in peers:
        if peer.shape == own.shape:
            total[...] += peer[...].astype(f32)
            continue
        side = peer.shape[1] // cols
        for part in range(side):
            some = slice(part * rows // side, (part + 1) * rows // side)
            total[some, cols:] += peer[:, part * cols : (part + 1) * cols].astype(f32)
    turned = total[...].T
    conv[...] = turned[:cols]
    up[...] = turned[cols:]


def xor_pairs(count, bits):
    return [(i, i ^ bits) for i in range(count)]


def core_sum(partial, send):
    groups, block, channels = send.shape
    got = lax.ppermute(send, "face", xor_pairs(lax.axis_size("face"), 1))
    shape = (groups // 2, block, channels)
    return kernel_call(core_kernel, [sds(shape, f32), sds(shape, bf16)], [], 0, partial, got)


def plane_swap(message, step):
    faces = lax.axis_size("face")
    orders = halving(faces)
    return lax.ppermute(message, "face", [(i, i ^ 2 << orders[i % 2][step]) for i in range(faces)])


def plane_sum(own, got):
    half, block, channels = own.shape
    shape = (half // 2, block, channels)
    return kernel_call(plane_kernel, [sds(shape, f32), sds(shape, bf16)], [], 0, own, got)


def conv_band_swap(conv, got):
    bands = lax.axis_size("band")
    _, block, channels = conv.shape
    shape = (block, channels // 2)
    own, message = kernel_call(
        conv_band_kernel, [sds(shape, f32), sds(shape, bf16)],
        [pltpu.VMEM((bands, block, channels // bands), f32)], 0, conv, got,
    )
    return own, lax.ppermute(message, "band", xor_pairs(bands, 1))


def band_sum(conv, got_conv, up, got_up):
    bands = lax.axis_size("band")
    _, block, channels = up.shape
    cols = channels // bands
    side = packing(block, cols)
    shapes = [(block // side, cols * side) if k % 2 else (block, 2 * cols) for k in range(bands)]
    own, *messages = kernel_call(
        band_kernel, [sds(shapes[0], f32)] + [sds(shape, bf16) for shape in shapes[1:]],
        [pltpu.VMEM((bands, block, cols), f32)], 0, conv, got_conv, up, got_up,
    )
    order = sorted(range(1, bands), key=lambda k: (k % 2, -k))
    got = [lax.ppermute(messages[k - 1], "band", xor_pairs(bands, k)) for k in order]
    return [
        a.T
        for a in kernel_call(
            last_kernel, [sds((cols, block), f32)] * 2, [pltpu.VMEM(shapes[0], f32)], 0, own, *got
        )
    ]


def after(value, *others):
    return lax.optimization_barrier((value, *others))[0]


def swap(first, second, axis, wrap):
    one, two = pairs(lax.axis_size(axis), wrap)
    return lax.ppermute(first, axis, one), lax.ppermute(second, axis, two)


def local(coarse, skip, up_weight, conv_weight, cotangent):
    n_rows, n_cols, channels = coarse.shape
    rows, cols, _ = skip.shape
    at = Layout(n_rows, n_cols)
    faces = lax.axis_size("face")
    groups, block = faces // 2, 9 * channels // faces

    flat = halves(rows * cols, channels)
    message = sds((at.face_size, channels), bf16)
    edges = pltpu.VMEM(message.shape, f32)
    first, second, cotangent, skip, coarse = kernel_call(
        face_message,
        [message, message, sds(cotangent.shape, bf16), sds(skip.shape, bf16), sds(coarse.shape, bf16)],
        [flat, edges, edges, pltpu.SemaphoreType.DMA((3,))],
        0, coarse, skip, cotangent, far=(0, 1, 2),
    )
    first, second = swap(first, second, "face", True)
    side = sds(message.shape, f32)
    message = sds((at.band_size, channels), bf16)
    edges = pltpu.VMEM(message.shape, f32)
    first, second, left, right = kernel_call(
        band_message, [message, message, side, side], [edges, edges],
        0, coarse, skip, cotangent, first, second,
    )
    first, second = swap(first, second, "band", False)

    cells = n_rows * n_cols
    stride = cols + 2 * MARGIN
    padded = halves((rows + 2) * stride, channels)
    shift_shape = (3, rows + 2, cols, channels)
    whole = -(-cells // 256) * 256 // n_cols
    part = sds((9 * channels, channels), f32)
    blocks = [
        sds(shift_shape, bf16), sds((2, whole + 1, n_cols, channels), bf16),
        sds(skip.shape, bf16), sds((rows * cols, channels), f32), part,
    ]
    *inner, last_pre, conv_weight, grad_act = kernel_call(
        inner_kernel,
        [
            *blocks, sds((cols, channels), f32), sds(conv_weight.shape, bf16),
            sds((rows * cols, channels), f32),
        ],
        [halves(rows * stride, channels), flat, pltpu.SemaphoreType.DMA],
        0, coarse, skip, cotangent, left, right, up_weight, conv_weight, far=(6,),
    )
    send = sds((groups, block, channels), bf16)
    side = sds(message.shape, f32)
    shifted, near, act, slope, part_conv, send_conv, upper, lower = kernel_call(
        act_kernel, [*blocks, send, side, side],
        [halves(stride, channels), halves(cols, channels)],
        0, second, first, right, up_weight, last_pre, *inner, changed={5 + i: i for i in range(5)},
    )
    phases = kernel_call(
        grad_kernel, [sds((2, 2, whole, n_cols, channels), bf16)], [flat],
        0, shifted, slope, grad_act, conv_weight,
    )[0]
    part_up, send_up = kernel_call(up_kernel, [part, send], [], 0, near, phases)
    own_conv, to_conv = core_sum(after(part_conv, send_up), send_conv)
    got_conv = plane_swap(to_conv, 0)
    own_up, to_up = core_sum(after(part_up, to_conv), send_up)
    got_up = plane_swap(to_up, 0)
    ring_act, ring_grad = kernel_call(
        ring_kernel,
        [
            sds((at.ring_size, channels), f32),
            sds((channels // LANES, at.grad_size, LANES), f32),
        ],
        [halves(at.ring_size, channels), halves((rows + 3) * stride, channels)],
        0, coarse, cotangent, after(left, to_up), right, upper, lower, conv_weight, up_weight,
    )
    own_conv = after(own_conv, ring_act)
    steps = (faces // 2).bit_length() - 1
    for step in range(1, steps):
        own_conv, to_conv = plane_sum(own_conv, got_conv)
        got_conv = plane_swap(to_conv, step)
        if step == 1:
            decoded = kernel_call(
                decoded_kernel, [sds(skip.shape, bf16)], [padded, pltpu.VMEM(shift_shape, bf16)],
                0, act, after(ring_act, to_conv), conv_weight,
            )[0]
            own_up = after(own_up, decoded)
        own_up, to_up = plane_sum(own_up, got_up)
        got_up = plane_swap(to_up, step)
        if step == 1:
            grad_coarse = kernel_call(
                coarse_kernel, [sds(coarse.shape, bf16)],
                [
                    halves(n_rows * (n_cols + 2 * MARGIN), channels),
                    pltpu.VMEM((4, n_rows + 1, n_cols, channels), bf16),
                ],
                0, phases, after(ring_grad, to_up), up_weight,
            )[0]
            own_up = after(own_up, grad_coarse)
    own_conv, got_conv = conv_band_swap(after(own_conv, to_up), got_conv)
    grad_conv, grad_up = band_sum(own_conv, got_conv, own_up, got_up)
    return (decoded, grad_coarse, grad_up, grad_conv)


def solution(mesh):
    return jax.shard_map(
        local,
        mesh=mesh,
        in_specs=(
            P("band", "face", None),
            P("band", "face", None),
            P(),
            P(),
            P("band", "face", None),
        ),
        out_specs=(
            P("band", "face", None),
            P("band", "face", None),
            P("face", "band"),
            P("face", "band"),
        ),
        check_vma=False,
    )
```

```python
import jax
import jax.numpy as jnp
from jax import lax
from jax.experimental import pallas as pl
from jax.experimental.pallas import tpu as pltpu
from jax.sharding import PartitionSpec as P

f32, bf16 = jnp.float32, jnp.bfloat16
forward_taps = ((1, 1), (0, 0), (1, 0))
backward_taps = ((1, 0), (0, 1), (1, 1))
MARGIN = 8
LANES = 128


def sds(shape, dtype):
    return jax.ShapeDtypeStruct(shape, dtype)


def kernel_call(body, outs, scratch, flops, *args, far=(), changed=None):
    vmem = pl.BlockSpec(memory_space=pltpu.VMEM)
    hbm = pl.BlockSpec(memory_space=pltpu.HBM)
    moved = sum(a.size * a.dtype.itemsize for a in args)
    moved += sum(a.size * a.dtype.itemsize for a in outs)
    args = [
        pltpu.with_memory_space_constraint(a, pltpu.HBM) if i in far else a
        for i, a in enumerate(args)
    ]
    return pl.pallas_call(
        body,
        out_shape=tuple(outs),
        in_specs=[hbm if i in far else vmem for i in range(len(args))],
        out_specs=tuple(vmem for _ in outs),
        scratch_shapes=scratch,
        input_output_aliases=changed or {},
        compiler_params=pltpu.CompilerParams(vmem_limit_bytes=28 * 2**20),
        cost_estimate=pl.CostEstimate(flops=flops, bytes_accessed=moved, transcendentals=0),
    )(*args)


def place_of():
    face = lax.axis_index("face")
    return lax.rem(face, 2), lax.div(face, 2), lax.axis_index("band"), lax.axis_size("band")


def dot(a, b):
    return jnp.dot(a, b, preferred_element_type=f32)


def dot_nt(a, b):
    return lax.dot_general(a, b, (((1,), (1,)), ((), ())), preferred_element_type=f32)


def pairs(count, wrap):
    first = [(i, i ^ 1) for i in range(count)]
    second = []
    for i in range(count):
        j = i + 1 if i % 2 else i - 1
        if wrap or 0 <= j < count:
            second.append((i, j % count))
    return first, second


def up16(n):
    return (n + 15) // 16 * 16


def halves(n_rows, channels):
    return pltpu.VMEM((channels // LANES, n_rows, LANES), f32)


def put(ref, start, value, step=1):
    for part in range(ref.shape[0]):
        rows = pl.ds(start, value.shape[0], stride=step if step > 1 else None)
        ref[part, rows, :] = value[:, part * LANES : (part + 1) * LANES]


def get(ref, start, count, step=1):
    rows = pl.ds(start, count, stride=step if step > 1 else None)
    return jnp.concatenate([ref[part, rows, :] for part in range(ref.shape[0])], axis=1)


def fill(ref, start, value):
    ref[start : start + value.shape[0], :] = value


def other_core(send, *terms):
    core = place_of()[0]
    groups, block, _ = send.shape
    for group in range(groups):
        theirs = pl.multiple_of((2 * group + 1 - core) * block, 16)
        send[group] = sum(term[pl.ds(theirs, block), :] for term in terms).astype(bf16)


class Layout:
    def __init__(self, n_rows, n_cols):
        rows, cols = 2 * n_rows, 2 * n_cols
        self.cot, self.cot_2, self.skip, self.coarse = 0, rows, 2 * rows, 3 * rows
        self.face_size = up16(3 * rows + n_rows)
        self.row_cot, self.row_cot_2, self.row_skip = 0, cols, 2 * cols
        self.row_coarse, self.corner = 3 * cols, 3 * cols + n_cols
        self.band_size = self.corner + 16
        ring = (cols + 2 + 7) // 8 * 8
        self.top, self.bottom, self.left, self.right = 0, ring, 2 * ring, 2 * ring + rows
        self.ring_size = up16(2 * ring + 2 * rows)
        self.grad_left, self.grad_size = ring, up16(ring + rows)


COT, COT_2, SKIP, COARSE = (0, 1, 2), (3, 4, 5), (6, None, 7), (8, None, 9)


def face_message(coarse, skip, cot, first, second, cot_v, skip_v, coarse_v, flat, before, after, sems):
    rows, cols, _ = cot.shape
    n_rows, n_cols, _ = coarse.shape
    at = Layout(n_rows, n_cols)
    copies = [
        pltpu.make_async_copy(source, target, sems.at[i])
        for i, (source, target) in enumerate(((cot, cot_v), (skip, skip_v), (coarse, coarse_v)))
    ]
    for copy in copies:
        copy.start()
    before[...] = jnp.zeros_like(before)
    after[...] = jnp.zeros_like(after)
    for copy, array, start, start_2 in (
        (copies[0], cot_v, at.cot, at.cot_2), (copies[1], skip_v, at.skip, None), (copies[2], coarse_v, at.coarse, None),
    ):
        copy.wait()
        n, width, channels = array.shape
        put(flat, 0, array[:, :16, :].astype(f32)[:, :8, :].reshape(n * 8, channels))
        put(flat, n * 8, array[:, width - 16 :, :].astype(f32)[:, 8:, :].reshape(n * 8, channels))
        fill(before, start, get(flat, 0, n, 8))
        fill(after, start, get(flat, n * 8 + 7, n, 8))
        if start_2 is not None:
            fill(after, start_2, get(flat, n * 8 + 6, n, 8))
    even = place_of()[0] == 0
    first[...] = jnp.where(even, after[...], before[...]).astype(bf16)
    second[...] = jnp.where(even, before[...], after[...]).astype(bf16)


def band_message(coarse, skip, cot, got_first, got_second, first, second, left, right, before, after):
    rows, cols, channels = cot.shape
    n_rows, n_cols, _ = coarse.shape
    at = Layout(n_rows, n_cols)
    even = place_of()[0] == 0
    one, two = got_first[...].astype(f32), got_second[...].astype(f32)
    left[...] = jnp.where(even, two, one)
    right[...] = jnp.where(even, one, two)
    for message, row, row_2, cell in ((before, 0, None, 0), (after, rows - 1, rows - 2, n_rows - 1)):
        fill(message, at.row_cot, cot[row].astype(f32))
        if row_2 is None:
            fill(message, at.row_cot_2, jnp.zeros((cols, channels), f32))
        else:
            fill(message, at.row_cot_2, cot[row_2].astype(f32))
        fill(message, at.row_skip, skip[row].astype(f32))
        fill(message, at.row_coarse, coarse[cell].astype(f32))
        fill(message, at.corner, jnp.zeros((16, channels), f32))
        corners = [
            (COT[0], left, at.cot + row), (COT[1], left, at.cot_2 + row), (COT[2], right, at.cot + row),
            (SKIP[0], left, at.skip + row), (SKIP[2], right, at.skip + row),
            (COARSE[0], left, at.coarse + cell), (COARSE[2], right, at.coarse + cell),
        ]
        if row_2 is not None:
            corners += [
                (COT_2[0], left, at.cot + row_2), (COT_2[1], left, at.cot_2 + row_2),
                (COT_2[2], right, at.cot + row_2),
            ]
        for corner, side, source in corners:
            fill(message, at.corner + corner, side[source : source + 1, :])
    even = lax.rem(place_of()[2], 2) == 0
    first[...] = jnp.where(even, after[...], before[...]).astype(bf16)
    second[...] = jnp.where(even, before[...], after[...]).astype(bf16)


def early_kernel(cot, conv_w, conv_v, grad_act, centre, sem):
    rows, cols, channels = cot.shape
    copy = pltpu.make_async_copy(conv_w, conv_v, sem)
    copy.start()
    for row in (0, rows + 1):
        centre[row] = jnp.zeros((cols, channels), bf16)
    centre[pl.ds(1, rows)] = cot[...]
    copy.wait()
    total = jnp.zeros((rows * cols, channels), f32)
    for k in range(3):
        source = centre[pl.ds(2 - k, rows)].reshape(-1, channels)
        total = total + dot_nt(source, conv_v[k, 1])
    grad_act[...] = total


def inner_kernel(
    coarse, skip, cot, left, right, up_w, conv_w, grad_centre,
    shifted, near, act, slope, partial, last_pre, grad_act, padded, pre,
):
    n_rows, n_cols, channels = coarse.shape
    rows, cols, _ = skip.shape
    at = Layout(n_rows, n_cols)
    stride = cols + 2 * MARGIN
    for row in range(n_rows):
        near[0, row] = coarse[row]
        put(padded, row * stride, coarse[row].astype(f32))
    put(padded, n_cols, right[at.coarse : at.coarse + n_rows, :], stride)
    for row in range(n_rows):
        near[1, row] = get(padded, row * stride + 1, n_cols).astype(bf16)
    for row in range(n_rows, near.shape[1]):
        for side in range(2):
            near[side, row] = jnp.zeros((n_cols, channels), bf16)
    sums = {}
    for k in range(3):
        row_phase, row_off = forward_taps[k]
        for l in range(3):
            col_phase, col_off = forward_taps[l]
            source = near[col_off, pl.ds(row_off, n_rows)].reshape(n_rows * n_cols, channels)
            term = dot(source, up_w[k, l])
            name = (row_phase, col_phase)
            sums[name] = sums[name] + term if name in sums else term
    for (row_phase, col_phase), total in sums.items():
        for row in range(n_rows):
            start = (2 * row + row_phase) * cols + col_phase
            put(pre, start, total[row * n_cols : (row + 1) * n_cols], 2)
    for row in range(rows):
        put(padded, row * stride + MARGIN, cot[row].astype(f32))
    put(padded, MARGIN - 1, left[at.cot : at.cot + rows, :], stride)
    put(padded, MARGIN + cols, right[at.cot : at.cot + rows, :], stride)
    for row in range(rows):
        for shift in (0, 2):
            start = row * stride + MARGIN - 1 + shift
            shifted[shift, row + 1] = get(padded, start, cols).astype(bf16)
        shifted[1, row + 1] = cot[row]
    for shift in range(3):
        shifted[shift, 0] = jnp.zeros((cols, channels), bf16)
        shifted[shift, rows + 1] = jnp.zeros((cols, channels), bf16)
    preact = get(pre, 0, rows * cols) + skip[...].reshape(rows * cols, channels).astype(f32)
    last_pre[...] = preact[(rows - 1) * cols :]
    sigma = jax.nn.sigmoid(preact)
    value = preact * sigma
    slope[...] = sigma + value * (1.0 - sigma)
    row_of = lax.broadcasted_iota(jnp.int32, value.shape, 0)
    act_flat = jnp.where(row_of < (rows - 1) * cols, value, 0.0).astype(bf16)
    act[...] = act_flat.reshape(act.shape)
    act_t = act_flat.T
    for k in range(3):
        for l in range(3):
            source = shifted[2 - l, pl.ds(2 - k, rows)].reshape(-1, channels)
            partial[pl.ds((3 * k + l) * channels, channels), :] = dot(act_t, source)
    total = grad_centre[...]
    for k in range(3):
        for l in (0, 2):
            source = shifted[2 - l, pl.ds(2 - k, rows)].reshape(-1, channels)
            total = total + dot_nt(source, conv_w[k, l])
    grad_act[...] = total


def act_kernel(
    got_first, got_second, right, up_w, last_pre, partial, shifted_in, near_in, act_in, slope_in,
    shifted, near, act, slope, extra, send, upper, lower, padded, pre,
):
    rows, cols, channels = act.shape
    n_rows, n_cols = rows // 2, cols // 2
    at = Layout(n_rows, n_cols)
    even = lax.rem(place_of()[2], 2) == 0
    one, two = got_first[...].astype(f32), got_second[...].astype(f32)
    upper[...] = jnp.where(even, two, one)
    lower[...] = jnp.where(even, one, two)
    below = lower[at.row_coarse : at.row_coarse + n_cols, :]
    corner = at.corner + COARSE[2]
    put(padded, 0, below)
    put(padded, n_cols, lower[corner : corner + 1, :])
    cells = [below.astype(bf16), get(padded, 1, n_cols).astype(bf16)]
    near[0, n_rows] = cells[0]
    near[1, n_rows] = cells[1]
    put(pre, 0, dot(cells[0], up_w[0, 1]), 2)
    put(pre, 1, dot(cells[1], up_w[0, 0]) + dot(cells[0], up_w[0, 2]), 2)
    preact = last_pre[...] + get(pre, 0, cols)
    sigma = jax.nn.sigmoid(preact)
    value = preact * sigma
    slope[(rows - 1) * cols :, :] = sigma + value * (1.0 - sigma)
    last = value.astype(bf16)
    act[rows - 1] = last
    for row, message in ((0, upper), (rows + 1, lower)):
        centre = message[at.row_cot : at.row_cot + cols, :]
        put(padded, MARGIN, centre)
        for col, one in ((-1, COT[0]), (cols, COT[2])):
            put(padded, MARGIN + col, message[at.corner + one : at.corner + one + 1, :])
        shifted[0, row] = get(padded, MARGIN - 1, cols).astype(bf16)
        shifted[1, row] = centre.astype(bf16)
        shifted[2, row] = get(padded, MARGIN + 1, cols).astype(bf16)
    last_t = last.T
    both_t = jnp.concatenate([last, act_in[0]], axis=0).T
    for k in range(3):
        for l in range(3):
            beside = shifted[2 - l, rows + 1 - k]
            if k == 2:
                term = dot(both_t, jnp.concatenate([beside, shifted[2 - l, 0]], axis=0))
            else:
                term = dot(last_t, beside)
            extra[pl.ds((3 * k + l) * channels, channels), :] = term
    other_core(send, partial, extra)


def grad_kernel(shifted, slope, grad_act, conv_w, phases, fine):
    rows, cols = shifted.shape[1] - 2, shifted.shape[2]
    channels = shifted.shape[3]
    n_rows, n_cols = rows // 2, cols // 2
    first = jnp.zeros((cols, channels), f32)
    last = jnp.zeros((cols, channels), f32)
    for l in range(3):
        first = first + dot_nt(shifted[2 - l, 0], conv_w[2, l])
        last = last + dot_nt(shifted[2 - l, rows + 1], conv_w[0, l])
    cells = rows * cols
    put(fine, 0, (grad_act[...] * slope[...]).astype(bf16).astype(f32))
    total = (grad_act[:cols, :] + first) * slope[:cols, :]
    put(fine, 0, total.astype(bf16).astype(f32))
    total = (grad_act[cells - cols :, :] + last) * slope[cells - cols :, :]
    put(fine, cells - cols, total.astype(bf16).astype(f32))
    whole = phases.shape[2]
    for row_phase in range(2):
        for col_phase in range(2):
            for row in range(n_rows):
                start = (2 * row + row_phase) * cols + col_phase
                phases[row_phase, col_phase, row] = get(fine, start, n_cols, 2).astype(bf16)
            for row in range(n_rows, whole):
                phases[row_phase, col_phase, row] = jnp.zeros((n_cols, channels), bf16)


def up_kernel(near, phases, partial, send):
    _, _, whole, n_cols, channels = phases.shape
    turned = {}
    for row_off in range(2):
        for col_off in range(2):
            cells = near[col_off, pl.ds(row_off, whole)]
            turned[row_off, col_off] = cells.reshape(whole * n_cols, channels).T
    for k in range(3):
        row_phase, row_off = forward_taps[k]
        for l in range(3):
            col_phase, col_off = forward_taps[l]
            source = phases[row_phase, col_phase].reshape(whole * n_cols, channels)
            partial[pl.ds((3 * k + l) * channels, channels), :] = dot(
                turned[row_off, col_off], source
            )
    other_core(send, partial)


def ring_kernel(
    coarse, cot, left, right, upper, lower, conv_w, up_w, ring_act, ring_grad, ring, wide,
):
    rows, cols, channels = cot.shape
    n_rows, n_cols = rows // 2, cols // 2
    at = Layout(n_rows, n_cols)
    stride, step = cols + 2 * MARGIN, n_cols + 2 * MARGIN
    _, _, band, n_bands = place_of()
    has_upper, has_lower = band > 0, band < n_bands - 1

    def corner(message, which):
        return message[at.corner + which : at.corner + which + 1, :]

    def cell(i, j):
        return (i + 1) * step + MARGIN + j

    for row in range(n_rows):
        put(wide, cell(row, 0), coarse[row].astype(f32))
    for row, message in ((-1, upper), (n_rows, lower)):
        put(wide, cell(row, 0), message[at.row_coarse : at.row_coarse + n_cols, :])
        put(wide, cell(row, -1), corner(message, COARSE[0]))
        put(wide, cell(row, n_cols), corner(message, COARSE[2]))
    put(wide, cell(0, -1), left[at.coarse : at.coarse + n_rows, :], step)
    put(wide, cell(0, n_cols), right[at.coarse : at.coarse + n_rows, :], step)
    total = jnp.zeros((at.ring_size, channels), f32)
    for k in range(3):
        for l in range(3):
            put(ring, 0, jnp.zeros((at.ring_size, channels), f32))
            for base, i in ((at.bottom, n_rows),) if k == 1 else ((at.top, k // 2 * -1),):
                start = cell(i, -1 if l == 2 else 0)
                put(ring, base + (l == 1), get(wide, start, n_cols + 1), 2)
            base, j = (at.right, n_cols) if l == 1 else (at.left, -(l // 2))
            start = cell(1 if k == 0 else 0, j)
            put(ring, base + (k != 1), get(wide, start, n_rows, step), 2)
            total = total + dot(get(ring, 0, at.ring_size).astype(bf16), up_w[k, l])
    put(ring, 0, jnp.zeros((at.ring_size, channels), f32))
    for base, message in ((at.top, upper), (at.bottom, lower)):
        put(ring, base + 1, message[at.row_skip : at.row_skip + cols, :])
        put(ring, base, corner(message, SKIP[0]))
        put(ring, base + cols + 1, corner(message, SKIP[2]))
    put(ring, at.left, left[at.skip : at.skip + rows, :])
    put(ring, at.right, right[at.skip : at.skip + rows, :])
    preact = total + get(ring, 0, at.ring_size)
    sigma = jax.nn.sigmoid(preact)
    value = preact * sigma
    slope = sigma + value * (1.0 - sigma)
    value = value.astype(bf16).astype(f32)
    ring_act[...] = value
    for base, exists in ((at.top, has_upper), (at.bottom, has_lower)):
        strip = value[base : base + cols + 2]
        ring_act[base : base + cols + 2, :] = jnp.where(exists, strip, 0.0)

    def fine(p, q):
        return (p + 2) * stride + MARGIN + q

    for row in range(rows):
        put(wide, fine(row, 0), cot[row].astype(f32))
    for row, message, start, which in (
        (-1, upper, at.row_cot, COT), (-2, upper, at.row_cot_2, COT_2), (rows, lower, at.row_cot, COT),
    ):
        put(wide, fine(row, 0), message[start : start + cols, :])
        for col, one in ((-1, which[0]), (-2, which[1]), (cols, which[2])):
            put(wide, fine(row, col), corner(message, one))
    put(wide, fine(0, -1), left[at.cot : at.cot + rows, :], stride)
    put(wide, fine(0, -2), left[at.cot_2 : at.cot_2 + rows, :], stride)
    put(wide, fine(0, cols), right[at.cot : at.cot + rows, :], stride)
    total = jnp.zeros((at.grad_size, channels), f32)
    for k in range(3):
        for l in range(3):
            put(ring, at.top, get(wide, fine(-k, -l), cols + 1))
            put(ring, at.grad_left, get(wide, fine(1 - k, -l), rows, stride))
            source = get(ring, 0, at.grad_size).astype(bf16)
            total = total + dot_nt(source, conv_w[k, l])
    strip = (total[: cols + 1] * slope[at.top : at.top + cols + 1]).astype(bf16).astype(f32)
    put(ring_grad, at.top, jnp.where(has_upper, strip, 0.0))
    strip = total[at.grad_left : at.grad_left + rows] * slope[at.left : at.left + rows]
    put(ring_grad, at.grad_left, strip.astype(bf16).astype(f32))


def decoded_kernel(act, ring_act, conv_w, decoded, padded, shifted):
    rows, cols, channels = act.shape
    at = Layout(rows // 2, cols // 2)
    stride = cols + 2 * MARGIN
    for row in range(rows):
        put(padded, (row + 1) * stride + MARGIN, act[row].astype(f32))
    for row, base in ((0, at.top), (rows + 1, at.bottom)):
        put(padded, row * stride + MARGIN - 1, ring_act[base : base + cols + 2, :])
    put(padded, stride + MARGIN - 1, ring_act[at.left : at.left + rows, :], stride)
    put(padded, stride + MARGIN + cols, ring_act[at.right : at.right + rows, :], stride)
    for row in range(rows + 2):
        for shift in range(3):
            start = row * stride + MARGIN - 1 + shift
            shifted[shift, row] = get(padded, start, cols).astype(bf16)
    total = jnp.zeros((rows * cols, channels), f32)
    for k in range(3):
        for l in range(3):
            source = shifted[l, pl.ds(k, rows)].reshape(-1, channels)
            total = total + dot(source, conv_w[k, l])
    decoded[...] = total.astype(bf16).reshape(decoded.shape)

def coarse_kernel(phases, ring_grad, up_w, coarse_out, padded, moved):
    n_rows, n_cols, channels = coarse_out.shape
    at = Layout(n_rows, n_cols)
    stride = n_cols + 2 * MARGIN
    for phase, start in ((0, 1), (1, 2), (2, 0)):
        moved[phase, 0] = get(ring_grad, at.top + start, n_cols, 2).astype(bf16)
    for phase in range(2):
        for row in range(n_rows):
            moved[phase, 1 + row] = phases[1, phase, row]
    for row_phase in range(2):
        for row in range(n_rows):
            put(padded, row * stride + MARGIN, phases[row_phase, 1, row].astype(f32))
        put(padded, MARGIN - 1, get(ring_grad, at.grad_left + row_phase, n_rows, 2), stride)
        for row in range(n_rows):
            cells = get(padded, row * stride + MARGIN - 1, n_cols).astype(bf16)
            if row_phase:
                moved[2, 1 + row] = cells
            else:
                moved[3, row] = cells
    total = jnp.zeros((n_rows * n_cols, channels), f32)
    for k in range(3):
        for l in range(3):
            if k == 1:
                if l == 0:
                    source = moved[3, pl.ds(0, n_rows)]
                else:
                    source = phases[0, l - 1, pl.ds(0, n_rows)]
            else:
                source = moved[(2, 0, 1)[l], pl.ds(k // 2, n_rows)]
            total = total + dot_nt(source.reshape(n_rows * n_cols, channels), up_w[k, l])
    coarse_out[...] = total.astype(bf16).reshape(coarse_out.shape)


def halving(count):
    bits = (count // 2).bit_length() - 1
    return [[(step + core) % bits for step in range(bits)] for core in range(2)]


def mask_of(slot, order):
    last = len(order) - 1
    return sum(1 << bit for step, bit in enumerate(order) if slot >> (last - step) & 1)


def core_kernel(*refs):
    *terms, got, own, message = refs
    slots, half, block = got.shape[0], own.shape[0], got.shape[1]
    core, chip, _, _ = place_of()
    even, odd = halving(2 * slots)
    for slot in range(slots):
        target = chip ^ jnp.where(core == 0, mask_of(slot, even), mask_of(slot, odd))
        mine = pl.multiple_of((2 * target + core) * block, 16)
        total = sum(term[pl.ds(mine, block), :] for term in terms) + got[target].astype(f32)
        if slot < half:
            own[slot] = total
        else:
            message[slot - half] = total.astype(bf16)


def plane_kernel(before, got, own, message):
    half = own.shape[0]
    for slot in range(2 * half):
        total = before[slot] + got[slot].astype(f32)
        if slot < half:
            own[slot] = total
        else:
            message[slot - half] = total.astype(bf16)


def band_kernel(conv, got_conv, up, got_up, own, *refs):
    n_bands, messages, cut = len(refs), refs[:-1], refs[-1]
    conv_total = conv[0] + got_conv[0].astype(f32)
    up_total = up[0] + got_up[0].astype(f32)
    cols = conv_total.shape[1] // n_bands
    for band in range(n_bands):
        cut[band, :, :cols] = conv_total[:, band * cols : (band + 1) * cols]
        cut[band, :, cols:] = up_total[:, band * cols : (band + 1) * cols]
    band = place_of()[2]
    own[...] = cut[band]
    for k, message in enumerate(messages):
        message[...] = cut[lax.rem(band + k + 1, n_bands)].astype(bf16)


def last_kernel(own, *refs):
    peers, (conv, up) = refs[:-2], refs[-2:]
    total = own[...]
    for peer in peers:
        total = total + peer[...].astype(f32)
    turned = total.T
    conv[...] = turned[: conv.shape[0]]
    up[...] = turned[conv.shape[0] :]


def xor_pairs(count, bits):
    return [(i, i ^ bits) for i in range(count)]


def core_sum(send, *terms):
    groups, block, channels = send.shape
    got = lax.ppermute(send, "face", xor_pairs(lax.axis_size("face"), 1))
    shape = (groups // 2, block, channels)
    return kernel_call(core_kernel, [sds(shape, f32), sds(shape, bf16)], [], 0, *terms, got)


def plane_swap(message, step):
    faces = lax.axis_size("face")
    orders = halving(faces)
    return lax.ppermute(message, "face", [(i, i ^ 2 << orders[i % 2][step]) for i in range(faces)])


def plane_sum(own, got):
    half, block, channels = own.shape
    shape = (half // 2, block, channels)
    return kernel_call(plane_kernel, [sds(shape, f32), sds(shape, bf16)], [], 0, own, got)


def band_sum(conv, got_conv, up, got_up):
    bands = lax.axis_size("band")
    _, block, channels = conv.shape
    cols = channels // bands
    shape = (block, 2 * cols)
    own, *messages = kernel_call(
        band_kernel, [sds(shape, f32)] + [sds(shape, bf16)] * (bands - 1),
        [pltpu.VMEM((bands,) + shape, f32)], 0, conv, got_conv, up, got_up,
    )
    got = [
        lax.ppermute(messages[k - 1], "band", [(i, (i + k) % bands) for i in range(bands)])
        for k in range(1, bands)
    ]
    return [a.T for a in kernel_call(last_kernel, [sds((cols, block), f32)] * 2, [], 0, own, *got)]


def after(value, *others):
    return lax.optimization_barrier((value, *others))[0]


def swap(first, second, axis, wrap):
    one, two = pairs(lax.axis_size(axis), wrap)
    return lax.ppermute(first, axis, one), lax.ppermute(second, axis, two)


def local(coarse, skip, up_weight, conv_weight, cotangent):
    n_rows, n_cols, channels = coarse.shape
    rows, cols, _ = skip.shape
    at = Layout(n_rows, n_cols)
    faces = lax.axis_size("face")
    groups, block = faces // 2, 9 * channels // faces

    flat = halves(rows * cols, channels)
    message = sds((at.face_size, channels), bf16)
    edges = pltpu.VMEM(message.shape, f32)
    first, second, cotangent, skip, coarse = kernel_call(
        face_message,
        [message, message, sds(cotangent.shape, bf16), sds(skip.shape, bf16), sds(coarse.shape, bf16)],
        [flat, edges, edges, pltpu.SemaphoreType.DMA((3,))],
        0, coarse, skip, cotangent, far=(0, 1, 2),
    )
    first, second = swap(first, second, "face", True)
    conv_weight, grad_centre = kernel_call(
        early_kernel,
        [sds(conv_weight.shape, bf16), sds((rows * cols, channels), f32)],
        [pltpu.VMEM((rows + 2, cols, channels), bf16), pltpu.SemaphoreType.DMA],
        0, cotangent, conv_weight, far=(1,),
    )
    side = sds(message.shape, f32)
    message = sds((at.band_size, channels), bf16)
    edges = pltpu.VMEM(message.shape, f32)
    first, second, left, right = kernel_call(
        band_message, [message, message, side, side], [edges, edges],
        0, coarse, skip, after(cotangent, grad_centre), first, second,
    )
    first, second = swap(first, second, "band", False)

    cells = n_rows * n_cols
    stride = cols + 2 * MARGIN
    padded = halves((rows + 2) * stride, channels)
    shift_shape = (3, rows + 2, cols, channels)
    whole = -(-cells // 256) * 256 // n_cols
    part = sds((9 * channels, channels), f32)
    blocks = [
        sds(shift_shape, bf16), sds((2, whole + 1, n_cols, channels), bf16),
        sds(skip.shape, bf16), sds((rows * cols, channels), f32), part,
    ]
    *inner, part_conv, last_pre, grad_act = kernel_call(
        inner_kernel,
        [
            *blocks, sds((cols, channels), f32), sds((rows * cols, channels), f32),
        ],
        [halves(rows * stride, channels), flat],
        0, coarse, skip, cotangent, left, right, up_weight, conv_weight, grad_centre,
    )
    send = sds((groups, block, channels), bf16)
    side = sds(message.shape, f32)
    shifted, near, act, slope, extra_conv, send_conv, upper, lower = kernel_call(
        act_kernel, [*blocks, send, side, side],
        [halves(stride, channels), halves(cols, channels)],
        0, first, second, right, up_weight, last_pre, part_conv, *inner,
        changed={6 + i: i for i in range(4)},
    )
    phases = kernel_call(
        grad_kernel, [sds((2, 2, whole, n_cols, channels), bf16)], [flat],
        0, shifted, slope, grad_act, conv_weight,
    )[0]
    part_up, send_up = kernel_call(up_kernel, [part, send], [], 0, near, phases)
    own_conv, to_conv = core_sum(send_conv, after(part_conv, send_up), extra_conv)
    got_conv = plane_swap(to_conv, 0)
    own_up, to_up = core_sum(send_up, after(part_up, to_conv))
    got_up = plane_swap(to_up, 0)
    ring_act, ring_grad = kernel_call(
        ring_kernel,
        [
            sds((at.ring_size, channels), f32),
            sds((channels // LANES, at.grad_size, LANES), f32),
        ],
        [halves(at.ring_size, channels), halves((rows + 3) * stride, channels)],
        0, coarse, cotangent, after(left, to_up), right, upper, lower, conv_weight, up_weight,
    )
    own_conv = after(own_conv, ring_act)
    steps = (faces // 2).bit_length() - 1
    for step in range(1, steps):
        own_conv, to_conv = plane_sum(own_conv, got_conv)
        got_conv = plane_swap(to_conv, step)
        if step == 1:
            decoded = kernel_call(
                decoded_kernel, [sds(skip.shape, bf16)], [padded, pltpu.VMEM(shift_shape, bf16)],
                0, act, after(ring_act, to_conv), conv_weight,
            )[0]
            own_up = after(own_up, decoded)
        own_up, to_up = plane_sum(own_up, got_up)
        got_up = plane_swap(to_up, step)
        if step == 1:
            grad_coarse = kernel_call(
                coarse_kernel, [sds(coarse.shape, bf16)],
                [
                    halves(n_rows * (n_cols + 2 * MARGIN), channels),
                    pltpu.VMEM((4, n_rows + 1, n_cols, channels), bf16),
                ],
                0, phases, after(ring_grad, to_up), up_weight,
            )[0]
            own_up = after(own_up, grad_coarse)
    grad_conv, grad_up = band_sum(own_conv, got_conv, own_up, got_up)
    return (decoded, grad_coarse, grad_up, grad_conv)


def solution(mesh):
    return jax.shard_map(
        local,
        mesh=mesh,
        in_specs=(
            P("band", "face", None),
            P("band", "face", None),
            P(),
            P(),
            P("band", "face", None),
        ),
        out_specs=(
            P("band", "face", None),
            P("band", "face", None),
            P("face", "band"),
            P("face", "band"),
        ),
        check_vma=False,
    )
```

```python
import jax
import jax.numpy as jnp
from jax import lax
from jax.experimental import pallas as pl
from jax.experimental.pallas import tpu as pltpu
from jax.sharding import PartitionSpec as P

f32, bf16 = jnp.float32, jnp.bfloat16
forward_taps = ((1, 1), (0, 0), (1, 0))
backward_taps = ((1, 0), (0, 1), (1, 1))
MARGIN = 8
LANES = 128


def sds(shape, dtype):
    return jax.ShapeDtypeStruct(shape, dtype)


def kernel_call(body, outs, scratch, flops, *args, far=(), changed=None):
    vmem = pl.BlockSpec(memory_space=pltpu.VMEM)
    hbm = pl.BlockSpec(memory_space=pltpu.HBM)
    moved = sum(a.size * a.dtype.itemsize for a in args)
    moved += sum(a.size * a.dtype.itemsize for a in outs)
    args = [
        pltpu.with_memory_space_constraint(a, pltpu.HBM) if i in far else a
        for i, a in enumerate(args)
    ]
    return pl.pallas_call(
        body,
        out_shape=tuple(outs),
        in_specs=[hbm if i in far else vmem for i in range(len(args))],
        out_specs=tuple(vmem for _ in outs),
        scratch_shapes=scratch,
        input_output_aliases=changed or {},
        compiler_params=pltpu.CompilerParams(vmem_limit_bytes=28 * 2**20),
        cost_estimate=pl.CostEstimate(flops=flops, bytes_accessed=moved, transcendentals=0),
    )(*args)


def place_of():
    face = lax.axis_index("face")
    return lax.rem(face, 2), lax.div(face, 2), lax.axis_index("band"), lax.axis_size("band")


def dot(a, b):
    return jnp.dot(a, b, preferred_element_type=f32)


def dot_nt(a, b):
    return lax.dot_general(a, b, (((1,), (1,)), ((), ())), preferred_element_type=f32)


def pairs(count, wrap):
    first = [(i, i ^ 1) for i in range(count)]
    second = []
    for i in range(count):
        j = i + 1 if i % 2 else i - 1
        if wrap or 0 <= j < count:
            second.append((i, j % count))
    return first, second


def up16(n):
    return (n + 15) // 16 * 16


def halves(n_rows, channels):
    return pltpu.VMEM((channels // LANES, n_rows, LANES), f32)


def put(ref, start, value, step=1):
    for part in range(ref.shape[0]):
        rows = pl.ds(start, value.shape[0], stride=step if step > 1 else None)
        ref[part, rows, :] = value[:, part * LANES : (part + 1) * LANES]


def get(ref, start, count, step=1):
    rows = pl.ds(start, count, stride=step if step > 1 else None)
    return jnp.concatenate([ref[part, rows, :] for part in range(ref.shape[0])], axis=1)


def fill(ref, start, value):
    ref[start : start + value.shape[0], :] = value


def other_core(send, *terms):
    core = place_of()[0]
    groups, block, _ = send.shape
    for group in range(groups):
        theirs = pl.multiple_of((2 * group + 1 - core) * block, 16)
        send[group] = sum(term[pl.ds(theirs, block), :] for term in terms).astype(bf16)


class Layout:
    def __init__(self, n_rows, n_cols):
        rows, cols = 2 * n_rows, 2 * n_cols
        self.cot, self.cot_2, self.skip, self.coarse = 0, rows, 2 * rows, 3 * rows
        self.face_size = up16(3 * rows + n_rows)
        self.row_cot, self.row_cot_2, self.row_skip = 0, cols, 2 * cols
        self.row_coarse, self.corner = 3 * cols, 3 * cols + n_cols
        self.band_size = self.corner + 16
        ring = (cols + 2 + 7) // 8 * 8
        self.top, self.bottom, self.left, self.right = 0, ring, 2 * ring, 2 * ring + rows
        self.ring_size = up16(2 * ring + 2 * rows)
        self.grad_left, self.grad_size = ring, up16(ring + rows)


COT, COT_2, SKIP, COARSE = (0, 1, 2), (3, 4, 5), (6, None, 7), (8, None, 9)


def face_message(coarse, skip, cot, first, second, cot_v, skip_v, coarse_v, flat, before, after, sems):
    rows, cols, _ = cot.shape
    n_rows, n_cols, _ = coarse.shape
    at = Layout(n_rows, n_cols)
    copies = [
        pltpu.make_async_copy(source, target, sems.at[i])
        for i, (source, target) in enumerate(((cot, cot_v), (skip, skip_v), (coarse, coarse_v)))
    ]
    for copy in copies:
        copy.start()
    before[...] = jnp.zeros_like(before)
    after[...] = jnp.zeros_like(after)
    for copy, array, start, start_2 in (
        (copies[0], cot_v, at.cot, at.cot_2), (copies[1], skip_v, at.skip, None), (copies[2], coarse_v, at.coarse, None),
    ):
        copy.wait()
        n, width, channels = array.shape
        put(flat, 0, array[:, :16, :].astype(f32)[:, :8, :].reshape(n * 8, channels))
        put(flat, n * 8, array[:, width - 16 :, :].astype(f32)[:, 8:, :].reshape(n * 8, channels))
        fill(before, start, get(flat, 0, n, 8))
        fill(after, start, get(flat, n * 8 + 7, n, 8))
        if start_2 is not None:
            fill(after, start_2, get(flat, n * 8 + 6, n, 8))
    even = place_of()[0] == 0
    first[...] = jnp.where(even, after[...], before[...]).astype(bf16)
    second[...] = jnp.where(even, before[...], after[...]).astype(bf16)


def band_message(coarse, skip, cot, got_first, got_second, first, second, left, right, before, after):
    rows, cols, channels = cot.shape
    n_rows, n_cols, _ = coarse.shape
    at = Layout(n_rows, n_cols)
    even = place_of()[0] == 0
    one, two = got_first[...].astype(f32), got_second[...].astype(f32)
    left[...] = jnp.where(even, two, one)
    right[...] = jnp.where(even, one, two)
    for message, row, row_2, cell in ((before, 0, None, 0), (after, rows - 1, rows - 2, n_rows - 1)):
        fill(message, at.row_cot, cot[row].astype(f32))
        if row_2 is None:
            fill(message, at.row_cot_2, jnp.zeros((cols, channels), f32))
        else:
            fill(message, at.row_cot_2, cot[row_2].astype(f32))
        fill(message, at.row_skip, skip[row].astype(f32))
        fill(message, at.row_coarse, coarse[cell].astype(f32))
        fill(message, at.corner, jnp.zeros((16, channels), f32))
        corners = [
            (COT[0], left, at.cot + row), (COT[1], left, at.cot_2 + row), (COT[2], right, at.cot + row),
            (SKIP[0], left, at.skip + row), (SKIP[2], right, at.skip + row),
            (COARSE[0], left, at.coarse + cell), (COARSE[2], right, at.coarse + cell),
        ]
        if row_2 is not None:
            corners += [
                (COT_2[0], left, at.cot + row_2), (COT_2[1], left, at.cot_2 + row_2),
                (COT_2[2], right, at.cot + row_2),
            ]
        for corner, side, source in corners:
            fill(message, at.corner + corner, side[source : source + 1, :])
    even = lax.rem(place_of()[2], 2) == 0
    first[...] = jnp.where(even, after[...], before[...]).astype(bf16)
    second[...] = jnp.where(even, before[...], after[...]).astype(bf16)


def early_kernel(cot, conv_w, conv_v, grad_act, centre, sem):
    rows, cols, channels = cot.shape
    copy = pltpu.make_async_copy(conv_w, conv_v, sem)
    copy.start()
    for row in (0, rows + 1):
        centre[row] = jnp.zeros((cols, channels), bf16)
    centre[pl.ds(1, rows)] = cot[...]
    copy.wait()
    total = jnp.zeros((rows * cols, channels), f32)
    for k in range(3):
        source = centre[pl.ds(2 - k, rows)].reshape(-1, channels)
        total = total + dot_nt(source, conv_v[k, 1])
    grad_act[...] = total


def inner_kernel(
    coarse, skip, cot, left, right, up_w, conv_w, grad_centre,
    shifted, near, act, slope, partial, send, last_pre, grad_act, padded, pre,
):
    n_rows, n_cols, channels = coarse.shape
    rows, cols, _ = skip.shape
    at = Layout(n_rows, n_cols)
    stride = cols + 2 * MARGIN
    for row in range(n_rows):
        near[0, row] = coarse[row]
        put(padded, row * stride, coarse[row].astype(f32))
    put(padded, n_cols, right[at.coarse : at.coarse + n_rows, :], stride)
    for row in range(n_rows):
        near[1, row] = get(padded, row * stride + 1, n_cols).astype(bf16)
    for row in range(n_rows, near.shape[1]):
        for side in range(2):
            near[side, row] = jnp.zeros((n_cols, channels), bf16)
    sums = {}
    for k in range(3):
        row_phase, row_off = forward_taps[k]
        for l in range(3):
            col_phase, col_off = forward_taps[l]
            source = near[col_off, pl.ds(row_off, n_rows)].reshape(n_rows * n_cols, channels)
            term = dot(source, up_w[k, l])
            name = (row_phase, col_phase)
            sums[name] = sums[name] + term if name in sums else term
    for (row_phase, col_phase), total in sums.items():
        for row in range(n_rows):
            start = (2 * row + row_phase) * cols + col_phase
            put(pre, start, total[row * n_cols : (row + 1) * n_cols], 2)
    for row in range(rows):
        put(padded, row * stride + MARGIN, cot[row].astype(f32))
    put(padded, MARGIN - 1, left[at.cot : at.cot + rows, :], stride)
    put(padded, MARGIN + cols, right[at.cot : at.cot + rows, :], stride)
    for row in range(rows):
        for shift in (0, 2):
            start = row * stride + MARGIN - 1 + shift
            shifted[shift, row + 1] = get(padded, start, cols).astype(bf16)
        shifted[1, row + 1] = cot[row]
    for shift in range(3):
        shifted[shift, 0] = jnp.zeros((cols, channels), bf16)
        shifted[shift, rows + 1] = jnp.zeros((cols, channels), bf16)
    preact = get(pre, 0, rows * cols) + skip[...].reshape(rows * cols, channels).astype(f32)
    last_pre[...] = preact[(rows - 1) * cols :]
    sigma = jax.nn.sigmoid(preact)
    value = preact * sigma
    slope[...] = sigma + value * (1.0 - sigma)
    row_of = lax.broadcasted_iota(jnp.int32, value.shape, 0)
    act_flat = jnp.where(row_of < (rows - 1) * cols, value, 0.0).astype(bf16)
    act[...] = act_flat.reshape(act.shape)
    act_t = act_flat.T
    for k in range(3):
        for l in range(3):
            source = shifted[2 - l, pl.ds(2 - k, rows)].reshape(-1, channels)
            partial[pl.ds((3 * k + l) * channels, channels), :] = dot(act_t, source)
    other_core(send, partial)
    total = grad_centre[...]
    for k in range(3):
        source = shifted[0, pl.ds(2 - k, rows)].reshape(-1, channels)
        total = total + dot_nt(source, conv_w[k, 2])
    grad_act[...] = total


def act_kernel(
    got_first, got_second, right, up_w, last_pre, shifted_in, near_in, act_in, slope_in,
    shifted, near, act, slope, edge, upper, lower, padded, pre,
):
    rows, cols, channels = act.shape
    n_rows, n_cols = rows // 2, cols // 2
    at = Layout(n_rows, n_cols)
    even = lax.rem(place_of()[2], 2) == 0
    one, two = got_first[...].astype(f32), got_second[...].astype(f32)
    upper[...] = jnp.where(even, two, one)
    lower[...] = jnp.where(even, one, two)
    below = lower[at.row_coarse : at.row_coarse + n_cols, :]
    corner = at.corner + COARSE[2]
    put(padded, 0, below)
    put(padded, n_cols, lower[corner : corner + 1, :])
    cells = [below.astype(bf16), get(padded, 1, n_cols).astype(bf16)]
    near[0, n_rows] = cells[0]
    near[1, n_rows] = cells[1]
    put(pre, 0, dot(cells[0], up_w[0, 1]), 2)
    put(pre, 1, dot(cells[1], up_w[0, 0]) + dot(cells[0], up_w[0, 2]), 2)
    preact = last_pre[...] + get(pre, 0, cols)
    sigma = jax.nn.sigmoid(preact)
    value = preact * sigma
    slope[(rows - 1) * cols :, :] = sigma + value * (1.0 - sigma)
    last = value.astype(bf16)
    act[rows - 1] = last
    for row, message in ((0, upper), (rows + 1, lower)):
        centre = message[at.row_cot : at.row_cot + cols, :]
        put(padded, MARGIN, centre)
        for col, one in ((-1, COT[0]), (cols, COT[2])):
            put(padded, MARGIN + col, message[at.corner + one : at.corner + one + 1, :])
        shifted[0, row] = get(padded, MARGIN - 1, cols).astype(bf16)
        shifted[1, row] = centre.astype(bf16)
        shifted[2, row] = get(padded, MARGIN + 1, cols).astype(bf16)
    edge[0] = last
    edge[1] = act_in[0]
    for shift in range(3):
        for place, row in enumerate((0, rows - 1, rows, rows + 1)):
            edge[2 + 4 * shift + place] = shifted[shift, row]


def grad_kernel(shifted, slope, grad_act, conv_w, phases, fine):
    rows, cols = shifted.shape[1] - 2, shifted.shape[2]
    channels = shifted.shape[3]
    n_rows, n_cols = rows // 2, cols // 2
    cells = rows * cols
    total = grad_act[...]
    for k in range(3):
        source = shifted[2, pl.ds(2 - k, rows)].reshape(cells, channels)
        total = total + dot_nt(source, conv_w[k, 0])
    first = jnp.zeros((cols, channels), f32)
    last = jnp.zeros((cols, channels), f32)
    for l in (1, 2):
        first = first + dot_nt(shifted[2 - l, 0], conv_w[2, l])
        last = last + dot_nt(shifted[2 - l, rows + 1], conv_w[0, l])
    put(fine, 0, (total * slope[...]).astype(bf16).astype(f32))
    put(fine, 0, ((total[:cols] + first) * slope[:cols, :]).astype(bf16).astype(f32))
    edge = (total[cells - cols :] + last) * slope[cells - cols :, :]
    put(fine, cells - cols, edge.astype(bf16).astype(f32))
    whole = phases.shape[2]
    for row_phase in range(2):
        for col_phase in range(2):
            for row in range(n_rows):
                start = (2 * row + row_phase) * cols + col_phase
                phases[row_phase, col_phase, row] = get(fine, start, n_cols, 2).astype(bf16)
            for row in range(n_rows, whole):
                phases[row_phase, col_phase, row] = jnp.zeros((n_cols, channels), bf16)


def up_kernel(near, phases, partial, send):
    _, _, whole, n_cols, channels = phases.shape
    turned = {}
    for row_off in range(2):
        for col_off in range(2):
            cells = near[col_off, pl.ds(row_off, whole)]
            turned[row_off, col_off] = cells.reshape(whole * n_cols, channels).T
    for k in range(3):
        row_phase, row_off = forward_taps[k]
        for l in range(3):
            col_phase, col_off = forward_taps[l]
            source = phases[row_phase, col_phase].reshape(whole * n_cols, channels)
            partial[pl.ds((3 * k + l) * channels, channels), :] = dot(
                turned[row_off, col_off], source
            )
    other_core(send, partial)


def ring_kernel(
    coarse, cot, left, right, upper, lower, conv_w, up_w, ring_act, ring_grad, ring, wide,
):
    rows, cols, channels = cot.shape
    n_rows, n_cols = rows // 2, cols // 2
    at = Layout(n_rows, n_cols)
    stride, step = cols + 2 * MARGIN, n_cols + 2 * MARGIN
    _, _, band, n_bands = place_of()
    has_upper, has_lower = band > 0, band < n_bands - 1

    def corner(message, which):
        return message[at.corner + which : at.corner + which + 1, :]

    def cell(i, j):
        return (i + 1) * step + MARGIN + j

    for row in range(n_rows):
        put(wide, cell(row, 0), coarse[row].astype(f32))
    for row, message in ((-1, upper), (n_rows, lower)):
        put(wide, cell(row, 0), message[at.row_coarse : at.row_coarse + n_cols, :])
        put(wide, cell(row, -1), corner(message, COARSE[0]))
        put(wide, cell(row, n_cols), corner(message, COARSE[2]))
    put(wide, cell(0, -1), left[at.coarse : at.coarse + n_rows, :], step)
    put(wide, cell(0, n_cols), right[at.coarse : at.coarse + n_rows, :], step)
    total = jnp.zeros((at.ring_size, channels), f32)
    for k in range(3):
        for l in range(3):
            put(ring, 0, jnp.zeros((at.ring_size, channels), f32))
            for base, i in ((at.bottom, n_rows),) if k == 1 else ((at.top, k // 2 * -1),):
                start = cell(i, -1 if l == 2 else 0)
                put(ring, base + (l == 1), get(wide, start, n_cols + 1), 2)
            base, j = (at.right, n_cols) if l == 1 else (at.left, -(l // 2))
            start = cell(1 if k == 0 else 0, j)
            put(ring, base + (k != 1), get(wide, start, n_rows, step), 2)
            total = total + dot(get(ring, 0, at.ring_size).astype(bf16), up_w[k, l])
    put(ring, 0, jnp.zeros((at.ring_size, channels), f32))
    for base, message in ((at.top, upper), (at.bottom, lower)):
        put(ring, base + 1, message[at.row_skip : at.row_skip + cols, :])
        put(ring, base, corner(message, SKIP[0]))
        put(ring, base + cols + 1, corner(message, SKIP[2]))
    put(ring, at.left, left[at.skip : at.skip + rows, :])
    put(ring, at.right, right[at.skip : at.skip + rows, :])
    preact = total + get(ring, 0, at.ring_size)
    sigma = jax.nn.sigmoid(preact)
    value = preact * sigma
    slope = sigma + value * (1.0 - sigma)
    value = value.astype(bf16).astype(f32)
    ring_act[...] = value
    for base, exists in ((at.top, has_upper), (at.bottom, has_lower)):
        strip = value[base : base + cols + 2]
        ring_act[base : base + cols + 2, :] = jnp.where(exists, strip, 0.0)

    def fine(p, q):
        return (p + 2) * stride + MARGIN + q

    for row in range(rows):
        put(wide, fine(row, 0), cot[row].astype(f32))
    for row, message, start, which in (
        (-1, upper, at.row_cot, COT), (-2, upper, at.row_cot_2, COT_2), (rows, lower, at.row_cot, COT),
    ):
        put(wide, fine(row, 0), message[start : start + cols, :])
        for col, one in ((-1, which[0]), (-2, which[1]), (cols, which[2])):
            put(wide, fine(row, col), corner(message, one))
    put(wide, fine(0, -1), left[at.cot : at.cot + rows, :], stride)
    put(wide, fine(0, -2), left[at.cot_2 : at.cot_2 + rows, :], stride)
    put(wide, fine(0, cols), right[at.cot : at.cot + rows, :], stride)
    total = jnp.zeros((at.grad_size, channels), f32)
    for k in range(3):
        for l in range(3):
            put(ring, at.top, get(wide, fine(-k, -l), cols + 1))
            put(ring, at.grad_left, get(wide, fine(1 - k, -l), rows, stride))
            source = get(ring, 0, at.grad_size).astype(bf16)
            total = total + dot_nt(source, conv_w[k, l])
    strip = (total[: cols + 1] * slope[at.top : at.top + cols + 1]).astype(bf16).astype(f32)
    put(ring_grad, at.top, jnp.where(has_upper, strip, 0.0))
    strip = total[at.grad_left : at.grad_left + rows] * slope[at.left : at.left + rows]
    put(ring_grad, at.grad_left, strip.astype(bf16).astype(f32))


def decoded_kernel(act, ring_act, conv_w, decoded, padded, shifted):
    rows, cols, channels = act.shape
    at = Layout(rows // 2, cols // 2)
    stride = cols + 2 * MARGIN
    for row in range(rows):
        put(padded, (row + 1) * stride + MARGIN, act[row].astype(f32))
    for row, base in ((0, at.top), (rows + 1, at.bottom)):
        put(padded, row * stride + MARGIN - 1, ring_act[base : base + cols + 2, :])
    put(padded, stride + MARGIN - 1, ring_act[at.left : at.left + rows, :], stride)
    put(padded, stride + MARGIN + cols, ring_act[at.right : at.right + rows, :], stride)
    for row in range(rows + 2):
        for shift in range(3):
            start = row * stride + MARGIN - 1 + shift
            shifted[shift, row] = get(padded, start, cols).astype(bf16)
    total = jnp.zeros((rows * cols, channels), f32)
    for k in range(3):
        for l in range(3):
            source = shifted[l, pl.ds(k, rows)].reshape(-1, channels)
            total = total + dot(source, conv_w[k, l])
    decoded[...] = total.astype(bf16).reshape(decoded.shape)

def coarse_kernel(phases, ring_grad, up_w, coarse_out, padded, moved):
    n_rows, n_cols, channels = coarse_out.shape
    at = Layout(n_rows, n_cols)
    stride = n_cols + 2 * MARGIN
    for phase, start in ((0, 1), (1, 2), (2, 0)):
        moved[phase, 0] = get(ring_grad, at.top + start, n_cols, 2).astype(bf16)
    for phase in range(2):
        for row in range(n_rows):
            moved[phase, 1 + row] = phases[1, phase, row]
    for row_phase in range(2):
        for row in range(n_rows):
            put(padded, row * stride + MARGIN, phases[row_phase, 1, row].astype(f32))
        put(padded, MARGIN - 1, get(ring_grad, at.grad_left + row_phase, n_rows, 2), stride)
        for row in range(n_rows):
            cells = get(padded, row * stride + MARGIN - 1, n_cols).astype(bf16)
            if row_phase:
                moved[2, 1 + row] = cells
            else:
                moved[3, row] = cells
    total = jnp.zeros((n_rows * n_cols, channels), f32)
    for k in range(3):
        for l in range(3):
            if k == 1:
                if l == 0:
                    source = moved[3, pl.ds(0, n_rows)]
                else:
                    source = phases[0, l - 1, pl.ds(0, n_rows)]
            else:
                source = moved[(2, 0, 1)[l], pl.ds(k // 2, n_rows)]
            total = total + dot_nt(source.reshape(n_rows * n_cols, channels), up_w[k, l])
    coarse_out[...] = total.astype(bf16).reshape(coarse_out.shape)


def halving(count):
    bits = (count // 2).bit_length() - 1
    return [[(step + core) % bits for step in range(bits)] for core in range(2)]


def mask_of(slot, order):
    last = len(order) - 1
    return sum(1 << bit for step, bit in enumerate(order) if slot >> (last - step) & 1)


def edge_kernel(partial, got, edge, got_edge, own, message, extra):
    channels, block = partial.shape[1], got.shape[1]
    zero = jnp.zeros(edge.shape[1:], bf16)
    sides = (edge, got_edge)
    rows_t = jnp.concatenate([side[row] for side in sides for row in range(2)], axis=0).T

    def add_blocks(core):
        for tap in range(9):
            first = 2 + 4 * (2 - tap % 3)
            beside = []
            for side in sides:
                beside += [side[first + 3 - tap // 3], side[first] if tap >= 6 else zero]
            beside = jnp.concatenate(beside, axis=0)
            start = tap * channels
            for mine in range(start // block, -(-(start + channels) // block)):
                if mine % 2 == core:
                    low = max(start, mine * block)
                    high = min(start + channels, (mine + 1) * block)
                    extra[low:high, :] = dot(rows_t[low - start : high - start], beside)

    for core in range(2):
        pl.when(place_of()[0] == core)(lambda core=core: add_blocks(core))
    core_kernel(partial, extra, got, own, message)


def core_kernel(*refs):
    *terms, got, own, message = refs
    slots, half, block = got.shape[0], own.shape[0], got.shape[1]
    core, chip, _, _ = place_of()
    even, odd = halving(2 * slots)
    for slot in range(slots):
        target = chip ^ jnp.where(core == 0, mask_of(slot, even), mask_of(slot, odd))
        mine = pl.multiple_of((2 * target + core) * block, 16)
        total = sum(term[pl.ds(mine, block), :] for term in terms) + got[target].astype(f32)
        if slot < half:
            own[slot] = total
        else:
            message[slot - half] = total.astype(bf16)


def plane_kernel(before, got, own, message):
    half = own.shape[0]
    for slot in range(2 * half):
        total = before[slot] + got[slot].astype(f32)
        if slot < half:
            own[slot] = total
        else:
            message[slot - half] = total.astype(bf16)


def band_kernel(conv, got_conv, up, got_up, own, *refs):
    n_bands, messages, cut = len(refs), refs[:-1], refs[-1]
    conv_total = conv[0] + got_conv[0].astype(f32)
    up_total = up[0] + got_up[0].astype(f32)
    cols = conv_total.shape[1] // n_bands
    for band in range(n_bands):
        cut[band, :, :cols] = conv_total[:, band * cols : (band + 1) * cols]
        cut[band, :, cols:] = up_total[:, band * cols : (band + 1) * cols]
    band = place_of()[2]
    own[...] = cut[band]
    for k, message in enumerate(messages):
        message[...] = cut[lax.rem(band + k + 1, n_bands)].astype(bf16)


def last_kernel(own, *refs):
    peers, (conv, up) = refs[:-2], refs[-2:]
    total = own[...]
    for peer in peers:
        total = total + peer[...].astype(f32)
    turned = total.T
    conv[...] = turned[: conv.shape[0]]
    up[...] = turned[conv.shape[0] :]


def xor_pairs(count, bits):
    return [(i, i ^ bits) for i in range(count)]


def core_swap(send):
    return lax.ppermute(send, "face", xor_pairs(lax.axis_size("face"), 1))


def core_sum(body, scratch, partial, got, *rest):
    groups, block, channels = got.shape
    shape = (groups // 2, block, channels)
    outs = [sds(shape, f32), sds(shape, bf16)]
    return kernel_call(body, outs, scratch, 0, partial, got, *rest)


def plane_swap(message, step):
    faces = lax.axis_size("face")
    orders = halving(faces)
    return lax.ppermute(message, "face", [(i, i ^ 2 << orders[i % 2][step]) for i in range(faces)])


def plane_sum(own, got):
    half, block, channels = own.shape
    shape = (half // 2, block, channels)
    return kernel_call(plane_kernel, [sds(shape, f32), sds(shape, bf16)], [], 0, own, got)


def band_sum(conv, got_conv, up, got_up):
    bands = lax.axis_size("band")
    _, block, channels = conv.shape
    cols = channels // bands
    shape = (block, 2 * cols)
    own, *messages = kernel_call(
        band_kernel, [sds(shape, f32)] + [sds(shape, bf16)] * (bands - 1),
        [pltpu.VMEM((bands,) + shape, f32)], 0, conv, got_conv, up, got_up,
    )
    got = [
        lax.ppermute(messages[k - 1], "band", [(i, (i + k) % bands) for i in range(bands)])
        for k in range(1, bands)
    ]
    return [a.T for a in kernel_call(last_kernel, [sds((cols, block), f32)] * 2, [], 0, own, *got)]


def after(value, *others):
    return lax.optimization_barrier((value, *others))[0]


def swap(first, second, axis, wrap):
    one, two = pairs(lax.axis_size(axis), wrap)
    return lax.ppermute(first, axis, one), lax.ppermute(second, axis, two)


def local(coarse, skip, up_weight, conv_weight, cotangent):
    n_rows, n_cols, channels = coarse.shape
    rows, cols, _ = skip.shape
    at = Layout(n_rows, n_cols)
    faces = lax.axis_size("face")
    groups, block = faces // 2, 9 * channels // faces

    flat = halves(rows * cols, channels)
    message = sds((at.face_size, channels), bf16)
    edges = pltpu.VMEM(message.shape, f32)
    first, second, cotangent, skip, coarse = kernel_call(
        face_message,
        [message, message, sds(cotangent.shape, bf16), sds(skip.shape, bf16), sds(coarse.shape, bf16)],
        [flat, edges, edges, pltpu.SemaphoreType.DMA((3,))],
        0, coarse, skip, cotangent, far=(0, 1, 2),
    )
    first, second = swap(first, second, "face", True)
    conv_weight, grad_centre = kernel_call(
        early_kernel,
        [sds(conv_weight.shape, bf16), sds((rows * cols, channels), f32)],
        [pltpu.VMEM((rows + 2, cols, channels), bf16), pltpu.SemaphoreType.DMA],
        0, cotangent, conv_weight, far=(1,),
    )
    side = sds(message.shape, f32)
    message = sds((at.band_size, channels), bf16)
    edges = pltpu.VMEM(message.shape, f32)
    first, second, left, right = kernel_call(
        band_message, [message, message, side, side], [edges, edges],
        0, coarse, skip, after(cotangent, grad_centre), first, second,
    )
    first, second = swap(first, second, "band", False)

    cells = n_rows * n_cols
    stride = cols + 2 * MARGIN
    padded = halves((rows + 2) * stride, channels)
    shift_shape = (3, rows + 2, cols, channels)
    whole = -(-cells // 256) * 256 // n_cols
    part = sds((9 * channels, channels), f32)
    send = sds((groups, block, channels), bf16)
    blocks = [
        sds(shift_shape, bf16), sds((2, whole + 1, n_cols, channels), bf16),
        sds(skip.shape, bf16), sds((rows * cols, channels), f32), part,
    ]
    *inner, part_conv, send_conv, last_pre, grad_act = kernel_call(
        inner_kernel,
        [
            *blocks, send, sds((cols, channels), f32), sds((rows * cols, channels), f32),
        ],
        [halves(rows * stride, channels), flat],
        0, coarse, skip, cotangent, left, right, up_weight, conv_weight, grad_centre,
    )
    side = sds(message.shape, f32)
    got_conv = core_swap(send_conv)
    edge = sds((14, cols, channels), bf16)
    shifted, near, act, slope, edge, upper, lower = kernel_call(
        act_kernel, [*blocks[:-1], edge, side, side],
        [halves(stride, channels), halves(cols, channels)],
        10**11, first, second, right, up_weight, last_pre, *inner, changed={5 + i: i for i in range(4)},
    )
    phases = kernel_call(
        grad_kernel, [sds((2, 2, whole, n_cols, channels), bf16)], [flat],
        0, shifted, slope, grad_act, conv_weight,
    )[0]
    part_up, send_up = kernel_call(up_kernel, [part, send], [], 0, near, phases)
    own_conv, to_conv = core_sum(
        edge_kernel, [pltpu.VMEM(part.shape, f32)], after(part_conv, send_up), got_conv, edge, core_swap(edge)
    )
    got_conv = plane_swap(to_conv, 0)
    own_up, to_up = core_sum(core_kernel, [], part_up, core_swap(after(send_up, to_conv)))
    got_up = plane_swap(to_up, 0)
    ring_act, ring_grad = kernel_call(
        ring_kernel,
        [
            sds((at.ring_size, channels), f32),
            sds((channels // LANES, at.grad_size, LANES), f32),
        ],
        [halves(at.ring_size, channels), halves((rows + 3) * stride, channels)],
        0, coarse, cotangent, after(left, to_up), right, upper, lower, conv_weight, up_weight,
    )
    own_conv = after(own_conv, ring_act)
    steps = (faces // 2).bit_length() - 1
    for step in range(1, steps):
        own_conv, to_conv = plane_sum(own_conv, got_conv)
        got_conv = plane_swap(to_conv, step)
        if step == 1:
            decoded = kernel_call(
                decoded_kernel, [sds(skip.shape, bf16)], [padded, pltpu.VMEM(shift_shape, bf16)],
                0, act, after(ring_act, to_conv), conv_weight,
            )[0]
            own_up = after(own_up, decoded)
        own_up, to_up = plane_sum(own_up, got_up)
        got_up = plane_swap(to_up, step)
        if step == 1:
            grad_coarse = kernel_call(
                coarse_kernel, [sds(coarse.shape, bf16)],
                [
                    halves(n_rows * (n_cols + 2 * MARGIN), channels),
                    pltpu.VMEM((4, n_rows + 1, n_cols, channels), bf16),
                ],
                0, phases, after(ring_grad, to_up), up_weight,
            )[0]
            own_up = after(own_up, grad_coarse)
    grad_conv, grad_up = band_sum(own_conv, got_conv, own_up, got_up)
    return (decoded, grad_coarse, grad_up, grad_conv)


def solution(mesh):
    return jax.shard_map(
        local,
        mesh=mesh,
        in_specs=(
            P("band", "face", None),
            P("band", "face", None),
            P(),
            P(),
            P("band", "face", None),
        ),
        out_specs=(
            P("band", "face", None),
            P("band", "face", None),
            P("face", "band"),
            P("face", "band"),
        ),
        check_vma=False,
    )
```

```python
import jax
import jax.numpy as jnp
from jax import lax
from jax.experimental import pallas as pl
from jax.experimental.pallas import tpu as pltpu
from jax.sharding import PartitionSpec as P

f32, bf16 = jnp.float32, jnp.bfloat16
forward_taps = ((1, 1), (0, 0), (1, 0))
backward_taps = ((1, 0), (0, 1), (1, 1))
MARGIN = 8
LANES = 128


def sds(shape, dtype):
    return jax.ShapeDtypeStruct(shape, dtype)


def kernel_call(body, outs, scratch, flops, *args, far=(), changed=None):
    vmem = pl.BlockSpec(memory_space=pltpu.VMEM)
    hbm = pl.BlockSpec(memory_space=pltpu.HBM)
    moved = sum(a.size * a.dtype.itemsize for a in args)
    moved += sum(a.size * a.dtype.itemsize for a in outs)
    args = [
        pltpu.with_memory_space_constraint(a, pltpu.HBM) if i in far else a
        for i, a in enumerate(args)
    ]
    return pl.pallas_call(
        body,
        out_shape=tuple(outs),
        in_specs=[hbm if i in far else vmem for i in range(len(args))],
        out_specs=tuple(vmem for _ in outs),
        scratch_shapes=scratch,
        input_output_aliases=changed or {},
        compiler_params=pltpu.CompilerParams(vmem_limit_bytes=28 * 2**20),
        cost_estimate=pl.CostEstimate(flops=flops, bytes_accessed=moved, transcendentals=0),
    )(*args)


def place_of():
    face = lax.axis_index("face")
    return lax.rem(face, 2), lax.div(face, 2), lax.axis_index("band"), lax.axis_size("band")


def dot(a, b):
    return jnp.dot(a, b, preferred_element_type=f32)


def dot_nt(a, b):
    return lax.dot_general(a, b, (((1,), (1,)), ((), ())), preferred_element_type=f32)


def pairs(count, wrap):
    first = [(i, i ^ 1) for i in range(count)]
    second = []
    for i in range(count):
        j = i + 1 if i % 2 else i - 1
        if wrap or 0 <= j < count:
            second.append((i, j % count))
    return first, second


def up16(n):
    return (n + 15) // 16 * 16


def halves(n_rows, channels):
    return pltpu.VMEM((channels // LANES, n_rows, LANES), f32)


def put(ref, start, value, step=1):
    for part in range(ref.shape[0]):
        rows = pl.ds(start, value.shape[0], stride=step if step > 1 else None)
        ref[part, rows, :] = value[:, part * LANES : (part + 1) * LANES]


def get(ref, start, count, step=1):
    rows = pl.ds(start, count, stride=step if step > 1 else None)
    return jnp.concatenate([ref[part, rows, :] for part in range(ref.shape[0])], axis=1)


def fill(ref, start, value):
    ref[start : start + value.shape[0], :] = value


def other_core(send, *terms):
    core = place_of()[0]
    groups, block, _ = send.shape
    for group in range(groups):
        theirs = pl.multiple_of((2 * group + 1 - core) * block, 16)
        send[group] = sum(term[pl.ds(theirs, block), :] for term in terms).astype(bf16)


class Layout:
    def __init__(self, n_rows, n_cols):
        rows, cols = 2 * n_rows, 2 * n_cols
        self.cot, self.cot_2, self.skip, self.coarse = 0, rows, 2 * rows, 3 * rows
        self.face_size = up16(3 * rows + n_rows)
        self.row_cot, self.row_cot_2, self.row_skip = 0, cols, 2 * cols
        self.row_coarse, self.corner = 3 * cols, 3 * cols + n_cols
        self.band_size = self.corner + 16
        ring = (cols + 2 + 7) // 8 * 8
        self.top, self.bottom, self.left, self.right = 0, ring, 2 * ring, 2 * ring + rows
        self.ring_size = up16(2 * ring + 2 * rows)
        self.grad_left, self.grad_size = ring, up16(ring + rows)


COT, COT_2, SKIP, COARSE = (0, 1, 2), (3, 4, 5), (6, None, 7), (8, None, 9)


def face_message(coarse, skip, cot, first, second, cot_v, skip_v, coarse_v, flat, before, after, sems):
    rows, cols, _ = cot.shape
    n_rows, n_cols, _ = coarse.shape
    at = Layout(n_rows, n_cols)
    copies = [
        pltpu.make_async_copy(source, target, sems.at[i])
        for i, (source, target) in enumerate(((cot, cot_v), (skip, skip_v), (coarse, coarse_v)))
    ]
    for copy in copies:
        copy.start()
    before[...] = jnp.zeros_like(before)
    after[...] = jnp.zeros_like(after)
    for copy, array, start, start_2 in (
        (copies[0], cot_v, at.cot, at.cot_2), (copies[1], skip_v, at.skip, None), (copies[2], coarse_v, at.coarse, None),
    ):
        copy.wait()
        n, width, channels = array.shape
        put(flat, 0, array[:, :16, :].astype(f32)[:, :8, :].reshape(n * 8, channels))
        put(flat, n * 8, array[:, width - 16 :, :].astype(f32)[:, 8:, :].reshape(n * 8, channels))
        fill(before, start, get(flat, 0, n, 8))
        fill(after, start, get(flat, n * 8 + 7, n, 8))
        if start_2 is not None:
            fill(after, start_2, get(flat, n * 8 + 6, n, 8))
    even = place_of()[0] == 0
    first[...] = jnp.where(even, after[...], before[...]).astype(bf16)
    second[...] = jnp.where(even, before[...], after[...]).astype(bf16)


def band_message(coarse, skip, cot, got_first, got_second, first, second, left, right, before, after):
    rows, cols, channels = cot.shape
    n_rows, n_cols, _ = coarse.shape
    at = Layout(n_rows, n_cols)
    even = place_of()[0] == 0
    one, two = got_first[...].astype(f32), got_second[...].astype(f32)
    left[...] = jnp.where(even, two, one)
    right[...] = jnp.where(even, one, two)
    for message, row, row_2, cell in ((before, 0, None, 0), (after, rows - 1, rows - 2, n_rows - 1)):
        fill(message, at.row_cot, cot[row].astype(f32))
        if row_2 is None:
            fill(message, at.row_cot_2, jnp.zeros((cols, channels), f32))
        else:
            fill(message, at.row_cot_2, cot[row_2].astype(f32))
        fill(message, at.row_skip, skip[row].astype(f32))
        fill(message, at.row_coarse, coarse[cell].astype(f32))
        fill(message, at.corner, jnp.zeros((16, channels), f32))
        corners = [
            (COT[0], left, at.cot + row), (COT[1], left, at.cot_2 + row), (COT[2], right, at.cot + row),
            (SKIP[0], left, at.skip + row), (SKIP[2], right, at.skip + row),
            (COARSE[0], left, at.coarse + cell), (COARSE[2], right, at.coarse + cell),
        ]
        if row_2 is not None:
            corners += [
                (COT_2[0], left, at.cot + row_2), (COT_2[1], left, at.cot_2 + row_2),
                (COT_2[2], right, at.cot + row_2),
            ]
        for corner, side, source in corners:
            fill(message, at.corner + corner, side[source : source + 1, :])
    even = lax.rem(place_of()[2], 2) == 0
    first[...] = jnp.where(even, after[...], before[...]).astype(bf16)
    second[...] = jnp.where(even, before[...], after[...]).astype(bf16)


def early_kernel(cot, conv_w, conv_v, grad_act, centre, sem):
    rows, cols, channels = cot.shape
    copy = pltpu.make_async_copy(conv_w, conv_v, sem)
    copy.start()
    for row in (0, rows + 1):
        centre[row] = jnp.zeros((cols, channels), bf16)
    centre[pl.ds(1, rows)] = cot[...]
    copy.wait()
    total = jnp.zeros((rows * cols, channels), f32)
    for k in range(3):
        source = centre[pl.ds(2 - k, rows)].reshape(-1, channels)
        total = total + dot_nt(source, conv_v[k, 1])
    grad_act[...] = total


def inner_kernel(
    coarse, skip, cot, left, right, up_w, conv_w, grad_centre,
    shifted, near, act, slope, partial, send, last_pre, grad_act, padded, pre,
):
    n_rows, n_cols, channels = coarse.shape
    rows, cols, _ = skip.shape
    at = Layout(n_rows, n_cols)
    stride = cols + 2 * MARGIN
    for row in range(n_rows):
        near[0, row] = coarse[row]
        put(padded, row * stride, coarse[row].astype(f32))
    put(padded, n_cols, right[at.coarse : at.coarse + n_rows, :], stride)
    for row in range(n_rows):
        near[1, row] = get(padded, row * stride + 1, n_cols).astype(bf16)
    for row in range(n_rows, near.shape[1]):
        for side in range(2):
            near[side, row] = jnp.zeros((n_cols, channels), bf16)
    sums = {}
    for k in range(3):
        row_phase, row_off = forward_taps[k]
        for l in range(3):
            col_phase, col_off = forward_taps[l]
            source = near[col_off, pl.ds(row_off, n_rows)].reshape(n_rows * n_cols, channels)
            term = dot(source, up_w[k, l])
            name = (row_phase, col_phase)
            sums[name] = sums[name] + term if name in sums else term
    for (row_phase, col_phase), total in sums.items():
        for row in range(n_rows):
            start = (2 * row + row_phase) * cols + col_phase
            put(pre, start, total[row * n_cols : (row + 1) * n_cols], 2)
    for row in range(rows):
        put(padded, row * stride + MARGIN, cot[row].astype(f32))
    put(padded, MARGIN - 1, left[at.cot : at.cot + rows, :], stride)
    put(padded, MARGIN + cols, right[at.cot : at.cot + rows, :], stride)
    for row in range(rows):
        for shift in (0, 2):
            start = row * stride + MARGIN - 1 + shift
            shifted[shift, row + 1] = get(padded, start, cols).astype(bf16)
        shifted[1, row + 1] = cot[row]
    for shift in range(3):
        shifted[shift, 0] = jnp.zeros((cols, channels), bf16)
        shifted[shift, rows + 1] = jnp.zeros((cols, channels), bf16)
    preact = get(pre, 0, rows * cols) + skip[...].reshape(rows * cols, channels).astype(f32)
    last_pre[...] = preact[(rows - 1) * cols :]
    sigma = jax.nn.sigmoid(preact)
    value = preact * sigma
    slope[...] = sigma + value * (1.0 - sigma)
    row_of = lax.broadcasted_iota(jnp.int32, value.shape, 0)
    act_flat = jnp.where(row_of < (rows - 1) * cols, value, 0.0).astype(bf16)
    act[...] = act_flat.reshape(act.shape)
    act_t = act_flat.T
    for k in range(3):
        for l in range(3):
            source = shifted[2 - l, pl.ds(2 - k, rows)].reshape(-1, channels)
            partial[pl.ds((3 * k + l) * channels, channels), :] = dot(act_t, source)
    other_core(send, partial)
    total = grad_centre[...]
    for k in range(3):
        source = shifted[0, pl.ds(2 - k, rows)].reshape(-1, channels)
        total = total + dot_nt(source, conv_w[k, 2])
    grad_act[...] = total


def act_kernel(
    got_first, got_second, right, up_w, last_pre, shifted_in, near_in, act_in, slope_in,
    shifted, near, act, slope, edge, upper, lower, padded, pre,
):
    rows, cols, channels = act.shape
    n_rows, n_cols = rows // 2, cols // 2
    at = Layout(n_rows, n_cols)
    even = lax.rem(place_of()[2], 2) == 0
    one, two = got_first[...].astype(f32), got_second[...].astype(f32)
    upper[...] = jnp.where(even, two, one)
    lower[...] = jnp.where(even, one, two)
    below = lower[at.row_coarse : at.row_coarse + n_cols, :]
    corner = at.corner + COARSE[2]
    put(padded, 0, below)
    put(padded, n_cols, lower[corner : corner + 1, :])
    cells = [below.astype(bf16), get(padded, 1, n_cols).astype(bf16)]
    near[0, n_rows] = cells[0]
    near[1, n_rows] = cells[1]
    put(pre, 0, dot(cells[0], up_w[0, 1]), 2)
    put(pre, 1, dot(cells[1], up_w[0, 0]) + dot(cells[0], up_w[0, 2]), 2)
    preact = last_pre[...] + get(pre, 0, cols)
    sigma = jax.nn.sigmoid(preact)
    value = preact * sigma
    slope[(rows - 1) * cols :, :] = sigma + value * (1.0 - sigma)
    last = value.astype(bf16)
    act[rows - 1] = last
    for row, message in ((0, upper), (rows + 1, lower)):
        centre = message[at.row_cot : at.row_cot + cols, :]
        put(padded, MARGIN, centre)
        for col, one in ((-1, COT[0]), (cols, COT[2])):
            put(padded, MARGIN + col, message[at.corner + one : at.corner + one + 1, :])
        shifted[0, row] = get(padded, MARGIN - 1, cols).astype(bf16)
        shifted[1, row] = centre.astype(bf16)
        shifted[2, row] = get(padded, MARGIN + 1, cols).astype(bf16)
    edge[0] = last
    edge[1] = act_in[0]
    for shift in range(3):
        for place, row in enumerate((0, rows - 1, rows, rows + 1)):
            edge[2 + 4 * shift + place] = shifted[shift, row]


def grad_kernel(shifted, slope, grad_act, conv_w, phases, fine):
    rows, cols = shifted.shape[1] - 2, shifted.shape[2]
    channels = shifted.shape[3]
    n_rows, n_cols = rows // 2, cols // 2
    cells = rows * cols
    total = grad_act[...]
    for k in range(3):
        source = shifted[2, pl.ds(2 - k, rows)].reshape(cells, channels)
        total = total + dot_nt(source, conv_w[k, 0])
    first = jnp.zeros((cols, channels), f32)
    last = jnp.zeros((cols, channels), f32)
    for l in (1, 2):
        first = first + dot_nt(shifted[2 - l, 0], conv_w[2, l])
        last = last + dot_nt(shifted[2 - l, rows + 1], conv_w[0, l])
    put(fine, 0, (total * slope[...]).astype(bf16).astype(f32))
    put(fine, 0, ((total[:cols] + first) * slope[:cols, :]).astype(bf16).astype(f32))
    edge = (total[cells - cols :] + last) * slope[cells - cols :, :]
    put(fine, cells - cols, edge.astype(bf16).astype(f32))
    whole = phases.shape[2]
    for row_phase in range(2):
        for col_phase in range(2):
            for row in range(n_rows):
                start = (2 * row + row_phase) * cols + col_phase
                phases[row_phase, col_phase, row] = get(fine, start, n_cols, 2).astype(bf16)
            for row in range(n_rows, whole):
                phases[row_phase, col_phase, row] = jnp.zeros((n_cols, channels), bf16)


def up_kernel(near, phases, partial, send):
    _, _, whole, n_cols, channels = phases.shape
    turned = {}
    for row_off in range(2):
        for col_off in range(2):
            cells = near[col_off, pl.ds(row_off, whole)]
            turned[row_off, col_off] = cells.reshape(whole * n_cols, channels).T
    for k in range(3):
        row_phase, row_off = forward_taps[k]
        for l in range(3):
            col_phase, col_off = forward_taps[l]
            source = phases[row_phase, col_phase].reshape(whole * n_cols, channels)
            partial[pl.ds((3 * k + l) * channels, channels), :] = dot(
                turned[row_off, col_off], source
            )
    other_core(send, partial)


def ring_kernel(
    coarse, cot, left, right, upper, lower, conv_w, up_w, ring_act, ring_grad, ring, wide,
):
    rows, cols, channels = cot.shape
    n_rows, n_cols = rows // 2, cols // 2
    at = Layout(n_rows, n_cols)
    stride, step = cols + 2 * MARGIN, n_cols + 2 * MARGIN
    _, _, band, n_bands = place_of()
    has_upper, has_lower = band > 0, band < n_bands - 1

    def corner(message, which):
        return message[at.corner + which : at.corner + which + 1, :]

    def cell(i, j):
        return (i + 1) * step + MARGIN + j

    for row in range(n_rows):
        put(wide, cell(row, 0), coarse[row].astype(f32))
    for row, message in ((-1, upper), (n_rows, lower)):
        put(wide, cell(row, 0), message[at.row_coarse : at.row_coarse + n_cols, :])
        put(wide, cell(row, -1), corner(message, COARSE[0]))
        put(wide, cell(row, n_cols), corner(message, COARSE[2]))
    put(wide, cell(0, -1), left[at.coarse : at.coarse + n_rows, :], step)
    put(wide, cell(0, n_cols), right[at.coarse : at.coarse + n_rows, :], step)
    total = jnp.zeros((at.ring_size, channels), f32)
    for k in range(3):
        for l in range(3):
            put(ring, 0, jnp.zeros((at.ring_size, channels), f32))
            for base, i in ((at.bottom, n_rows),) if k == 1 else ((at.top, k // 2 * -1),):
                start = cell(i, -1 if l == 2 else 0)
                put(ring, base + (l == 1), get(wide, start, n_cols + 1), 2)
            base, j = (at.right, n_cols) if l == 1 else (at.left, -(l // 2))
            start = cell(1 if k == 0 else 0, j)
            put(ring, base + (k != 1), get(wide, start, n_rows, step), 2)
            total = total + dot(get(ring, 0, at.ring_size).astype(bf16), up_w[k, l])
    put(ring, 0, jnp.zeros((at.ring_size, channels), f32))
    for base, message in ((at.top, upper), (at.bottom, lower)):
        put(ring, base + 1, message[at.row_skip : at.row_skip + cols, :])
        put(ring, base, corner(message, SKIP[0]))
        put(ring, base + cols + 1, corner(message, SKIP[2]))
    put(ring, at.left, left[at.skip : at.skip + rows, :])
    put(ring, at.right, right[at.skip : at.skip + rows, :])
    preact = total + get(ring, 0, at.ring_size)
    sigma = jax.nn.sigmoid(preact)
    value = preact * sigma
    slope = sigma + value * (1.0 - sigma)
    value = value.astype(bf16).astype(f32)
    ring_act[...] = value
    for base, exists in ((at.top, has_upper), (at.bottom, has_lower)):
        strip = value[base : base + cols + 2]
        ring_act[base : base + cols + 2, :] = jnp.where(exists, strip, 0.0)

    def fine(p, q):
        return (p + 2) * stride + MARGIN + q

    for row in range(rows):
        put(wide, fine(row, 0), cot[row].astype(f32))
    for row, message, start, which in (
        (-1, upper, at.row_cot, COT), (-2, upper, at.row_cot_2, COT_2), (rows, lower, at.row_cot, COT),
    ):
        put(wide, fine(row, 0), message[start : start + cols, :])
        for col, one in ((-1, which[0]), (-2, which[1]), (cols, which[2])):
            put(wide, fine(row, col), corner(message, one))
    put(wide, fine(0, -1), left[at.cot : at.cot + rows, :], stride)
    put(wide, fine(0, -2), left[at.cot_2 : at.cot_2 + rows, :], stride)
    put(wide, fine(0, cols), right[at.cot : at.cot + rows, :], stride)
    total = jnp.zeros((at.grad_size, channels), f32)
    for k in range(3):
        for l in range(3):
            put(ring, at.top, get(wide, fine(-k, -l), cols + 1))
            put(ring, at.grad_left, get(wide, fine(1 - k, -l), rows, stride))
            source = get(ring, 0, at.grad_size).astype(bf16)
            total = total + dot_nt(source, conv_w[k, l])
    strip = (total[: cols + 1] * slope[at.top : at.top + cols + 1]).astype(bf16).astype(f32)
    put(ring_grad, at.top, jnp.where(has_upper, strip, 0.0))
    strip = total[at.grad_left : at.grad_left + rows] * slope[at.left : at.left + rows]
    put(ring_grad, at.grad_left, strip.astype(bf16).astype(f32))


def decoded_kernel(act, ring_act, conv_w, decoded, padded, shifted):
    rows, cols, channels = act.shape
    at = Layout(rows // 2, cols // 2)
    stride = cols + 2 * MARGIN
    for row in range(rows):
        put(padded, (row + 1) * stride + MARGIN, act[row].astype(f32))
    for row, base in ((0, at.top), (rows + 1, at.bottom)):
        put(padded, row * stride + MARGIN - 1, ring_act[base : base + cols + 2, :])
    put(padded, stride + MARGIN - 1, ring_act[at.left : at.left + rows, :], stride)
    put(padded, stride + MARGIN + cols, ring_act[at.right : at.right + rows, :], stride)
    for row in range(rows + 2):
        for shift in range(3):
            start = row * stride + MARGIN - 1 + shift
            shifted[shift, row] = get(padded, start, cols).astype(bf16)
    total = jnp.zeros((rows * cols, channels), f32)
    for k in range(3):
        for l in range(3):
            source = shifted[l, pl.ds(k, rows)].reshape(-1, channels)
            total = total + dot(source, conv_w[k, l])
    decoded[...] = total.astype(bf16).reshape(decoded.shape)

def coarse_kernel(phases, ring_grad, up_w, coarse_out, padded, moved):
    n_rows, n_cols, channels = coarse_out.shape
    at = Layout(n_rows, n_cols)
    stride = n_cols + 2 * MARGIN
    for phase, start in ((0, 1), (1, 2), (2, 0)):
        moved[phase, 0] = get(ring_grad, at.top + start, n_cols, 2).astype(bf16)
    for phase in range(2):
        for row in range(n_rows):
            moved[phase, 1 + row] = phases[1, phase, row]
    for row_phase in range(2):
        for row in range(n_rows):
            put(padded, row * stride + MARGIN, phases[row_phase, 1, row].astype(f32))
        put(padded, MARGIN - 1, get(ring_grad, at.grad_left + row_phase, n_rows, 2), stride)
        for row in range(n_rows):
            cells = get(padded, row * stride + MARGIN - 1, n_cols).astype(bf16)
            if row_phase:
                moved[2, 1 + row] = cells
            else:
                moved[3, row] = cells
    total = jnp.zeros((n_rows * n_cols, channels), f32)
    for k in range(3):
        for l in range(3):
            if k == 1:
                if l == 0:
                    source = moved[3, pl.ds(0, n_rows)]
                else:
                    source = phases[0, l - 1, pl.ds(0, n_rows)]
            else:
                source = moved[(2, 0, 1)[l], pl.ds(k // 2, n_rows)]
            total = total + dot_nt(source.reshape(n_rows * n_cols, channels), up_w[k, l])
    coarse_out[...] = total.astype(bf16).reshape(coarse_out.shape)


def halving(count):
    bits = (count // 2).bit_length() - 1
    return [[(step + core) % bits for step in range(bits)] for core in range(2)]


def mask_of(slot, order):
    last = len(order) - 1
    return sum(1 << bit for step, bit in enumerate(order) if slot >> (last - step) & 1)


def edge_kernel(partial, got, edge, got_edge, own, message, extra):
    channels, block = partial.shape[1], got.shape[1]
    zero = jnp.zeros(edge.shape[1:], bf16)
    sides = (edge, got_edge)
    rows_t = jnp.concatenate([side[row] for side in sides for row in range(2)], axis=0).T

    def add_blocks(core):
        for tap in range(9):
            first = 2 + 4 * (2 - tap % 3)
            beside = []
            for side in sides:
                beside += [side[first + 3 - tap // 3], side[first] if tap >= 6 else zero]
            beside = jnp.concatenate(beside, axis=0)
            start = tap * channels
            for mine in range(start // block, -(-(start + channels) // block)):
                if mine % 2 == core:
                    low = max(start, mine * block)
                    high = min(start + channels, (mine + 1) * block)
                    extra[low:high, :] = dot(rows_t[low - start : high - start], beside)

    for core in range(2):
        pl.when(place_of()[0] == core)(lambda core=core: add_blocks(core))
    core_kernel(partial, extra, got, own, message)


def core_kernel(*refs):
    *terms, got, own, message = refs
    slots, half, block = got.shape[0], own.shape[0], got.shape[1]
    core, chip, _, _ = place_of()
    even, odd = halving(2 * slots)
    for slot in range(slots):
        target = chip ^ jnp.where(core == 0, mask_of(slot, even), mask_of(slot, odd))
        mine = pl.multiple_of((2 * target + core) * block, 16)
        total = sum(term[pl.ds(mine, block), :] for term in terms) + got[target].astype(f32)
        if slot < half:
            own[slot] = total
        else:
            message[slot - half] = total.astype(bf16)


def plane_kernel(before, got, own, message):
    half = own.shape[0]
    for slot in range(2 * half):
        total = before[slot] + got[slot].astype(f32)
        if slot < half:
            own[slot] = total
        else:
            message[slot - half] = total.astype(bf16)


def band_kernel(conv, got_conv, up, got_up, own, *refs):
    n_bands, messages, cut = len(refs), refs[:-1], refs[-1]
    conv_total = conv[0] + got_conv[0].astype(f32)
    up_total = up[0] + got_up[0].astype(f32)
    cols = conv_total.shape[1] // n_bands
    for band in range(n_bands):
        cut[band, :, :cols] = conv_total[:, band * cols : (band + 1) * cols]
        cut[band, :, cols:] = up_total[:, band * cols : (band + 1) * cols]
    band = place_of()[2]
    own[...] = cut[band]
    for k, message in enumerate(messages):
        message[...] = cut[band ^ (k + 1)].astype(bf16)


def last_kernel(own, *refs):
    peers, (conv, up) = refs[:-2], refs[-2:]
    total = own[...]
    for peer in peers:
        total = total + peer[...].astype(f32)
    turned = total.T
    conv[...] = turned[: conv.shape[0]]
    up[...] = turned[conv.shape[0] :]


def xor_pairs(count, bits):
    return [(i, i ^ bits) for i in range(count)]


def core_swap(send):
    return lax.ppermute(send, "face", xor_pairs(lax.axis_size("face"), 1))


def core_sum(body, scratch, partial, got, *rest):
    groups, block, channels = got.shape
    shape = (groups // 2, block, channels)
    outs = [sds(shape, f32), sds(shape, bf16)]
    return kernel_call(body, outs, scratch, 0, partial, got, *rest)


def plane_swap(message, step):
    faces = lax.axis_size("face")
    orders = halving(faces)
    return lax.ppermute(message, "face", [(i, i ^ 2 << orders[i % 2][step]) for i in range(faces)])


def plane_sum(own, got):
    half, block, channels = own.shape
    shape = (half // 2, block, channels)
    return kernel_call(plane_kernel, [sds(shape, f32), sds(shape, bf16)], [], 0, own, got)


def band_sum(conv, got_conv, up, got_up):
    bands = lax.axis_size("band")
    _, block, channels = conv.shape
    cols = channels // bands
    shape = (block, 2 * cols)
    own, *messages = kernel_call(
        band_kernel, [sds(shape, f32)] + [sds(shape, bf16)] * (bands - 1),
        [pltpu.VMEM((bands,) + shape, f32)], 0, conv, got_conv, up, got_up,
    )
    got = [
        lax.ppermute(messages[k - 1], "band", xor_pairs(bands, k))
        for k in (3, 2, 1)
    ]
    return [a.T for a in kernel_call(last_kernel, [sds((cols, block), f32)] * 2, [], 0, own, *got)]


def after(value, *others):
    return lax.optimization_barrier((value, *others))[0]


def swap(first, second, axis, wrap):
    one, two = pairs(lax.axis_size(axis), wrap)
    return lax.ppermute(first, axis, one), lax.ppermute(second, axis, two)


def local(coarse, skip, up_weight, conv_weight, cotangent):
    n_rows, n_cols, channels = coarse.shape
    rows, cols, _ = skip.shape
    at = Layout(n_rows, n_cols)
    faces = lax.axis_size("face")
    groups, block = faces // 2, 9 * channels // faces

    flat = halves(rows * cols, channels)
    message = sds((at.face_size, channels), bf16)
    edges = pltpu.VMEM(message.shape, f32)
    first, second, cotangent, skip, coarse = kernel_call(
        face_message,
        [message, message, sds(cotangent.shape, bf16), sds(skip.shape, bf16), sds(coarse.shape, bf16)],
        [flat, edges, edges, pltpu.SemaphoreType.DMA((3,))],
        0, coarse, skip, cotangent, far=(0, 1, 2),
    )
    first, second = swap(first, second, "face", True)
    conv_weight, grad_centre = kernel_call(
        early_kernel,
        [sds(conv_weight.shape, bf16), sds((rows * cols, channels), f32)],
        [pltpu.VMEM((rows + 2, cols, channels), bf16), pltpu.SemaphoreType.DMA],
        0, cotangent, conv_weight, far=(1,),
    )
    side = sds(message.shape, f32)
    message = sds((at.band_size, channels), bf16)
    edges = pltpu.VMEM(message.shape, f32)
    first, second, left, right = kernel_call(
        band_message, [message, message, side, side], [edges, edges],
        0, coarse, skip, after(cotangent, grad_centre), first, second,
    )
    first, second = swap(first, second, "band", False)

    cells = n_rows * n_cols
    stride = cols + 2 * MARGIN
    padded = halves((rows + 2) * stride, channels)
    shift_shape = (3, rows + 2, cols, channels)
    whole = -(-cells // 256) * 256 // n_cols
    part = sds((9 * channels, channels), f32)
    send = sds((groups, block, channels), bf16)
    blocks = [
        sds(shift_shape, bf16), sds((2, whole + 1, n_cols, channels), bf16),
        sds(skip.shape, bf16), sds((rows * cols, channels), f32), part,
    ]
    *inner, part_conv, send_conv, last_pre, grad_act = kernel_call(
        inner_kernel,
        [
            *blocks, send, sds((cols, channels), f32), sds((rows * cols, channels), f32),
        ],
        [halves(rows * stride, channels), flat],
        0, coarse, skip, cotangent, left, right, up_weight, conv_weight, grad_centre,
    )
    side = sds(message.shape, f32)
    got_conv = core_swap(send_conv)
    edge = sds((14, cols, channels), bf16)
    shifted, near, act, slope, edge, upper, lower = kernel_call(
        act_kernel, [*blocks[:-1], edge, side, side],
        [halves(stride, channels), halves(cols, channels)],
        10**11, first, second, right, up_weight, last_pre, *inner, changed={5 + i: i for i in range(4)},
    )
    phases = kernel_call(
        grad_kernel, [sds((2, 2, whole, n_cols, channels), bf16)], [flat],
        0, shifted, slope, grad_act, conv_weight,
    )[0]
    part_up, send_up = kernel_call(up_kernel, [part, send], [], 0, near, phases)
    own_conv, to_conv = core_sum(
        edge_kernel, [pltpu.VMEM(part.shape, f32)], after(part_conv, send_up), got_conv, edge, core_swap(edge)
    )
    got_conv = plane_swap(to_conv, 0)
    own_up, to_up = core_sum(core_kernel, [], part_up, core_swap(after(send_up, to_conv)))
    got_up = plane_swap(to_up, 0)
    ring_act, ring_grad = kernel_call(
        ring_kernel,
        [
            sds((at.ring_size, channels), f32),
            sds((channels // LANES, at.grad_size, LANES), f32),
        ],
        [halves(at.ring_size, channels), halves((rows + 3) * stride, channels)],
        0, coarse, cotangent, after(left, to_up), right, upper, lower, conv_weight, up_weight,
    )
    own_conv = after(own_conv, ring_act)
    steps = (faces // 2).bit_length() - 1
    for step in range(1, steps):
        own_conv, to_conv = plane_sum(own_conv, got_conv)
        got_conv = plane_swap(to_conv, step)
        if step == 1:
            decoded = kernel_call(
                decoded_kernel, [sds(skip.shape, bf16)], [padded, pltpu.VMEM(shift_shape, bf16)],
                0, act, after(ring_act, to_conv), conv_weight,
            )[0]
            own_up = after(own_up, decoded)
        own_up, to_up = plane_sum(own_up, got_up)
        got_up = plane_swap(to_up, step)
        if step == 1:
            grad_coarse = kernel_call(
                coarse_kernel, [sds(coarse.shape, bf16)],
                [
                    halves(n_rows * (n_cols + 2 * MARGIN), channels),
                    pltpu.VMEM((4, n_rows + 1, n_cols, channels), bf16),
                ],
                0, phases, after(ring_grad, to_up), up_weight,
            )[0]
            own_up = after(own_up, grad_coarse)
    grad_conv, grad_up = band_sum(own_conv, got_conv, own_up, got_up)
    return (decoded, grad_coarse, grad_up, grad_conv)


def solution(mesh):
    return jax.shard_map(
        local,
        mesh=mesh,
        in_specs=(
            P("band", "face", None),
            P("band", "face", None),
            P(),
            P(),
            P("band", "face", None),
        ),
        out_specs=(
            P("band", "face", None),
            P("band", "face", None),
            P("face", "band"),
            P("face", "band"),
        ),
        check_vma=False,
    )
```

```python
import jax
import jax.numpy as jnp
from jax import lax
from jax.experimental import pallas as pl
from jax.experimental.pallas import tpu as pltpu
from jax.sharding import PartitionSpec as P

f32, bf16 = jnp.float32, jnp.bfloat16
forward_taps = ((1, 1), (0, 0), (1, 0))
backward_taps = ((1, 0), (0, 1), (1, 1))
MARGIN = 8
LANES = 128


def sds(shape, dtype):
    return jax.ShapeDtypeStruct(shape, dtype)


def kernel_call(body, outs, scratch, flops, *args, far=(), changed=None):
    vmem = pl.BlockSpec(memory_space=pltpu.VMEM)
    hbm = pl.BlockSpec(memory_space=pltpu.HBM)
    moved = sum(a.size * a.dtype.itemsize for a in args)
    moved += sum(a.size * a.dtype.itemsize for a in outs)
    args = [
        pltpu.with_memory_space_constraint(a, pltpu.HBM) if i in far else a
        for i, a in enumerate(args)
    ]
    return pl.pallas_call(
        body,
        out_shape=tuple(outs),
        in_specs=[hbm if i in far else vmem for i in range(len(args))],
        out_specs=tuple(vmem for _ in outs),
        scratch_shapes=scratch,
        input_output_aliases=changed or {},
        compiler_params=pltpu.CompilerParams(vmem_limit_bytes=28 * 2**20),
        cost_estimate=pl.CostEstimate(flops=flops, bytes_accessed=moved, transcendentals=0),
    )(*args)


def place_of():
    face = lax.axis_index("face")
    return lax.rem(face, 2), lax.div(face, 2), lax.axis_index("band"), lax.axis_size("band")


def dot(a, b):
    return jnp.dot(a, b, preferred_element_type=f32)


def dot_nt(a, b):
    return lax.dot_general(a, b, (((1,), (1,)), ((), ())), preferred_element_type=f32)


def pairs(count, wrap):
    first = [(i, i ^ 1) for i in range(count)]
    second = []
    for i in range(count):
        j = i + 1 if i % 2 else i - 1
        if wrap or 0 <= j < count:
            second.append((i, j % count))
    return first, second


def up16(n):
    return (n + 15) // 16 * 16


def halves(n_rows, channels):
    return pltpu.VMEM((channels // LANES, n_rows, LANES), f32)


def put(ref, start, value, step=1):
    for part in range(ref.shape[0]):
        rows = pl.ds(start, value.shape[0], stride=step if step > 1 else None)
        ref[part, rows, :] = value[:, part * LANES : (part + 1) * LANES]


def get(ref, start, count, step=1):
    rows = pl.ds(start, count, stride=step if step > 1 else None)
    return jnp.concatenate([ref[part, rows, :] for part in range(ref.shape[0])], axis=1)


def fill(ref, start, value):
    ref[start : start + value.shape[0], :] = value


def other_core(send, *terms):
    core = place_of()[0]
    groups, block, _ = send.shape
    for group in range(groups):
        theirs = pl.multiple_of((2 * group + 1 - core) * block, 16)
        send[group] = sum(term[pl.ds(theirs, block), :] for term in terms).astype(bf16)


class Layout:
    def __init__(self, n_rows, n_cols):
        rows, cols = 2 * n_rows, 2 * n_cols
        self.cot, self.cot_2, self.skip, self.coarse = 0, rows, 2 * rows, 3 * rows
        self.face_size = up16(3 * rows + n_rows)
        self.row_cot, self.row_cot_2, self.row_skip = 0, cols, 2 * cols
        self.row_coarse, self.corner = 3 * cols, 3 * cols + n_cols
        self.band_size = self.corner + 16
        ring = (cols + 2 + 7) // 8 * 8
        self.top, self.bottom, self.left, self.right = 0, ring, 2 * ring, 2 * ring + rows
        self.ring_size = up16(2 * ring + 2 * rows)
        self.grad_left, self.grad_size = ring, up16(ring + rows)


COT, COT_2, SKIP, COARSE = (0, 1, 2), (3, 4, 5), (6, None, 7), (8, None, 9)


def face_message(coarse, skip, cot, first, second, cot_v, skip_v, coarse_v, flat, before, after, sems):
    rows, cols, _ = cot.shape
    n_rows, n_cols, _ = coarse.shape
    at = Layout(n_rows, n_cols)
    copies = [
        pltpu.make_async_copy(source, target, sems.at[i])
        for i, (source, target) in enumerate(((cot, cot_v), (skip, skip_v), (coarse, coarse_v)))
    ]
    for copy in copies:
        copy.start()
    before[...] = jnp.zeros_like(before)
    after[...] = jnp.zeros_like(after)
    for copy, array, start, start_2 in (
        (copies[0], cot_v, at.cot, at.cot_2), (copies[1], skip_v, at.skip, None), (copies[2], coarse_v, at.coarse, None),
    ):
        copy.wait()
        n, width, channels = array.shape
        put(flat, 0, array[:, :16, :].astype(f32)[:, :8, :].reshape(n * 8, channels))
        put(flat, n * 8, array[:, width - 16 :, :].astype(f32)[:, 8:, :].reshape(n * 8, channels))
        fill(before, start, get(flat, 0, n, 8))
        fill(after, start, get(flat, n * 8 + 7, n, 8))
        if start_2 is not None:
            fill(after, start_2, get(flat, n * 8 + 6, n, 8))
    even = place_of()[0] == 0
    first[...] = jnp.where(even, after[...], before[...]).astype(bf16)
    second[...] = jnp.where(even, before[...], after[...]).astype(bf16)


def band_message(coarse, skip, cot, got_first, got_second, first, second, left, right, before, after):
    rows, cols, channels = cot.shape
    n_rows, n_cols, _ = coarse.shape
    at = Layout(n_rows, n_cols)
    even = place_of()[0] == 0
    one, two = got_first[...].astype(f32), got_second[...].astype(f32)
    left[...] = jnp.where(even, two, one)
    right[...] = jnp.where(even, one, two)
    for message, row, row_2, cell in ((before, 0, None, 0), (after, rows - 1, rows - 2, n_rows - 1)):
        fill(message, at.row_cot, cot[row].astype(f32))
        if row_2 is None:
            fill(message, at.row_cot_2, jnp.zeros((cols, channels), f32))
        else:
            fill(message, at.row_cot_2, cot[row_2].astype(f32))
        fill(message, at.row_skip, skip[row].astype(f32))
        fill(message, at.row_coarse, coarse[cell].astype(f32))
        fill(message, at.corner, jnp.zeros((16, channels), f32))
        corners = [
            (COT[0], left, at.cot + row), (COT[1], left, at.cot_2 + row), (COT[2], right, at.cot + row),
            (SKIP[0], left, at.skip + row), (SKIP[2], right, at.skip + row),
            (COARSE[0], left, at.coarse + cell), (COARSE[2], right, at.coarse + cell),
        ]
        if row_2 is not None:
            corners += [
                (COT_2[0], left, at.cot + row_2), (COT_2[1], left, at.cot_2 + row_2),
                (COT_2[2], right, at.cot + row_2),
            ]
        for corner, side, source in corners:
            fill(message, at.corner + corner, side[source : source + 1, :])
    even = lax.rem(place_of()[2], 2) == 0
    first[...] = jnp.where(even, after[...], before[...]).astype(bf16)
    second[...] = jnp.where(even, before[...], after[...]).astype(bf16)


def early_kernel(cot, conv_w, conv_v, grad_act, centre, sem):
    rows, cols, channels = cot.shape
    copy = pltpu.make_async_copy(conv_w, conv_v, sem)
    copy.start()
    for row in (0, rows + 1):
        centre[row] = jnp.zeros((cols, channels), bf16)
    centre[pl.ds(1, rows)] = cot[...]
    copy.wait()
    total = jnp.zeros((rows * cols, channels), f32)
    for k in range(3):
        source = centre[pl.ds(2 - k, rows)].reshape(-1, channels)
        total = total + dot_nt(source, conv_v[k, 1])
    grad_act[...] = total


def inner_kernel(
    coarse, skip, cot, left, right, up_w, conv_w, grad_centre,
    shifted, near, act, slope, partial, send, last_pre, grad_act, padded, pre,
):
    n_rows, n_cols, channels = coarse.shape
    rows, cols, _ = skip.shape
    at = Layout(n_rows, n_cols)
    stride = cols + 2 * MARGIN
    for row in range(n_rows):
        near[0, row] = coarse[row]
        put(padded, row * stride, coarse[row].astype(f32))
    put(padded, n_cols, right[at.coarse : at.coarse + n_rows, :], stride)
    for row in range(n_rows):
        near[1, row] = get(padded, row * stride + 1, n_cols).astype(bf16)
    for row in range(n_rows, near.shape[1]):
        for side in range(2):
            near[side, row] = jnp.zeros((n_cols, channels), bf16)
    sums = {}
    for k in range(3):
        row_phase, row_off = forward_taps[k]
        for l in range(3):
            col_phase, col_off = forward_taps[l]
            source = near[col_off, pl.ds(row_off, n_rows)].reshape(n_rows * n_cols, channels)
            term = dot(source, up_w[k, l])
            name = (row_phase, col_phase)
            sums[name] = sums[name] + term if name in sums else term
    for (row_phase, col_phase), total in sums.items():
        for row in range(n_rows):
            start = (2 * row + row_phase) * cols + col_phase
            put(pre, start, total[row * n_cols : (row + 1) * n_cols], 2)
    for row in range(rows):
        put(padded, row * stride + MARGIN, cot[row].astype(f32))
    put(padded, MARGIN - 1, left[at.cot : at.cot + rows, :], stride)
    put(padded, MARGIN + cols, right[at.cot : at.cot + rows, :], stride)
    for row in range(rows):
        for shift in (0, 2):
            start = row * stride + MARGIN - 1 + shift
            shifted[shift, row + 1] = get(padded, start, cols).astype(bf16)
        shifted[1, row + 1] = cot[row]
    for shift in range(3):
        shifted[shift, 0] = jnp.zeros((cols, channels), bf16)
        shifted[shift, rows + 1] = jnp.zeros((cols, channels), bf16)
    preact = get(pre, 0, rows * cols) + skip[...].reshape(rows * cols, channels).astype(f32)
    last_pre[...] = preact[(rows - 1) * cols :]
    sigma = jax.nn.sigmoid(preact)
    value = preact * sigma
    slope[...] = sigma + value * (1.0 - sigma)
    row_of = lax.broadcasted_iota(jnp.int32, value.shape, 0)
    act_flat = jnp.where(row_of < (rows - 1) * cols, value, 0.0).astype(bf16)
    act[...] = act_flat.reshape(act.shape)
    act_t = act_flat.T
    for k in range(3):
        for l in range(3):
            source = shifted[2 - l, pl.ds(2 - k, rows)].reshape(-1, channels)
            partial[pl.ds((3 * k + l) * channels, channels), :] = dot(act_t, source)
    other_core(send, partial)
    total = grad_centre[...]
    for k in range(3):
        source = shifted[0, pl.ds(2 - k, rows)].reshape(-1, channels)
        total = total + dot_nt(source, conv_w[k, 2])
    grad_act[...] = total


def act_kernel(
    got_first, got_second, right, up_w, last_pre, shifted_in, near_in, act_in, slope_in,
    shifted, near, act, slope, edge, upper, lower, padded, pre,
):
    rows, cols, channels = act.shape
    n_rows, n_cols = rows // 2, cols // 2
    at = Layout(n_rows, n_cols)
    even = lax.rem(place_of()[2], 2) == 0
    one, two = got_first[...].astype(f32), got_second[...].astype(f32)
    upper[...] = jnp.where(even, two, one)
    lower[...] = jnp.where(even, one, two)
    below = lower[at.row_coarse : at.row_coarse + n_cols, :]
    corner = at.corner + COARSE[2]
    put(padded, 0, below)
    put(padded, n_cols, lower[corner : corner + 1, :])
    cells = [below.astype(bf16), get(padded, 1, n_cols).astype(bf16)]
    near[0, n_rows] = cells[0]
    near[1, n_rows] = cells[1]
    put(pre, 0, dot(cells[0], up_w[0, 1]), 2)
    put(pre, 1, dot(cells[1], up_w[0, 0]) + dot(cells[0], up_w[0, 2]), 2)
    preact = last_pre[...] + get(pre, 0, cols)
    sigma = jax.nn.sigmoid(preact)
    value = preact * sigma
    slope[(rows - 1) * cols :, :] = sigma + value * (1.0 - sigma)
    last = value.astype(bf16)
    act[rows - 1] = last
    for row, message in ((0, upper), (rows + 1, lower)):
        centre = message[at.row_cot : at.row_cot + cols, :]
        put(padded, MARGIN, centre)
        for col, one in ((-1, COT[0]), (cols, COT[2])):
            put(padded, MARGIN + col, message[at.corner + one : at.corner + one + 1, :])
        shifted[0, row] = get(padded, MARGIN - 1, cols).astype(bf16)
        shifted[1, row] = centre.astype(bf16)
        shifted[2, row] = get(padded, MARGIN + 1, cols).astype(bf16)
    edge[0] = last
    edge[1] = act_in[0]
    for shift in range(3):
        for place, row in enumerate((0, rows - 1, rows, rows + 1)):
            edge[2 + 4 * shift + place] = shifted[shift, row]


def grad_kernel(shifted, slope, grad_act, conv_w, phases, fine):
    rows, cols = shifted.shape[1] - 2, shifted.shape[2]
    channels = shifted.shape[3]
    n_rows, n_cols = rows // 2, cols // 2
    cells = rows * cols
    total = grad_act[...]
    for k in range(3):
        source = shifted[2, pl.ds(2 - k, rows)].reshape(cells, channels)
        total = total + dot_nt(source, conv_w[k, 0])
    first = jnp.zeros((cols, channels), f32)
    last = jnp.zeros((cols, channels), f32)
    for l in (1, 2):
        first = first + dot_nt(shifted[2 - l, 0], conv_w[2, l])
        last = last + dot_nt(shifted[2 - l, rows + 1], conv_w[0, l])
    put(fine, 0, (total * slope[...]).astype(bf16).astype(f32))
    put(fine, 0, ((total[:cols] + first) * slope[:cols, :]).astype(bf16).astype(f32))
    edge = (total[cells - cols :] + last) * slope[cells - cols :, :]
    put(fine, cells - cols, edge.astype(bf16).astype(f32))
    whole = phases.shape[2]
    for row_phase in range(2):
        for col_phase in range(2):
            for row in range(n_rows):
                start = (2 * row + row_phase) * cols + col_phase
                phases[row_phase, col_phase, row] = get(fine, start, n_cols, 2).astype(bf16)
            for row in range(n_rows, whole):
                phases[row_phase, col_phase, row] = jnp.zeros((n_cols, channels), bf16)


def up_kernel(near, phases, partial, send):
    _, _, whole, n_cols, channels = phases.shape
    turned = {}
    for row_off in range(2):
        for col_off in range(2):
            cells = near[col_off, pl.ds(row_off, whole)]
            turned[row_off, col_off] = cells.reshape(whole * n_cols, channels).T
    for k in range(3):
        row_phase, row_off = forward_taps[k]
        for l in range(3):
            col_phase, col_off = forward_taps[l]
            source = phases[row_phase, col_phase].reshape(whole * n_cols, channels)
            partial[pl.ds((3 * k + l) * channels, channels), :] = dot(
                turned[row_off, col_off], source
            )
    other_core(send, partial)


def ring_kernel(
    coarse, cot, left, right, upper, lower, conv_w, up_w, ring_act, ring_grad, ring, wide,
):
    rows, cols, channels = cot.shape
    n_rows, n_cols = rows // 2, cols // 2
    at = Layout(n_rows, n_cols)
    stride, step = cols + 2 * MARGIN, n_cols + 2 * MARGIN
    _, _, band, n_bands = place_of()
    has_upper, has_lower = band > 0, band < n_bands - 1

    def corner(message, which):
        return message[at.corner + which : at.corner + which + 1, :]

    def cell(i, j):
        return (i + 1) * step + MARGIN + j

    for row in range(n_rows):
        put(wide, cell(row, 0), coarse[row].astype(f32))
    for row, message in ((-1, upper), (n_rows, lower)):
        put(wide, cell(row, 0), message[at.row_coarse : at.row_coarse + n_cols, :])
        put(wide, cell(row, -1), corner(message, COARSE[0]))
        put(wide, cell(row, n_cols), corner(message, COARSE[2]))
    put(wide, cell(0, -1), left[at.coarse : at.coarse + n_rows, :], step)
    put(wide, cell(0, n_cols), right[at.coarse : at.coarse + n_rows, :], step)
    total = jnp.zeros((at.ring_size, channels), f32)
    for k in range(3):
        for l in range(3):
            put(ring, 0, jnp.zeros((at.ring_size, channels), f32))
            for base, i in ((at.bottom, n_rows),) if k == 1 else ((at.top, k // 2 * -1),):
                start = cell(i, -1 if l == 2 else 0)
                put(ring, base + (l == 1), get(wide, start, n_cols + 1), 2)
            base, j = (at.right, n_cols) if l == 1 else (at.left, -(l // 2))
            start = cell(1 if k == 0 else 0, j)
            put(ring, base + (k != 1), get(wide, start, n_rows, step), 2)
            total = total + dot(get(ring, 0, at.ring_size).astype(bf16), up_w[k, l])
    put(ring, 0, jnp.zeros((at.ring_size, channels), f32))
    for base, message in ((at.top, upper), (at.bottom, lower)):
        put(ring, base + 1, message[at.row_skip : at.row_skip + cols, :])
        put(ring, base, corner(message, SKIP[0]))
        put(ring, base + cols + 1, corner(message, SKIP[2]))
    put(ring, at.left, left[at.skip : at.skip + rows, :])
    put(ring, at.right, right[at.skip : at.skip + rows, :])
    preact = total + get(ring, 0, at.ring_size)
    sigma = jax.nn.sigmoid(preact)
    value = preact * sigma
    slope = sigma + value * (1.0 - sigma)
    value = value.astype(bf16).astype(f32)
    ring_act[...] = value
    for base, exists in ((at.top, has_upper), (at.bottom, has_lower)):
        strip = value[base : base + cols + 2]
        ring_act[base : base + cols + 2, :] = jnp.where(exists, strip, 0.0)

    def fine(p, q):
        return (p + 2) * stride + MARGIN + q

    for row in range(rows):
        put(wide, fine(row, 0), cot[row].astype(f32))
    for row, message, start, which in (
        (-1, upper, at.row_cot, COT), (-2, upper, at.row_cot_2, COT_2), (rows, lower, at.row_cot, COT),
    ):
        put(wide, fine(row, 0), message[start : start + cols, :])
        for col, one in ((-1, which[0]), (-2, which[1]), (cols, which[2])):
            put(wide, fine(row, col), corner(message, one))
    put(wide, fine(0, -1), left[at.cot : at.cot + rows, :], stride)
    put(wide, fine(0, -2), left[at.cot_2 : at.cot_2 + rows, :], stride)
    put(wide, fine(0, cols), right[at.cot : at.cot + rows, :], stride)
    total = jnp.zeros((at.grad_size, channels), f32)
    for k in range(3):
        for l in range(3):
            put(ring, at.top, get(wide, fine(-k, -l), cols + 1))
            put(ring, at.grad_left, get(wide, fine(1 - k, -l), rows, stride))
            source = get(ring, 0, at.grad_size).astype(bf16)
            total = total + dot_nt(source, conv_w[k, l])
    strip = (total[: cols + 1] * slope[at.top : at.top + cols + 1]).astype(bf16).astype(f32)
    put(ring_grad, at.top, jnp.where(has_upper, strip, 0.0))
    strip = total[at.grad_left : at.grad_left + rows] * slope[at.left : at.left + rows]
    put(ring_grad, at.grad_left, strip.astype(bf16).astype(f32))


def decoded_kernel(act, ring_act, conv_w, decoded, padded, shifted):
    rows, cols, channels = act.shape
    at = Layout(rows // 2, cols // 2)
    stride = cols + 2 * MARGIN
    for row in range(rows):
        put(padded, (row + 1) * stride + MARGIN, act[row].astype(f32))
    for row, base in ((0, at.top), (rows + 1, at.bottom)):
        put(padded, row * stride + MARGIN - 1, ring_act[base : base + cols + 2, :])
    put(padded, stride + MARGIN - 1, ring_act[at.left : at.left + rows, :], stride)
    put(padded, stride + MARGIN + cols, ring_act[at.right : at.right + rows, :], stride)
    for row in range(rows + 2):
        for shift in range(3):
            start = row * stride + MARGIN - 1 + shift
            shifted[shift, row] = get(padded, start, cols).astype(bf16)
    total = jnp.zeros((rows * cols, channels), f32)
    for k in range(3):
        for l in range(3):
            source = shifted[l, pl.ds(k, rows)].reshape(-1, channels)
            total = total + dot(source, conv_w[k, l])
    decoded[...] = total.astype(bf16).reshape(decoded.shape)

def coarse_kernel(phases, ring_grad, up_w, coarse_out, padded, moved):
    n_rows, n_cols, channels = coarse_out.shape
    at = Layout(n_rows, n_cols)
    stride = n_cols + 2 * MARGIN
    for phase, start in ((0, 1), (1, 2), (2, 0)):
        moved[phase, 0] = get(ring_grad, at.top + start, n_cols, 2).astype(bf16)
    for phase in range(2):
        for row in range(n_rows):
            moved[phase, 1 + row] = phases[1, phase, row]
    for row_phase in range(2):
        for row in range(n_rows):
            put(padded, row * stride + MARGIN, phases[row_phase, 1, row].astype(f32))
        put(padded, MARGIN - 1, get(ring_grad, at.grad_left + row_phase, n_rows, 2), stride)
        for row in range(n_rows):
            cells = get(padded, row * stride + MARGIN - 1, n_cols).astype(bf16)
            if row_phase:
                moved[2, 1 + row] = cells
            else:
                moved[3, row] = cells
    total = jnp.zeros((n_rows * n_cols, channels), f32)
    for k in range(3):
        for l in range(3):
            if k == 1:
                if l == 0:
                    source = moved[3, pl.ds(0, n_rows)]
                else:
                    source = phases[0, l - 1, pl.ds(0, n_rows)]
            else:
                source = moved[(2, 0, 1)[l], pl.ds(k // 2, n_rows)]
            total = total + dot_nt(source.reshape(n_rows * n_cols, channels), up_w[k, l])
    coarse_out[...] = total.astype(bf16).reshape(coarse_out.shape)


def halving(count):
    bits = (count // 2).bit_length() - 1
    return [[(step + core) % bits for step in range(bits)] for core in range(2)]


def mask_of(slot, order):
    last = len(order) - 1
    return sum(1 << bit for step, bit in enumerate(order) if slot >> (last - step) & 1)


def edge_kernel(partial, got, edge, got_edge, own, message, extra):
    channels, block = partial.shape[1], got.shape[1]
    zero = jnp.zeros(edge.shape[1:], bf16)
    sides = (edge, got_edge)
    rows_t = jnp.concatenate([side[row] for side in sides for row in range(2)], axis=0).T

    def add_blocks(core):
        for tap in range(9):
            first = 2 + 4 * (2 - tap % 3)
            beside = []
            for side in sides:
                beside += [side[first + 3 - tap // 3], side[first] if tap >= 6 else zero]
            beside = jnp.concatenate(beside, axis=0)
            start = tap * channels
            for mine in range(start // block, -(-(start + channels) // block)):
                if mine % 2 == core:
                    low = max(start, mine * block)
                    high = min(start + channels, (mine + 1) * block)
                    extra[low:high, :] = dot(rows_t[low - start : high - start], beside)

    for core in range(2):
        pl.when(place_of()[0] == core)(lambda core=core: add_blocks(core))
    core_kernel(partial, extra, got, own, message)


def core_kernel(*refs):
    *terms, got, own, message = refs
    slots, half, block = got.shape[0], own.shape[0], got.shape[1]
    core, chip, _, _ = place_of()
    even, odd = halving(2 * slots)
    for slot in range(slots):
        target = chip ^ jnp.where(core == 0, mask_of(slot, even), mask_of(slot, odd))
        mine = pl.multiple_of((2 * target + core) * block, 16)
        total = sum(term[pl.ds(mine, block), :] for term in terms) + got[target].astype(f32)
        if slot < half:
            own[slot] = total
        else:
            message[slot - half] = total.astype(bf16)


def plane_kernel(before, got, own, message):
    half = own.shape[0]
    for slot in range(2 * half):
        total = before[slot] + got[slot].astype(f32)
        if slot < half:
            own[slot] = total
        else:
            message[slot - half] = total.astype(bf16)


def band_kernel(conv, got_conv, up, got_up, own, *refs):
    n_bands, messages, cut = len(refs), refs[:-1], refs[-1]
    conv_total = conv[0] + got_conv[0].astype(f32)
    up_total = up[0] + got_up[0].astype(f32)
    cols = conv_total.shape[1] // n_bands
    for band in range(n_bands):
        cut[band, :, :cols] = conv_total[:, band * cols : (band + 1) * cols]
        cut[band, :, cols:] = up_total[:, band * cols : (band + 1) * cols]
    band = place_of()[2]
    own[...] = cut[band]
    for k, message in enumerate(messages):
        message[...] = cut[band ^ (k + 1)].astype(bf16)


def last_kernel(own, *refs):
    peers, (conv, up) = refs[:-2], refs[-2:]
    total = own[...]
    for peer in peers:
        total = total + peer[...].astype(f32)
    turned = total.T
    conv[...] = turned[: conv.shape[0]]
    up[...] = turned[conv.shape[0] :]


def xor_pairs(count, bits):
    return [(i, i ^ bits) for i in range(count)]


def core_swap(send):
    return lax.ppermute(send, "face", xor_pairs(lax.axis_size("face"), 1))


def core_sum(body, scratch, partial, got, *rest):
    groups, block, channels = got.shape
    shape = (groups // 2, block, channels)
    outs = [sds(shape, f32), sds(shape, bf16)]
    cost = 10**11 if rest else 0
    return kernel_call(body, outs, scratch, cost, partial, got, *rest)


def plane_swap(message, step):
    faces = lax.axis_size("face")
    orders = halving(faces)
    return lax.ppermute(message, "face", [(i, i ^ 2 << orders[i % 2][step]) for i in range(faces)])


def plane_sum(own, got):
    half, block, channels = own.shape
    shape = (half // 2, block, channels)
    return kernel_call(plane_kernel, [sds(shape, f32), sds(shape, bf16)], [], 0, own, got)


def band_sum(conv, got_conv, up, got_up):
    bands = lax.axis_size("band")
    _, block, channels = conv.shape
    cols = channels // bands
    shape = (block, 2 * cols)
    own, *messages = kernel_call(
        band_kernel, [sds(shape, f32)] + [sds(shape, bf16)] * (bands - 1),
        [pltpu.VMEM((bands,) + shape, f32)], 0, conv, got_conv, up, got_up,
    )
    got = [
        lax.ppermute(messages[k - 1], "band", xor_pairs(bands, k))
        for k in (3, 2, 1)
    ]
    return [a.T for a in kernel_call(last_kernel, [sds((cols, block), f32)] * 2, [], 0, own, *got)]


def after(value, *others):
    return lax.optimization_barrier((value, *others))[0]


def swap(first, second, axis, wrap):
    one, two = pairs(lax.axis_size(axis), wrap)
    return lax.ppermute(first, axis, one), lax.ppermute(second, axis, two)


def local(coarse, skip, up_weight, conv_weight, cotangent):
    n_rows, n_cols, channels = coarse.shape
    rows, cols, _ = skip.shape
    at = Layout(n_rows, n_cols)
    faces = lax.axis_size("face")
    groups, block = faces // 2, 9 * channels // faces

    flat = halves(rows * cols, channels)
    message = sds((at.face_size, channels), bf16)
    edges = pltpu.VMEM(message.shape, f32)
    first, second, cotangent, skip, coarse = kernel_call(
        face_message,
        [message, message, sds(cotangent.shape, bf16), sds(skip.shape, bf16), sds(coarse.shape, bf16)],
        [flat, edges, edges, pltpu.SemaphoreType.DMA((3,))],
        0, coarse, skip, cotangent, far=(0, 1, 2),
    )
    first, second = swap(first, second, "face", True)
    conv_weight, grad_centre = kernel_call(
        early_kernel,
        [sds(conv_weight.shape, bf16), sds((rows * cols, channels), f32)],
        [pltpu.VMEM((rows + 2, cols, channels), bf16), pltpu.SemaphoreType.DMA],
        0, cotangent, conv_weight, far=(1,),
    )
    side = sds(message.shape, f32)
    message = sds((at.band_size, channels), bf16)
    edges = pltpu.VMEM(message.shape, f32)
    first, second, left, right = kernel_call(
        band_message, [message, message, side, side], [edges, edges],
        0, coarse, skip, after(cotangent, grad_centre), first, second,
    )
    first, second = swap(first, second, "band", False)

    cells = n_rows * n_cols
    stride = cols + 2 * MARGIN
    padded = halves((rows + 2) * stride, channels)
    shift_shape = (3, rows + 2, cols, channels)
    whole = -(-cells // 256) * 256 // n_cols
    part = sds((9 * channels, channels), f32)
    send = sds((groups, block, channels), bf16)
    blocks = [
        sds(shift_shape, bf16), sds((2, whole + 1, n_cols, channels), bf16),
        sds(skip.shape, bf16), sds((rows * cols, channels), f32), part,
    ]
    *inner, part_conv, send_conv, last_pre, grad_act = kernel_call(
        inner_kernel,
        [
            *blocks, send, sds((cols, channels), f32), sds((rows * cols, channels), f32),
        ],
        [halves(rows * stride, channels), flat],
        0, coarse, skip, cotangent, left, right, up_weight, conv_weight, grad_centre,
    )
    side = sds(message.shape, f32)
    got_conv = core_swap(send_conv)
    edge = sds((14, cols, channels), bf16)
    shifted, near, act, slope, edge, upper, lower = kernel_call(
        act_kernel, [*blocks[:-1], edge, side, side],
        [halves(stride, channels), halves(cols, channels)],
        10**11, first, second, right, up_weight, last_pre, *inner, changed={5 + i: i for i in range(4)},
    )
    phases = kernel_call(
        grad_kernel, [sds((2, 2, whole, n_cols, channels), bf16)], [flat],
        0, shifted, slope, grad_act, conv_weight,
    )[0]
    part_up, send_up = kernel_call(up_kernel, [part, send], [], 0, near, phases)
    own_conv, to_conv = core_sum(
        edge_kernel, [pltpu.VMEM(part.shape, f32)], after(part_conv, send_up), got_conv, edge, core_swap(edge)
    )
    got_conv = plane_swap(to_conv, 0)
    own_up, to_up = core_sum(core_kernel, [], after(part_up, to_conv), core_swap(send_up))
    got_up = plane_swap(to_up, 0)
    ring_act, ring_grad = kernel_call(
        ring_kernel,
        [
            sds((at.ring_size, channels), f32),
            sds((channels // LANES, at.grad_size, LANES), f32),
        ],
        [halves(at.ring_size, channels), halves((rows + 3) * stride, channels)],
        0, coarse, cotangent, after(left, to_up), right, upper, lower, conv_weight, up_weight,
    )
    decoded = kernel_call(
        decoded_kernel, [sds(skip.shape, bf16)], [padded, pltpu.VMEM(shift_shape, bf16)],
        0, act, ring_act, conv_weight,
    )[0]
    own_conv = after(own_conv, decoded)
    steps = (faces // 2).bit_length() - 1
    for step in range(1, steps):
        own_conv, to_conv = plane_sum(own_conv, got_conv)
        got_conv = plane_swap(to_conv, step)
        own_up, to_up = plane_sum(own_up, got_up)
        got_up = plane_swap(to_up, step)
        if step == 1:
            grad_coarse = kernel_call(
                coarse_kernel, [sds(coarse.shape, bf16)],
                [
                    halves(n_rows * (n_cols + 2 * MARGIN), channels),
                    pltpu.VMEM((4, n_rows + 1, n_cols, channels), bf16),
                ],
                0, phases, after(ring_grad, to_up), up_weight,
            )[0]
            own_up = after(own_up, grad_coarse)
    grad_conv, grad_up = band_sum(own_conv, got_conv, own_up, got_up)
    return (decoded, grad_coarse, grad_up, grad_conv)


def solution(mesh):
    return jax.shard_map(
        local,
        mesh=mesh,
        in_specs=(
            P("band", "face", None),
            P("band", "face", None),
            P(),
            P(),
            P("band", "face", None),
        ),
        out_specs=(
            P("band", "face", None),
            P("band", "face", None),
            P("face", "band"),
            P("face", "band"),
        ),
        check_vma=False,
    )
```

```python
import jax
import jax.numpy as jnp
from jax import lax
from jax.experimental import pallas as pl
from jax.experimental.pallas import tpu as pltpu
from jax.sharding import PartitionSpec as P

f32, bf16 = jnp.float32, jnp.bfloat16
forward_taps = ((1, 1), (0, 0), (1, 0))
backward_taps = ((1, 0), (0, 1), (1, 1))
MARGIN = 8
LANES = 128


def sds(shape, dtype):
    return jax.ShapeDtypeStruct(shape, dtype)


def kernel_call(body, outs, scratch, flops, *args, far=(), changed=None):
    vmem = pl.BlockSpec(memory_space=pltpu.VMEM)
    hbm = pl.BlockSpec(memory_space=pltpu.HBM)
    moved = sum(a.size * a.dtype.itemsize for a in args)
    moved += sum(a.size * a.dtype.itemsize for a in outs)
    args = [
        pltpu.with_memory_space_constraint(a, pltpu.HBM) if i in far else a
        for i, a in enumerate(args)
    ]
    return pl.pallas_call(
        body,
        out_shape=tuple(outs),
        in_specs=[hbm if i in far else vmem for i in range(len(args))],
        out_specs=tuple(vmem for _ in outs),
        scratch_shapes=scratch,
        input_output_aliases=changed or {},
        compiler_params=pltpu.CompilerParams(vmem_limit_bytes=28 * 2**20),
        cost_estimate=pl.CostEstimate(flops=flops, bytes_accessed=moved, transcendentals=0),
    )(*args)


def place_of():
    face = lax.axis_index("face")
    return lax.rem(face, 2), lax.div(face, 2), lax.axis_index("band"), lax.axis_size("band")


def dot(a, b):
    return jnp.dot(a, b, preferred_element_type=f32)


def dot_nt(a, b):
    return lax.dot_general(a, b, (((1,), (1,)), ((), ())), preferred_element_type=f32)


def pairs(count, wrap):
    first = [(i, i ^ 1) for i in range(count)]
    second = []
    for i in range(count):
        j = i + 1 if i % 2 else i - 1
        if wrap or 0 <= j < count:
            second.append((i, j % count))
    return first, second


def up16(n):
    return (n + 15) // 16 * 16


def halves(n_rows, channels):
    return pltpu.VMEM((channels // LANES, n_rows, LANES), f32)


def put(ref, start, value, step=1):
    for part in range(ref.shape[0]):
        rows = pl.ds(start, value.shape[0], stride=step if step > 1 else None)
        ref[part, rows, :] = value[:, part * LANES : (part + 1) * LANES]


def get(ref, start, count, step=1):
    rows = pl.ds(start, count, stride=step if step > 1 else None)
    return jnp.concatenate([ref[part, rows, :] for part in range(ref.shape[0])], axis=1)


def fill(ref, start, value):
    ref[start : start + value.shape[0], :] = value


def other_core(send, *terms):
    core = place_of()[0]
    groups, block, _ = send.shape
    for group in range(groups):
        theirs = pl.multiple_of((2 * group + 1 - core) * block, 16)
        send[group] = sum(term[pl.ds(theirs, block), :] for term in terms).astype(bf16)


class Layout:
    def __init__(self, n_rows, n_cols):
        rows, cols = 2 * n_rows, 2 * n_cols
        self.cot, self.cot_2, self.skip, self.coarse = 0, rows, 2 * rows, 3 * rows
        self.face_size = up16(3 * rows + n_rows)
        self.row_cot, self.row_cot_2, self.row_skip = 0, cols, 2 * cols
        self.row_coarse, self.corner = 3 * cols, 3 * cols + n_cols
        self.band_size = self.corner + 16
        ring = (cols + 2 + 7) // 8 * 8
        self.top, self.bottom, self.left, self.right = 0, ring, 2 * ring, 2 * ring + rows
        self.ring_size = up16(2 * ring + 2 * rows)
        self.grad_left, self.grad_size = ring, up16(ring + rows)


COT, COT_2, SKIP, COARSE = (0, 1, 2), (3, 4, 5), (6, None, 7), (8, None, 9)


def face_message(coarse, skip, cot, first, second, cot_v, skip_v, coarse_v, flat, before, after, sems):
    rows, cols, _ = cot.shape
    n_rows, n_cols, _ = coarse.shape
    at = Layout(n_rows, n_cols)
    copies = [
        pltpu.make_async_copy(source, target, sems.at[i])
        for i, (source, target) in enumerate(((cot, cot_v), (skip, skip_v), (coarse, coarse_v)))
    ]
    for copy in copies:
        copy.start()
    before[...] = jnp.zeros_like(before)
    after[...] = jnp.zeros_like(after)
    for copy, array, start, start_2 in (
        (copies[0], cot_v, at.cot, at.cot_2), (copies[1], skip_v, at.skip, None), (copies[2], coarse_v, at.coarse, None),
    ):
        copy.wait()
        n, width, channels = array.shape
        put(flat, 0, array[:, :16, :].astype(f32)[:, :8, :].reshape(n * 8, channels))
        put(flat, n * 8, array[:, width - 16 :, :].astype(f32)[:, 8:, :].reshape(n * 8, channels))
        fill(before, start, get(flat, 0, n, 8))
        fill(after, start, get(flat, n * 8 + 7, n, 8))
        if start_2 is not None:
            fill(after, start_2, get(flat, n * 8 + 6, n, 8))
    even = place_of()[0] == 0
    first[...] = jnp.where(even, after[...], before[...]).astype(bf16)
    second[...] = jnp.where(even, before[...], after[...]).astype(bf16)


def band_message(coarse, skip, cot, got_first, got_second, first, second, left, right, before, after):
    rows, cols, channels = cot.shape
    n_rows, n_cols, _ = coarse.shape
    at = Layout(n_rows, n_cols)
    even = place_of()[0] == 0
    one, two = got_first[...].astype(f32), got_second[...].astype(f32)
    left[...] = jnp.where(even, two, one)
    right[...] = jnp.where(even, one, two)
    for message, row, row_2, cell in ((before, 0, None, 0), (after, rows - 1, rows - 2, n_rows - 1)):
        fill(message, at.row_cot, cot[row].astype(f32))
        if row_2 is None:
            fill(message, at.row_cot_2, jnp.zeros((cols, channels), f32))
        else:
            fill(message, at.row_cot_2, cot[row_2].astype(f32))
        fill(message, at.row_skip, skip[row].astype(f32))
        fill(message, at.row_coarse, coarse[cell].astype(f32))
        fill(message, at.corner, jnp.zeros((16, channels), f32))
        corners = [
            (COT[0], left, at.cot + row), (COT[1], left, at.cot_2 + row), (COT[2], right, at.cot + row),
            (SKIP[0], left, at.skip + row), (SKIP[2], right, at.skip + row),
            (COARSE[0], left, at.coarse + cell), (COARSE[2], right, at.coarse + cell),
        ]
        if row_2 is not None:
            corners += [
                (COT_2[0], left, at.cot + row_2), (COT_2[1], left, at.cot_2 + row_2),
                (COT_2[2], right, at.cot + row_2),
            ]
        for corner, side, source in corners:
            fill(message, at.corner + corner, side[source : source + 1, :])
    even = lax.rem(place_of()[2], 2) == 0
    first[...] = jnp.where(even, after[...], before[...]).astype(bf16)
    second[...] = jnp.where(even, before[...], after[...]).astype(bf16)


def early_kernel(cot, conv_w, conv_v, grad_act, centre, sem):
    rows, cols, channels = cot.shape
    copy = pltpu.make_async_copy(conv_w, conv_v, sem)
    copy.start()
    for row in (0, rows + 1):
        centre[row] = jnp.zeros((cols, channels), bf16)
    centre[pl.ds(1, rows)] = cot[...]
    copy.wait()
    total = jnp.zeros((rows * cols, channels), f32)
    for k in range(3):
        source = centre[pl.ds(2 - k, rows)].reshape(-1, channels)
        total = total + dot_nt(source, conv_v[k, 1])
    grad_act[...] = total


def inner_kernel(
    coarse, skip, cot, left, right, up_w, conv_w, grad_centre,
    shifted, near, act, slope, partial, send, last_pre, grad_act, padded, pre,
):
    n_rows, n_cols, channels = coarse.shape
    rows, cols, _ = skip.shape
    at = Layout(n_rows, n_cols)
    stride = cols + 2 * MARGIN
    for row in range(n_rows):
        near[0, row] = coarse[row]
        put(padded, row * stride, coarse[row].astype(f32))
    put(padded, n_cols, right[at.coarse : at.coarse + n_rows, :], stride)
    for row in range(n_rows):
        near[1, row] = get(padded, row * stride + 1, n_cols).astype(bf16)
    for row in range(n_rows, near.shape[1]):
        for side in range(2):
            near[side, row] = jnp.zeros((n_cols, channels), bf16)
    sums = {}
    for k in range(3):
        row_phase, row_off = forward_taps[k]
        for l in range(3):
            col_phase, col_off = forward_taps[l]
            source = near[col_off, pl.ds(row_off, n_rows)].reshape(n_rows * n_cols, channels)
            term = dot(source, up_w[k, l])
            name = (row_phase, col_phase)
            sums[name] = sums[name] + term if name in sums else term
    for (row_phase, col_phase), total in sums.items():
        for row in range(n_rows):
            start = (2 * row + row_phase) * cols + col_phase
            put(pre, start, total[row * n_cols : (row + 1) * n_cols], 2)
    for row in range(rows):
        put(padded, row * stride + MARGIN, cot[row].astype(f32))
    put(padded, MARGIN - 1, left[at.cot : at.cot + rows, :], stride)
    put(padded, MARGIN + cols, right[at.cot : at.cot + rows, :], stride)
    for row in range(rows):
        for shift in (0, 2):
            start = row * stride + MARGIN - 1 + shift
            shifted[shift, row + 1] = get(padded, start, cols).astype(bf16)
        shifted[1, row + 1] = cot[row]
    for shift in range(3):
        shifted[shift, 0] = jnp.zeros((cols, channels), bf16)
        shifted[shift, rows + 1] = jnp.zeros((cols, channels), bf16)
    preact = get(pre, 0, rows * cols) + skip[...].reshape(rows * cols, channels).astype(f32)
    last_pre[...] = preact[(rows - 1) * cols :]
    sigma = jax.nn.sigmoid(preact)
    value = preact * sigma
    slope[...] = sigma + value * (1.0 - sigma)
    row_of = lax.broadcasted_iota(jnp.int32, value.shape, 0)
    act_flat = jnp.where(row_of < (rows - 1) * cols, value, 0.0).astype(bf16)
    act[...] = act_flat.reshape(act.shape)
    act_t = act_flat.T
    for k in range(3):
        for l in range(3):
            source = shifted[2 - l, pl.ds(2 - k, rows)].reshape(-1, channels)
            partial[pl.ds((3 * k + l) * channels, channels), :] = dot(act_t, source)
    other_core(send, partial)
    total = grad_centre[...]
    for k in range(3):
        source = shifted[0, pl.ds(2 - k, rows)].reshape(-1, channels)
        total = total + dot_nt(source, conv_w[k, 2])
    grad_act[...] = total


def act_kernel(
    got_first, got_second, right, up_w, last_pre, shifted_in, near_in, act_in, slope_in,
    shifted, near, act, slope, edge, upper, lower, padded, pre,
):
    rows, cols, channels = act.shape
    n_rows, n_cols = rows // 2, cols // 2
    at = Layout(n_rows, n_cols)
    even = lax.rem(place_of()[2], 2) == 0
    one, two = got_first[...].astype(f32), got_second[...].astype(f32)
    upper[...] = jnp.where(even, two, one)
    lower[...] = jnp.where(even, one, two)
    below = lower[at.row_coarse : at.row_coarse + n_cols, :]
    corner = at.corner + COARSE[2]
    put(padded, 0, below)
    put(padded, n_cols, lower[corner : corner + 1, :])
    cells = [below.astype(bf16), get(padded, 1, n_cols).astype(bf16)]
    near[0, n_rows] = cells[0]
    near[1, n_rows] = cells[1]
    put(pre, 0, dot(cells[0], up_w[0, 1]), 2)
    put(pre, 1, dot(cells[1], up_w[0, 0]) + dot(cells[0], up_w[0, 2]), 2)
    preact = last_pre[...] + get(pre, 0, cols)
    sigma = jax.nn.sigmoid(preact)
    value = preact * sigma
    slope[(rows - 1) * cols :, :] = sigma + value * (1.0 - sigma)
    last = value.astype(bf16)
    act[rows - 1] = last
    for row, message in ((0, upper), (rows + 1, lower)):
        centre = message[at.row_cot : at.row_cot + cols, :]
        put(padded, MARGIN, centre)
        for col, one in ((-1, COT[0]), (cols, COT[2])):
            put(padded, MARGIN + col, message[at.corner + one : at.corner + one + 1, :])
        shifted[0, row] = get(padded, MARGIN - 1, cols).astype(bf16)
        shifted[1, row] = centre.astype(bf16)
        shifted[2, row] = get(padded, MARGIN + 1, cols).astype(bf16)
    edge[0] = last
    edge[1] = act_in[0]
    for shift in range(3):
        for place, row in enumerate((0, rows - 1, rows, rows + 1)):
            edge[2 + 4 * shift + place] = shifted[shift, row]


def grad_kernel(shifted, slope, grad_act, conv_w, phases, fine):
    rows, cols = shifted.shape[1] - 2, shifted.shape[2]
    channels = shifted.shape[3]
    n_rows, n_cols = rows // 2, cols // 2
    cells = rows * cols
    total = grad_act[...]
    for k in range(3):
        source = shifted[2, pl.ds(2 - k, rows)].reshape(cells, channels)
        total = total + dot_nt(source, conv_w[k, 0])
    first = jnp.zeros((cols, channels), f32)
    last = jnp.zeros((cols, channels), f32)
    for l in (1, 2):
        first = first + dot_nt(shifted[2 - l, 0], conv_w[2, l])
        last = last + dot_nt(shifted[2 - l, rows + 1], conv_w[0, l])
    put(fine, 0, (total * slope[...]).astype(bf16).astype(f32))
    put(fine, 0, ((total[:cols] + first) * slope[:cols, :]).astype(bf16).astype(f32))
    edge = (total[cells - cols :] + last) * slope[cells - cols :, :]
    put(fine, cells - cols, edge.astype(bf16).astype(f32))
    whole = phases.shape[2]
    for row_phase in range(2):
        for col_phase in range(2):
            for row in range(n_rows):
                start = (2 * row + row_phase) * cols + col_phase
                phases[row_phase, col_phase, row] = get(fine, start, n_cols, 2).astype(bf16)
            for row in range(n_rows, whole):
                phases[row_phase, col_phase, row] = jnp.zeros((n_cols, channels), bf16)


def up_kernel(near, phases, partial, send):
    _, _, whole, n_cols, channels = phases.shape
    turned = {}
    for row_off in range(2):
        for col_off in range(2):
            cells = near[col_off, pl.ds(row_off, whole)]
            turned[row_off, col_off] = cells.reshape(whole * n_cols, channels).T
    for k in range(3):
        row_phase, row_off = forward_taps[k]
        for l in range(3):
            col_phase, col_off = forward_taps[l]
            source = phases[row_phase, col_phase].reshape(whole * n_cols, channels)
            partial[pl.ds((3 * k + l) * channels, channels), :] = dot(
                turned[row_off, col_off], source
            )
    other_core(send, partial)


def ring_kernel(
    coarse, cot, left, right, upper, lower, conv_w, up_w, ring_act, ring_grad, ring, wide,
):
    rows, cols, channels = cot.shape
    n_rows, n_cols = rows // 2, cols // 2
    at = Layout(n_rows, n_cols)
    stride, step = cols + 2 * MARGIN, n_cols + 2 * MARGIN
    _, _, band, n_bands = place_of()
    has_upper, has_lower = band > 0, band < n_bands - 1

    def corner(message, which):
        return message[at.corner + which : at.corner + which + 1, :]

    def cell(i, j):
        return (i + 1) * step + MARGIN + j

    for row in range(n_rows):
        put(wide, cell(row, 0), coarse[row].astype(f32))
    for row, message in ((-1, upper), (n_rows, lower)):
        put(wide, cell(row, 0), message[at.row_coarse : at.row_coarse + n_cols, :])
        put(wide, cell(row, -1), corner(message, COARSE[0]))
        put(wide, cell(row, n_cols), corner(message, COARSE[2]))
    put(wide, cell(0, -1), left[at.coarse : at.coarse + n_rows, :], step)
    put(wide, cell(0, n_cols), right[at.coarse : at.coarse + n_rows, :], step)
    total = jnp.zeros((at.ring_size, channels), f32)
    for k in range(3):
        for l in range(3):
            put(ring, 0, jnp.zeros((at.ring_size, channels), f32))
            for base, i in ((at.bottom, n_rows),) if k == 1 else ((at.top, k // 2 * -1),):
                start = cell(i, -1 if l == 2 else 0)
                put(ring, base + (l == 1), get(wide, start, n_cols + 1), 2)
            base, j = (at.right, n_cols) if l == 1 else (at.left, -(l // 2))
            start = cell(1 if k == 0 else 0, j)
            put(ring, base + (k != 1), get(wide, start, n_rows, step), 2)
            total = total + dot(get(ring, 0, at.ring_size).astype(bf16), up_w[k, l])
    put(ring, 0, jnp.zeros((at.ring_size, channels), f32))
    for base, message in ((at.top, upper), (at.bottom, lower)):
        put(ring, base + 1, message[at.row_skip : at.row_skip + cols, :])
        put(ring, base, corner(message, SKIP[0]))
        put(ring, base + cols + 1, corner(message, SKIP[2]))
    put(ring, at.left, left[at.skip : at.skip + rows, :])
    put(ring, at.right, right[at.skip : at.skip + rows, :])
    preact = total + get(ring, 0, at.ring_size)
    sigma = jax.nn.sigmoid(preact)
    value = preact * sigma
    slope = sigma + value * (1.0 - sigma)
    value = value.astype(bf16).astype(f32)
    ring_act[...] = value
    for base, exists in ((at.top, has_upper), (at.bottom, has_lower)):
        strip = value[base : base + cols + 2]
        ring_act[base : base + cols + 2, :] = jnp.where(exists, strip, 0.0)

    def fine(p, q):
        return (p + 2) * stride + MARGIN + q

    for row in range(rows):
        put(wide, fine(row, 0), cot[row].astype(f32))
    for row, message, start, which in (
        (-1, upper, at.row_cot, COT), (-2, upper, at.row_cot_2, COT_2), (rows, lower, at.row_cot, COT),
    ):
        put(wide, fine(row, 0), message[start : start + cols, :])
        for col, one in ((-1, which[0]), (-2, which[1]), (cols, which[2])):
            put(wide, fine(row, col), corner(message, one))
    put(wide, fine(0, -1), left[at.cot : at.cot + rows, :], stride)
    put(wide, fine(0, -2), left[at.cot_2 : at.cot_2 + rows, :], stride)
    put(wide, fine(0, cols), right[at.cot : at.cot + rows, :], stride)
    total = jnp.zeros((at.grad_size, channels), f32)
    for k in range(3):
        for l in range(3):
            put(ring, at.top, get(wide, fine(-k, -l), cols + 1))
            put(ring, at.grad_left, get(wide, fine(1 - k, -l), rows, stride))
            source = get(ring, 0, at.grad_size).astype(bf16)
            total = total + dot_nt(source, conv_w[k, l])
    strip = (total[: cols + 1] * slope[at.top : at.top + cols + 1]).astype(bf16).astype(f32)
    put(ring_grad, at.top, jnp.where(has_upper, strip, 0.0))
    strip = total[at.grad_left : at.grad_left + rows] * slope[at.left : at.left + rows]
    put(ring_grad, at.grad_left, strip.astype(bf16).astype(f32))


def decoded_kernel(act, ring_act, conv_w, decoded, padded, shifted):
    rows, cols, channels = act.shape
    at = Layout(rows // 2, cols // 2)
    stride = cols + 2 * MARGIN
    for row in range(rows):
        put(padded, (row + 1) * stride + MARGIN, act[row].astype(f32))
    for row, base in ((0, at.top), (rows + 1, at.bottom)):
        put(padded, row * stride + MARGIN - 1, ring_act[base : base + cols + 2, :])
    put(padded, stride + MARGIN - 1, ring_act[at.left : at.left + rows, :], stride)
    put(padded, stride + MARGIN + cols, ring_act[at.right : at.right + rows, :], stride)
    for row in range(rows + 2):
        for shift in range(3):
            start = row * stride + MARGIN - 1 + shift
            shifted[shift, row] = get(padded, start, cols).astype(bf16)
    total = jnp.zeros((rows * cols, channels), f32)
    for k in range(3):
        for l in range(3):
            source = shifted[l, pl.ds(k, rows)].reshape(-1, channels)
            total = total + dot(source, conv_w[k, l])
    decoded[...] = total.astype(bf16).reshape(decoded.shape)

def coarse_kernel(phases, ring_grad, up_w, coarse_out, padded, moved):
    n_rows, n_cols, channels = coarse_out.shape
    at = Layout(n_rows, n_cols)
    stride = n_cols + 2 * MARGIN
    for phase, start in ((0, 1), (1, 2), (2, 0)):
        moved[phase, 0] = get(ring_grad, at.top + start, n_cols, 2).astype(bf16)
    for phase in range(2):
        for row in range(n_rows):
            moved[phase, 1 + row] = phases[1, phase, row]
    for row_phase in range(2):
        for row in range(n_rows):
            put(padded, row * stride + MARGIN, phases[row_phase, 1, row].astype(f32))
        put(padded, MARGIN - 1, get(ring_grad, at.grad_left + row_phase, n_rows, 2), stride)
        for row in range(n_rows):
            cells = get(padded, row * stride + MARGIN - 1, n_cols).astype(bf16)
            if row_phase:
                moved[2, 1 + row] = cells
            else:
                moved[3, row] = cells
    total = jnp.zeros((n_rows * n_cols, channels), f32)
    for k in range(3):
        for l in range(3):
            if k == 1:
                if l == 0:
                    source = moved[3, pl.ds(0, n_rows)]
                else:
                    source = phases[0, l - 1, pl.ds(0, n_rows)]
            else:
                source = moved[(2, 0, 1)[l], pl.ds(k // 2, n_rows)]
            total = total + dot_nt(source.reshape(n_rows * n_cols, channels), up_w[k, l])
    coarse_out[...] = total.astype(bf16).reshape(coarse_out.shape)


def halving(count):
    bits = (count // 2).bit_length() - 1
    return [[(step + core) % bits for step in range(bits)] for core in range(2)]


def mask_of(slot, order):
    last = len(order) - 1
    return sum(1 << bit for step, bit in enumerate(order) if slot >> (last - step) & 1)


def edge_kernel(partial, got, edge, got_edge, own, message, extra):
    channels, block = partial.shape[1], got.shape[1]
    zero = jnp.zeros(edge.shape[1:], bf16)
    sides = (edge, got_edge)
    rows_t = jnp.concatenate([side[row] for side in sides for row in range(2)], axis=0).T

    def add_blocks(core):
        for tap in range(9):
            first = 2 + 4 * (2 - tap % 3)
            beside = []
            for side in sides:
                beside += [side[first + 3 - tap // 3], side[first] if tap >= 6 else zero]
            beside = jnp.concatenate(beside, axis=0)
            start = tap * channels
            for mine in range(start // block, -(-(start + channels) // block)):
                if mine % 2 == core:
                    low = max(start, mine * block)
                    high = min(start + channels, (mine + 1) * block)
                    extra[low:high, :] = dot(rows_t[low - start : high - start], beside)

    for core in range(2):
        pl.when(place_of()[0] == core)(lambda core=core: add_blocks(core))
    core_kernel(partial, extra, got, own, message)


def core_kernel(*refs):
    *terms, got, own, message = refs
    slots, half, block = got.shape[0], own.shape[0], got.shape[1]
    core, chip, _, _ = place_of()
    even, odd = halving(2 * slots)
    for slot in range(slots):
        target = chip ^ jnp.where(core == 0, mask_of(slot, even), mask_of(slot, odd))
        mine = pl.multiple_of((2 * target + core) * block, 16)
        total = sum(term[pl.ds(mine, block), :] for term in terms) + got[target].astype(f32)
        if slot < half:
            own[slot] = total
        else:
            message[slot - half] = total.astype(bf16)


def plane_kernel(before, got, own, message):
    half = own.shape[0]
    for slot in range(2 * half):
        total = before[slot] + got[slot].astype(f32)
        if slot < half:
            own[slot] = total
        else:
            message[slot - half] = total.astype(bf16)


def band_kernel(conv, got_conv, up, got_up, own, *refs):
    n_bands, messages, cut = len(refs), refs[:-1], refs[-1]
    conv_total = conv[0] + got_conv[0].astype(f32)
    up_total = up[0] + got_up[0].astype(f32)
    cols = conv_total.shape[1] // n_bands
    for band in range(n_bands):
        cut[band, :, :cols] = conv_total[:, band * cols : (band + 1) * cols]
        cut[band, :, cols:] = up_total[:, band * cols : (band + 1) * cols]
    band = place_of()[2]
    own[...] = cut[band]
    for k, message in enumerate(messages):
        message[...] = cut[band ^ (k + 1)].astype(bf16)


def last_kernel(own, *refs):
    peers, (conv, up) = refs[:-2], refs[-2:]
    total = own[...]
    for peer in peers:
        total = total + peer[...].astype(f32)
    turned = total.T
    conv[...] = turned[: conv.shape[0]]
    up[...] = turned[conv.shape[0] :]


def xor_pairs(count, bits):
    return [(i, i ^ bits) for i in range(count)]


def core_swap(send):
    return lax.ppermute(send, "face", xor_pairs(lax.axis_size("face"), 1))


def core_sum(body, scratch, partial, got, *rest):
    groups, block, channels = got.shape
    shape = (groups // 2, block, channels)
    outs = [sds(shape, f32), sds(shape, bf16)]
    cost = 10**11 if rest else 0
    return kernel_call(body, outs, scratch, cost, partial, got, *rest)


def plane_swap(message, step):
    faces = lax.axis_size("face")
    orders = halving(faces)
    return lax.ppermute(message, "face", [(i, i ^ 2 << orders[i % 2][step]) for i in range(faces)])


def plane_sum(own, got):
    half, block, channels = own.shape
    shape = (half // 2, block, channels)
    return kernel_call(plane_kernel, [sds(shape, f32), sds(shape, bf16)], [], 0, own, got)


def band_sum(conv, got_conv, up, got_up):
    bands = lax.axis_size("band")
    _, block, channels = conv.shape
    cols = channels // bands
    shape = (block, 2 * cols)
    own, *messages = kernel_call(
        band_kernel, [sds(shape, f32)] + [sds(shape, bf16)] * (bands - 1),
        [pltpu.VMEM((bands,) + shape, f32)], 0, conv, got_conv, up, got_up,
    )
    got = [
        lax.ppermute(messages[k - 1], "band", xor_pairs(bands, k))
        for k in (3, 2, 1)
    ]
    return [a.T for a in kernel_call(last_kernel, [sds((cols, block), f32)] * 2, [], 0, own, *got)]


def after(value, *others):
    return lax.optimization_barrier((value, *others))[0]


def swap(first, second, axis, wrap):
    one, two = pairs(lax.axis_size(axis), wrap)
    return lax.ppermute(first, axis, one), lax.ppermute(second, axis, two)


def local(coarse, skip, up_weight, conv_weight, cotangent):
    n_rows, n_cols, channels = coarse.shape
    rows, cols, _ = skip.shape
    at = Layout(n_rows, n_cols)
    faces = lax.axis_size("face")
    groups, block = faces // 2, 9 * channels // faces

    flat = halves(rows * cols, channels)
    message = sds((at.face_size, channels), bf16)
    edges = pltpu.VMEM(message.shape, f32)
    first, second, cotangent, skip, coarse = kernel_call(
        face_message,
        [message, message, sds(cotangent.shape, bf16), sds(skip.shape, bf16), sds(coarse.shape, bf16)],
        [flat, edges, edges, pltpu.SemaphoreType.DMA((3,))],
        0, coarse, skip, cotangent, far=(0, 1, 2),
    )
    first, second = swap(first, second, "face", True)
    conv_weight, grad_centre = kernel_call(
        early_kernel,
        [sds(conv_weight.shape, bf16), sds((rows * cols, channels), f32)],
        [pltpu.VMEM((rows + 2, cols, channels), bf16), pltpu.SemaphoreType.DMA],
        0, cotangent, conv_weight, far=(1,),
    )
    side = sds(message.shape, f32)
    message = sds((at.band_size, channels), bf16)
    edges = pltpu.VMEM(message.shape, f32)
    first, second, left, right = kernel_call(
        band_message, [message, message, side, side], [edges, edges],
        0, coarse, skip, after(cotangent, grad_centre), first, second,
    )
    first, second = swap(first, second, "band", False)

    cells = n_rows * n_cols
    stride = cols + 2 * MARGIN
    padded = halves((rows + 2) * stride, channels)
    shift_shape = (3, rows + 2, cols, channels)
    whole = -(-cells // 256) * 256 // n_cols
    part = sds((9 * channels, channels), f32)
    send = sds((groups, block, channels), bf16)
    blocks = [
        sds(shift_shape, bf16), sds((2, whole + 1, n_cols, channels), bf16),
        sds(skip.shape, bf16), sds((rows * cols, channels), f32), part,
    ]
    *inner, part_conv, send_conv, last_pre, grad_act = kernel_call(
        inner_kernel,
        [
            *blocks, send, sds((cols, channels), f32), sds((rows * cols, channels), f32),
        ],
        [halves(rows * stride, channels), flat],
        0, coarse, skip, cotangent, left, right, up_weight, conv_weight, grad_centre,
    )
    side = sds(message.shape, f32)
    got_conv = core_swap(send_conv)
    edge = sds((14, cols, channels), bf16)
    shifted, near, act, slope, edge, upper, lower = kernel_call(
        act_kernel, [*blocks[:-1], edge, side, side],
        [halves(stride, channels), halves(cols, channels)],
        10**11, first, second, right, up_weight, last_pre, *inner, changed={5 + i: i for i in range(4)},
    )
    phases = kernel_call(
        grad_kernel, [sds((2, 2, whole, n_cols, channels), bf16)], [flat],
        0, shifted, slope, grad_act, conv_weight,
    )[0]
    part_up, send_up = kernel_call(up_kernel, [part, send], [], 0, near, phases)
    own_conv, to_conv = core_sum(
        edge_kernel, [pltpu.VMEM(part.shape, f32)], after(part_conv, send_up), got_conv, edge, core_swap(edge)
    )
    got_conv = plane_swap(to_conv, 0)
    own_up, to_up = core_sum(core_kernel, [], after(part_up, to_conv), core_swap(send_up))
    got_up = plane_swap(to_up, 0)
    ring_act, ring_grad = kernel_call(
        ring_kernel,
        [
            sds((at.ring_size, channels), f32),
            sds((channels // LANES, at.grad_size, LANES), f32),
        ],
        [halves(at.ring_size, channels), halves((rows + 3) * stride, channels)],
        0, coarse, cotangent, after(left, to_up), right, upper, lower, conv_weight, up_weight,
    )
    decoded = kernel_call(
        decoded_kernel, [sds(skip.shape, bf16)], [padded, pltpu.VMEM(shift_shape, bf16)],
        0, act, ring_act, conv_weight,
    )[0]
    own_conv = after(own_conv, decoded)
    steps = (faces // 2).bit_length() - 1
    for step in range(1, steps):
        own_conv, to_conv = plane_sum(own_conv, got_conv)
        got_conv = plane_swap(to_conv, step)
        if step == 1:
            grad_coarse = kernel_call(
                coarse_kernel, [sds(coarse.shape, bf16)],
                [
                    halves(n_rows * (n_cols + 2 * MARGIN), channels),
                    pltpu.VMEM((4, n_rows + 1, n_cols, channels), bf16),
                ],
                0, phases, after(ring_grad, to_conv), up_weight,
            )[0]
            own_up = after(own_up, grad_coarse)
        own_up, to_up = plane_sum(own_up, got_up)
        got_up = plane_swap(to_up, step)
    grad_conv, grad_up = band_sum(own_conv, got_conv, own_up, got_up)
    return (decoded, grad_coarse, grad_up, grad_conv)


def solution(mesh):
    return jax.shard_map(
        local,
        mesh=mesh,
        in_specs=(
            P("band", "face", None),
            P("band", "face", None),
            P(),
            P(),
            P("band", "face", None),
        ),
        out_specs=(
            P("band", "face", None),
            P("band", "face", None),
            P("face", "band"),
            P("face", "band"),
        ),
        check_vma=False,
    )
```

```python
import jax
import jax.numpy as jnp
from jax import lax
from jax.experimental import pallas as pl
from jax.experimental.pallas import tpu as pltpu
from jax.sharding import PartitionSpec as P

f32, bf16 = jnp.float32, jnp.bfloat16
forward_taps = ((1, 1), (0, 0), (1, 0))
backward_taps = ((1, 0), (0, 1), (1, 1))
MARGIN = 8
LANES = 128


def sds(shape, dtype):
    return jax.ShapeDtypeStruct(shape, dtype)


def kernel_call(body, outs, scratch, flops, *args, far=(), changed=None):
    vmem = pl.BlockSpec(memory_space=pltpu.VMEM)
    hbm = pl.BlockSpec(memory_space=pltpu.HBM)
    moved = sum(a.size * a.dtype.itemsize for a in args)
    moved += sum(a.size * a.dtype.itemsize for a in outs)
    args = [
        pltpu.with_memory_space_constraint(a, pltpu.HBM) if i in far else a
        for i, a in enumerate(args)
    ]
    return pl.pallas_call(
        body,
        out_shape=tuple(outs),
        in_specs=[hbm if i in far else vmem for i in range(len(args))],
        out_specs=tuple(vmem for _ in outs),
        scratch_shapes=scratch,
        input_output_aliases=changed or {},
        compiler_params=pltpu.CompilerParams(vmem_limit_bytes=28 * 2**20),
        cost_estimate=pl.CostEstimate(flops=flops, bytes_accessed=moved, transcendentals=0),
    )(*args)


def place_of():
    face = lax.axis_index("face")
    return lax.rem(face, 2), lax.div(face, 2), lax.axis_index("band"), lax.axis_size("band")


def dot(a, b):
    return jnp.dot(a, b, preferred_element_type=f32)


def dot_nt(a, b):
    return lax.dot_general(a, b, (((1,), (1,)), ((), ())), preferred_element_type=f32)


def pairs(count, wrap):
    first = [(i, i ^ 1) for i in range(count)]
    second = []
    for i in range(count):
        j = i + 1 if i % 2 else i - 1
        if wrap or 0 <= j < count:
            second.append((i, j % count))
    return first, second


def up16(n):
    return (n + 15) // 16 * 16


def halves(n_rows, channels):
    return pltpu.VMEM((channels // LANES, n_rows, LANES), f32)


def put(ref, start, value, step=1):
    for part in range(ref.shape[0]):
        rows = pl.ds(start, value.shape[0], stride=step if step > 1 else None)
        ref[part, rows, :] = value[:, part * LANES : (part + 1) * LANES]


def get(ref, start, count, step=1):
    rows = pl.ds(start, count, stride=step if step > 1 else None)
    return jnp.concatenate([ref[part, rows, :] for part in range(ref.shape[0])], axis=1)


def fill(ref, start, value):
    ref[start : start + value.shape[0], :] = value


def other_core(send, *terms):
    core = place_of()[0]
    groups, block, _ = send.shape
    for group in range(groups):
        theirs = pl.multiple_of((2 * group + 1 - core) * block, 16)
        send[group] = sum(term[pl.ds(theirs, block), :] for term in terms).astype(bf16)


class Layout:
    def __init__(self, n_rows, n_cols):
        rows, cols = 2 * n_rows, 2 * n_cols
        self.cot, self.cot_2, self.skip, self.coarse = 0, rows, 2 * rows, 3 * rows
        self.face_size = up16(3 * rows + n_rows)
        self.row_cot, self.row_cot_2, self.row_skip = 0, cols, 2 * cols
        self.row_coarse, self.corner = 3 * cols, 3 * cols + n_cols
        self.band_size = self.corner + 16
        ring = (cols + 2 + 7) // 8 * 8
        self.top, self.bottom, self.left, self.right = 0, ring, 2 * ring, 2 * ring + rows
        self.ring_size = up16(2 * ring + 2 * rows)
        self.grad_left, self.grad_size = ring, up16(ring + rows)


COT, COT_2, SKIP, COARSE = (0, 1, 2), (3, 4, 5), (6, None, 7), (8, None, 9)


def face_message(coarse, skip, cot, first, second, cot_v, skip_v, coarse_v, flat, before, after, sems):
    rows, cols, _ = cot.shape
    n_rows, n_cols, _ = coarse.shape
    at = Layout(n_rows, n_cols)
    copies = [
        pltpu.make_async_copy(source, target, sems.at[i])
        for i, (source, target) in enumerate(((cot, cot_v), (skip, skip_v), (coarse, coarse_v)))
    ]
    for copy in copies:
        copy.start()
    before[...] = jnp.zeros_like(before)
    after[...] = jnp.zeros_like(after)
    for copy, array, start, start_2 in (
        (copies[0], cot_v, at.cot, at.cot_2), (copies[1], skip_v, at.skip, None), (copies[2], coarse_v, at.coarse, None),
    ):
        copy.wait()
        n, width, channels = array.shape
        put(flat, 0, array[:, :16, :].astype(f32)[:, :8, :].reshape(n * 8, channels))
        put(flat, n * 8, array[:, width - 16 :, :].astype(f32)[:, 8:, :].reshape(n * 8, channels))
        fill(before, start, get(flat, 0, n, 8))
        fill(after, start, get(flat, n * 8 + 7, n, 8))
        if start_2 is not None:
            fill(after, start_2, get(flat, n * 8 + 6, n, 8))
    even = place_of()[0] == 0
    first[...] = jnp.where(even, after[...], before[...]).astype(bf16)
    second[...] = jnp.where(even, before[...], after[...]).astype(bf16)


def band_message(coarse, skip, cot, got_first, got_second, first, second, left, right, before, after):
    rows, cols, channels = cot.shape
    n_rows, n_cols, _ = coarse.shape
    at = Layout(n_rows, n_cols)
    even = place_of()[0] == 0
    one, two = got_first[...].astype(f32), got_second[...].astype(f32)
    left[...] = jnp.where(even, two, one)
    right[...] = jnp.where(even, one, two)
    for message, row, row_2, cell in ((before, 0, None, 0), (after, rows - 1, rows - 2, n_rows - 1)):
        fill(message, at.row_cot, cot[row].astype(f32))
        if row_2 is None:
            fill(message, at.row_cot_2, jnp.zeros((cols, channels), f32))
        else:
            fill(message, at.row_cot_2, cot[row_2].astype(f32))
        fill(message, at.row_skip, skip[row].astype(f32))
        fill(message, at.row_coarse, coarse[cell].astype(f32))
        fill(message, at.corner, jnp.zeros((16, channels), f32))
        corners = [
            (COT[0], left, at.cot + row), (COT[1], left, at.cot_2 + row), (COT[2], right, at.cot + row),
            (SKIP[0], left, at.skip + row), (SKIP[2], right, at.skip + row),
            (COARSE[0], left, at.coarse + cell), (COARSE[2], right, at.coarse + cell),
        ]
        if row_2 is not None:
            corners += [
                (COT_2[0], left, at.cot + row_2), (COT_2[1], left, at.cot_2 + row_2),
                (COT_2[2], right, at.cot + row_2),
            ]
        for corner, side, source in corners:
            fill(message, at.corner + corner, side[source : source + 1, :])
    even = lax.rem(place_of()[2], 2) == 0
    first[...] = jnp.where(even, after[...], before[...]).astype(bf16)
    second[...] = jnp.where(even, before[...], after[...]).astype(bf16)


def early_kernel(cot, conv_w, conv_v, grad_act, centre, sem):
    rows, cols, channels = cot.shape
    copy = pltpu.make_async_copy(conv_w, conv_v, sem)
    copy.start()
    for row in (0, rows + 1):
        centre[row] = jnp.zeros((cols, channels), bf16)
    centre[pl.ds(1, rows)] = cot[...]
    copy.wait()
    total = jnp.zeros((rows * cols, channels), f32)
    for k in range(3):
        source = centre[pl.ds(2 - k, rows)].reshape(-1, channels)
        total = total + dot_nt(source, conv_v[k, 1])
    grad_act[...] = total


def inner_kernel(
    coarse, skip, cot, left, right, up_w, conv_w, grad_centre,
    shifted, near, act, slope, partial, send, last_pre, grad_act, padded, pre,
):
    n_rows, n_cols, channels = coarse.shape
    rows, cols, _ = skip.shape
    at = Layout(n_rows, n_cols)
    stride = cols + 2 * MARGIN
    for row in range(n_rows):
        near[0, row] = coarse[row]
        put(padded, row * stride, coarse[row].astype(f32))
    put(padded, n_cols, right[at.coarse : at.coarse + n_rows, :], stride)
    for row in range(n_rows):
        near[1, row] = get(padded, row * stride + 1, n_cols).astype(bf16)
    for row in range(n_rows, near.shape[1]):
        for side in range(2):
            near[side, row] = jnp.zeros((n_cols, channels), bf16)
    sums = {}
    for k in range(3):
        row_phase, row_off = forward_taps[k]
        for l in range(3):
            col_phase, col_off = forward_taps[l]
            source = near[col_off, pl.ds(row_off, n_rows)].reshape(n_rows * n_cols, channels)
            term = dot(source, up_w[k, l])
            name = (row_phase, col_phase)
            sums[name] = sums[name] + term if name in sums else term
    for (row_phase, col_phase), total in sums.items():
        for row in range(n_rows):
            start = (2 * row + row_phase) * cols + col_phase
            put(pre, start, total[row * n_cols : (row + 1) * n_cols], 2)
    for row in range(rows):
        put(padded, row * stride + MARGIN, cot[row].astype(f32))
    put(padded, MARGIN - 1, left[at.cot : at.cot + rows, :], stride)
    put(padded, MARGIN + cols, right[at.cot : at.cot + rows, :], stride)
    for row in range(rows):
        for shift in (0, 2):
            start = row * stride + MARGIN - 1 + shift
            shifted[shift, row + 1] = get(padded, start, cols).astype(bf16)
        shifted[1, row + 1] = cot[row]
    for shift in range(3):
        shifted[shift, 0] = jnp.zeros((cols, channels), bf16)
        shifted[shift, rows + 1] = jnp.zeros((cols, channels), bf16)
    preact = get(pre, 0, rows * cols) + skip[...].reshape(rows * cols, channels).astype(f32)
    last_pre[...] = preact[(rows - 1) * cols :]
    sigma = jax.nn.sigmoid(preact)
    value = preact * sigma
    slope[...] = sigma + value * (1.0 - sigma)
    row_of = lax.broadcasted_iota(jnp.int32, value.shape, 0)
    act_flat = jnp.where(row_of < (rows - 1) * cols, value, 0.0).astype(bf16)
    act[...] = act_flat.reshape(act.shape)
    act_t = act_flat.T
    for k in range(3):
        for l in range(3):
            source = shifted[2 - l, pl.ds(2 - k, rows)].reshape(-1, channels)
            partial[pl.ds((3 * k + l) * channels, channels), :] = dot(act_t, source)
    other_core(send, partial)
    total = grad_centre[...]
    for k in range(3):
        source = shifted[0, pl.ds(2 - k, rows)].reshape(-1, channels)
        total = total + dot_nt(source, conv_w[k, 2])
    grad_act[...] = total


def act_kernel(
    got_first, got_second, right, up_w, last_pre, shifted_in, near_in, act_in, slope_in,
    shifted, near, act, slope, edge, upper, lower, padded, pre,
):
    rows, cols, channels = act.shape
    n_rows, n_cols = rows // 2, cols // 2
    at = Layout(n_rows, n_cols)
    even = lax.rem(place_of()[2], 2) == 0
    one, two = got_first[...].astype(f32), got_second[...].astype(f32)
    upper[...] = jnp.where(even, two, one)
    lower[...] = jnp.where(even, one, two)
    below = lower[at.row_coarse : at.row_coarse + n_cols, :]
    corner = at.corner + COARSE[2]
    put(padded, 0, below)
    put(padded, n_cols, lower[corner : corner + 1, :])
    cells = [below.astype(bf16), get(padded, 1, n_cols).astype(bf16)]
    near[0, n_rows] = cells[0]
    near[1, n_rows] = cells[1]
    put(pre, 0, dot(cells[0], up_w[0, 1]), 2)
    put(pre, 1, dot(cells[1], up_w[0, 0]) + dot(cells[0], up_w[0, 2]), 2)
    preact = last_pre[...] + get(pre, 0, cols)
    sigma = jax.nn.sigmoid(preact)
    value = preact * sigma
    slope[(rows - 1) * cols :, :] = sigma + value * (1.0 - sigma)
    last = value.astype(bf16)
    act[rows - 1] = last
    for row, message in ((0, upper), (rows + 1, lower)):
        centre = message[at.row_cot : at.row_cot + cols, :]
        put(padded, MARGIN, centre)
        for col, one in ((-1, COT[0]), (cols, COT[2])):
            put(padded, MARGIN + col, message[at.corner + one : at.corner + one + 1, :])
        shifted[0, row] = get(padded, MARGIN - 1, cols).astype(bf16)
        shifted[1, row] = centre.astype(bf16)
        shifted[2, row] = get(padded, MARGIN + 1, cols).astype(bf16)
    edge[0] = last
    edge[1] = act_in[0]
    for shift in range(3):
        for place, row in enumerate((0, rows - 1, rows, rows + 1)):
            edge[2 + 4 * shift + place] = shifted[shift, row]


def grad_kernel(shifted, slope, grad_act, conv_w, phases, fine):
    rows, cols = shifted.shape[1] - 2, shifted.shape[2]
    channels = shifted.shape[3]
    n_rows, n_cols = rows // 2, cols // 2
    cells = rows * cols
    total = grad_act[...]
    for k in range(3):
        source = shifted[2, pl.ds(2 - k, rows)].reshape(cells, channels)
        total = total + dot_nt(source, conv_w[k, 0])
    first = jnp.zeros((cols, channels), f32)
    last = jnp.zeros((cols, channels), f32)
    for l in (1, 2):
        first = first + dot_nt(shifted[2 - l, 0], conv_w[2, l])
        last = last + dot_nt(shifted[2 - l, rows + 1], conv_w[0, l])
    put(fine, 0, (total * slope[...]).astype(bf16).astype(f32))
    put(fine, 0, ((total[:cols] + first) * slope[:cols, :]).astype(bf16).astype(f32))
    edge = (total[cells - cols :] + last) * slope[cells - cols :, :]
    put(fine, cells - cols, edge.astype(bf16).astype(f32))
    whole = phases.shape[2]
    for row_phase in range(2):
        for col_phase in range(2):
            for row in range(n_rows):
                start = (2 * row + row_phase) * cols + col_phase
                phases[row_phase, col_phase, row] = get(fine, start, n_cols, 2).astype(bf16)
            for row in range(n_rows, whole):
                phases[row_phase, col_phase, row] = jnp.zeros((n_cols, channels), bf16)


def up_kernel(near, phases, partial, send):
    _, _, whole, n_cols, channels = phases.shape
    turned = {}
    for row_off in range(2):
        for col_off in range(2):
            cells = near[col_off, pl.ds(row_off, whole)]
            turned[row_off, col_off] = cells.reshape(whole * n_cols, channels).T
    for k in range(3):
        row_phase, row_off = forward_taps[k]
        for l in range(3):
            col_phase, col_off = forward_taps[l]
            source = phases[row_phase, col_phase].reshape(whole * n_cols, channels)
            partial[pl.ds((3 * k + l) * channels, channels), :] = dot(
                turned[row_off, col_off], source
            )
    other_core(send, partial)


def ring_kernel(
    coarse, cot, left, right, upper, lower, conv_w, up_w, ring_act, ring_grad, ring, wide,
):
    rows, cols, channels = cot.shape
    n_rows, n_cols = rows // 2, cols // 2
    at = Layout(n_rows, n_cols)
    stride, step = cols + 2 * MARGIN, n_cols + 2 * MARGIN
    _, _, band, n_bands = place_of()
    has_upper, has_lower = band > 0, band < n_bands - 1

    def corner(message, which):
        return message[at.corner + which : at.corner + which + 1, :]

    def cell(i, j):
        return (i + 1) * step + MARGIN + j

    for row in range(n_rows):
        put(wide, cell(row, 0), coarse[row].astype(f32))
    for row, message in ((-1, upper), (n_rows, lower)):
        put(wide, cell(row, 0), message[at.row_coarse : at.row_coarse + n_cols, :])
        put(wide, cell(row, -1), corner(message, COARSE[0]))
        put(wide, cell(row, n_cols), corner(message, COARSE[2]))
    put(wide, cell(0, -1), left[at.coarse : at.coarse + n_rows, :], step)
    put(wide, cell(0, n_cols), right[at.coarse : at.coarse + n_rows, :], step)
    total = jnp.zeros((at.ring_size, channels), f32)
    for k in range(3):
        for l in range(3):
            put(ring, 0, jnp.zeros((at.ring_size, channels), f32))
            for base, i in ((at.bottom, n_rows),) if k == 1 else ((at.top, k // 2 * -1),):
                start = cell(i, -1 if l == 2 else 0)
                put(ring, base + (l == 1), get(wide, start, n_cols + 1), 2)
            base, j = (at.right, n_cols) if l == 1 else (at.left, -(l // 2))
            start = cell(1 if k == 0 else 0, j)
            put(ring, base + (k != 1), get(wide, start, n_rows, step), 2)
            total = total + dot(get(ring, 0, at.ring_size).astype(bf16), up_w[k, l])
    put(ring, 0, jnp.zeros((at.ring_size, channels), f32))
    for base, message in ((at.top, upper), (at.bottom, lower)):
        put(ring, base + 1, message[at.row_skip : at.row_skip + cols, :])
        put(ring, base, corner(message, SKIP[0]))
        put(ring, base + cols + 1, corner(message, SKIP[2]))
    put(ring, at.left, left[at.skip : at.skip + rows, :])
    put(ring, at.right, right[at.skip : at.skip + rows, :])
    preact = total + get(ring, 0, at.ring_size)
    sigma = jax.nn.sigmoid(preact)
    value = preact * sigma
    slope = sigma + value * (1.0 - sigma)
    value = value.astype(bf16).astype(f32)
    ring_act[...] = value
    for base, exists in ((at.top, has_upper), (at.bottom, has_lower)):
        strip = value[base : base + cols + 2]
        ring_act[base : base + cols + 2, :] = jnp.where(exists, strip, 0.0)

    def fine(p, q):
        return (p + 2) * stride + MARGIN + q

    for row in range(rows):
        put(wide, fine(row, 0), cot[row].astype(f32))
    for row, message, start, which in (
        (-1, upper, at.row_cot, COT), (-2, upper, at.row_cot_2, COT_2), (rows, lower, at.row_cot, COT),
    ):
        put(wide, fine(row, 0), message[start : start + cols, :])
        for col, one in ((-1, which[0]), (-2, which[1]), (cols, which[2])):
            put(wide, fine(row, col), corner(message, one))
    put(wide, fine(0, -1), left[at.cot : at.cot + rows, :], stride)
    put(wide, fine(0, -2), left[at.cot_2 : at.cot_2 + rows, :], stride)
    put(wide, fine(0, cols), right[at.cot : at.cot + rows, :], stride)
    total = jnp.zeros((at.grad_size, channels), f32)
    for k in range(3):
        for l in range(3):
            put(ring, at.top, get(wide, fine(-k, -l), cols + 1))
            put(ring, at.grad_left, get(wide, fine(1 - k, -l), rows, stride))
            source = get(ring, 0, at.grad_size).astype(bf16)
            total = total + dot_nt(source, conv_w[k, l])
    strip = (total[: cols + 1] * slope[at.top : at.top + cols + 1]).astype(bf16).astype(f32)
    put(ring_grad, at.top, jnp.where(has_upper, strip, 0.0))
    strip = total[at.grad_left : at.grad_left + rows] * slope[at.left : at.left + rows]
    put(ring_grad, at.grad_left, strip.astype(bf16).astype(f32))


def decoded_kernel(act, ring_act, conv_w, decoded, padded, shifted):
    rows, cols, channels = act.shape
    at = Layout(rows // 2, cols // 2)
    stride = cols + 2 * MARGIN
    for row in range(rows):
        put(padded, (row + 1) * stride + MARGIN, act[row].astype(f32))
    for row, base in ((0, at.top), (rows + 1, at.bottom)):
        put(padded, row * stride + MARGIN - 1, ring_act[base : base + cols + 2, :])
    put(padded, stride + MARGIN - 1, ring_act[at.left : at.left + rows, :], stride)
    put(padded, stride + MARGIN + cols, ring_act[at.right : at.right + rows, :], stride)
    for row in range(rows + 2):
        for shift in range(3):
            start = row * stride + MARGIN - 1 + shift
            shifted[shift, row] = get(padded, start, cols).astype(bf16)
    total = jnp.zeros((rows * cols, channels), f32)
    for k in range(3):
        for l in range(3):
            source = shifted[l, pl.ds(k, rows)].reshape(-1, channels)
            total = total + dot(source, conv_w[k, l])
    decoded[...] = total.astype(bf16).reshape(decoded.shape)

def coarse_kernel(phases, ring_grad, up_w, coarse_out, padded, moved):
    n_rows, n_cols, channels = coarse_out.shape
    at = Layout(n_rows, n_cols)
    stride = n_cols + 2 * MARGIN
    for phase, start in ((0, 1), (1, 2), (2, 0)):
        moved[phase, 0] = get(ring_grad, at.top + start, n_cols, 2).astype(bf16)
    for phase in range(2):
        for row in range(n_rows):
            moved[phase, 1 + row] = phases[1, phase, row]
    for row_phase in range(2):
        for row in range(n_rows):
            put(padded, row * stride + MARGIN, phases[row_phase, 1, row].astype(f32))
        put(padded, MARGIN - 1, get(ring_grad, at.grad_left + row_phase, n_rows, 2), stride)
        for row in range(n_rows):
            cells = get(padded, row * stride + MARGIN - 1, n_cols).astype(bf16)
            if row_phase:
                moved[2, 1 + row] = cells
            else:
                moved[3, row] = cells
    total = jnp.zeros((n_rows * n_cols, channels), f32)
    for k in range(3):
        for l in range(3):
            if k == 1:
                if l == 0:
                    source = moved[3, pl.ds(0, n_rows)]
                else:
                    source = phases[0, l - 1, pl.ds(0, n_rows)]
            else:
                source = moved[(2, 0, 1)[l], pl.ds(k // 2, n_rows)]
            total = total + dot_nt(source.reshape(n_rows * n_cols, channels), up_w[k, l])
    coarse_out[...] = total.astype(bf16).reshape(coarse_out.shape)


def halving(count):
    bits = (count // 2).bit_length() - 1
    return [[(step + core) % bits for step in range(bits)] for core in range(2)]


def mask_of(slot, order):
    last = len(order) - 1
    return sum(1 << bit for step, bit in enumerate(order) if slot >> (last - step) & 1)


def edge_kernel(partial, got, edge, got_edge, own, message, extra):
    channels, block = partial.shape[1], got.shape[1]
    zero = jnp.zeros(edge.shape[1:], bf16)
    sides = (edge, got_edge)
    rows_t = jnp.concatenate([side[row] for side in sides for row in range(2)], axis=0).T

    def add_blocks(core):
        for tap in range(9):
            first = 2 + 4 * (2 - tap % 3)
            beside = []
            for side in sides:
                beside += [side[first + 3 - tap // 3], side[first] if tap >= 6 else zero]
            beside = jnp.concatenate(beside, axis=0)
            start = tap * channels
            for mine in range(start // block, -(-(start + channels) // block)):
                if mine % 2 == core:
                    low = max(start, mine * block)
                    high = min(start + channels, (mine + 1) * block)
                    extra[low:high, :] = dot(rows_t[low - start : high - start], beside)

    for core in range(2):
        pl.when(place_of()[0] == core)(lambda core=core: add_blocks(core))
    core_kernel(partial, extra, got, own, message)


def core_kernel(*refs):
    *terms, got, own, message = refs
    slots, half, block = got.shape[0], own.shape[0], got.shape[1]
    core, chip, _, _ = place_of()
    even, odd = halving(2 * slots)
    for slot in range(slots):
        target = chip ^ jnp.where(core == 0, mask_of(slot, even), mask_of(slot, odd))
        mine = pl.multiple_of((2 * target + core) * block, 16)
        total = sum(term[pl.ds(mine, block), :] for term in terms) + got[target].astype(f32)
        if slot < half:
            own[slot] = total
        else:
            message[slot - half] = total.astype(bf16)


def plane_kernel(before, got, own, message):
    half = own.shape[0]
    for slot in range(2 * half):
        total = before[slot] + got[slot].astype(f32)
        if slot < half:
            own[slot] = total
        else:
            message[slot - half] = total.astype(bf16)


def band_kernel(conv, got_conv, up, got_up, own, *refs):
    n_bands, messages, cut = len(refs), refs[:-1], refs[-1]
    conv_total = conv[0] + got_conv[0].astype(f32)
    up_total = up[0] + got_up[0].astype(f32)
    cols = conv_total.shape[1] // n_bands
    for band in range(n_bands):
        cut[band, :, :cols] = conv_total[:, band * cols : (band + 1) * cols]
        cut[band, :, cols:] = up_total[:, band * cols : (band + 1) * cols]
    band = place_of()[2]
    own[...] = cut[band]
    for k, message in enumerate(messages):
        message[...] = cut[band ^ (k + 1)].astype(bf16)


def last_kernel(own, *refs):
    peers, (conv, up) = refs[:-2], refs[-2:]
    total = own[...]
    for peer in peers:
        total = total + peer[...].astype(f32)
    turned = total.T
    conv[...] = turned[: conv.shape[0]]
    up[...] = turned[conv.shape[0] :]


def xor_pairs(count, bits):
    return [(i, i ^ bits) for i in range(count)]


def core_swap(send):
    return lax.ppermute(send, "face", xor_pairs(lax.axis_size("face"), 1))


def core_sum(body, scratch, partial, got, *rest):
    groups, block, channels = got.shape
    shape = (groups // 2, block, channels)
    outs = [sds(shape, f32), sds(shape, bf16)]
    cost = 10**11 if rest else 0
    return kernel_call(body, outs, scratch, cost, partial, got, *rest)


def plane_swap(message, step):
    faces = lax.axis_size("face")
    orders = halving(faces)
    return lax.ppermute(message, "face", [(i, i ^ 2 << orders[i % 2][step]) for i in range(faces)])


def plane_sum(own, got):
    half, block, channels = own.shape
    shape = (half // 2, block, channels)
    return kernel_call(plane_kernel, [sds(shape, f32), sds(shape, bf16)], [], 0, own, got)


def band_sum(conv, got_conv, up, got_up):
    bands = lax.axis_size("band")
    _, block, channels = conv.shape
    cols = channels // bands
    shape = (block, 2 * cols)
    own, *messages = kernel_call(
        band_kernel, [sds(shape, f32)] + [sds(shape, bf16)] * (bands - 1),
        [pltpu.VMEM((bands,) + shape, f32)], 0, conv, got_conv, up, got_up,
    )
    got = [
        lax.ppermute(messages[k - 1], "band", xor_pairs(bands, k))
        for k in (3, 2, 1)
    ]
    return [a.T for a in kernel_call(last_kernel, [sds((cols, block), f32)] * 2, [], 0, own, *got)]


def after(value, *others):
    return lax.optimization_barrier((value, *others))[0]


def swap(first, second, axis, wrap):
    one, two = pairs(lax.axis_size(axis), wrap)
    return lax.ppermute(first, axis, one), lax.ppermute(second, axis, two)


def local(coarse, skip, up_weight, conv_weight, cotangent):
    n_rows, n_cols, channels = coarse.shape
    rows, cols, _ = skip.shape
    at = Layout(n_rows, n_cols)
    faces = lax.axis_size("face")
    groups, block = faces // 2, 9 * channels // faces

    flat = halves(rows * cols, channels)
    message = sds((at.face_size, channels), bf16)
    edges = pltpu.VMEM(message.shape, f32)
    first, second, cotangent, skip, coarse = kernel_call(
        face_message,
        [message, message, sds(cotangent.shape, bf16), sds(skip.shape, bf16), sds(coarse.shape, bf16)],
        [flat, edges, edges, pltpu.SemaphoreType.DMA((3,))],
        0, coarse, skip, cotangent, far=(0, 1, 2),
    )
    first, second = swap(first, second, "face", True)
    conv_weight, grad_centre = kernel_call(
        early_kernel,
        [sds(conv_weight.shape, bf16), sds((rows * cols, channels), f32)],
        [pltpu.VMEM((rows + 2, cols, channels), bf16), pltpu.SemaphoreType.DMA],
        0, cotangent, conv_weight, far=(1,),
    )
    side = sds(message.shape, f32)
    message = sds((at.band_size, channels), bf16)
    edges = pltpu.VMEM(message.shape, f32)
    first, second, left, right = kernel_call(
        band_message, [message, message, side, side], [edges, edges],
        0, coarse, skip, after(cotangent, grad_centre), first, second,
    )
    first, second = swap(first, second, "band", False)

    cells = n_rows * n_cols
    stride = cols + 2 * MARGIN
    padded = halves((rows + 2) * stride, channels)
    shift_shape = (3, rows + 2, cols, channels)
    whole = -(-cells // 256) * 256 // n_cols
    part = sds((9 * channels, channels), f32)
    send = sds((groups, block, channels), bf16)
    blocks = [
        sds(shift_shape, bf16), sds((2, whole + 1, n_cols, channels), bf16),
        sds(skip.shape, bf16), sds((rows * cols, channels), f32), part,
    ]
    *inner, part_conv, send_conv, last_pre, grad_act = kernel_call(
        inner_kernel,
        [
            *blocks, send, sds((cols, channels), f32), sds((rows * cols, channels), f32),
        ],
        [halves(rows * stride, channels), flat],
        0, coarse, skip, cotangent, left, right, up_weight, conv_weight, grad_centre,
    )
    side = sds(message.shape, f32)
    got_conv = core_swap(send_conv)
    edge = sds((14, cols, channels), bf16)
    shifted, near, act, slope, edge, upper, lower = kernel_call(
        act_kernel, [*blocks[:-1], edge, side, side],
        [halves(stride, channels), halves(cols, channels)],
        10**11, first, second, right, up_weight, last_pre, *inner, changed={5 + i: i for i in range(4)},
    )
    phases = kernel_call(
        grad_kernel, [sds((2, 2, whole, n_cols, channels), bf16)], [flat],
        0, shifted, slope, grad_act, conv_weight,
    )[0]
    part_up, send_up = kernel_call(up_kernel, [part, send], [], 0, near, phases)
    own_conv, to_conv = core_sum(
        edge_kernel, [pltpu.VMEM(part.shape, f32)], after(part_conv, send_up), got_conv, edge, core_swap(edge)
    )
    got_conv = plane_swap(to_conv, 0)
    own_up, to_up = core_sum(core_kernel, [], after(part_up, to_conv), core_swap(send_up))
    got_up = plane_swap(to_up, 0)
    ring_act, ring_grad = kernel_call(
        ring_kernel,
        [
            sds((at.ring_size, channels), f32),
            sds((channels // LANES, at.grad_size, LANES), f32),
        ],
        [halves(at.ring_size, channels), halves((rows + 3) * stride, channels)],
        0, coarse, cotangent, after(left, to_up), right, upper, lower, conv_weight, up_weight,
    )
    decoded = kernel_call(
        decoded_kernel, [sds(skip.shape, bf16)], [padded, pltpu.VMEM(shift_shape, bf16)],
        0, act, ring_act, conv_weight,
    )[0]
    own_conv = after(own_conv, decoded)
    steps = (faces // 2).bit_length() - 1
    for step in range(1, steps):
        own_conv, to_conv = plane_sum(own_conv, got_conv)
        got_conv = plane_swap(to_conv, step)
        own_up, to_up = plane_sum(own_up, got_up)
        got_up = plane_swap(to_up, step)
        if step == 1:
            grad_coarse = kernel_call(
                coarse_kernel, [sds(coarse.shape, bf16)],
                [
                    halves(n_rows * (n_cols + 2 * MARGIN), channels),
                    pltpu.VMEM((4, n_rows + 1, n_cols, channels), bf16),
                ],
                0, phases, after(ring_grad, to_up), up_weight,
            )[0]
    grad_conv, grad_up = band_sum(own_conv, got_conv, own_up, got_up)
    return (decoded, grad_coarse, grad_up, grad_conv)


def solution(mesh):
    return jax.shard_map(
        local,
        mesh=mesh,
        in_specs=(
            P("band", "face", None),
            P("band", "face", None),
            P(),
            P(),
            P("band", "face", None),
        ),
        out_specs=(
            P("band", "face", None),
            P("band", "face", None),
            P("face", "band"),
            P("face", "band"),
        ),
        check_vma=False,
    )
```
